128 devices in a mesh: batch: 4 (over y_lo, core), seq: 16 (over z, x), tensor: 2 (over y_hi).
Axes of the slice: x: 4, y: 4 (y_hi: 2, y_lo: 2; y = y_hi * 2 + y_lo), z: 4, core: 2. Of those that a mesh axis runs over, the one named last changes fastest.
Arguments:
- latents: bfloat16 [64, 512, 1024], P(('batch', 'seq'), 'tensor'), may hold values from -6 to 6
- pixels: bfloat16 [64, 4096, 261], P('batch', ('seq', 'tensor')), may hold values from -6 to 6
- crop_bounds: int32 [64, 2], P(('batch', 'seq')), may hold values from 0 to 4096, as said below
- key_mask: int32 [64, 4096], P(('batch', 'seq')), may hold values 0 or 1
- query_gain: bfloat16 [1024], replicated, may hold values from 0.25 to 1.75
- pixel_gain: bfloat16 [261], replicated, may hold values from 0.25 to 1.75
- cross_gain: bfloat16 [1024], replicated, may hold values from 0.25 to 1.75
- attend_gain: bfloat16 [1024], replicated, may hold values from 0.25 to 1.75
- feed_gain: bfloat16 [1024], replicated, may hold values from 0.25 to 1.75
- query_weight: bfloat16 [1024, 1024], replicated, may hold values from -0.1875 to 0.1875
- key_weight: bfloat16 [261, 1024], replicated, may hold values from -0.375 to 0.375
- value_weight: bfloat16 [261, 1024], replicated, may hold values from -0.375 to 0.375
- cross_out: bfloat16 [1024, 1024], replicated, may hold values from -6 to 6
- cross_up: bfloat16 [1024, 1024], replicated, may hold values from -0.1875 to 0.1875
- cross_down: bfloat16 [1024, 1024], replicated, may hold values from -0.1875 to 0.1875
- self_attend: bfloat16 [3, 1024, 1024], P(None, None, 'tensor'), may hold values from -0.1875 to 0.1875
- self_out: bfloat16 [1024, 1024], P('tensor'), may hold values from -2.5 to 2.5
- self_up: bfloat16 [1024, 1024], P(None, 'tensor'), may hold values from -0.1875 to 0.1875
- self_down: bfloat16 [1024, 1024], P('tensor'), may hold values from -0.1875 to 0.1875
- cotangent: bfloat16 [64, 512, 1024], P(('batch', 'seq'), 'tensor'), may hold values from -6 to 6
Outputs:
- latents_out: bfloat16 [64, 512, 1024], P(('batch', 'seq'), 'tensor')
- latents_grad: float32 [64, 512, 1024], P(('batch', 'seq'), 'tensor')
- pixels_grad: float32 [64, 4096, 261], P('batch', ('seq', 'tensor'))
- querygain_grad: float32 [1024], P(('seq', 'tensor'))
- pixelgain_grad: float32 [261], replicated
- crossgain_grad: float32 [1024], P(('seq', 'tensor'))
- attendgain_grad: float32 [1024], P(('seq', 'tensor'))
- feedgain_grad: float32 [1024], P(('seq', 'tensor'))
- queryweight_grad: float32 [1024, 1024], P(('seq', 'tensor'))
- keyweight_grad: float32 [261, 1024], P(None, ('seq', 'tensor'))
- valueweight_grad: float32 [261, 1024], P(None, ('seq', 'tensor'))
- crossout_grad: float32 [1024, 1024], P(('seq', 'tensor'))
- crossup_grad: float32 [1024, 1024], P(('seq', 'tensor'))
- crossdown_grad: float32 [1024, 1024], P(('seq', 'tensor'))
- selfattend_grad: float32 [3, 1024, 1024], P(None, 'seq', 'tensor')
- selfout_grad: float32 [1024, 1024], P('tensor', 'seq')
- selfup_grad: float32 [1024, 1024], P('seq', 'tensor')
- selfdown_grad: float32 [1024, 1024], P('tensor', 'seq')
The draws below stay inside these ranges and needn't reach their ends.
Inputs may be any that keep to these rules, and one draw needn't show every extreme that they name: crop_bounds[i] = (start, count): image i's crop keeps pixel rows start to start + count - 1; count >= 2048 and start + count <= 4096.
All inputs are finite; a program needn't handle non-finite values. No bound on the sum of `key_mask` on one device may be relied on, other than what follows from the above.
Results may differ from the reference program's by a relative error of at most 0.033.
Values may be sent and summed in bfloat16 or wider, within the bound.
A program may use at most 192 MiB of HBM per device.

```python
import math
import jax
import jax.numpy as jnp
from jax import lax

LATENT_WIDTH = 1024
PIXEL_WIDTH = 261
FEED_WIDTH = 1024
HEAD_COUNT = 8
HEAD_WIDTH = 128
LATENT_COUNT = 512
PIXEL_ROWS = 4096
IMAGE_TOTAL = 64


def draw_crop_bounds(key, part):
    key = jax.random.fold_in(key, 11)
    length_key, start_key, choose_key = jax.random.split(key, 3)
    lengths = jax.random.randint(length_key, (IMAGE_TOTAL,), PIXEL_ROWS // 2, PIXEL_ROWS + 1)
    forced_slot = jax.random.randint(choose_key, (), 0, 4)
    full_crop = jnp.arange(IMAGE_TOTAL, dtype=jnp.int32) % 4 == forced_slot
    lengths = jnp.where(full_crop, PIXEL_ROWS, lengths)
    starts = jax.random.randint(start_key, (IMAGE_TOTAL,), 0, PIXEL_ROWS + 1) % (PIXEL_ROWS - lengths + 1)
    return jnp.stack([starts, lengths], axis=1).astype(jnp.int32)


def with_ends(array, own_key, smallest, top_value):
    shape = array.shape
    place = [jax.random.randint(jax.random.fold_in(own_key, axis), (), 0, shape[axis]) for axis in range(len(shape))]
    array = array.at[tuple(place)].set(smallest)
    longest = shape.index(max(shape))
    place[longest] = (place[longest] + 1) % shape[longest]
    return array.at[tuple(place)].set(top_value)


def levels(rng, dims, shards, least, largest):
    def one(axis_at, shards_of):
        draws = jax.random.uniform(jax.random.fold_in(jax.random.fold_in(rng, 6), axis_at), (shards_of,), jnp.float32, least / len(shards), largest / len(shards))
        return jnp.repeat(jnp.exp(draws), dims[axis_at] // shards_of).reshape((-1,) + (1,) * (len(dims) - axis_at - 1))

    factor_of = one(*shards[0])
    for cut in shards[1:]:
        factor_of = factor_of * one(*cut)
    return factor_of


def normal_values(stream_key, extent, width, limit, cuts=(), held_as=jnp.bfloat16):
    entries = jax.random.normal(stream_key, extent, jnp.float32) * width
    if len(cuts) > 0:
        entries = levels(stream_key, extent, cuts, -0.22, 0.18) * entries
    return jnp.clip(entries, min=-limit, max=limit).astype(held_as)


def setup_inputs(seed: int = 0) -> dict:
    streams_of = jax.random.split(jax.random.key(seed), 21)
    return {
        "latents": normal_values(streams_of[0], (IMAGE_TOTAL, LATENT_COUNT, LATENT_WIDTH), 1.0, 6.0, ((0, 64), (1, 2))),
        "pixels": normal_values(streams_of[1], (IMAGE_TOTAL, PIXEL_ROWS, PIXEL_WIDTH), 1.0, 6.0, ((0, 4), (1, 32))),
        "crop_bounds": draw_crop_bounds(jax.random.fold_in(streams_of[20], 71), 0),
        "key_mask": with_ends((jax.random.randint(streams_of[3], (IMAGE_TOTAL, PIXEL_ROWS), 0, 8) < 7).astype(jnp.int32), jax.random.fold_in(streams_of[3], 1), 0, 1),
        "query_gain": jnp.clip(1.0 + 0.15 * jax.random.normal(streams_of[4], (LATENT_WIDTH,), jnp.float32), 0.25, 1.75).astype(jnp.bfloat16),
        "pixel_gain": jnp.clip(1.0 + 0.15 * jax.random.normal(streams_of[5], (PIXEL_WIDTH,), jnp.float32), 0.25, 1.75).astype(jnp.bfloat16),
        "cross_gain": jnp.clip(1.0 + 0.15 * jax.random.normal(streams_of[6], (LATENT_WIDTH,), jnp.float32), 0.25, 1.75).astype(jnp.bfloat16),
        "attend_gain": jnp.clip(1.0 + 0.15 * jax.random.normal(streams_of[7], (LATENT_WIDTH,), jnp.float32), 0.25, 1.75).astype(jnp.bfloat16),
        "feed_gain": jnp.clip(1.0 + 0.15 * jax.random.normal(streams_of[8], (LATENT_WIDTH,), jnp.float32), 0.25, 1.75).astype(jnp.bfloat16),
        "query_weight": normal_values(streams_of[9], (LATENT_WIDTH, LATENT_WIDTH), LATENT_WIDTH ** -0.5, 0.1875),
        "key_weight": normal_values(streams_of[10], (PIXEL_WIDTH, LATENT_WIDTH), PIXEL_WIDTH ** -0.5, 0.375),
        "value_weight": normal_values(streams_of[11], (PIXEL_WIDTH, LATENT_WIDTH), PIXEL_WIDTH ** -0.5, 0.375),
        "cross_out": normal_values(streams_of[12], (LATENT_WIDTH, LATENT_WIDTH), (max(1, 4 * LATENT_WIDTH // PIXEL_ROWS)) ** -0.5, 6.0),
        "cross_up": normal_values(streams_of[13], (LATENT_WIDTH, FEED_WIDTH), LATENT_WIDTH ** -0.5, 0.1875),
        "cross_down": normal_values(streams_of[14], (FEED_WIDTH, LATENT_WIDTH), FEED_WIDTH ** -0.5, 0.1875),
        "self_attend": normal_values(streams_of[15], (3, LATENT_WIDTH, LATENT_WIDTH), LATENT_WIDTH ** -0.5, 0.1875, ((2, 2),)),
        "self_out": normal_values(streams_of[16], (LATENT_WIDTH, LATENT_WIDTH), (max(1, 3 * LATENT_WIDTH // LATENT_COUNT)) ** -0.5, 2.5, ((0, 2),)),
        "self_up": normal_values(streams_of[17], (LATENT_WIDTH, FEED_WIDTH), LATENT_WIDTH ** -0.5, 0.1875, ((1, 2),)),
        "self_down": normal_values(streams_of[18], (FEED_WIDTH, LATENT_WIDTH), FEED_WIDTH ** -0.5, 0.1875, ((0, 2),)),
        "cotangent": normal_values(streams_of[19], (IMAGE_TOTAL, LATENT_COUNT, LATENT_WIDTH), 1.0, 6.0, ((0, 64), (1, 2))),
    }


@jax.custom_vjp
def low(v):
    return lax.optimization_barrier(v.astype(jnp.bfloat16)).astype(jnp.float32)

@jax.custom_vjp
def low_back(v):
    return v

def low_keep(v):
    return (low(v), None)

def low_pass(kept, grad):
    return (grad,)

def back_keep(v):
    return (v, None)

def back_low(kept, grad):
    return (low(grad),)
low.defvjp(low_keep, low_pass)
low_back.defvjp(back_keep, back_low)
EPS = 1e-05
MASKED = -1000000000.0
HIGHEST = lax.Precision.HIGHEST

def round_both(values):
    return low(low_back(values))

def product(operand, another):
    return jnp.dot(operand, another, precision=HIGHEST)

def normed(values, weighting):
    average = lax.optimization_barrier(jnp.mean(values, axis=-1, keepdims=True))
    centered = values - average
    spread = lax.optimization_barrier(jnp.mean(centered * centered, axis=-1, keepdims=True))
    return centered * lax.rsqrt(spread + EPS) * weighting

def feed_forward(values, weighting, up_weight, down_weight):
    hidden = low_back(product(low(normed(values, weighting)), up_weight))
    return low_back(product(low(jax.nn.gelu(hidden)), down_weight))

def self_attention(values, weighting, project, output):
    rows_low = low(normed(values, weighting))
    head_query = round_both(product(rows_low, project[0])).reshape(LATENT_COUNT, HEAD_COUNT, HEAD_WIDTH)
    head_key = round_both(product(rows_low, project[1])).reshape(LATENT_COUNT, HEAD_COUNT, HEAD_WIDTH)
    head_value = round_both(product(rows_low, project[2])).reshape(LATENT_COUNT, HEAD_COUNT, HEAD_WIDTH)
    dotted = jnp.einsum('qhd,khd->hqk', head_query, head_key, precision=HIGHEST) * (1.0 / math.sqrt(HEAD_WIDTH))
    softened = low(jax.nn.softmax(low_back(dotted), axis=-1))
    mixture = round_both(jnp.einsum('hqk,khd->qhd', softened, head_value, precision=HIGHEST))
    return low_back(product(mixture.reshape(LATENT_COUNT, LATENT_WIDTH), output))

def image_forward(params, latent, pixel_rows, kept_rows):
    query_gain, pixel_gain, cross_gain, attend_gain, feed_gain, query_weight, key_weight, value_weight, cross_out, cross_up, cross_down, self_attend, self_out, self_up, self_down = params
    queries = round_both(product(low(normed(latent, query_gain)), query_weight))
    pixel_low = round_both(normed(pixel_rows, pixel_gain))
    keys_all = round_both(product(pixel_low, key_weight))
    values = round_both(product(pixel_low, value_weight))
    dotted = product(queries, keys_all.T) * (1.0 / math.sqrt(LATENT_WIDTH))
    scores = low_back(jnp.where(kept_rows[None, :], dotted, MASKED))
    softened = low(jax.nn.softmax(scores, axis=-1))
    attended = round_both(product(softened, values))
    after_cross = latent + low_back(product(attended, cross_out))
    after_mlp = after_cross + feed_forward(after_cross, cross_gain, cross_up, cross_down)
    after_attend = after_mlp + self_attention(after_mlp, attend_gain, self_attend, self_out)
    return after_attend + feed_forward(after_attend, feed_gain, self_up, self_down)

def reference(latents, pixels, crop_bounds, key_mask, query_gain, pixel_gain, cross_gain, attend_gain, feed_gain, query_weight, key_weight, value_weight, cross_out, cross_up, cross_down, self_attend, self_out, self_up, self_down, cotangent):
    params = tuple((weight_in.astype(jnp.float32) for weight_in in (query_gain, pixel_gain, cross_gain, attend_gain, feed_gain, query_weight, key_weight, value_weight, cross_out, cross_up, cross_down, self_attend, self_out, self_up, self_down)))
    positions = jnp.arange(PIXEL_ROWS, dtype=jnp.int32)

    def one_image(totals, sliced):
        latent, pixel_rows, bounds, key_marks, tangent = sliced
        kept_rows = (positions >= bounds[0]) & (positions < bounds[0] + bounds[1]) & (key_marks == 1)

        def forward(weights_all, latent_in, pixel_in):
            return image_forward(weights_all, latent_in, pixel_in, kept_rows)
        result, pullback = jax.vjp(forward, params, latent.astype(jnp.float32), pixel_rows.astype(jnp.float32))
        gradients, latent_grad, pixel_grad = pullback(tangent.astype(jnp.float32))
        totals = jax.tree.map(lambda earlier, current: earlier + current, totals, gradients)
        return (totals, (result.astype(jnp.bfloat16), latent_grad, pixel_grad))
    start_sums = tuple((jnp.zeros_like(weight_in) for weight_in in params))
    totals, (latents_out, latents_grad, pixels_grad) = lax.scan(one_image, start_sums, (latents, pixels, crop_bounds, key_mask, cotangent))
    return (latents_out, latents_grad, pixels_grad, totals[0], totals[1], totals[2], totals[3], totals[4], totals[5], totals[6], totals[7], totals[8], totals[9], totals[10], totals[11], totals[12], totals[13], totals[14])
```

```python
import functools
import math

import jax
import jax.numpy as jnp
from jax import lax
from jax.experimental import pallas as pl
from jax.experimental.pallas import tpu as pltpu
from jax.sharding import PartitionSpec as P

HEAD_WIDTH = 128
EPS = 1e-05
MASKED = -1000000000.0
MESH = pl.DeviceIdType.MESH
F32 = jnp.float32
B16 = jnp.bfloat16
LANES = 128
PAD = 272
WIDE = 1024
CYCLE = ("XA", "XB", "ZA", "ZB", "T")

SIBLING = [(0, 1), (1, 0), (2, 3), (3, 2)]
TURN = [(l * 4 + c * 2 + t, l * 4 + t * 2 + c) for l in range(2) for c in range(2) for t in range(2)]


def sibling(x):
    return lax.ppermute(x, "batch", SIBLING)


def turned(x):
    return lax.ppermute(x, ("batch", "tensor"), TURN)


def norm_parts(values):
    average = jnp.mean(values, axis=-1, keepdims=True)
    centered = values - average
    spread = jnp.mean(centered * centered, axis=-1, keepdims=True)
    inverse = lax.rsqrt(spread + EPS)
    return centered * inverse, inverse


def norm_back(high, inverse, gain, grad):
    a = grad * gain
    back = (
        a - jnp.mean(a, axis=-1, keepdims=True) - high * jnp.mean(a * high, axis=-1, keepdims=True)
    ) * inverse
    return back, jnp.sum(grad * high, axis=0)


def dot(a, b):
    return jnp.dot(a, b, preferred_element_type=F32)


def dot_t(a, b):
    return lax.dot_general(a, b, (((1,), (1,)), ((), ())), preferred_element_type=F32)


def tdot(a, b):
    return lax.dot_general(a, b, (((0,), (0,)), ((), ())), preferred_element_type=F32)


def flip(p):
    return p + 1 - 2 * lax.rem(p, 2)


def place():
    b, s, t = lax.axis_index("batch"), lax.axis_index("seq"), lax.axis_index("tensor")
    return lax.div(b, 2), lax.rem(b, 2), s, t


def spread_kernel(home_ref, out_ref, send, recv, fsend, frecv, own):
    l, c, s, t = place()
    seq = 16
    base = pl.multiple_of(c * (seq * LANES), LANES)
    far = pl.multiple_of(t * (seq * LANES), LANES)
    sib = (2 * l + 1 - c, s, t)

    barrier = pltpu.get_barrier_semaphore()

    def peer(k):
        return (2 * l + t, lax.rem(s + k, seq), c)

    @pl.when(c != t)
    def _():
        pl.semaphore_signal(barrier, inc=1, device_id=peer(0), device_id_type=MESH)

    for k in range(1, seq):
        pl.semaphore_signal(barrier, inc=1, device_id=peer(k), device_id_type=MESH)
    pl.semaphore_signal(barrier, inc=1, device_id=sib, device_id_type=MESH)

    @pl.when(c != t)
    def _():
        pl.semaphore_wait(barrier, seq + 1)

    @pl.when(c == t)
    def _():
        pl.semaphore_wait(barrier, seq)

    def away(k):
        return pltpu.make_async_remote_copy(
            src_ref=home_ref.at[lax.rem(s + k, seq)],
            dst_ref=out_ref.at[:, pl.ds(pl.multiple_of(far + s * LANES, LANES), LANES)],
            send_sem=send.at[k],
            recv_sem=recv.at[k],
            device_id=peer(k),
            device_id_type=MESH,
        )

    local = pltpu.make_async_copy(
        home_ref.at[s], out_ref.at[:, pl.ds(pl.multiple_of(base + s * LANES, LANES), LANES)], own
    )

    def onward(k):
        at = pl.multiple_of(base + lax.rem(s - k + seq, seq) * LANES, LANES)
        return pltpu.make_async_remote_copy(
            src_ref=out_ref.at[:, pl.ds(at, LANES)],
            dst_ref=out_ref.at[:, pl.ds(at, LANES)],
            send_sem=fsend.at[k],
            recv_sem=frecv.at[k],
            device_id=sib,
            device_id_type=MESH,
        )

    @pl.when(c != t)
    def _():
        away(0).start()

    @pl.when(c == t)
    def _():
        local.start()

    for k in range(1, seq):
        away(k).start()

    @pl.when(c != t)
    def _():
        away(0).wait()

    @pl.when(c == t)
    def _():
        local.wait()

    onward(0).start()
    for k in range(1, seq):
        away(k).wait_recv()
        onward(k).start()
    for k in range(1, seq):
        away(k).wait_send()
    for k in range(seq):
        onward(k).wait()


def spread(home):
    seq = home.shape[0]
    return pl.pallas_call(
        spread_kernel,
        out_shape=jax.ShapeDtypeStruct((PAD, 2 * seq * LANES), B16),
        in_specs=[pl.BlockSpec(memory_space=pl.ANY)],
        out_specs=pl.BlockSpec(memory_space=pl.ANY),
        scratch_shapes=[pltpu.SemaphoreType.DMA((seq,))] * 4 + [pltpu.SemaphoreType.DMA],
        compiler_params=pltpu.CompilerParams(collective_id=0, has_side_effects=True),
        name="spread",
    )(home)


def weight_kernel(xa_at, at_ref, x_ref, y_ref, o_ref):
    r = tdot(x_ref[...], y_ref[...]).astype(o_ref.dtype)
    swap = lax.rem(at_ref[1] + pl.program_id(2), 2) == 1
    first, second = r[:64], r[64:]
    slot = [0, 0, 0, 0]
    o_ref[tuple(slot)] = jnp.where(swap, second, first)
    slot[xa_at] = 1
    o_ref[tuple(slot)] = jnp.where(swap, first, second)


def weight_grad(x, y, order, at):
    bits = [bit for bit in order if bit != "T"]
    rows, width = x.shape[0], y.shape[1]

    def x_map(za, zb, xb, at_ref):
        z, x_ = at_ref[0], at_ref[1]
        z = z + za * (1 - 2 * lax.rem(z, 2))
        z = z + zb * (3 - 2 * z)
        x_ = x_ + xb * (3 - 2 * x_)
        return 0, z * 2 + lax.div(x_, 2)

    def o_map(za, zb, xb, at_ref):
        where = {"ZA": za, "ZB": zb, "XB": xb, "XA": 0}
        return tuple(where[bit] for bit in bits) + (0, 0)

    block = tuple(2 if bit == "XA" else 1 for bit in bits) + (64, width)
    out = pl.pallas_call(
        functools.partial(weight_kernel, bits.index("XA")),
        out_shape=jax.ShapeDtypeStruct((2, 2, 2, 2, 64, width), B16),
        grid_spec=pltpu.PrefetchScalarGridSpec(
            num_scalar_prefetch=1,
            grid=(2, 2, 2),
            in_specs=[
                pl.BlockSpec((rows, LANES), x_map),
                pl.BlockSpec((rows, width), lambda za, zb, xb, at_ref: (0, 0)),
            ],
            out_specs=pl.BlockSpec(block, o_map),
        ),
        compiler_params=pltpu.CompilerParams(vmem_limit_bytes=32 * 1024 * 1024),
        cost_estimate=pl.CostEstimate(
            flops=2 * rows * WIDE * width,
            bytes_accessed=2 * (rows * WIDE + rows * width + WIDE * width),
            transcendentals=0,
        ),
        name="weight_grad",
    )(at, x, y)
    return out.reshape(16, 64, width)


def block_order(order, z, x):
    bits = [bit for bit in order if bit != "T"]
    places = []
    for code in range(16):
        where = {bit: (code >> (3 - j)) & 1 for j, bit in enumerate(bits)}
        zz = flip(z) if where["ZA"] else z
        zz = 3 - zz if where["ZB"] else zz
        xx = flip(x) if where["XA"] else x
        xx = 3 - xx if where["XB"] else xx
        places.append(zz * 4 + xx)
    return jnp.stack(places)


GROUPS = (
    ("mine", ("selfup", "selfdown")),
    ("own", ("selfout", "selfattend0")),
    ("own", ("selfattend1", "selfattend2")),
    ("pair", ("crossdown", "crossup")),
    ("pair", ("crossout", "late")),
)


def order_of(g):
    return CYCLE[g:] + CYCLE[:g]


ORDERS = {name: order_of(g) for g, (_, names) in enumerate(GROUPS) for name in names}


def add_rows(into, here, there, count):
    def step(i, carry):
        into[i] = (here[i].astype(F32) + there[i].astype(F32)).astype(into.dtype)
        return carry

    lax.fori_loop(0, count, step, 0)


def reduce_kernel(plan, sems, *refs):
    l, c, s, t = place()
    z, x = lax.div(s, 4), lax.rem(s, 4)
    seq = 16
    n_items = sum(len(names) for _, names in GROUPS)
    items = refs[:n_items]
    grad_ref, gain_ref = refs[n_items : n_items + 2]
    at = n_items + 2
    outs = refs[at : at + n_items]
    home_ref, gain_out = refs[at + n_items : at + n_items + 2]
    at += n_items + 2
    scratch = list(refs[at:])
    send, recv, local = scratch[:3]
    grad_own, grad_in, gain_buf, gain_in = scratch[3:7]
    scratch = scratch[7:]

    partner = {
        "XA": (2 * l + c, z * 4 + flip(x), t),
        "XB": (2 * l + c, z * 4 + 3 - x, t),
        "ZA": (2 * l + c, flip(z) * 4 + x, t),
        "ZB": (2 * l + c, (3 - z) * 4 + x, t),
        "T": (2 * l + c, s, 1 - t),
        "L": (2 * (1 - l) + c, s, t),
        "C": (2 * l + 1 - c, s, t),
    }

    def peer(k):
        return (2 * l + t, lax.rem(s + k, seq), c)

    barrier = pltpu.get_barrier_semaphore()
    for device in partner.values():
        pl.semaphore_signal(barrier, inc=1, device_id=device, device_id_type=MESH)
    for k in range(1, seq):
        pl.semaphore_signal(barrier, inc=1, device_id=peer(k), device_id_type=MESH)

    @pl.when(c != t)
    def _():
        pl.semaphore_signal(barrier, inc=1, device_id=peer(0), device_id_type=MESH)
        pl.semaphore_wait(barrier, len(partner) + seq)

    @pl.when(c == t)
    def _():
        pl.semaphore_wait(barrier, len(partner) + seq - 1)

    used = [0, 0]
    waits = []

    def remote(src, dst, device):
        i = used[0]
        used[0] += 1
        copy = pltpu.make_async_remote_copy(
            src_ref=src, dst_ref=dst, send_sem=send.at[i], recv_sem=recv.at[i], device_id=device, device_id_type=MESH
        )
        copy.start()
        waits.append(copy)
        return copy

    def here(src, dst):
        i = used[1]
        used[1] += 1
        copy = pltpu.make_async_copy(src, dst, local.at[i])
        copy.start()
        return copy

    half = seq * LANES
    mine = pl.ds(pl.multiple_of(c * half, LANES), half)
    other = pl.ds(pl.multiple_of((1 - c) * half, LANES), half)
    grad_copy = remote(grad_ref.at[:, other], grad_in, partner["C"])
    grad_load = here(grad_ref.at[:, mine], grad_own)

    buffers, starts = [], []
    item = 0
    for g, (kind, names) in enumerate(GROUPS):
        buf, from_sib = scratch[plan[g]["buf"]], scratch[plan[g]["sib"]] if plan[g]["sib"] is not None else None
        buffers.append(buf)
        own = []
        for j, _ in enumerate(names):
            ref = items[item]
            item += 1
            to = pl.ds(j * 512, 512)
            if kind == "pair":
                for h in range(2):
                    rows = pl.ds(32 * h, 32)
                    own.append(here(ref.at[:, rows, pl.ds(pl.multiple_of(512 * c, LANES), 512)], buf.at[h, :, :, to]).wait)
                    own.append(
                        remote(
                            ref.at[:, rows, pl.ds(pl.multiple_of(512 * (1 - c), LANES), 512)],
                            from_sib.at[h, :, :, to],
                            partner["C"],
                        ).wait_recv
                    )
            else:
                keep, give = pl.ds(pl.multiple_of(32 * c, 32), 32), pl.ds(pl.multiple_of(32 * (1 - c), 32), 32)
                for k in range(2 if kind == "mine" else 1):
                    h = c if k == 0 else 1 - c
                    columns = pl.ds(512 * k, 512)
                    own.append(here(ref.at[:, keep, columns], buf.at[h, :, :, to]).wait)
                    target = from_sib if kind == "mine" else buf
                    own.append(remote(ref.at[:, give, columns], target.at[h, :, :, to], partner["C"]).wait_recv)
        starts.append(own)

    grad_load.wait()
    grad_copy.wait_recv()

    def grad_step(i, carry):
        rows = pl.ds(pl.multiple_of(i * 16, 16), 16)
        grad_own[rows, :] = (grad_own[rows, :].astype(F32) + grad_in[rows, :].astype(F32)).astype(B16)
        return carry

    lax.fori_loop(0, PAD // 16, grad_step, 0)

    first = used[0]
    used[0] += seq

    def homeward(k):
        to = lax.rem(s + k, seq)
        return pltpu.make_async_remote_copy(
            src_ref=grad_own.at[:, pl.ds(pl.multiple_of(to * LANES, LANES), LANES)],
            dst_ref=home_ref.at[s],
            send_sem=send.at[first + k],
            recv_sem=recv.at[first + k],
            device_id=peer(k),
            device_id_type=MESH,
        )

    last_local = used[1]
    used[1] += 1
    stay = pltpu.make_async_copy(
        grad_own.at[:, pl.ds(pl.multiple_of(s * LANES, LANES), LANES)], home_ref.at[s], local.at[last_local]
    )

    @pl.when(c != t)
    def _():
        homeward(0).start()

    @pl.when(c == t)
    def _():
        stay.start()

    for k in range(1, seq):
        homeward(k).start()

    gain_buf[0] = gain_ref[...]
    gain_steps = ("XA", "XB", "ZA", "ZB", "T", "L", "C")

    state = []
    for g, (kind, names) in enumerate(GROUPS):
        for wait in starts[g]:
            wait()
        buf = buffers[g]
        if plan[g]["sib"] is not None:
            from_sib = scratch[plan[g]["sib"]]
            for h in range(2):
                add_rows(buf.at[h], buf.at[h], from_sib.at[h], seq)
        state.append({"buf": buf, "split": True, "n": seq})

    def begin(g, k):
        now = state[g]
        order = order_of(g)
        into = scratch[plan[g]["steps"][k]]
        bit = order[k] if k < 5 else "L"
        n = now["n"]
        if bit == "T":
            copy = remote(now["buf"].at[1 - t, pl.ds(0, n)], into, partner["T"])
        elif bit == "L":
            copy = remote(now["buf"].at[pl.ds(0, 1)], into, partner["L"])
        elif now["split"]:
            copy = remote(now["buf"].at[:, pl.ds(n // 2, n // 2)], into, partner[bit])
        else:
            copy = remote(now["buf"].at[pl.ds(n // 2, n // 2)], into, partner[bit])
        now["copy"], now["bit"], now["into"] = copy, bit, into

    def finish(g, k):
        now = state[g]
        now["copy"].wait_recv()
        bit, n, into = now["bit"], now["n"], now["into"]
        if bit == "T":
            after = scratch[plan[g]["after"]]
            add_rows(after, now["buf"].at[t], into, n)
            now["buf"], now["split"] = after, False
        elif bit == "L":
            after = scratch[plan[g]["last"]]
            add_rows(after, now["buf"], into, 1)
            now["buf"] = after
        else:
            n = n // 2
            if now["split"]:
                for h in range(2):
                    add_rows(now["buf"].at[h], now["buf"].at[h], into.at[h], n)
            else:
                add_rows(now["buf"], now["buf"], into, n)
            now["n"] = n

    gain_copy = None
    for k in range(7):
        if k > 0:
            gain_copy.wait_recv()
            gain_buf[k] = gain_buf[k - 1] + gain_in[k - 1]
        gain_copy = remote(gain_buf.at[k], gain_in.at[k], partner[gain_steps[k]])
        for g in range(len(GROUPS)):
            if 0 < k < 7:
                finish(g, k - 1)
            if k < 6:
                begin(g, k)
    gain_copy.wait_recv()
    gain_out[...] = gain_buf[6] + gain_in[6]

    item = 0
    ends = []
    for g, (kind, names) in enumerate(GROUPS):
        final = state[g]["buf"]
        for j, _ in enumerate(names):
            if kind == "pair":
                dst = outs[item].at[:, pl.ds(pl.multiple_of(512 * c, LANES), 512)]
            else:
                dst = outs[item].at[pl.ds(pl.multiple_of(32 * c, 32), 32), :]
            src = final.at[0, :, pl.ds(j * 512, 512)]
            ends.append(remote(src, dst, partner["C"]).wait_recv)
            ends.append(here(src, dst).wait)
            item += 1
    for wait in ends:
        wait()

    @pl.when(c != t)
    def _():
        homeward(0).wait()

    @pl.when(c == t)
    def _():
        stay.wait()

    for k in range(1, seq):
        homeward(k).wait()
    for copy in waits:
        copy.wait_send()
    assert used[0] <= sems[0] and used[1] <= sems[1]


def reduce_all(items, grad, gain):
    scratch, plan = [], []

    def room(*shape):
        scratch.append(pltpu.VMEM(shape, B16))
        return len(scratch) - 1

    for g, (kind, names) in enumerate(GROUPS):
        width = 512 * len(names)
        here = {"buf": room(2, 16, 32, width), "sib": room(2, 16, 32, width) if kind != "own" else None}
        steps, n, split = [], 16, True
        for bit in order_of(g):
            if bit == "T":
                split = False
                steps.append(room(n, 32, width))
                here["after"] = room(n, 32, width)
            else:
                n //= 2
                steps.append(room(2, n, 32, width) if split else room(n, 32, width))
        steps.append(room(1, 32, width))
        here["last"] = room(1, 32, width)
        here["steps"] = steps
        plan.append(here)
    names = [name for _, group in GROUPS for name in group]
    kinds = {name: kind for kind, group in GROUPS for name in group}
    out_shape = [
        jax.ShapeDtypeStruct((32, 1024) if kinds[name] == "pair" else (64, 512), B16) for name in names
    ]
    out_shape += [jax.ShapeDtypeStruct((16, PAD, LANES), B16), jax.ShapeDtypeStruct(gain.shape, F32)]
    sems = (128, 64)
    anywhere = pl.BlockSpec(memory_space=pl.ANY)
    vmem = pl.BlockSpec(memory_space=pltpu.VMEM)
    result = pl.pallas_call(
        functools.partial(reduce_kernel, plan, sems),
        out_shape=out_shape,
        in_specs=[anywhere] * (len(names) + 1) + [vmem],
        out_specs=[anywhere] * (len(names) + 1) + [vmem],
        scratch_shapes=[
            pltpu.SemaphoreType.DMA((sems[0],)),
            pltpu.SemaphoreType.DMA((sems[0],)),
            pltpu.SemaphoreType.DMA((sems[1],)),
            pltpu.VMEM((PAD, 16 * LANES), B16),
            pltpu.VMEM((PAD, 16 * LANES), B16),
            pltpu.VMEM((7,) + gain.shape, F32),
            pltpu.VMEM((7,) + gain.shape, F32),
        ]
        + scratch,
        compiler_params=pltpu.CompilerParams(
            collective_id=1, has_side_effects=True, vmem_limit_bytes=56 * 1024 * 1024
        ),
        name="reduce_all",
    )(*[items[name] for name in names], grad, gain)
    return dict(zip(names, result)), result[-2], result[-1]


def shards(
    latents,
    pixels,
    crop_bounds,
    key_mask,
    query_gain,
    pixel_gain,
    cross_gain,
    attend_gain,
    feed_gain,
    query_weight,
    key_weight,
    value_weight,
    cross_out,
    cross_up,
    cross_down,
    self_attend,
    self_out,
    self_up,
    self_down,
    cotangent,
):
    channels = pixels.shape[2]
    rows = pixels.shape[1]
    pixel_total = key_mask.shape[1]
    latent_half = latents.shape[1]
    heads = self_attend.shape[2] // HEAD_WIDTH
    cross_scale = 1.0 / math.sqrt(latents.shape[2])
    self_scale = 1.0 / math.sqrt(HEAD_WIDTH)
    l, c, s, t = place()
    z, x = lax.div(s, 4), lax.rem(s, 4)
    at = jnp.stack([z, x]).astype(jnp.int32)

    latent_in = turned(latents)[0].astype(F32)
    cot = turned(cotangent)[0]
    attend_w = turned(self_attend)
    out_mine = turned(self_out)
    up_mine = turned(self_up)
    down_mine = turned(self_down)
    out_all = jnp.concatenate([out_mine, sibling(out_mine)], axis=0)
    up_all = jnp.concatenate([up_mine, sibling(up_mine)], axis=1)
    down_all = jnp.concatenate([down_mine, sibling(down_mine)], axis=0)

    pixel_high, pixel_inverse = norm_parts(pixels.astype(F32))
    pixel_low = (pixel_high * pixel_gain.astype(F32)).astype(B16)
    home = jnp.pad(jnp.swapaxes(pixel_low, 1, 2), ((0, 0), (0, PAD - channels), (0, 0)))
    picture = spread(home)

    positions = jnp.arange(pixel_total, dtype=jnp.int32)
    start, count = crop_bounds[0, 0], crop_bounds[0, 1]
    kept = (positions >= start) & (positions < start + count) & (key_mask[0] == 1)
    kept = jnp.swapaxes(kept.reshape(16, 2, rows), 0, 1).reshape(1, pixel_total).astype(F32)
    kept = jnp.where(c == t, kept, sibling(kept))
    any_kept = jnp.max(kept)
    keep_rows = kept > 0.5

    query_high, query_inverse = norm_parts(latent_in)
    query_low = (query_high * query_gain.astype(F32)).astype(B16)
    queries = dot(query_low, query_weight).astype(B16)
    key_wide = jnp.pad(key_weight, ((0, PAD - channels), (0, 0)))
    value_wide = jnp.pad(value_weight, ((0, PAD - channels), (0, 0)))
    asked = (dot_t(queries, key_wide) * cross_scale).astype(B16)
    scores = jnp.where(keep_rows, dot(asked, picture), MASKED)
    top = jnp.max(scores, axis=-1, keepdims=True)
    raised = jnp.exp(scores - top)
    inverse_total = 1.0 / jnp.sum(raised, axis=-1, keepdims=True)
    raised_low = raised.astype(B16)
    mixed_pixels = dot_t(raised_low, picture) * inverse_total
    mixed_low = mixed_pixels.astype(B16)
    attended = dot(mixed_low, value_wide).astype(B16)
    after_cross = latent_in + dot(attended, cross_out)
    cross_high, cross_inverse = norm_parts(after_cross)
    cross_in = (cross_high * cross_gain.astype(F32)).astype(B16)
    cross_hidden = dot(cross_in, cross_up)
    cross_act, cross_act_pull = jax.vjp(jax.nn.gelu, cross_hidden)
    cross_act = cross_act.astype(B16)
    after_mlp = after_cross + dot(cross_act, cross_down)

    attend_high, attend_inverse = norm_parts(after_mlp)
    attend_own = (attend_high * attend_gain.astype(F32)).astype(B16)
    attend_in = jnp.concatenate([attend_own, sibling(attend_own)], axis=0)
    projected = jnp.einsum("ld,cde->cle", attend_in, attend_w, preferred_element_type=F32).astype(B16)
    projected = projected.reshape(3, 2 * latent_half, heads, HEAD_WIDTH)
    self_query, self_key, self_value = projected[0], projected[1], projected[2]
    dotted = jnp.einsum("qhd,khd->hqk", self_query, self_key, preferred_element_type=F32) * self_scale
    self_probs = jax.nn.softmax(dotted, axis=-1)
    self_probs_low = self_probs.astype(B16)
    self_mixed = jnp.einsum("hqk,khd->qhd", self_probs_low, self_value, preferred_element_type=F32)
    self_mixed = self_mixed.astype(B16).reshape(2 * latent_half, heads * HEAD_WIDTH)
    mixed_other = sibling(self_mixed[latent_half:])
    mixed_rows = jnp.concatenate([self_mixed[:latent_half], mixed_other], axis=1)
    after_attend = after_mlp + dot(mixed_rows, out_all)

    feed_high, feed_inverse = norm_parts(after_attend)
    feed_in = (feed_high * feed_gain.astype(F32)).astype(B16)
    feed_hidden = dot(feed_in, up_all)
    feed_act, feed_act_pull = jax.vjp(jax.nn.gelu, feed_hidden)
    feed_act = feed_act.astype(B16)
    latents_out = (after_attend + dot(feed_act, down_all)).astype(B16)

    items = {}

    def item(name, a, b):
        items[name] = weight_grad(a, b, ORDERS[name], at)

    item("selfdown", cot, feed_act)
    (feed_hidden_grad,) = feed_act_pull(dot_t(cot, down_all))
    feed_hidden_low = feed_hidden_grad.astype(B16)
    item("selfup", feed_in, feed_hidden_low)
    back, feedgain = norm_back(
        feed_high, feed_inverse, feed_gain.astype(F32), dot_t(feed_hidden_low, up_all)
    )
    attend_grad = cot.astype(F32) + back
    branch_own = attend_grad.astype(B16)
    branch = jnp.concatenate([branch_own, sibling(branch_own)], axis=0)
    item("selfout", branch, self_mixed)
    mixed_grad = dot_t(branch, out_mine).astype(B16).reshape(2 * latent_half, heads, HEAD_WIDTH)
    probs_grad = jnp.einsum("qhd,khd->hqk", mixed_grad, self_value, preferred_element_type=F32)
    value_grad = jnp.einsum("hqk,qhd->khd", self_probs_low, mixed_grad, preferred_element_type=F32)
    score_grad = (
        self_probs * (probs_grad - jnp.sum(self_probs * probs_grad, axis=-1, keepdims=True))
    ).astype(B16)
    query_grad = jnp.einsum("hqk,khd->qhd", score_grad, self_key, preferred_element_type=F32) * self_scale
    key_grad = jnp.einsum("hqk,qhd->khd", score_grad, self_query, preferred_element_type=F32) * self_scale
    projected_grad = [
        v.astype(B16).reshape(2 * latent_half, heads * HEAD_WIDTH) for v in (query_grad, key_grad, value_grad)
    ]
    rows_grad = 0
    for k in range(3):
        item("selfattend%d" % k, attend_in, projected_grad[k])
        rows_grad = rows_grad + dot_t(projected_grad[k], attend_w[k])
    rows_grad = rows_grad[:latent_half] + sibling(rows_grad[latent_half:].astype(B16)).astype(F32)
    back, attendgain = norm_back(attend_high, attend_inverse, attend_gain.astype(F32), rows_grad)
    mlp_grad = attend_grad + back
    mlp_branch = mlp_grad.astype(B16)
    item("crossdown", cross_act, mlp_branch)
    (cross_hidden_grad,) = cross_act_pull(dot_t(mlp_branch, cross_down))
    cross_hidden_low = cross_hidden_grad.astype(B16)
    item("crossup", cross_in, cross_hidden_low)
    back, crossgain = norm_back(
        cross_high, cross_inverse, cross_gain.astype(F32), dot_t(cross_hidden_low, cross_up)
    )
    cross_grad = mlp_grad + back
    cross_branch = cross_grad.astype(B16)
    item("crossout", attended, cross_branch)
    attended_grad = dot_t(cross_branch, cross_out).astype(B16)
    mixed_pull = dot_t(attended_grad, value_wide).astype(B16)
    row_dot = jnp.sum(mixed_pull.astype(F32) * mixed_pixels, axis=-1, keepdims=True)
    turn = (raised_low.astype(F32) * (dot(mixed_pull, picture) - row_dot)).astype(B16)
    turned_sum = dot_t(turn, picture) * (inverse_total * any_kept)
    asked_grad = (turned_sum * cross_scale).astype(B16)
    asked_part = (asked.astype(F32) * (inverse_total * any_kept)).astype(B16)
    mixed_part = (mixed_pull.astype(F32) * inverse_total).astype(B16)
    picture_grad = (tdot(asked_part, turn) + tdot(mixed_part, raised_low)).astype(B16)
    pixelgain = jnp.sum(
        asked.astype(F32) * turned_sum + mixed_pull.astype(F32) * mixed_pixels, axis=0
    )[:channels] / pixel_gain.astype(F32)
    queries_grad = dot(asked_grad, key_wide).astype(B16)
    back, querygain = norm_back(
        query_high, query_inverse, query_gain.astype(F32), dot_t(queries_grad, query_weight)
    )
    latents_grad = cross_grad + back

    late = [
        weight_grad(query_low, asked_grad, ORDERS["late"], at),
        weight_grad(queries, asked_grad, ORDERS["late"], at),
        weight_grad(attended_grad, mixed_low, ORDERS["late"], at),
    ]
    gains = jnp.stack([querygain, crossgain, attendgain, feedgain], axis=-1).astype(B16).reshape(16, 64, 4)
    gains = jnp.take(gains, block_order(ORDERS["late"], z, x), axis=0)
    fill = jnp.zeros((16, 64, WIDE - 3 * PAD - 4), B16)
    items["late"] = jnp.concatenate(late + [gains, fill], axis=-1)
    gain_block = jnp.zeros((8, 384), F32).at[0, :channels].set(pixelgain)

    sums, picture_home, pixelgain_sum = reduce_all(items, picture_grad, gain_block)

    pixel_grad = jnp.swapaxes(picture_home[:, :channels], 1, 2).astype(F32)
    a = pixel_grad * pixel_gain.astype(F32)
    pixels_grad = (
        a
        - jnp.mean(a, axis=-1, keepdims=True)
        - pixel_high * jnp.mean(a * pixel_high, axis=-1, keepdims=True)
    ) * pixel_inverse

    late_sum = sums["late"]
    queryweight_grad = dot(late_sum[:, :PAD], key_wide)
    keyweight_grad = late_sum[:, PAD : PAD + channels].astype(F32).T
    valueweight_grad = late_sum[:, 2 * PAD : 2 * PAD + channels].astype(F32).T
    gain_sums = late_sum[:, 3 * PAD : 3 * PAD + 4].astype(F32)
    return (
        turned(latents_out)[None],
        turned(latents_grad.astype(B16)).astype(F32)[None],
        pixels_grad,
        gain_sums[:, 0],
        pixelgain_sum[0, :channels],
        gain_sums[:, 1],
        gain_sums[:, 2],
        gain_sums[:, 3],
        queryweight_grad,
        keyweight_grad,
        valueweight_grad,
        sums["crossout"].astype(F32),
        sums["crossup"].astype(F32),
        sums["crossdown"].astype(F32),
        jnp.stack([sums["selfattend%d" % k].astype(F32) for k in range(3)]),
        sums["selfout"].astype(F32).T,
        sums["selfup"].astype(F32),
        sums["selfdown"].astype(F32).T,
    )


def solution(mesh):
    in_specs = (
        P(("batch", "seq"), "tensor", None),
        P("batch", ("seq", "tensor"), None),
        P(("batch", "seq"), None),
        P(("batch", "seq"), None),
        P(),
        P(),
        P(),
        P(),
        P(),
        P(),
        P(),
        P(),
        P(),
        P(),
        P(),
        P(None, None, "tensor"),
        P("tensor", None),
        P(None, "tensor"),
        P("tensor", None),
        P(("batch", "seq"), "tensor", None),
    )
    out_specs = (
        P(("batch", "seq"), "tensor", None),
        P(("batch", "seq"), "tensor", None),
        P("batch", ("seq", "tensor"), None),
        P(("seq", "tensor")),
        P(),
        P(("seq", "tensor")),
        P(("seq", "tensor")),
        P(("seq", "tensor")),
        P(("seq", "tensor"), None),
        P(None, ("seq", "tensor")),
        P(None, ("seq", "tensor")),
        P(("seq", "tensor"), None),
        P(("seq", "tensor"), None),
        P(("seq", "tensor"), None),
        P(None, "seq", "tensor"),
        P("tensor", "seq"),
        P("seq", "tensor"),
        P("tensor", "seq"),
    )
    return jax.shard_map(shards, mesh=mesh, in_specs=in_specs, out_specs=out_specs, check_vma=False)
```

```python
import functools
import math

import jax
import jax.numpy as jnp
from jax import lax
from jax.experimental import pallas as pl
from jax.experimental.pallas import tpu as pltpu
from jax.sharding import PartitionSpec as P

HEAD_WIDTH = 128
EPS = 1e-05
MASKED = -1000000000.0
MESH = pl.DeviceIdType.MESH
F32 = jnp.float32
B16 = jnp.bfloat16
LANES = 128
PAD = 272
WIDE = 1024
CYCLE = ("XA", "XB", "ZA", "ZB", "T")

SIBLING = [(0, 1), (1, 0), (2, 3), (3, 2)]
ACROSS = [
    (l * 4 + c * 2 + t, (1 - l) * 4 + c * 2 + 1 - t) for l in range(2) for c in range(2) for t in range(2)
]


def sibling(x):
    return lax.ppermute(x, "batch", SIBLING)


def across(x):
    return lax.ppermute(x, ("batch", "tensor"), ACROSS)


def norm_parts(values):
    average = jnp.mean(values, axis=-1, keepdims=True)
    centered = values - average
    spread = jnp.mean(centered * centered, axis=-1, keepdims=True)
    inverse = lax.rsqrt(spread + EPS)
    return centered * inverse, inverse


def norm_back(high, inverse, gain, grad):
    a = grad * gain
    back = (
        a - jnp.mean(a, axis=-1, keepdims=True) - high * jnp.mean(a * high, axis=-1, keepdims=True)
    ) * inverse
    return back, jnp.sum(grad * high, axis=0)


def dot(a, b):
    return jnp.dot(a, b, preferred_element_type=F32)


def dot_t(a, b):
    return lax.dot_general(a, b, (((1,), (1,)), ((), ())), preferred_element_type=F32)


def tdot(a, b):
    return lax.dot_general(a, b, (((0,), (0,)), ((), ())), preferred_element_type=F32)


def flip(p):
    return p + 1 - 2 * lax.rem(p, 2)


def place():
    b, s, t = lax.axis_index("batch"), lax.axis_index("seq"), lax.axis_index("tensor")
    return lax.div(b, 2), lax.rem(b, 2), s, t


def spread_kernel(home_ref, kept_ref, lat_ref, cot_ref, out_ref, kept_out, lat_out, cot_out, send, recv, fsend, frecv, own):
    l, c, s, t = place()
    seq = 16
    base = pl.multiple_of(c * (seq * LANES), LANES)
    far = pl.multiple_of(t * (seq * LANES), LANES)
    sib = (2 * l + 1 - c, s, t)

    barrier = pltpu.get_barrier_semaphore()

    def peer(k):
        return (2 * l + t, lax.rem(s + k, seq), c)

    @pl.when(c != t)
    def _():
        pl.semaphore_signal(barrier, inc=1, device_id=peer(0), device_id_type=MESH)

    for k in range(1, seq):
        pl.semaphore_signal(barrier, inc=1, device_id=peer(k), device_id_type=MESH)
    pl.semaphore_signal(barrier, inc=1, device_id=sib, device_id_type=MESH)

    @pl.when(c != t)
    def _():
        pl.semaphore_wait(barrier, seq + 1)

    @pl.when(c == t)
    def _():
        pl.semaphore_wait(barrier, seq)

    def remote(src, dst, i, device):
        return pltpu.make_async_remote_copy(
            src_ref=src, dst_ref=dst, send_sem=send.at[i], recv_sem=recv.at[i], device_id=device, device_id_type=MESH
        )

    def away(k):
        return remote(
            home_ref.at[lax.rem(s + k, seq)],
            out_ref.at[:, pl.ds(pl.multiple_of(far + s * LANES, LANES), LANES)],
            k,
            peer(k),
        )

    turned = [(lat_ref, lat_out), (cot_ref, cot_out)]
    moves = [remote(src, dst, seq + i, peer(0)) for i, (src, dst) in enumerate(turned)]
    stays = [
        pltpu.make_async_copy(src, dst, own.at[1 + i])
        for i, (src, dst) in enumerate(turned + [(kept_ref, kept_out)])
    ]
    kept_move = remote(kept_ref, kept_out, seq + 2, sib)
    local = pltpu.make_async_copy(
        home_ref.at[s], out_ref.at[:, pl.ds(pl.multiple_of(base + s * LANES, LANES), LANES)], own.at[0]
    )

    def onward(k):
        at = pl.multiple_of(base + lax.rem(s - k + seq, seq) * LANES, LANES)
        return pltpu.make_async_remote_copy(
            src_ref=out_ref.at[:, pl.ds(at, LANES)],
            dst_ref=out_ref.at[:, pl.ds(at, LANES)],
            send_sem=fsend.at[k],
            recv_sem=frecv.at[k],
            device_id=sib,
            device_id_type=MESH,
        )

    @pl.when(c != t)
    def _():
        moves[0].start()
        away(0).start()

    @pl.when(c == t)
    def _():
        local.start()
        for copy in stays:
            copy.start()
        kept_move.start()

    for k in range(1, seq):
        away(k).start()

    @pl.when(c != t)
    def _():
        moves[1].start()
        away(0).wait()

    @pl.when(c == t)
    def _():
        local.wait()

    onward(0).start()
    for k in range(1, seq):
        away(k).wait_recv()
        onward(k).start()
    for k in range(1, seq):
        away(k).wait_send()
    for k in range(seq):
        onward(k).wait()

    @pl.when(c != t)
    def _():
        for copy in moves:
            copy.wait()
        kept_move.wait_recv()

    @pl.when(c == t)
    def _():
        for copy in stays:
            copy.wait()
        kept_move.wait_send()


def spread(home, kept, lat, cot):
    seq = home.shape[0]
    anywhere = pl.BlockSpec(memory_space=pl.ANY)
    return pl.pallas_call(
        spread_kernel,
        out_shape=[
            jax.ShapeDtypeStruct((PAD, 2 * seq * LANES), B16),
            jax.ShapeDtypeStruct(kept.shape, kept.dtype),
            jax.ShapeDtypeStruct(lat.shape, lat.dtype),
            jax.ShapeDtypeStruct(cot.shape, cot.dtype),
        ],
        in_specs=[anywhere] * 4,
        out_specs=[anywhere] * 4,
        scratch_shapes=[
            pltpu.SemaphoreType.DMA((seq + 3,)),
            pltpu.SemaphoreType.DMA((seq + 3,)),
            pltpu.SemaphoreType.DMA((seq,)),
            pltpu.SemaphoreType.DMA((seq,)),
            pltpu.SemaphoreType.DMA((4,)),
        ],
        compiler_params=pltpu.CompilerParams(collective_id=0, has_side_effects=True),
        name="spread",
    )(home, kept, lat, cot)


GROUPS = (
    ("heads", (("selfdown", (("cot", "feed_act"),)), ("selfup", (("feed_in", "feed_back"),)))),
    ("heads", (("selfout", (("branch", "mixed"),)), ("selfattend0", (("attend_in", "back0"),)))),
    ("heads", (("selfattend1", (("attend_in", "back1"),)), ("selfattend2", (("attend_in", "back2"),)))),
    ("rows", (("crossdown", (("cross_act", "mlp_branch"),)), ("crossup", (("cross_in", "cross_back"),)))),
    ("rows", (("crossout", (("attended", "cross_branch"),)), ("late", (("late_x", "late_y"), ("attended_grad", "mixed_pixels"))))),
)
OPERANDS = {
    "cot": "rows",
    "feed_act": "quarter",
    "feed_in": "rows",
    "feed_back": "quarter",
    "branch": "whole",
    "mixed": "whole",
    "attend_in": "whole",
    "back0": "whole",
    "back1": "whole",
    "back2": "whole",
    "cross_act": "rows",
    "mlp_branch": "half",
    "cross_in": "rows",
    "cross_back": "half",
    "attended": "rows",
    "cross_branch": "half",
    "late_x": "given",
    "late_y": "rows",
    "attended_grad": "rows",
    "mixed_pixels": "given",
}
INPUTS = [part for name, how in OPERANDS.items() for part in ((name, name + "_give") if how == "given" else (name,))]
ITEMS = [name for _, group in GROUPS for name, _ in group]
Y_OPERANDS = {y for _, group in GROUPS for _, pairs in group for _, y in pairs}


def order_of(g):
    return CYCLE[g:] + CYCLE[:g]


def add_rows(into, here, there, count):
    def step(i, carry):
        into[i] = (here[i].astype(F32) + there[i].astype(F32)).astype(into.dtype)
        return carry

    lax.fori_loop(0, count, step, 0)


def reduce_kernel(plan, sems, *refs):
    l, c, s, t = place()
    z, x = lax.div(s, 4), lax.rem(s, 4)
    seq = 16
    refs = list(refs)

    def take(n):
        part = refs[:n]
        del refs[:n]
        return part

    given = dict(zip(INPUTS, take(len(INPUTS))))
    grad_ref, gain_ref, lat_ref, latgrad_ref = take(4)
    outs = dict(zip(ITEMS, take(len(ITEMS))))
    home_ref, gain_out, lat_home, latgrad_home = take(4)
    send, recv, local = take(3)
    grad_own, grad_in, gain_buf, gain_in = take(4)
    held = dict(zip(OPERANDS, take(len(OPERANDS))))
    scratch = refs

    partner = {
        "XA": (2 * l + c, z * 4 + flip(x), t),
        "XB": (2 * l + c, z * 4 + 3 - x, t),
        "ZA": (2 * l + c, flip(z) * 4 + x, t),
        "ZB": (2 * l + c, (3 - z) * 4 + x, t),
        "T": (2 * l + c, s, 1 - t),
        "L": (2 * (1 - l) + c, s, t),
        "C": (2 * l + 1 - c, s, t),
    }

    def peer(k):
        return (2 * l + t, lax.rem(s + k, seq), c)

    barrier = pltpu.get_barrier_semaphore()
    for device in partner.values():
        pl.semaphore_signal(barrier, inc=1, device_id=device, device_id_type=MESH)
    for k in range(1, seq):
        pl.semaphore_signal(barrier, inc=1, device_id=peer(k), device_id_type=MESH)

    @pl.when(c != t)
    def _():
        pl.semaphore_signal(barrier, inc=1, device_id=peer(0), device_id_type=MESH)
        pl.semaphore_wait(barrier, len(partner) + seq)

    @pl.when(c == t)
    def _():
        pl.semaphore_wait(barrier, len(partner) + seq - 1)

    used = [0, 0]
    waits = []

    def remote_of(src, dst, device):
        i = used[0]
        used[0] += 1
        return pltpu.make_async_remote_copy(
            src_ref=src, dst_ref=dst, send_sem=send.at[i], recv_sem=recv.at[i], device_id=device, device_id_type=MESH
        )

    def remote(src, dst, device):
        copy = remote_of(src, dst, device)
        copy.start()
        waits.append(copy)
        return copy

    def here_of(src, dst):
        i = used[1]
        used[1] += 1
        return pltpu.make_async_copy(src, dst, local.at[i])

    def here(src, dst):
        copy = here_of(src, dst)
        copy.start()
        return copy

    half = seq * LANES
    mine = pl.ds(pl.multiple_of(c * half, LANES), half)
    other = pl.ds(pl.multiple_of((1 - c) * half, LANES), half)
    grad_copy = remote(grad_ref.at[:, other], grad_in, partner["C"])
    grad_load = here(grad_ref.at[:, mine], grad_own)

    ready = {}
    top, low = pl.ds(0, 256), pl.ds(256, 256)
    for name, how in OPERANDS.items():
        ref, to = given[name], held[name]
        if how == "whole":
            ready[name] = [here(ref, to).wait]
        elif how in ("rows", "given"):
            give = given[name + "_give"] if how == "given" else ref
            ready[name] = [here(ref, to.at[top]).wait, remote(give, to.at[low], partner["C"]).wait_recv]
        elif how == "half":
            keep = pl.ds(pl.multiple_of(512 * c, LANES), 512)
            give = pl.ds(pl.multiple_of(512 * (1 - c), LANES), 512)
            ready[name] = [
                here(ref.at[:, keep], to.at[top]).wait,
                remote(ref.at[:, give], to.at[low], partner["C"]).wait_recv,
            ]
        else:
            keep = pl.ds(pl.multiple_of(256 * c, LANES), 256)
            give = pl.ds(pl.multiple_of(256 * (1 - c), LANES), 256)
            left, right = pl.ds(0, 256), pl.ds(256, 256)
            ready[name] = [
                here(ref.at[:, keep], to.at[top, left]).wait,
                here(ref.at[:, pl.ds(512, 256)], to.at[top, right]).wait,
                remote(ref.at[:, give], to.at[low, left], partner["C"]).wait_recv,
                remote(ref.at[:, pl.ds(768, 256)], to.at[low, right], partner["C"]).wait_recv,
            ]

    turned = [(lat_ref, lat_home), (latgrad_ref, latgrad_home)]
    moves = [remote_of(src, dst, peer(0)) for src, dst in turned]
    stays = [here_of(src, dst) for src, dst in turned]

    def product(g, j, pairs):
        kind = GROUPS[g][0]
        buf = scratch[plan[g]["buf"]]
        bits = [bit for bit in order_of(g) if bit != "T"]
        weight = {bit: 8 >> k for k, bit in enumerate(bits)}
        for a, b in pairs:
            for name in (a, b):
                for wait in ready.pop(name, ()):
                    wait()

        def step(i, carry):
            za, zb, xb = lax.div(i, 4), lax.rem(lax.div(i, 2), 2), lax.rem(i, 2)
            zz = z + za * (1 - 2 * lax.rem(z, 2))
            zz = zz + zb * (3 - 2 * zz)
            xx = x + xb * (3 - 2 * x)
            columns = pl.ds(pl.multiple_of((zz * 2 + lax.div(xx, 2)) * LANES, LANES), LANES)
            odd = lax.rem(xx, 2)
            r = tdot(held[pairs[0][0]][:, columns], held[pairs[0][1]][...])
            for a, b in pairs[1:]:
                r = r + tdot(held[a][:, columns], held[b][...])
            r = r.astype(B16)
            base = za * weight["ZA"] + zb * weight["ZB"] + xb * weight["XB"]
            for part, xa in ((r[:64], odd), (r[64:], 1 - odd)):
                idx = base + xa * weight["XA"]
                if kind == "heads":
                    to = pl.ds(j * 256, 256)
                    buf[t, idx, :, to] = part[:, :256]
                    buf[1 - t, idx, :, to] = part[:, 256:]
                else:
                    to = pl.ds(j * 512, 512)
                    buf[0, idx, :, to] = part[:32]
                    buf[1, idx, :, to] = part[32:]
            return carry

        lax.fori_loop(0, 8, step, 0)

    state = []

    def begin(g, k):
        now = state[g]
        order = order_of(g)
        into = scratch[plan[g]["steps"][k]]
        bit = order[k] if k < 5 else "L"
        n = now["n"]
        if bit == "T":
            copy = remote(now["buf"].at[1 - t, pl.ds(0, n)], into, partner["T"])
        elif bit == "L":
            copy = remote(now["buf"].at[pl.ds(0, 1)], into, partner["L"])
        elif now["split"]:
            copy = remote(now["buf"].at[:, pl.ds(n // 2, n // 2)], into, partner[bit])
        else:
            copy = remote(now["buf"].at[pl.ds(n // 2, n // 2)], into, partner[bit])
        now["copy"], now["bit"], now["into"] = copy, bit, into

    def finish(g, k):
        now = state[g]
        now["copy"].wait_recv()
        bit, n, into = now["bit"], now["n"], now["into"]
        if bit == "T":
            after = scratch[plan[g]["after"]]
            add_rows(after, now["buf"].at[t], into, n)
            now["buf"], now["split"] = after, False
        elif bit == "L":
            after = scratch[plan[g]["last"]]
            add_rows(after, now["buf"], into, 1)
            now["buf"] = after
        else:
            n = n // 2
            if now["split"]:
                for h in range(2):
                    add_rows(now["buf"].at[h], now["buf"].at[h], into.at[h], n)
            else:
                add_rows(now["buf"], now["buf"], into, n)
            now["n"] = n

    first, last_local = used[0], used[1]
    used[0] += seq
    used[1] += 1

    def homeward(k):
        to = lax.rem(s + k, seq)
        return pltpu.make_async_remote_copy(
            src_ref=grad_own.at[:, pl.ds(pl.multiple_of(to * LANES, LANES), LANES)],
            dst_ref=home_ref.at[s],
            send_sem=send.at[first + k],
            recv_sem=recv.at[first + k],
            device_id=peer(k),
            device_id_type=MESH,
        )

    stay = pltpu.make_async_copy(
        grad_own.at[:, pl.ds(pl.multiple_of(s * LANES, LANES), LANES)], home_ref.at[s], local.at[last_local]
    )

    def pixels_home():
        grad_load.wait()
        grad_copy.wait_recv()

        def grad_step(i, carry):
            rows = pl.ds(pl.multiple_of(i * 16, 16), 16)
            grad_own[rows, :] = (grad_own[rows, :].astype(F32) + grad_in[rows, :].astype(F32)).astype(B16)
            return carry

        lax.fori_loop(0, PAD // 16, grad_step, 0)

        @pl.when(c != t)
        def _():
            for copy in moves:
                copy.start()
            homeward(0).start()

        @pl.when(c == t)
        def _():
            for copy in stays:
                copy.start()
            stay.start()

        for k in range(1, seq):
            homeward(k).start()

    for g, (kind, group) in enumerate(GROUPS):
        state.append({"buf": scratch[plan[g]["buf"]], "split": True, "n": seq})
        for j, (name, pairs) in enumerate(group):
            product(g, j, pairs)
        begin(g, 0)
        if g == 0:
            pixels_home()

    gain_buf[0] = gain_ref[...]
    gain_steps = ("XA", "XB", "ZA", "ZB", "T", "L", "C")
    gain_copy = None
    for k in range(7):
        if k > 0:
            gain_copy.wait_recv()
            gain_buf[k] = gain_buf[k - 1] + gain_in[k - 1]
        gain_copy = remote(gain_buf.at[k], gain_in.at[k], partner[gain_steps[k]])
        for g in range(len(GROUPS)):
            if 0 < k < 7:
                finish(g, k - 1)
            if 0 < k < 6:
                begin(g, k)
    gain_copy.wait_recv()
    gain_out[...] = gain_buf[6] + gain_in[6]

    ends = []
    for g, (kind, group) in enumerate(GROUPS):
        final = state[g]["buf"]
        for j, (name, _) in enumerate(group):
            width = 256 if kind == "heads" else 512
            dst = outs[name].at[:, pl.ds(pl.multiple_of(width * c, LANES), width)]
            src = final.at[0, :, pl.ds(j * width, width)]
            ends.append(remote(src, dst, partner["C"]).wait_recv)
            ends.append(here(src, dst).wait)
    for wait in ends:
        wait()

    @pl.when(c != t)
    def _():
        for copy in moves:
            copy.wait()
        homeward(0).wait()

    @pl.when(c == t)
    def _():
        for copy in stays:
            copy.wait()
        stay.wait()

    for k in range(1, seq):
        homeward(k).wait()
    for copy in waits:
        copy.wait_send()
    assert used[0] <= sems[0] and used[1] <= sems[1]


def reduce_all(given, grad, gain, lat, latgrad):
    scratch, plan = [], []

    def room(*shape):
        scratch.append(pltpu.VMEM(shape, B16))
        return len(scratch) - 1

    for g, (kind, group) in enumerate(GROUPS):
        rows, width = (64, 256 * len(group)) if kind == "heads" else (32, 512 * len(group))
        plan_g = {"buf": room(2, 16, rows, width)}
        steps, n, split = [], 16, True
        for bit in order_of(g):
            if bit == "T":
                split = False
                steps.append(room(n, rows, width))
                plan_g["after"] = room(n, rows, width)
            else:
                n //= 2
                steps.append(room(2, n, rows, width) if split else room(n, rows, width))
        steps.append(room(1, rows, width))
        plan_g["last"] = room(1, rows, width)
        plan_g["steps"] = steps
        plan.append(plan_g)
    kinds = {name: kind for kind, group in GROUPS for name, _ in group}
    out_shape = [jax.ShapeDtypeStruct((32, 1024) if kinds[name] == "rows" else (64, 512), B16) for name in ITEMS]
    out_shape += [
        jax.ShapeDtypeStruct((16, PAD, LANES), B16),
        jax.ShapeDtypeStruct(gain.shape, F32),
        jax.ShapeDtypeStruct(lat.shape, lat.dtype),
        jax.ShapeDtypeStruct(latgrad.shape, latgrad.dtype),
    ]
    sems = (128, 64)
    anywhere = pl.BlockSpec(memory_space=pl.ANY)
    vmem = pl.BlockSpec(memory_space=pltpu.VMEM)
    result = pl.pallas_call(
        functools.partial(reduce_kernel, plan, sems),
        out_shape=out_shape,
        in_specs=[anywhere] * (len(INPUTS) + 1) + [vmem] + [anywhere] * 2,
        out_specs=[anywhere] * (len(ITEMS) + 1) + [vmem] + [anywhere] * 2,
        scratch_shapes=[
            pltpu.SemaphoreType.DMA((sems[0],)),
            pltpu.SemaphoreType.DMA((sems[0],)),
            pltpu.SemaphoreType.DMA((sems[1],)),
            pltpu.VMEM((PAD, 16 * LANES), B16),
            pltpu.VMEM((PAD, 16 * LANES), B16),
            pltpu.VMEM((7,) + gain.shape, F32),
            pltpu.VMEM((7,) + gain.shape, F32),
        ]
        + [pltpu.VMEM((512, 512 if name in Y_OPERANDS else 1024), B16) for name in OPERANDS]
        + scratch,
        compiler_params=pltpu.CompilerParams(
            collective_id=1, has_side_effects=True, vmem_limit_bytes=60 * 1024 * 1024
        ),
        name="reduce_all",
    )(*[given[name] for name in INPUTS], grad, gain, lat, latgrad)
    return dict(zip(ITEMS, result)), *result[len(ITEMS) :]


def shards(
    latents,
    pixels,
    crop_bounds,
    key_mask,
    query_gain,
    pixel_gain,
    cross_gain,
    attend_gain,
    feed_gain,
    query_weight,
    key_weight,
    value_weight,
    cross_out,
    cross_up,
    cross_down,
    self_attend,
    self_out,
    self_up,
    self_down,
    cotangent,
):
    channels = pixels.shape[2]
    rows = pixels.shape[1]
    pixel_total = key_mask.shape[1]
    latent_half = latents.shape[1]
    heads = self_attend.shape[2] // HEAD_WIDTH
    cross_scale = 1.0 / math.sqrt(latents.shape[2])
    self_scale = 1.0 / math.sqrt(HEAD_WIDTH)
    l, c, s, t = place()

    def cut(v, k, n, axis):
        return lax.dynamic_slice_in_dim(v, k * n, n, axis)

    attend_own = cut(self_attend, c, 256, 2)
    attend_w = jnp.concatenate([attend_own, across(attend_own)], axis=2)
    out_far = across(cut(self_out, c, 256, 0))
    out_mine = jnp.concatenate([cut(self_out, c, 256, 0), out_far], axis=0)
    out_all = jnp.concatenate([out_mine, cut(self_out, 1 - c, 256, 0), sibling(out_far)], axis=0)
    up_far = across(cut(self_up, c, 256, 1))
    up_all = jnp.concatenate([self_up, up_far, sibling(up_far)], axis=1)
    down_far = across(cut(self_down, c, 256, 0))
    down_all = jnp.concatenate([self_down, down_far, sibling(down_far)], axis=0)

    pixel_high, pixel_inverse = norm_parts(pixels.astype(F32))
    pixel_low = (pixel_high * pixel_gain.astype(F32)).astype(B16)
    home = jnp.pad(jnp.swapaxes(pixel_low, 1, 2), ((0, 0), (0, PAD - channels), (0, 0)))
    positions = jnp.arange(pixel_total, dtype=jnp.int32)
    start, count = crop_bounds[0, 0], crop_bounds[0, 1]
    kept = (positions >= start) & (positions < start + count) & (key_mask[0] == 1)
    kept = jnp.swapaxes(kept.reshape(16, 2, rows), 0, 1).reshape(1, pixel_total).astype(F32)
    kept = jnp.broadcast_to(kept, (8, pixel_total))
    picture, kept, lat, cot = spread(home, kept, latents[0], cotangent[0])
    latent_in = lat.astype(F32)
    keep_rows = kept[:1] > 0.5
    any_kept = jnp.max(kept[:1])

    query_high, query_inverse = norm_parts(latent_in)
    query_low = (query_high * query_gain.astype(F32)).astype(B16)
    queries = dot(query_low, query_weight).astype(B16)
    key_wide = jnp.pad(key_weight, ((0, PAD - channels), (0, 0)))
    value_wide = jnp.pad(value_weight, ((0, PAD - channels), (0, 0)))
    asked = (dot_t(queries, key_wide) * cross_scale).astype(B16)
    scores = jnp.where(keep_rows, dot(asked, picture), MASKED)
    top = jnp.max(scores, axis=-1, keepdims=True)
    raised = jnp.exp(scores - top)
    inverse_total = 1.0 / jnp.sum(raised, axis=-1, keepdims=True)
    raised_low = raised.astype(B16)
    mixed_pixels = dot_t(raised_low, picture) * inverse_total
    mixed_low = mixed_pixels.astype(B16)
    attended = dot(mixed_low, value_wide).astype(B16)
    after_cross = latent_in + dot(attended, cross_out)
    cross_high, cross_inverse = norm_parts(after_cross)
    cross_in = (cross_high * cross_gain.astype(F32)).astype(B16)
    cross_hidden = dot(cross_in, cross_up)
    cross_act, cross_act_pull = jax.vjp(jax.nn.gelu, cross_hidden)
    cross_act = cross_act.astype(B16)
    after_mlp = after_cross + dot(cross_act, cross_down)

    attend_high, attend_inverse = norm_parts(after_mlp)
    attend_own = (attend_high * attend_gain.astype(F32)).astype(B16)
    attend_in = jnp.concatenate([attend_own, sibling(attend_own)], axis=0)
    projected = jnp.einsum("ld,cde->cle", attend_in, attend_w, preferred_element_type=F32).astype(B16)
    projected = projected.reshape(3, 2 * latent_half, heads, HEAD_WIDTH)
    self_query, self_key, self_value = projected[0], projected[1], projected[2]
    dotted = jnp.einsum("qhd,khd->hqk", self_query, self_key, preferred_element_type=F32) * self_scale
    self_probs = jax.nn.softmax(dotted, axis=-1)
    self_probs_low = self_probs.astype(B16)
    self_mixed = jnp.einsum("hqk,khd->qhd", self_probs_low, self_value, preferred_element_type=F32)
    self_mixed = self_mixed.astype(B16).reshape(2 * latent_half, heads * HEAD_WIDTH)
    mixed_other = sibling(self_mixed[latent_half:])
    mixed_rows = jnp.concatenate([self_mixed[:latent_half], mixed_other], axis=1)
    after_attend = after_mlp + dot(mixed_rows, out_all)

    feed_high, feed_inverse = norm_parts(after_attend)
    feed_in = (feed_high * feed_gain.astype(F32)).astype(B16)
    feed_hidden = dot(feed_in, up_all)
    feed_act, feed_act_pull = jax.vjp(jax.nn.gelu, feed_hidden)
    feed_act = feed_act.astype(B16)
    latents_out = (after_attend + dot(feed_act, down_all)).astype(B16)

    (feed_hidden_grad,) = feed_act_pull(dot_t(cot, down_all))
    feed_back = feed_hidden_grad.astype(B16)
    back, feedgain = norm_back(feed_high, feed_inverse, feed_gain.astype(F32), dot_t(feed_back, up_all))
    attend_grad = cot.astype(F32) + back
    branch_own = attend_grad.astype(B16)
    branch = jnp.concatenate([branch_own, sibling(branch_own)], axis=0)
    mixed_grad = dot_t(branch, out_mine).astype(B16).reshape(2 * latent_half, heads, HEAD_WIDTH)
    probs_grad = jnp.einsum("qhd,khd->hqk", mixed_grad, self_value, preferred_element_type=F32)
    value_grad = jnp.einsum("hqk,qhd->khd", self_probs_low, mixed_grad, preferred_element_type=F32)
    score_grad = (
        self_probs * (probs_grad - jnp.sum(self_probs * probs_grad, axis=-1, keepdims=True))
    ).astype(B16)
    query_grad = jnp.einsum("hqk,khd->qhd", score_grad, self_key, preferred_element_type=F32) * self_scale
    key_grad = jnp.einsum("hqk,qhd->khd", score_grad, self_query, preferred_element_type=F32) * self_scale
    projected_grad = [
        v.astype(B16).reshape(2 * latent_half, heads * HEAD_WIDTH) for v in (query_grad, key_grad, value_grad)
    ]
    rows_grad = sum(dot_t(projected_grad[k], attend_w[k]) for k in range(3))
    rows_grad = rows_grad[:latent_half] + sibling(rows_grad[latent_half:].astype(B16)).astype(F32)
    back, attendgain = norm_back(attend_high, attend_inverse, attend_gain.astype(F32), rows_grad)
    mlp_grad = attend_grad + back
    mlp_branch = mlp_grad.astype(B16)
    (cross_hidden_grad,) = cross_act_pull(dot_t(mlp_branch, cross_down))
    cross_back = cross_hidden_grad.astype(B16)
    back, crossgain = norm_back(cross_high, cross_inverse, cross_gain.astype(F32), dot_t(cross_back, cross_up))
    cross_grad = mlp_grad + back
    cross_branch = cross_grad.astype(B16)
    attended_grad = dot_t(cross_branch, cross_out).astype(B16)
    mixed_pull = dot_t(attended_grad, value_wide).astype(B16)
    row_dot = jnp.sum(mixed_pull.astype(F32) * mixed_pixels, axis=-1, keepdims=True)
    turn = (raised_low.astype(F32) * (dot(mixed_pull, picture) - row_dot)).astype(B16)
    turned_sum = dot_t(turn, picture) * (inverse_total * any_kept)
    asked_grad = (turned_sum * cross_scale).astype(B16)
    asked_part = (asked.astype(F32) * (inverse_total * any_kept)).astype(B16)
    mixed_part = (mixed_pull.astype(F32) * inverse_total).astype(B16)
    picture_grad = (tdot(asked_part, turn) + tdot(mixed_part, raised_low)).astype(B16)
    pixelgain = jnp.sum(
        asked.astype(F32) * turned_sum + mixed_pull.astype(F32) * mixed_pixels, axis=0
    )[:channels] / pixel_gain.astype(F32)
    queries_grad = dot(asked_grad, key_wide).astype(B16)
    back, querygain = norm_back(
        query_high, query_inverse, query_gain.astype(F32), dot_t(queries_grad, query_weight)
    )
    latents_grad = (cross_grad + back).astype(B16)

    def nothing(width):
        return jnp.zeros((latent_half, width), B16)

    def mixed_columns(core):
        return jnp.concatenate(
            [nothing(PAD), mixed_low[:, 256:PAD], nothing(384 - 2 * PAD + 256), cut(mixed_low, core, LANES, 1)], axis=1
        )

    given = {
        "cot": cot,
        "feed_act": feed_act,
        "feed_in": feed_in,
        "feed_back": feed_back,
        "branch": branch,
        "mixed": self_mixed,
        "attend_in": attend_in,
        "back0": projected_grad[0],
        "back1": projected_grad[1],
        "back2": projected_grad[2],
        "cross_act": cross_act,
        "mlp_branch": mlp_branch,
        "cross_in": cross_in,
        "cross_back": cross_back,
        "attended": attended,
        "cross_branch": cross_branch,
        "late_x": jnp.where(c == 0, query_low, queries),
        "late_x_give": jnp.where(c == 0, queries, query_low),
        "late_y": jnp.pad(asked_grad, ((0, 0), (0, 512 - PAD))),
        "attended_grad": attended_grad,
        "mixed_pixels": mixed_columns(c),
        "mixed_pixels_give": mixed_columns(1 - c),
    }
    gains = jnp.zeros((8, WIDE), F32)
    for k, v in enumerate((querygain, crossgain, attendgain, feedgain)):
        gains = gains.at[k].set(v)
    gains = gains.at[4, :channels].set(pixelgain)

    sums, picture_home, gains, latents_out, latents_grad = reduce_all(
        given, picture_grad, gains, latents_out, latents_grad
    )

    pixel_grad = jnp.swapaxes(picture_home[:, :channels], 1, 2).astype(F32)
    a = pixel_grad * pixel_gain.astype(F32)
    pixels_grad = (
        a
        - jnp.mean(a, axis=-1, keepdims=True)
        - pixel_high * jnp.mean(a * pixel_high, axis=-1, keepdims=True)
    ) * pixel_inverse

    late_sum = sums["late"]
    queryweight_grad = dot(late_sum[:, :PAD], key_wide)
    keyweight_grad = late_sum[:, 512 : 512 + channels].astype(F32).T
    valueweight_grad = jnp.concatenate(
        [late_sum[:, 384:512], late_sum[:, 896:], late_sum[:, PAD : PAD + channels - 256]], axis=1
    ).astype(F32).T
    gain_sums = cut(gains[:4], 2 * s + t, 32, 1)
    return (
        latents_out[None],
        latents_grad.astype(F32)[None],
        pixels_grad,
        gain_sums[0],
        gains[4, :channels],
        gain_sums[1],
        gain_sums[2],
        gain_sums[3],
        queryweight_grad,
        keyweight_grad,
        valueweight_grad,
        sums["crossout"].astype(F32),
        sums["crossup"].astype(F32),
        sums["crossdown"].astype(F32),
        jnp.stack([sums["selfattend%d" % k].astype(F32) for k in range(3)]),
        sums["selfout"].astype(F32).T,
        sums["selfup"].astype(F32),
        sums["selfdown"].astype(F32).T,
    )


def solution(mesh):
    in_specs = (
        P(("batch", "seq"), "tensor", None),
        P("batch", ("seq", "tensor"), None),
        P(("batch", "seq"), None),
        P(("batch", "seq"), None),
        P(),
        P(),
        P(),
        P(),
        P(),
        P(),
        P(),
        P(),
        P(),
        P(),
        P(),
        P(None, None, "tensor"),
        P("tensor", None),
        P(None, "tensor"),
        P("tensor", None),
        P(("batch", "seq"), "tensor", None),
    )
    out_specs = (
        P(("batch", "seq"), "tensor", None),
        P(("batch", "seq"), "tensor", None),
        P("batch", ("seq", "tensor"), None),
        P(("seq", "tensor")),
        P(),
        P(("seq", "tensor")),
        P(("seq", "tensor")),
        P(("seq", "tensor")),
        P(("seq", "tensor"), None),
        P(None, ("seq", "tensor")),
        P(None, ("seq", "tensor")),
        P(("seq", "tensor"), None),
        P(("seq", "tensor"), None),
        P(("seq", "tensor"), None),
        P(None, "seq", "tensor"),
        P("tensor", "seq"),
        P("seq", "tensor"),
        P("tensor", "seq"),
    )
    return jax.shard_map(shards, mesh=mesh, in_specs=in_specs, out_specs=out_specs, check_vma=False)
```

```python
import functools
import math

import jax
import jax.numpy as jnp
from jax import lax
from jax.experimental import pallas as pl
from jax.experimental.pallas import tpu as pltpu
from jax.sharding import PartitionSpec as P

HEAD_WIDTH = 128
EPS = 1e-05
MASKED = -1000000000.0
MESH = pl.DeviceIdType.MESH
F32 = jnp.float32
B16 = jnp.bfloat16
LANES = 128
PAD = 272
WIDE = 1024
CYCLE = ("XA", "XB", "ZA", "ZB", "T")

def norm_parts(values):
    average = jnp.mean(values, axis=-1, keepdims=True)
    centered = values - average
    spread = jnp.mean(centered * centered, axis=-1, keepdims=True)
    inverse = lax.rsqrt(spread + EPS)
    return centered * inverse, inverse


def dot(a, b):
    return jnp.dot(a, b, preferred_element_type=F32)


def dot_t(a, b):
    return lax.dot_general(a, b, (((1,), (1,)), ((), ())), preferred_element_type=F32)


def tdot(a, b):
    return lax.dot_general(a, b, (((0,), (0,)), ((), ())), preferred_element_type=F32)


def flip(p):
    return p + 1 - 2 * lax.rem(p, 2)


def place():
    b, s, t = lax.axis_index("batch"), lax.axis_index("seq"), lax.axis_index("tensor")
    return lax.div(b, 2), lax.rem(b, 2), s, t


MIB = 1024 * 1024
ROWS = 256
GELU_K = math.sqrt(2.0 / math.pi)


def gelu(u):
    return 0.5 * u * (1.0 + jnp.tanh(GELU_K * (u + 0.044715 * u * u * u)))


def gelu_slope(u):
    th = jnp.tanh(GELU_K * (u + 0.044715 * u * u * u))
    return 0.5 * (1.0 + th) + 0.5 * u * (1.0 - th * th) * GELU_K * (1.0 + 3.0 * 0.044715 * u * u)


def loop(n, step):
    lax.fori_loop(0, n, lambda i, carry: (step(i), carry)[1], 0)


def block(i, n):
    return pl.ds(pl.multiple_of(i * n, n), n)


FRONT_HBM = (
    ("home", "kept", "latents", "cotangent", "self_attend", "self_out", "self_up", "self_down")
    + ("query_weight", "key_wide", "value_wide", "cross_out", "cross_up", "cross_down")
)
FRONT_VMEM = ("query_gain", "cross_gain", "attend_gain", "feed_gain")
FRONT_OUT = {
    "cot": ((ROWS, WIDE), B16),
    "feed_in": ((ROWS, WIDE), B16),
    "feed_act": ((ROWS, WIDE), B16),
    "feed_back": ((ROWS, WIDE), B16),
    "branch": ((512, WIDE), B16),
    "mixed": ((512, 512), B16),
    "attend_in": ((512, WIDE), B16),
    "back": ((512, 1536), B16),
    "cross_act": ((ROWS, WIDE), B16),
    "cross_in": ((ROWS, WIDE), B16),
    "attended": ((ROWS, WIDE), B16),
    "late_x": ((ROWS, WIDE), B16),
    "late_x_give": ((ROWS, WIDE), B16),
    "mixed_pixels": ((ROWS, 512), B16),
    "mixed_pixels_give": ((ROWS, 512), B16),
    "rows_grad": ((ROWS, WIDE), F32),
    "rows_grad_give": ((ROWS, WIDE), B16),
    "after_mlp": ((ROWS, WIDE), F32),
    "attend_grad": ((ROWS, WIDE), F32),
    "cross_hidden": ((ROWS, WIDE), F32),
    "after_cross": ((ROWS, WIDE), F32),
    "latents_turned": ((ROWS, WIDE), B16),
    "picture": ((PAD, 4096), B16),
    "raised": ((ROWS, 4096), B16),
    "mixed_f32": ((ROWS, PAD), F32),
    "asked": ((ROWS, PAD), B16),
    "latents_out": ((ROWS, WIDE), B16),
    "inverse_total": ((ROWS, 1), F32),
    "any_kept": ((1, 1), F32),
    "feedgain": ((1, WIDE), F32),
}
FRONT_OUT_VMEM = ("inverse_total", "any_kept", "feedgain")


def front_kernel(names, sems, *refs):
    l, c, s, t = place()
    seq = 16
    r = dict(zip(names, refs))
    send, recv, local = r["send"], r["recv"], r["local"]
    cross_scale = 1.0 / math.sqrt(WIDE)
    self_scale = 1.0 / math.sqrt(HEAD_WIDTH)
    sib = (2 * l + 1 - c, s, t)
    over = (2 * (1 - l) + c, s, 1 - t)
    beside = (2 * (1 - l) + c, s, t)

    def peer(k):
        return (2 * l + t, lax.rem(s + k, seq), c)

    barrier = pltpu.get_barrier_semaphore()
    for device in (sib, over, beside):
        pl.semaphore_signal(barrier, inc=1, device_id=device, device_id_type=MESH)
    for k in range(1, seq):
        pl.semaphore_signal(barrier, inc=1, device_id=peer(k), device_id_type=MESH)

    @pl.when(c != t)
    def _():
        pl.semaphore_signal(barrier, inc=1, device_id=peer(0), device_id_type=MESH)
        pl.semaphore_wait(barrier, 3 + seq)

    @pl.when(c == t)
    def _():
        pl.semaphore_wait(barrier, 2 + seq)

    used = [0, 0]
    waits, stores = [], []

    def remote_of(src, dst, device):
        i = used[0]
        used[0] += 1
        return pltpu.make_async_remote_copy(
            src_ref=src, dst_ref=dst, send_sem=send.at[i], recv_sem=recv.at[i], device_id=device, device_id_type=MESH
        )

    def remote(src, dst, device):
        copy = remote_of(src, dst, device)
        copy.start()
        waits.append(copy)
        return copy

    def here_of(src, dst):
        i = used[1]
        used[1] += 1
        return pltpu.make_async_copy(src, dst, local.at[i])

    def here(src, dst):
        copy = here_of(src, dst)
        copy.start()
        return copy

    def store(name, src):
        stores.append(here(src, r[name]))

    ready = {}

    def await_all(*wanted):
        for name in wanted:
            for wait in ready.pop(name, ()):
                wait()

    base = pl.multiple_of(c * (seq * LANES), LANES)
    far = pl.multiple_of(t * (seq * LANES), LANES)
    picture = r["v_picture"]

    def away_of(k):
        return remote_of(
            r["home"].at[lax.rem(s + k, seq)],
            picture.at[:, pl.ds(pl.multiple_of(far + s * LANES, LANES), LANES)],
            peer(k),
        )

    away = [away_of(k) for k in range(seq)]
    lat_move, cot_move = remote_of(r["latents"], r["v_lat"], peer(0)), remote_of(r["cotangent"], r["v_cot"], peer(0))
    kept_move = remote_of(r["kept"], r["v_kept"], sib)
    lat_stay, cot_stay = here_of(r["latents"], r["v_lat"]), here_of(r["cotangent"], r["v_cot"])
    kept_stay = here_of(r["kept"], r["v_kept"])
    picture_stay = here_of(r["home"].at[s], picture.at[:, pl.ds(pl.multiple_of(base + s * LANES, LANES), LANES)])

    @pl.when(c != t)
    def _():
        lat_move.start()
        away[0].start()

    @pl.when(c == t)
    def _():
        lat_stay.start()
        picture_stay.start()
        kept_stay.start()
        kept_move.start()
        cot_stay.start()

    for k in range(1, seq):
        away[k].start()

    mine, theirs = l, 1 - l

    def rows128(base_row, p):
        return pl.ds(pl.multiple_of(base_row + 128 * p, 128), 128)

    own256 = 256 * c
    own_columns = pl.ds(pl.multiple_of(own256, LANES), 256)
    attend_far, out_w, up_w, down_w = r["w_attend_far"], r["w_out"], r["w_up"], r["w_down"]

    def attend_piece(k, p):
        return attend_far.at[k, block(p, 512)]

    across = {}
    for k in range(3):
        across["attend%d" % k] = remote(
            r["self_attend"].at[k, block(theirs, 512), own_columns], attend_piece(k, theirs), over
        )

    @pl.when(c != t)
    def _():
        cot_move.start()

    across["out"] = remote(r["self_out"].at[rows128(own256, theirs)], out_w.at[rows128(256, theirs)], over)
    across["up"] = remote(
        r["self_up"].at[:, rows128(own256, theirs)], up_w.at[:, rows128(512, theirs)], over
    )
    across["down"] = remote(r["self_down"].at[rows128(own256, theirs)], down_w.at[rows128(512, theirs)], over)

    for name, to in (
        ("query_weight", "w_query"),
        ("key_wide", "w_key"),
        ("value_wide", "w_value"),
        ("cross_out", "w_cross_out"),
        ("cross_up", "w_cross_up"),
        ("cross_down", "w_cross_down"),
    ):
        ready[to] = [here(r[name], r[to]).wait]
    ready["attend_own"] = [here(r["self_attend"].at[:, :, own_columns], r["w_attend_own"]).wait]
    ready["out_own"] = [
        here(r["self_out"].at[pl.ds(pl.multiple_of(own256, LANES), 256)], out_w.at[pl.ds(0, 256)]).wait,
        here(r["self_out"].at[pl.ds(pl.multiple_of(256 - own256, LANES), 256)], out_w.at[pl.ds(512, 256)]).wait,
    ]
    ready["up_own"] = [here(r["self_up"], up_w.at[:, pl.ds(0, 512)]).wait]
    ready["down_own"] = [here(r["self_down"], down_w.at[pl.ds(0, 512)]).wait]

    places = {
        "attend0": lambda p: attend_piece(0, p),
        "attend1": lambda p: attend_piece(1, p),
        "attend2": lambda p: attend_piece(2, p),
        "out": lambda p: out_w.at[rows128(256, p)],
        "up": lambda p: up_w.at[:, rows128(512, p)],
        "down": lambda p: down_w.at[rows128(512, p)],
    }
    sib_places = {
        "out": lambda p: out_w.at[rows128(768, p)],
        "up": lambda p: up_w.at[:, rows128(768, p)],
        "down": lambda p: down_w.at[rows128(768, p)],
    }
    onward = {}

    def pass_on(*wanted):
        for name in wanted:
            across[name].wait_recv()
            at = places[name]
            onward[name] = [remote(at(mine), at(mine), beside)]
            if name in sib_places:
                to = sib_places[name]
                onward[name].append(remote(at(mine), to(mine), sib))

    def pass_rest(*wanted):
        for name in wanted:
            onward[name][0].wait_recv()
            if name in sib_places:
                at, to = places[name], sib_places[name]
                onward[name].append(remote(at(theirs), to(theirs), sib))

    def arrived(*wanted):
        for name in wanted:
            for copy in onward[name][1:]:
                copy.wait_recv()

    def norm_rows(value_ref, gain, out_ref, also=None):
        def step(i):
            rows = block(i, 64)
            v = value_ref[rows, :].astype(F32)
            high, _ = norm_parts(v)
            out_ref[rows, :] = (high * gain).astype(B16)

        loop(ROWS // 64, step)

    def each256(n, step):
        loop(n // 256, lambda i: step(block(i, 256)))

    @pl.when(c != t)
    def _():
        lat_move.wait_recv()

    @pl.when(c == t)
    def _():
        lat_stay.wait()

    store("latents_turned", r["v_lat"])
    query_low, queries = r["v_query_low"], r["v_queries"]
    norm_rows(r["v_lat"], r["query_gain"][...], query_low)
    await_all("w_query", "w_key")

    def query_step(columns):
        queries[:, columns] = dot(query_low[...], r["w_query"][:, columns]).astype(B16)

    each256(WIDE, query_step)
    r["v_asked"][...] = (dot_t(queries[...], r["w_key"][...]) * cross_scale).astype(B16)
    store("asked", r["v_asked"])
    late_a, late_b = here_of(query_low, r["late_x"]), here_of(queries, r["late_x_give"])
    late_c, late_d = here_of(query_low, r["late_x_give"]), here_of(queries, r["late_x"])

    @pl.when(c == 0)
    def _():
        late_a.start()
        late_b.start()

    @pl.when(c == 1)
    def _():
        late_c.start()
        late_d.start()

    def chunk(k):
        return picture.at[:, pl.ds(pl.multiple_of(base + lax.rem(s - k + seq, seq) * LANES, LANES), LANES)]

    @pl.when(c != t)
    def _():
        away[0].wait_recv()
        kept_move.wait_recv()

    @pl.when(c == t)
    def _():
        picture_stay.wait()
        kept_stay.wait()

    passed = [remote(chunk(0), chunk(0), sib)]
    for k in range(1, seq):
        away[k].wait_recv()
        passed.append(remote(chunk(k), chunk(k), sib))
    for copy in passed:
        copy.wait_recv()
    store("picture", picture)

    scores, raised = r["v_scores"], r["v_raised"]
    r["v_top"][...] = jnp.full((ROWS, 1), -3.0e38, F32)
    r["v_total"][...] = jnp.zeros((ROWS, 1), F32)
    r["v_mixed"][...] = jnp.zeros_like(r["v_mixed"])
    r["any_kept"][...] = jnp.max(r["v_kept"][0:1, :], axis=-1, keepdims=True)

    def score_step(i):
        columns = block(i, 512)
        value = dot(r["v_asked"][...], picture[:, columns])
        value = jnp.where(r["v_kept"][0:1, columns] > 0.5, value, MASKED)
        scores[:, columns] = value
        r["v_top"][...] = jnp.maximum(r["v_top"][...], jnp.max(value, axis=-1, keepdims=True))

    loop(8, score_step)

    def raise_step(i):
        columns = block(i, 512)
        value = jnp.exp(scores[:, columns] - r["v_top"][...])
        r["v_total"][...] += jnp.sum(value, axis=-1, keepdims=True)
        low = value.astype(B16)
        raised[:, columns] = low
        r["v_mixed"][...] += dot_t(low, picture[:, columns])

    loop(8, raise_step)
    store("raised", raised)
    inverse_total = 1.0 / r["v_total"][...]
    r["inverse_total"][...] = inverse_total
    mixed = r["v_mixed"][...] * inverse_total
    r["v_mixed"][...] = mixed
    store("mixed_f32", r["v_mixed"])
    r["v_mixed_wide"][...] = jnp.zeros_like(r["v_mixed_wide"])
    r["v_mixed_wide"][:, :PAD] = mixed
    tail = pltpu.roll(r["v_mixed_wide"][:, 256:384], 16, 1).astype(B16)
    for name, core in (("mixed_pixels", c), ("mixed_pixels_give", 1 - c)):
        ref = r["v_" + name]
        ref[:, :256] = jnp.zeros((ROWS, 256), B16)
        ref[:, 256:384] = tail
        ref[:, 384:] = r["v_mixed_wide"][:, pl.ds(pl.multiple_of(LANES * core, LANES), LANES)].astype(B16)
        store(name, ref)
    await_all("w_value", "w_cross_out")
    r["v_attended"][...] = dot(mixed.astype(B16), r["w_value"][...]).astype(B16)
    store("attended", r["v_attended"])

    def out_step(columns):
        r["v_after_cross"][:, columns] = r["v_lat"][:, columns].astype(F32) + dot(
            r["v_attended"][...], r["w_cross_out"][:, columns]
        )

    each256(WIDE, out_step)
    store("after_cross", r["v_after_cross"])
    pass_on("attend0")
    norm_rows(r["v_after_cross"], r["cross_gain"][...], r["v_cross_in"])
    store("cross_in", r["v_cross_in"])
    await_all("w_cross_up", "w_cross_down")

    def up_step(columns):
        hidden = dot(r["v_cross_in"][...], r["w_cross_up"][:, columns])
        r["v_hidden"][:, columns] = hidden
        r["v_cross_act"][:, columns] = gelu(hidden).astype(B16)

    each256(WIDE, up_step)
    store("cross_hidden", r["v_hidden"])
    store("cross_act", r["v_cross_act"])
    pass_on("attend1")

    def down_step(columns):
        r["v_after_mlp"][:, columns] = r["v_after_cross"][:, columns] + dot(
            r["v_cross_act"][...], r["w_cross_down"][:, columns]
        )

    each256(WIDE, down_step)
    store("after_mlp", r["v_after_mlp"])

    attend_in = r["v_attend_in"]
    top, low = pl.ds(0, ROWS), pl.ds(ROWS, ROWS)
    norm_rows(r["v_after_mlp"], r["attend_gain"][...], attend_in)
    attend_copy = remote(attend_in.at[top], attend_in.at[low], sib)
    await_all("attend_own")
    pass_on("attend2")
    attend_copy.wait_recv()
    store("attend_in", attend_in)
    projected, probs = r["v_projected"], r["v_probs"]

    def project(weights, at):
        for k in range(3):
            projected[k, :, pl.ds(at, 256)] = dot(attend_in[...], weights[k]).astype(B16)

    def attend(h):
        columns = block(h, HEAD_WIDTH)
        dotted = dot_t(projected[0, :, columns], projected[1, :, columns]) * self_scale
        value = jnp.exp(dotted - jnp.max(dotted, axis=-1, keepdims=True))
        value = (value * (1.0 / jnp.sum(value, axis=-1, keepdims=True))).astype(B16)
        probs[h] = value
        r["v_self"][:, columns] = dot(value, projected[2, :, columns]).astype(B16)

    project(r["w_attend_own"], 0)
    loop(2, attend)
    pass_rest("attend0", "attend1", "attend2")
    project(attend_far, 256)
    loop(2, lambda i: attend(i + 2))
    store("mixed", r["v_self"])
    self_copy = remote(r["v_self"].at[low], r["v_self_in"], sib)
    pass_on("out", "up")
    await_all("out_own")
    pass_rest("out")
    arrived("out")
    self_copy.wait_recv()

    def attended_step(columns):
        r["v_after_attend"][:, columns] = (
            r["v_after_mlp"][:, columns]
            + dot(r["v_self"][top, :], out_w[pl.ds(0, 512), columns])
            + dot(r["v_self_in"][...], out_w[pl.ds(512, 512), columns])
        )

    each256(WIDE, attended_step)

    norm_rows(r["v_after_attend"], r["feed_gain"][...], r["v_feed_in"])
    store("feed_in", r["v_feed_in"])

    @pl.when(c != t)
    def _():
        cot_move.wait_recv()

    @pl.when(c == t)
    def _():
        cot_stay.wait()

    store("cot", r["v_cot"])
    pass_on("down")
    await_all("up_own", "down_own")

    def feed_step(columns):
        hidden = dot(r["v_feed_in"][...], up_w[:, columns])
        r["v_feed_act"][:, columns] = gelu(hidden).astype(B16)
        pulled = dot_t(r["v_cot"][...], down_w[columns, :])
        r["v_feed_back"][:, columns] = (gelu_slope(hidden) * pulled).astype(B16)

    loop(2, lambda i: feed_step(block(i, 256)))
    pass_rest("up", "down")
    arrived("up", "down")
    loop(2, lambda i: feed_step(block(i + 2, 256)))
    store("feed_act", r["v_feed_act"])
    store("feed_back", r["v_feed_back"])

    def feed_pull(rows):
        r["v_tmp"][:, rows] = dot_t(r["v_feed_back"][...], up_w[rows, :])

    each256(WIDE, feed_pull)
    r["feedgain"][...] = jnp.zeros((1, WIDE), F32)
    branch = r["v_branch"]

    def feed_norm(i):
        rows = block(i, 64)
        high, inverse = norm_parts(r["v_after_attend"][rows, :])
        e = r["v_tmp"][rows, :]
        a = e * r["feed_gain"][...]
        back = (
            a - jnp.mean(a, axis=-1, keepdims=True) - high * jnp.mean(a * high, axis=-1, keepdims=True)
        ) * inverse
        r["feedgain"][...] += jnp.sum(e * high, axis=0, keepdims=True)
        total = r["v_cot"][rows, :].astype(F32) + back
        r["v_attend_grad"][rows, :] = total
        branch[rows, :] = total.astype(B16)

    loop(ROWS // 64, feed_norm)
    branch_copy = remote(branch.at[top], branch.at[low], sib)
    store("attend_grad", r["v_attend_grad"])

    def latents_step(columns):
        r["v_latents_out"][:, columns] = (
            r["v_after_attend"][:, columns] + dot(r["v_feed_act"][...], down_w[:, columns])
        ).astype(B16)

    each256(WIDE, latents_step)
    store("latents_out", r["v_latents_out"])
    branch_copy.wait_recv()
    store("branch", branch)

    def mixed_step(rows):
        r["v_self_grad"][:, rows] = dot_t(branch[...], out_w[rows, :]).astype(B16)

    loop(2, lambda i: mixed_step(block(i, 256)))
    back = r["v_back"]

    def attend_back(h):
        columns = block(h, HEAD_WIDTH)
        grad = r["v_self_grad"][:, columns]
        p = probs[h]
        g = dot_t(grad, projected[2, :, columns])
        p32 = p.astype(F32)
        change = (p32 * (g - jnp.sum(p32 * g, axis=-1, keepdims=True))).astype(B16)
        back[:, pl.ds(pl.multiple_of(h * HEAD_WIDTH, LANES), HEAD_WIDTH)] = (
            dot(change, projected[1, :, columns]) * self_scale
        ).astype(B16)
        back[:, pl.ds(pl.multiple_of(512 + h * HEAD_WIDTH, LANES), HEAD_WIDTH)] = (
            tdot(change, projected[0, :, columns]) * self_scale
        ).astype(B16)
        back[:, pl.ds(pl.multiple_of(1024 + h * HEAD_WIDTH, LANES), HEAD_WIDTH)] = tdot(p, grad).astype(B16)

    loop(4, attend_back)
    store("back", back)

    def rows_step(rows):
        total = 0
        for k in range(3):
            total = total + dot_t(back[:, pl.ds(512 * k, 256)], r["w_attend_own"][k, rows, :])
            total = total + dot_t(back[:, pl.ds(512 * k + 256, 256)], attend_far[k, rows, :])
        r["v_tmp"][:, rows] = total[:ROWS]
        r["v_rows_give"][:, rows] = total[ROWS:].astype(B16)

    each256(WIDE, rows_step)
    store("rows_grad", r["v_tmp"])
    store("rows_grad_give", r["v_rows_give"])

    @pl.when(c != t)
    def _():
        lat_move.wait_send()
        cot_move.wait_send()
        away[0].wait_send()

    @pl.when(c == t)
    def _():
        kept_move.wait_send()

    @pl.when(c == 0)
    def _():
        late_a.wait()
        late_b.wait()

    @pl.when(c == 1)
    def _():
        late_c.wait()
        late_d.wait()

    for k in range(1, seq):
        away[k].wait_send()
    for copy in waits:
        copy.wait_send()
    for copy in stores:
        copy.wait()
    assert not ready, tuple(ready)
    assert used[0] <= sems[0] and used[1] <= sems[1], used


def front(given):
    names, scratch = [], []

    def room(name, shape, dtype=B16):
        names.append(name)
        scratch.append(pltpu.VMEM(shape, dtype))

    sems = (64, 64)
    names += list(FRONT_HBM) + list(FRONT_VMEM) + list(FRONT_OUT)
    for name in ("send", "recv", "local"):
        names.append(name)
        scratch.append(pltpu.SemaphoreType.DMA((sems[1 if name == "local" else 0],)))
    for name in ("query", "cross_out", "cross_up", "cross_down", "out", "up", "down"):
        room("w_" + name, (WIDE, WIDE))
    for name in ("key", "value"):
        room("w_" + name, (PAD, WIDE))
    for name in ("attend_own", "attend_far"):
        room("w_" + name, (3, WIDE, 256))
    room("v_picture", (PAD, 4096))
    room("v_kept", (8, 4096), F32)
    room("v_scores", (ROWS, 4096), F32)
    room("v_raised", (ROWS, 4096))
    for name in ("lat", "cot", "query_low", "queries", "attended", "cross_in", "cross_act", "feed_in", "feed_act"):
        room("v_" + name, (ROWS, WIDE))
    for name in ("feed_back", "latents_out", "rows_give"):
        room("v_" + name, (ROWS, WIDE))
    for name in ("after_cross", "hidden", "after_mlp", "after_attend", "attend_grad", "tmp"):
        room("v_" + name, (ROWS, WIDE), F32)
    for name in ("attend_in", "branch"):
        room("v_" + name, (512, WIDE))
    room("v_projected", (3, 512, 512))
    room("v_probs", (4, 512, 512))
    room("v_self", (512, 512))
    room("v_self_in", (ROWS, 512))
    room("v_self_grad", (512, 512))
    room("v_back", (512, 1536))
    room("v_asked", (ROWS, PAD))
    room("v_top", (ROWS, 1), F32)
    room("v_total", (ROWS, 1), F32)
    room("v_mixed", (ROWS, PAD), F32)
    room("v_mixed_wide", (ROWS, 384), F32)
    room("v_mixed_pixels", (ROWS, 512))
    room("v_mixed_pixels_give", (ROWS, 512))
    anywhere = pl.BlockSpec(memory_space=pl.ANY)
    vmem = pl.BlockSpec(memory_space=pltpu.VMEM)
    result = pl.pallas_call(
        functools.partial(front_kernel, tuple(names), sems),
        out_shape=[jax.ShapeDtypeStruct(*spec) for spec in FRONT_OUT.values()],
        in_specs=[anywhere] * len(FRONT_HBM) + [vmem] * len(FRONT_VMEM),
        out_specs=[vmem if name in FRONT_OUT_VMEM else anywhere for name in FRONT_OUT],
        scratch_shapes=scratch,
        compiler_params=pltpu.CompilerParams(collective_id=0, has_side_effects=True, vmem_limit_bytes=63 * MIB),
        name="front",
    )(*[given[name] for name in FRONT_HBM + FRONT_VMEM])
    return dict(zip(FRONT_OUT, result))


SETS = ("S", "P", "Q")
WIDTHS = {"S": 384, "P": 256, "Q": 256}
DEPTHS = {"S": 64, "P": 32, "Q": 32}
PART_ORDERS = (
    ("XA", "ZA", "XB", "ZB"),
    ("ZA", "XB", "ZB", "XA"),
    ("XB", "ZB", "XA", "ZA"),
    ("ZB", "XA", "ZA", "XB"),
)
X_NAMES = ("cot", "feed_in", "branch", "attend_in", "cross_act", "cross_in", "attended", "late_x")
Y_NAMES = ("feed_act", "feed_back", "mixed", "back", "mixed_pixels")
HBM_INPUTS = (
    ("cot", "feed_in", "feed_act", "feed_back", "branch", "mixed", "attend_in", "back")
    + ("cross_act", "cross_in", "attended", "late_x", "late_x_give", "mixed_pixels", "mixed_pixels_give")
    + ("rows_grad", "rows_grad_give", "after_mlp", "attend_grad", "cross_hidden", "after_cross", "latents")
    + ("cross_down", "cross_up", "cross_out", "query_weight", "key_wide", "value_wide", "picture", "raised")
    + ("mixed_f32", "asked", "latents_out")
)
VMEM_INPUTS = ("inverse_total", "any_kept", "attend_gain", "cross_gain", "query_gain", "pixel_gain", "feedgain")


def back_kernel(names, sems, *refs):
    l, c, s, t = place()
    z, x = lax.div(s, 4), lax.rem(s, 4)
    seq = 16
    r = dict(zip(names, refs))
    send, recv, local = r["send"], r["recv"], r["local"]
    cross_scale = 1.0 / math.sqrt(WIDE)

    partner = {
        "XA": (2 * l + c, z * 4 + flip(x), t),
        "XB": (2 * l + c, z * 4 + 3 - x, t),
        "ZA": (2 * l + c, flip(z) * 4 + x, t),
        "ZB": (2 * l + c, (3 - z) * 4 + x, t),
        "T": (2 * l + c, s, 1 - t),
        "L": (2 * (1 - l) + c, s, t),
        "C": (2 * l + 1 - c, s, t),
    }

    def peer(k):
        return (2 * l + t, lax.rem(s + k, seq), c)

    barrier = pltpu.get_barrier_semaphore()
    for device in partner.values():
        pl.semaphore_signal(barrier, inc=1, device_id=device, device_id_type=MESH)
    for k in range(1, seq):
        pl.semaphore_signal(barrier, inc=1, device_id=peer(k), device_id_type=MESH)

    @pl.when(c != t)
    def _():
        pl.semaphore_signal(barrier, inc=1, device_id=peer(0), device_id_type=MESH)
        pl.semaphore_wait(barrier, len(partner) + seq)

    @pl.when(c == t)
    def _():
        pl.semaphore_wait(barrier, len(partner) + seq - 1)

    used = [0, 0]
    waits = []

    def remote_of(src, dst, device):
        i = used[0]
        used[0] += 1
        return pltpu.make_async_remote_copy(
            src_ref=src, dst_ref=dst, send_sem=send.at[i], recv_sem=recv.at[i], device_id=device, device_id_type=MESH
        )

    def remote(src, dst, device):
        copy = remote_of(src, dst, device)
        copy.start()
        waits.append(copy)
        return copy

    def here_of(src, dst):
        i = used[1]
        used[1] += 1
        return pltpu.make_async_copy(src, dst, local.at[i])

    def here(src, dst):
        copy = here_of(src, dst)
        copy.start()
        return copy

    ready = {}

    def await_all(*wanted):
        for name in wanted:
            for wait in ready.pop(name, ()):
                wait()

    sib = partner["C"]
    top, low = pl.ds(0, ROWS), pl.ds(ROWS, ROWS)
    keep512 = pl.ds(pl.multiple_of(512 * c, LANES), 512)
    give512 = pl.ds(pl.multiple_of(512 * (1 - c), LANES), 512)
    keep256 = pl.ds(pl.multiple_of(256 * c, LANES), 256)
    give256 = pl.ds(pl.multiple_of(256 * (1 - c), LANES), 256)
    left, right = pl.ds(0, 256), pl.ds(256, 256)

    def exchange_rows(name, give=None):
        ref, to = r[name], r["x_" + name]
        give = ref if give is None else r[give]
        ready["x_" + name] = [here(ref, to.at[top]).wait, remote(give, to.at[low], sib).wait_recv]

    def exchange_quarter(name):
        ref, to = r[name], r["y_" + name]
        ready["y_" + name] = [
            here(ref.at[:, keep256], to.at[top, left]).wait,
            here(ref.at[:, pl.ds(512, 256)], to.at[top, right]).wait,
            remote(ref.at[:, give256], to.at[low, left], sib).wait_recv,
            remote(ref.at[:, pl.ds(768, 256)], to.at[low, right], sib).wait_recv,
        ]

    def load(name, to, key=None):
        ready[key or name] = [here(r[name], to).wait]

    ready["rows_grad_sum"] = [remote(r["rows_grad_give"], r["v_rows_in"], sib).wait_recv]
    exchange_rows("cot")
    exchange_quarter("feed_act")
    exchange_rows("feed_in")
    exchange_quarter("feed_back")
    load("branch", r["x_branch"], "x_branch")
    load("mixed", r["y_mixed"], "y_mixed")
    load("attend_in", r["x_attend_in"], "x_attend_in")
    load("back", r["y_back"], "y_back")
    load("rows_grad", r["v_tmp"], "rows_grad")
    load("after_mlp", r["v_norm"], "after_mlp")
    load("attend_grad", r["v_grad"], "attend_grad")
    load("cross_down", r["w_down"], "w_down")
    load("cross_up", r["w_up"], "w_up")
    load("cross_hidden", r["v_hidden"], "cross_hidden")
    exchange_rows("cross_act")
    exchange_rows("cross_in")
    load("value_wide", r["w_value"], "w_value")
    load("picture", r["v_picture"], "picture")
    load("raised", r["v_raised"], "raised")
    load("mixed_f32", r["v_mixed"], "mixed_f32")
    load("asked", r["v_asked"], "asked")
    exchange_rows("attended")
    exchange_rows("late_x", "late_x_give")
    ready["y_mixed_pixels"] = [
        here(r["mixed_pixels"], r["y_mixed_pixels"].at[top]).wait,
        remote(r["mixed_pixels_give"], r["y_mixed_pixels"].at[low], sib).wait_recv,
    ]
    load("key_wide", r["w_key"], "w_key")
    load("latents", r["v_latents"], "latents")

    turned = [("latents_out", "latents_home"), ("v_latgrad", "latgrad_home")]
    moves = [remote_of(r[src], r[dst], peer(0)) for src, dst in turned]
    stays = [here_of(r[src], r[dst]) for src, dst in turned]

    class Part:
        def __init__(self, set_, q):
            self.set, self.q, self.stage, self.n, self.cur = set_, q, -1, seq, r["%s%d_buf" % (set_, q)]
            self.weight = {bit: 8 >> k for k, bit in enumerate(PART_ORDERS[q])}

        def index(self, za, zb, xa, xb):
            w = self.weight
            return za * w["ZA"] + zb * w["ZB"] + xa * w["XA"] + xb * w["XB"]

        def begin(self):
            self.stage += 1
            k, n, key = self.stage, self.n, "%s%d_" % (self.set, self.q)
            if k < 4:
                self.into = r[key + "in%d" % k]
                self.copy = remote(self.cur.at[:, pl.ds(n // 2, n // 2)], self.into, partner[PART_ORDERS[self.q][k]])
            elif k == 4:
                self.into = r[key + "in4"]
                self.copy = remote(self.cur.at[1 - t, 0], self.into, partner["T"])
            elif k == 5:
                self.into = r[key + "in5"]
                self.copy = remote(r[key + "sum4"], self.into, partner["L"])
            else:
                width = WIDTHS[self.set]
                dst = r["out_" + self.set].at[:, pl.ds(pl.multiple_of((4 * c + self.q) * width, LANES), width)]
                self.copy = remote(r[key + "sum5"], dst, partner["C"])
                self.copy_here = here(r[key + "sum5"], dst)

        def finish(self):
            self.copy.wait_recv()
            k, key = self.stage, "%s%d_" % (self.set, self.q)
            if k < 4:
                self.n //= 2
                cur, into = self.cur, self.into
                for h in range(2):

                    def step(i, h=h):
                        cur[h, i] = (cur[h, i].astype(F32) + into[h, i].astype(F32)).astype(B16)

                    if self.n > 1:
                        loop(self.n, step)
                    else:
                        step(0)
            elif k == 4:
                r[key + "sum4"][...] = (self.cur[t, 0].astype(F32) + self.into[...].astype(F32)).astype(B16)
            elif k == 5:
                r[key + "sum5"][...] = (r[key + "sum4"][...].astype(F32) + self.into[...].astype(F32)).astype(B16)
            else:
                self.copy_here.wait()

        def advance(self):
            self.finish()
            if self.stage < 6:
                self.begin()

    parts = {(set_, q): Part(set_, q) for set_ in SETS for q in range(4)}

    def advance(set_):
        for q in range(4):
            parts[set_, q].advance()

    def product(x_ref, y_ref, width, set_, pieces, add=False):
        block = 512 if width <= 512 else 256
        per = block // 256

        def step(i):
            columns = pl.ds(pl.multiple_of(i * block, block), block)
            whole = tdot(x_ref[:, columns], y_ref[...])
            for a in range(per):
                zz = i * per + a
                zb = lax.rem(lax.div(z, 2) + lax.div(zz, 2), 2)
                za = lax.rem(lax.rem(z, 2) + lax.rem(zz, 2) + zb, 2)
                for xx in range(4):
                    xb = lax.rem(lax.div(x, 2) + xx // 2, 2)
                    xa = lax.rem(lax.rem(x, 2) + xx % 2 + xb, 2)
                    at = (a * 4 + xx) * 64
                    for src, half, dst, n in pieces:
                        part = parts[set_, dst // WIDTHS[set_]]
                        to = pl.ds(dst % WIDTHS[set_], n)
                        idx = part.index(za, zb, xa, xb)
                        value = whole[at : at + 64, src : src + n]
                        if half is not None:
                            part.cur[half, idx, :, to] = value.astype(B16)
                        else:
                            for h in range(2):
                                piece = value[32 * h : 32 * h + 32]
                                if add:
                                    piece = piece + part.cur[h, idx, :, to].astype(F32)
                                part.cur[h, idx, :, to] = piece.astype(B16)

        loop(WIDE // block, step)

    def spread_pieces(src, half, dst, n, width):
        found = []
        while n > 0:
            m = min(n, width - dst % width)
            found.append((src, half, dst, m))
            src, dst, n = src + m, dst + m, n - m
        return found

    def heads(src, dst):
        return spread_pieces(src, t, dst, 256, 384) + spread_pieces(src + 256, 1 - t, dst, 256, 384)

    def rows_of(src, dst, n):
        return spread_pieces(src, None, dst, n, 256)

    await_all("x_cot", "y_feed_act")
    product(r["x_cot"], r["y_feed_act"], 512, "S", heads(0, 0))
    await_all("x_feed_in", "y_feed_back")
    product(r["x_feed_in"], r["y_feed_back"], 512, "S", heads(0, 256))
    parts["S", 0].begin()
    await_all("x_branch", "y_mixed")
    product(r["x_branch"], r["y_mixed"], 512, "S", heads(0, 512))
    parts["S", 1].begin()
    await_all("x_attend_in", "y_back")
    product(r["x_attend_in"], r["y_back"], 1536, "S", [p for k in range(3) for p in heads(512 * k, 768 + 256 * k)])
    parts["S", 2].begin()
    parts["S", 3].begin()

    out_w, query_w = r["x_cot"], r["x_branch"]
    out_w2, query_w2 = r["x_feed_in"], r["x_attend_in"]
    ready["w_out"] = [
        here(r["cross_out"].at[pl.ds(0, 512)], out_w).wait,
        here(r["cross_out"].at[pl.ds(512, 512)], out_w2).wait,
    ]
    ready["w_query"] = [
        here(r["query_weight"].at[pl.ds(0, 512)], query_w).wait,
        here(r["query_weight"].at[pl.ds(512, 512)], query_w2).wait,
    ]

    def norm_grad(value_ref, gain, slot, after):
        r["gains"][pl.ds(slot, 1), :] = jnp.zeros((1, WIDE), F32)

        def step(i):
            rows = pl.ds(pl.multiple_of(i * 64, 64), 64)
            v = value_ref[rows, :].astype(F32)
            high, inverse = norm_parts(v)
            e = r["v_tmp"][rows, :]
            a = e * gain
            back = (
                a - jnp.mean(a, axis=-1, keepdims=True) - high * jnp.mean(a * high, axis=-1, keepdims=True)
            ) * inverse
            r["gains"][pl.ds(slot, 1), :] += jnp.sum(e * high, axis=0, keepdims=True)
            total = r["v_grad"][rows, :] + back
            after(rows, total)

        loop(ROWS // 64, step)

    def keep_grad(low_ref):
        def after(rows, total):
            r["v_grad"][rows, :] = total
            low_ref[rows, :] = total.astype(B16)

        return after

    def pull(a_ref, pieces, store):
        at = 0
        for piece in pieces:
            n = piece.shape[0]

            def step(i, piece=piece, at=at):
                rows = pl.ds(pl.multiple_of(i * 256, 256), 256)
                store(pl.ds(pl.multiple_of(at + i * 256, 256), 256), dot_t(a_ref[...], piece[rows, :]))

            loop(n // 256, step)
            at += n

    def to_tmp(columns, value):
        r["v_tmp"][:, columns] = value

    r["gains"][...] = jnp.zeros_like(r["gains"])
    await_all("rows_grad", "rows_grad_sum", "after_mlp", "attend_grad")

    def sum_step(i):
        rows = pl.ds(pl.multiple_of(i * 64, 64), 64)
        r["v_tmp"][rows, :] += r["v_rows_in"][rows, :].astype(F32)

    loop(ROWS // 64, sum_step)
    norm_grad(r["v_norm"], r["attend_gain"][...], 2, keep_grad(r["v_branch"]))
    load("after_cross", r["v_norm"], "after_cross")
    ready["y_mlp"] = [
        here(r["v_branch"].at[:, keep512], r["y_mlp"].at[top]).wait,
        remote(r["v_branch"].at[:, give512], r["y_mlp"].at[low], sib).wait_recv,
    ]
    await_all("w_down", "cross_hidden")

    def hidden_store(columns, value):
        r["v_back"][:, columns] = (gelu_slope(r["v_hidden"][:, columns]) * value).astype(B16)

    pull(r["v_branch"], [r["w_down"]], hidden_store)
    ready["y_hidden"] = [
        here(r["v_back"].at[:, keep512], r["y_hidden"].at[top]).wait,
        remote(r["v_back"].at[:, give512], r["y_hidden"].at[low], sib).wait_recv,
    ]
    await_all("w_up")
    pull(r["v_back"], [r["w_up"]], to_tmp)
    await_all("after_cross")
    norm_grad(r["v_norm"], r["cross_gain"][...], 1, keep_grad(r["v_branch2"]))
    ready["y_out"] = [
        here(r["v_branch2"].at[:, keep512], r["y_out"].at[top]).wait,
        remote(r["v_branch2"].at[:, give512], r["y_out"].at[low], sib).wait_recv,
    ]
    await_all("x_cross_act", "y_mlp")
    product(r["x_cross_act"], r["y_mlp"], 512, "P", rows_of(0, 0, 512))
    parts["P", 0].begin()
    parts["P", 1].begin()
    await_all("x_cross_in", "y_hidden")
    product(r["x_cross_in"], r["y_hidden"], 512, "P", rows_of(0, 512, 512))
    parts["P", 2].begin()
    parts["P", 3].begin()
    advance("S")

    await_all("w_out")
    attended_grad = r["x_attended_grad"]

    def attended_store(columns, value):
        attended_grad[top, columns] = value.astype(B16)

    pull(r["v_branch2"], [out_w, out_w2], attended_store)
    ready["x_attended_grad"] = [remote(attended_grad.at[top], attended_grad.at[low], sib).wait_recv]
    await_all("w_value", "mixed_f32", "asked", "picture", "raised")
    mixed_pull = dot_t(attended_grad[top, :], r["w_value"][...])
    pull_low = mixed_pull.astype(B16)
    r["v_pull"][...] = pull_low
    pull_f32 = pull_low.astype(F32)
    r["v_dot"][...] = jnp.sum(pull_f32 * r["v_mixed"][...], axis=-1, keepdims=True)
    scale_any = r["inverse_total"][...] * r["any_kept"][...]
    r["v_asked_t"][...] = (r["v_asked"][...].astype(F32) * scale_any).T.astype(B16)
    r["v_pull_t"][...] = (pull_f32 * r["inverse_total"][...]).T.astype(B16)
    r["v_sum"][...] = jnp.zeros_like(r["v_sum"])
    half = seq * LANES

    def pixel_chunk(start, to, at):
        columns = pl.ds(start, 512)
        picture, raised = r["v_picture"][:, columns], r["v_raised"][:, columns]
        change = (raised.astype(F32) * (dot(r["v_pull"][...], picture) - r["v_dot"][...])).astype(B16)
        r["v_sum"][...] += dot_t(change, picture)
        to[:, pl.ds(at, 512)] = (dot(r["v_asked_t"][...], change) + dot(r["v_pull_t"][...], raised)).astype(B16)

    def far_step(i):
        pixel_chunk(pl.multiple_of((1 - c) * half + i * 512, 512), r["grad_far"], pl.multiple_of(i * 512, 512))

    def near_step(i):
        pixel_chunk(pl.multiple_of(c * half + i * 512, 512), r["grad_own"], pl.multiple_of(i * 512, 512))

    loop(4, far_step)
    grad_copy = remote(r["grad_far"], r["grad_in"], sib)
    advance("S")
    advance("P")
    loop(4, near_step)

    turned_sum = r["v_sum"][...] * scale_any
    r["y_late"][...] = jnp.zeros_like(r["y_late"])
    r["y_late_own"][...] = jnp.zeros_like(r["y_late_own"])
    r["y_late_own"][:, :PAD] = (turned_sum * cross_scale).astype(B16)
    ready["y_late"] = [
        here(r["y_late_own"], r["y_late"].at[top]).wait,
        remote(r["y_late_own"], r["y_late_in"], sib).wait_recv,
    ]
    r["gains"][4:5, :PAD] = (
        jnp.sum(r["v_asked"][...].astype(F32) * turned_sum + r["v_pull"][...].astype(F32) * r["v_mixed"][...], axis=0, keepdims=True)
        / r["pixel_gain"][...]
    )

    grad_copy.wait_recv()

    def grad_step(i):
        rows = pl.ds(pl.multiple_of(i * 16, 16), 16)
        r["grad_own"][rows, :] = (r["grad_own"][rows, :].astype(F32) + r["grad_in"][rows, :].astype(F32)).astype(B16)

    loop(PAD // 16, grad_step)
    first, last_local = used[0], used[1]
    used[0] += seq
    used[1] += 1

    def homeward(k):
        to = lax.rem(s + k, seq)
        return pltpu.make_async_remote_copy(
            src_ref=r["grad_own"].at[:, pl.ds(pl.multiple_of(to * LANES, LANES), LANES)],
            dst_ref=r["home"].at[s],
            send_sem=send.at[first + k],
            recv_sem=recv.at[first + k],
            device_id=peer(k),
            device_id_type=MESH,
        )

    stay = pltpu.make_async_copy(
        r["grad_own"].at[:, pl.ds(pl.multiple_of(s * LANES, LANES), LANES)], r["home"].at[s], local.at[last_local]
    )

    @pl.when(c != t)
    def _():
        homeward(0).start()

    @pl.when(c == t)
    def _():
        stay.start()

    for k in range(1, seq):
        homeward(k).start()

    await_all("x_attended", "y_out")
    product(r["x_attended"], r["y_out"], 512, "Q", rows_of(0, 0, 512))
    parts["Q", 0].begin()
    parts["Q", 1].begin()
    await_all("x_attended_grad", "y_mixed_pixels")
    product(r["x_attended_grad"], r["y_mixed_pixels"], 512, "Q", rows_of(0, 512, 512))
    await_all("x_late_x", "y_late")
    r["y_late"][low, :] = r["y_late_in"][...]
    product(r["x_late_x"], r["y_late"], 384, "Q", rows_of(0, 512, 384), add=True)
    parts["Q", 2].begin()
    parts["Q", 3].begin()
    advance("S")
    advance("P")

    await_all("w_key", "w_query", "latents")
    r["v_rows_in"][...] = dot(r["y_late_own"][:, :PAD], r["w_key"][...]).astype(B16)
    pull(r["v_rows_in"], [query_w, query_w2], to_tmp)

    def latents_after(rows, total):
        r["v_latgrad"][rows, :] = total.astype(B16)

    norm_grad(r["v_latents"], r["query_gain"][...], 0, latents_after)
    r["gains"][3:4, :] = r["feedgain"][...]

    @pl.when(c != t)
    def _():
        for copy in moves:
            copy.start()

    @pl.when(c == t)
    def _():
        for copy in stays:
            copy.start()

    gain_buf, gain_in = r["gain_buf"], r["gain_in"]
    gain_buf[0] = r["gains"][...]
    gain_steps = ("XA", "XB", "ZA", "ZB", "T", "L", "C")
    gain_copy = remote(gain_buf.at[0], gain_in.at[0], partner[gain_steps[0]])
    live = [parts[set_, q] for set_ in SETS for q in range(4)]
    k = 0
    while live or k < 7:
        if k < 7:
            gain_copy.wait_recv()
            total = gain_buf[k] + gain_in[k]
            k += 1
            if k < 7:
                gain_buf[k] = total
                gain_copy = remote(gain_buf.at[k], gain_in.at[k], partner[gain_steps[k]])
            else:
                r["out_gains"][...] = total
        left_over = []
        for part in live:
            last = part.stage == 6
            part.advance()
            if not last:
                left_over.append(part)
        live = left_over

    @pl.when(c != t)
    def _():
        for copy in moves:
            copy.wait()
        homeward(0).wait()

    @pl.when(c == t)
    def _():
        for copy in stays:
            copy.wait()
        stay.wait()

    for k in range(1, seq):
        homeward(k).wait()
    for copy in waits:
        copy.wait_send()
    assert not ready, tuple(ready)
    assert used[0] <= sems[0] and used[1] <= sems[1], used


def back_and_reduce(given):
    names, scratch = [], []

    def room(name, shape, dtype=B16):
        names.append(name)
        scratch.append(pltpu.VMEM(shape, dtype))

    outs = {
        "out_S": ((64, 8 * 384), B16),
        "out_P": ((32, 8 * 256), B16),
        "out_Q": ((32, 8 * 256), B16),
        "home": ((16, PAD, LANES), B16),
        "latents_home": ((ROWS, WIDE), B16),
        "latgrad_home": ((ROWS, WIDE), B16),
        "out_gains": ((8, WIDE), F32),
    }
    sems = (160, 96)
    names += list(HBM_INPUTS) + list(VMEM_INPUTS) + list(outs)
    for name in ("send", "recv", "local"):
        names.append(name)
        scratch.append(pltpu.SemaphoreType.DMA((sems[1 if name == "local" else 0],)))
    for name in X_NAMES + ("attended_grad",):
        room("x_" + name, (512, WIDE))
    for name in ("feed_act", "feed_back", "mixed", "mixed_pixels", "mlp", "hidden", "out"):
        room("y_" + name, (512, 512))
    room("y_back", (512, 1536))
    room("y_late", (512, 384))
    room("y_late_own", (ROWS, 384))
    room("y_late_in", (ROWS, 384))
    for name in ("w_down", "w_up"):
        room(name, (WIDE, WIDE))
    for name in ("w_key", "w_value"):
        room(name, (PAD, WIDE))
    for name in ("v_tmp", "v_norm", "v_grad", "v_hidden"):
        room(name, (ROWS, WIDE), F32)
    for name in ("v_rows_in", "v_branch", "v_branch2", "v_back", "v_latents", "v_latgrad"):
        room(name, (ROWS, WIDE))
    room("v_picture", (PAD, 4096))
    room("v_raised", (ROWS, 4096))
    room("v_mixed", (ROWS, PAD), F32)
    room("v_sum", (ROWS, PAD), F32)
    room("v_asked", (ROWS, PAD))
    room("v_pull", (ROWS, PAD))
    room("v_asked_t", (PAD, ROWS))
    room("v_pull_t", (PAD, ROWS))
    room("v_dot", (ROWS, 1), F32)
    for name in ("grad_own", "grad_far", "grad_in"):
        room(name, (PAD, 16 * LANES))
    room("gains", (8, WIDE), F32)
    room("gain_buf", (7, 8, WIDE), F32)
    room("gain_in", (7, 8, WIDE), F32)
    for set_ in SETS:
        for q in range(4):
            key, depth, width = "%s%d_" % (set_, q), DEPTHS[set_], WIDTHS[set_]
            room(key + "buf", (2, 16, depth, width))
            for k in range(4):
                room(key + "in%d" % k, (2, 8 >> k, depth, width))
            for name in ("in4", "in5", "sum4", "sum5"):
                room(key + name, (depth, width))
    anywhere = pl.BlockSpec(memory_space=pl.ANY)
    vmem = pl.BlockSpec(memory_space=pltpu.VMEM)
    result = pl.pallas_call(
        functools.partial(back_kernel, tuple(names), sems),
        out_shape=[jax.ShapeDtypeStruct(*spec) for spec in outs.values()],
        in_specs=[anywhere] * len(HBM_INPUTS) + [vmem] * len(VMEM_INPUTS),
        out_specs=[anywhere] * (len(outs) - 1) + [vmem],
        scratch_shapes=scratch,
        compiler_params=pltpu.CompilerParams(
            collective_id=1, has_side_effects=True, vmem_limit_bytes=63 * MIB
        ),
        name="back_and_reduce",
    )(*[given[name] for name in HBM_INPUTS + VMEM_INPUTS])
    return dict(zip(outs, result))


def shards(
    latents,
    pixels,
    crop_bounds,
    key_mask,
    query_gain,
    pixel_gain,
    cross_gain,
    attend_gain,
    feed_gain,
    query_weight,
    key_weight,
    value_weight,
    cross_out,
    cross_up,
    cross_down,
    self_attend,
    self_out,
    self_up,
    self_down,
    cotangent,
):
    channels = pixels.shape[2]
    rows = pixels.shape[1]
    pixel_total = key_mask.shape[1]
    l, c, s, t = place()

    def cut(v, k, n, axis):
        return lax.dynamic_slice_in_dim(v, k * n, n, axis)

    pixel_high, pixel_inverse = norm_parts(pixels.astype(F32))
    pixel_low = (pixel_high * pixel_gain.astype(F32)).astype(B16)
    home = jnp.pad(jnp.swapaxes(pixel_low, 1, 2), ((0, 0), (0, PAD - channels), (0, 0)))
    positions = jnp.arange(pixel_total, dtype=jnp.int32)
    start, count = crop_bounds[0, 0], crop_bounds[0, 1]
    kept = (positions >= start) & (positions < start + count) & (key_mask[0] == 1)
    kept = jnp.swapaxes(kept.reshape(16, 2, rows), 0, 1).reshape(1, pixel_total).astype(F32)
    kept = jnp.broadcast_to(kept, (8, pixel_total))
    key_wide = jnp.pad(key_weight, ((0, PAD - channels), (0, 0)))
    value_wide = jnp.pad(value_weight, ((0, PAD - channels), (0, 0)))
    shared = {
        "query_weight": query_weight,
        "key_wide": key_wide,
        "value_wide": value_wide,
        "cross_out": cross_out,
        "cross_up": cross_up,
        "cross_down": cross_down,
        "query_gain": query_gain.astype(F32)[None],
        "cross_gain": cross_gain.astype(F32)[None],
        "attend_gain": attend_gain.astype(F32)[None],
    }
    given = front(
        shared
        | {
            "home": home,
            "kept": kept,
            "latents": latents[0],
            "cotangent": cotangent[0],
            "self_attend": self_attend,
            "self_out": self_out,
            "self_up": self_up,
            "self_down": self_down,
            "feed_gain": feed_gain.astype(F32)[None],
        }
    )
    given = shared | given
    given["latents"] = given.pop("latents_turned")
    given["pixel_gain"] = jnp.pad(pixel_gain.astype(F32), (0, PAD - channels), constant_values=1.0)[None]
    done = back_and_reduce(given)
    picture_home, gains = done["home"], done["out_gains"]
    latents_out, latents_grad = done["latents_home"], done["latgrad_home"]
    out_s = done["out_S"].reshape(64, 2, 6, 256)
    heads_sums = [out_s[:, :, k].reshape(64, 512).astype(F32) for k in range(6)]
    out_p = done["out_P"].reshape(32, 2, 2, 512)
    out_q = done["out_Q"].reshape(32, 2, 2, 512)
    late_sum = out_q[:, :, 1].reshape(32, 1024)

    pixel_grad = jnp.swapaxes(picture_home[:, :channels], 1, 2).astype(F32)
    a = pixel_grad * pixel_gain.astype(F32)
    pixels_grad = (
        a
        - jnp.mean(a, axis=-1, keepdims=True)
        - pixel_high * jnp.mean(a * pixel_high, axis=-1, keepdims=True)
    ) * pixel_inverse

    queryweight_grad = dot(late_sum[:, :PAD], key_wide)
    keyweight_grad = late_sum[:, 512 : 512 + channels].astype(F32).T
    valueweight_grad = jnp.concatenate(
        [late_sum[:, 384:512], late_sum[:, 896:], late_sum[:, PAD : PAD + channels - 256]], axis=1
    ).astype(F32).T
    gain_sums = cut(gains[:4], 2 * s + t, 32, 1)
    return (
        latents_out[None],
        latents_grad.astype(F32)[None],
        pixels_grad,
        gain_sums[0],
        gains[4, :channels],
        gain_sums[1],
        gain_sums[2],
        gain_sums[3],
        queryweight_grad,
        keyweight_grad,
        valueweight_grad,
        out_q[:, :, 0].reshape(32, 1024).astype(F32),
        out_p[:, :, 1].reshape(32, 1024).astype(F32),
        out_p[:, :, 0].reshape(32, 1024).astype(F32),
        jnp.stack(heads_sums[3:]),
        heads_sums[2].T,
        heads_sums[1],
        heads_sums[0].T,
    )


def solution(mesh):
    in_specs = (
        P(("batch", "seq"), "tensor", None),
        P("batch", ("seq", "tensor"), None),
        P(("batch", "seq"), None),
        P(("batch", "seq"), None),
        P(),
        P(),
        P(),
        P(),
        P(),
        P(),
        P(),
        P(),
        P(),
        P(),
        P(),
        P(None, None, "tensor"),
        P("tensor", None),
        P(None, "tensor"),
        P("tensor", None),
        P(("batch", "seq"), "tensor", None),
    )
    out_specs = (
        P(("batch", "seq"), "tensor", None),
        P(("batch", "seq"), "tensor", None),
        P("batch", ("seq", "tensor"), None),
        P(("seq", "tensor")),
        P(),
        P(("seq", "tensor")),
        P(("seq", "tensor")),
        P(("seq", "tensor")),
        P(("seq", "tensor"), None),
        P(None, ("seq", "tensor")),
        P(None, ("seq", "tensor")),
        P(("seq", "tensor"), None),
        P(("seq", "tensor"), None),
        P(("seq", "tensor"), None),
        P(None, "seq", "tensor"),
        P("tensor", "seq"),
        P("seq", "tensor"),
        P("tensor", "seq"),
    )
    return jax.shard_map(shards, mesh=mesh, in_specs=in_specs, out_specs=out_specs, check_vma=False)
```

```python
import functools
import math

import jax
import jax.numpy as jnp
from jax import lax
from jax.experimental import pallas as pl
from jax.experimental.pallas import tpu as pltpu
from jax.sharding import PartitionSpec as P

HEAD_WIDTH = 128
EPS = 1e-05
MASKED = -1000000000.0
MESH = pl.DeviceIdType.MESH
F32 = jnp.float32
B16 = jnp.bfloat16
LANES = 128
PAD = 272
WIDE = 1024
CYCLE = ("XA", "XB", "ZA", "ZB", "T")

def norm_parts(values):
    average = jnp.mean(values, axis=-1, keepdims=True)
    centered = values - average
    spread = jnp.mean(centered * centered, axis=-1, keepdims=True)
    inverse = lax.rsqrt(spread + EPS)
    return centered * inverse, inverse


def dot(a, b):
    return jnp.dot(a, b, preferred_element_type=F32)


def dot_t(a, b):
    return lax.dot_general(a, b, (((1,), (1,)), ((), ())), preferred_element_type=F32)


def tdot(a, b):
    return lax.dot_general(a, b, (((0,), (0,)), ((), ())), preferred_element_type=F32)


def flip(p):
    return p + 1 - 2 * lax.rem(p, 2)


def place():
    b, s, t = lax.axis_index("batch"), lax.axis_index("seq"), lax.axis_index("tensor")
    return lax.div(b, 2), lax.rem(b, 2), s, t


MIB = 1024 * 1024
ROWS = 256
GELU_K = math.sqrt(2.0 / math.pi)


def gelu(u):
    return 0.5 * u * (1.0 + jnp.tanh(GELU_K * (u + 0.044715 * u * u * u)))


def gelu_slope(u):
    th = jnp.tanh(GELU_K * (u + 0.044715 * u * u * u))
    return 0.5 * (1.0 + th) + 0.5 * u * (1.0 - th * th) * GELU_K * (1.0 + 3.0 * 0.044715 * u * u)


def loop(n, step):
    lax.fori_loop(0, n, lambda i, carry: (step(i), carry)[1], 0)


def block(i, n):
    return pl.ds(pl.multiple_of(i * n, n), n)


FRONT_HBM = (
    ("pixels", "latents", "cotangent", "self_attend", "self_out", "self_up", "self_down")
    + ("query_weight", "cross_out", "cross_up", "cross_down")
)
FRONT_VMEM = ("norm_gains", "pixel_gain", "key_weight", "value_weight", "key_mask", "crop_bounds")
FRONT_OUT = {
    "cot": ((512, WIDE), B16),
    "cross_act": ((512, WIDE), B16),
    "cross_in": ((512, WIDE), B16),
    "attended": ((512, WIDE), B16),
    "late_x": ((512, WIDE), B16),
    "mixed_pixels": ((512, 512), B16),
    "mixed": ((512, 512), B16),
    "attend_in": ((512, WIDE), B16),
    "projected": ((3, 512, 512), B16),
    "probs": ((8, ROWS, 512), B16),
    "out_mine": ((512, WIDE), B16),
    "attend_far": ((3, WIDE, 256), B16),
    "up_far": ((WIDE, 512), B16),
    "down_far": ((512, WIDE), B16),
    "after_mlp": ((ROWS, WIDE), F32),
    "after_attend": ((ROWS, WIDE), F32),
    "cross_hidden": ((ROWS, WIDE), F32),
    "after_cross": ((ROWS, WIDE), F32),
    "latents_turned": ((ROWS, WIDE), B16),
    "picture": ((PAD, 4096), B16),
    "raised": ((8, ROWS, 512), B16),
    "mixed_f32": ((ROWS, PAD), F32),
    "asked": ((ROWS, PAD), B16),
    "key_wide": ((PAD, WIDE), B16),
    "value_wide": ((PAD, WIDE), B16),
    "inverse_total": ((ROWS, 1), F32),
    "any_kept": ((1, 1), F32),
}
FRONT_OUT_VMEM = ("inverse_total", "any_kept")


def front_kernel(names, sems, *refs):
    l, c, s, t = place()
    seq = 16
    r = dict(zip(names, refs))
    send, recv, local = r["send"], r["recv"], r["local"]
    cross_scale = 1.0 / math.sqrt(WIDE)
    self_scale = 1.0 / math.sqrt(HEAD_WIDTH)
    sib = (2 * l + 1 - c, s, t)
    over = (2 * (1 - l) + c, s, 1 - t)
    beside = (2 * (1 - l) + c, s, t)

    def peer(k):
        return (2 * l + t, lax.rem(s + k, seq), c)

    barrier = pltpu.get_barrier_semaphore()
    for device in (sib, over, beside):
        pl.semaphore_signal(barrier, inc=1, device_id=device, device_id_type=MESH)
    def plane(k):
        return (2 * l + c, lax.rem(s + k, seq), t)

    for k in range(1, seq):
        pl.semaphore_signal(barrier, inc=1, device_id=peer(k), device_id_type=MESH)
        pl.semaphore_signal(barrier, inc=1, device_id=plane(k), device_id_type=MESH)

    @pl.when(c != t)
    def _():
        pl.semaphore_signal(barrier, inc=1, device_id=peer(0), device_id_type=MESH)
        pl.semaphore_wait(barrier, 2 + 2 * seq)

    @pl.when(c == t)
    def _():
        pl.semaphore_wait(barrier, 1 + 2 * seq)

    used = [0, 0]
    waits, stores = [], []

    def remote_of(src, dst, device):
        i = used[0]
        used[0] += 1
        return pltpu.make_async_remote_copy(
            src_ref=src, dst_ref=dst, send_sem=send.at[i], recv_sem=recv.at[i], device_id=device, device_id_type=MESH
        )

    def remote(src, dst, device):
        copy = remote_of(src, dst, device)
        copy.start()
        waits.append(copy)
        return copy

    def here_of(src, dst):
        i = used[1]
        used[1] += 1
        return pltpu.make_async_copy(src, dst, local.at[i])

    def here(src, dst):
        copy = here_of(src, dst)
        copy.start()
        return copy

    def store(name, src):
        stores.append(here(src, r[name]))

    top, low = pl.ds(0, ROWS), pl.ds(ROWS, ROWS)
    shared = []

    def share(name, src, give=None):
        stores.append(here(src, r[name].at[top]))
        shared.append(remote(src if give is None else give, r[name].at[low], sib))

    ready = {}

    def await_all(*wanted):
        for name in wanted:
            for wait in ready.pop(name, ()):
                wait()

    base = pl.multiple_of(c * (seq * LANES), LANES)
    far = pl.multiple_of(t * (seq * LANES), LANES)
    picture = r["v_picture"]

    def away_of(k):
        return remote_of(
            r["v_home"].at[lax.rem(s + k, seq)],
            picture.at[:, pl.ds(pl.multiple_of(far + s * LANES, LANES), LANES)],
            peer(k),
        )

    away = [away_of(k) for k in range(seq)]
    lat_move, cot_move = remote_of(r["latents"], r["v_lat"], peer(0)), remote_of(r["cotangent"], r["v_cot"], peer(0))
    kept_move = remote_of(r["v_kept_own"], r["v_kept"], sib)
    lat_stay, cot_stay = here_of(r["latents"], r["v_lat"]), here_of(r["cotangent"], r["v_cot"])
    kept_stay = here_of(r["v_kept_own"], r["v_kept"])
    picture_stay = here_of(r["v_home"].at[s], picture.at[:, pl.ds(pl.multiple_of(base + s * LANES, LANES), LANES)])

    @pl.when(c != t)
    def _():
        lat_move.start()

    @pl.when(c == t)
    def _():
        lat_stay.start()
        cot_stay.start()

    pixels_copy = here(r["pixels"], r["v_pixels"])

    mine, theirs = l, 1 - l
    own256 = 256 * c
    own_columns = pl.ds(pl.multiple_of(own256, LANES), 256)
    attend_far, out_w, up_far, down_far = r["w_attend_far"], r["w_out"], r["w_up_far"], r["w_down_far"]
    left = pl.ds(0, 256)

    def rows16(base_row, piece):
        return pl.ds(pl.multiple_of(base_row + 16 * piece, 16), 16)

    shares = {
        "out": (lambda p: r["self_out"].at[rows16(own256, p)], lambda p: out_w.at[rows16(256, p)]),
        "up": (lambda p: r["self_up"].at[block(p, 64), own_columns], lambda p: up_far.at[block(p, 64), left]),
        "down": (lambda p: r["self_down"].at[rows16(own256, p)], lambda p: down_far.at[rows16(0, p)]),
    }
    first_piece = {name: remote(src(s), dst(s), over) for name, (src, dst) in shares.items()}

    def attend_piece(k, p):
        return attend_far.at[k, block(p, 512)]

    across = {}
    for k in range(3):
        across["attend%d" % k] = remote(
            r["self_attend"].at[k, block(theirs, 512), own_columns], attend_piece(k, theirs), over
        )
    onward = {}

    def pass_on(*wanted):
        for name in wanted:
            across[name].wait_recv()
            k = int(name[-1])
            onward[name] = remote(attend_piece(k, mine), attend_piece(k, mine), beside)

    def pass_rest(*wanted):
        for name in wanted:
            onward[name].wait_recv()

    pieces = {}

    def spread_pieces(*wanted):
        for name in wanted:
            first_piece[name].wait_recv()
            dst = shares[name][1]
            pieces[name] = [remote(dst(s), dst(s), plane(k)) for k in range(1, seq)]

    whole = {
        "out": (out_w.at[pl.ds(256, 256)], out_w.at[pl.ds(768, 256)]),
        "up": (up_far.at[:, left], up_far.at[:, pl.ds(256, 256)]),
        "down": (down_far.at[left], down_far.at[pl.ds(256, 256)]),
    }
    sib_quarter = {}

    def gather_pieces(*wanted):
        for name in wanted:
            for copy in pieces[name]:
                copy.wait_recv()
            sib_quarter[name] = remote(*whole[name], sib)

    def arrived(*wanted):
        for name in wanted:
            sib_quarter[name].wait_recv()

    @pl.when(c != t)
    def _():
        cot_move.start()

    pixels_copy.wait()
    pixels, normed = r["v_pixels"], r["v_normed"]
    channels = pixels.shape[0]
    some = 9

    def features(i):
        return pl.ds(i * some, some)

    def sum_step(i, total):
        return total + jnp.sum(pixels[features(i)].astype(F32), axis=0)

    zeros = jnp.zeros(pixels.shape[1:], F32)
    average = lax.fori_loop(0, channels // some, sum_step, zeros) * (1.0 / channels)

    def square_step(i, total):
        centered = pixels[features(i)].astype(F32) - average
        return total + jnp.sum(centered * centered, axis=0)

    spread = lax.fori_loop(0, channels // some, square_step, zeros) * (1.0 / channels)
    inverse = lax.rsqrt(spread + EPS)

    def norm_step(i):
        value = (pixels[features(i)].astype(F32) - average) * inverse * r["pixel_gain"][features(i)]
        normed[pl.ds(pl.multiple_of(i * (some * 16), 16), some * 16), :] = value.reshape(some * 16, LANES)

    loop(channels // some, norm_step)
    normed[channels * 16 :, :] = jnp.zeros(((PAD - channels) * 16, LANES), F32)

    def turn_image(k):
        image = lax.rem(s + k, seq)
        r["v_home"][image] = normed[pl.ds(image, PAD, stride=16), :].astype(B16)

    turn_image(0)

    @pl.when(c != t)
    def _():
        away[0].start()

    @pl.when(c == t)
    def _():
        picture_stay.start()

    for k in range(1, seq):
        turn_image(k)
        away[k].start()

    start, count = r["crop_bounds"][:, 0:1], r["crop_bounds"][:, 1:2]
    lanes = lax.broadcasted_iota(jnp.int32, (1, LANES), 1)
    for k in range(2 * seq):
        row = lanes + k * LANES
        keep = (row >= start) & (row < start + count) & (r["key_mask"][:, pl.ds(k * LANES, LANES)] == 1)
        to = pl.ds(((k % 2) * seq + k // 2) * LANES, LANES)
        r["v_kept_own"][:, to] = jnp.broadcast_to(jnp.where(keep, 1.0, 0.0), (8, LANES))

    @pl.when(c == t)
    def _():
        kept_stay.start()
        kept_move.start()

    for name in ("key", "value"):
        ref, to = r[name + "_weight"], r["w_" + name]
        to[:256, :] = ref[:256, :]
        to[256:, :] = jnp.concatenate(
            [ref[256:channels, :].astype(F32), jnp.zeros((PAD - channels, WIDE), F32)], axis=0
        ).astype(B16)
        store(name + "_wide", to)
    for name, to in (
        ("query_weight", "w_query"),
        ("cross_out", "w_cross_out"),
        ("cross_up", "w_cross_up"),
        ("cross_down", "w_cross_down"),
    ):
        ready[to] = [here(r[name], r[to]).wait]
    ready["attend_own"] = [here(r["self_attend"].at[:, :, own_columns], r["w_attend_own"]).wait]
    ready["out_own"] = [
        here(r["self_out"].at[pl.ds(pl.multiple_of(own256, LANES), 256)], out_w.at[pl.ds(0, 256)]).wait,
        here(r["self_out"].at[pl.ds(pl.multiple_of(256 - own256, LANES), 256)], out_w.at[pl.ds(512, 256)]).wait,
    ]

    spread_pieces("out", "up", "down")

    def norm_rows(value_ref, gain, out_ref, also=None):
        def step(i):
            rows = block(i, 64)
            v = value_ref[rows, :].astype(F32)
            high, _ = norm_parts(v)
            out_ref[rows, :] = (high * gain).astype(B16)

        loop(ROWS // 64, step)

    def each256(n, step):
        loop(n // 256, lambda i: step(block(i, 256)))

    @pl.when(c != t)
    def _():
        lat_move.wait_recv()

    @pl.when(c == t)
    def _():
        lat_stay.wait()

    store("latents_turned", r["v_lat"])
    query_low, queries = r["v_query_low"], r["v_queries"]
    norm_rows(r["v_lat"], r["norm_gains"][0:1, :], query_low)
    await_all("w_query")

    def query_step(columns):
        queries[:, columns] = dot(query_low[...], r["w_query"][:, columns]).astype(B16)

    each256(WIDE, query_step)
    r["v_asked"][...] = (dot_t(queries[...], r["w_key"][...]) * cross_scale).astype(B16)
    store("asked", r["v_asked"])
    late = r["late_x"]
    late_keep = [here_of(src, late.at[top]) for src in (query_low, queries)]
    late_give = [remote_of(src, late.at[low], sib) for src in (queries, query_low)]

    @pl.when(c == 0)
    def _():
        late_keep[0].start()
        late_give[0].start()

    @pl.when(c == 1)
    def _():
        late_keep[1].start()
        late_give[1].start()

    def chunk(k):
        return picture.at[:, pl.ds(pl.multiple_of(base + lax.rem(s - k + seq, seq) * LANES, LANES), LANES)]

    @pl.when(c != t)
    def _():
        away[0].wait_recv()
        kept_move.wait_recv()

    @pl.when(c == t)
    def _():
        picture_stay.wait()
        kept_stay.wait()

    passed = [remote(chunk(0), chunk(0), sib)]
    for k in range(1, seq):
        away[k].wait_recv()
        passed.append(remote(chunk(k), chunk(k), sib))
    for copy in passed:
        copy.wait_recv()
    store("picture", picture)

    scores, raised = r["v_scores"], r["v_raised"]
    r["v_top"][...] = jnp.full((ROWS, 1), -3.0e38, F32)
    r["v_total"][...] = jnp.zeros((ROWS, 1), F32)
    r["v_mixed"][...] = jnp.zeros_like(r["v_mixed"])
    r["any_kept"][...] = jnp.max(r["v_kept"][0:1, :], axis=-1, keepdims=True)

    def score_step(i):
        columns = block(i, 512)
        value = dot(r["v_asked"][...], picture[:, columns])
        value = jnp.where(r["v_kept"][0:1, columns] > 0.5, value, MASKED)
        scores[:, columns] = value
        r["v_top"][...] = jnp.maximum(r["v_top"][...], jnp.max(value, axis=-1, keepdims=True))

    loop(8, score_step)

    def raise_step(i):
        columns = block(i, 512)
        value = jnp.exp(scores[:, columns] - r["v_top"][...])
        r["v_total"][...] += jnp.sum(value, axis=-1, keepdims=True)
        value = value.astype(B16)
        raised[i] = value
        r["v_mixed"][...] += dot_t(value, picture[:, columns])

    loop(8, raise_step)
    store("raised", raised)
    inverse_total = 1.0 / r["v_total"][...]
    r["inverse_total"][...] = inverse_total
    mixed = r["v_mixed"][...] * inverse_total
    r["v_mixed"][...] = mixed
    store("mixed_f32", r["v_mixed"])
    r["v_mixed_wide"][...] = jnp.zeros_like(r["v_mixed_wide"])
    r["v_mixed_wide"][:, :PAD] = mixed
    tail = pltpu.roll(r["v_mixed_wide"][:, 256:384], 16, 1).astype(B16)
    for name, core in (("mixed_pixels", c), ("mixed_pixels_give", 1 - c)):
        ref = r["v_" + name]
        ref[:, :256] = jnp.zeros((ROWS, 256), B16)
        ref[:, 256:384] = tail
        ref[:, 384:] = r["v_mixed_wide"][:, pl.ds(pl.multiple_of(LANES * core, LANES), LANES)].astype(B16)
    share("mixed_pixels", r["v_mixed_pixels"], r["v_mixed_pixels_give"])
    await_all("w_cross_out")
    r["v_attended"][...] = dot(mixed.astype(B16), r["w_value"][...]).astype(B16)
    share("attended", r["v_attended"])

    def out_step(columns):
        r["v_after_cross"][:, columns] = r["v_lat"][:, columns].astype(F32) + dot(
            r["v_attended"][...], r["w_cross_out"][:, columns]
        )

    each256(WIDE, out_step)
    store("after_cross", r["v_after_cross"])
    pass_on("attend0")
    norm_rows(r["v_after_cross"], r["norm_gains"][1:2, :], r["v_cross_in"])
    share("cross_in", r["v_cross_in"])
    await_all("w_cross_up", "w_cross_down")

    def up_step(columns):
        hidden = dot(r["v_cross_in"][...], r["w_cross_up"][:, columns])
        r["v_hidden"][:, columns] = hidden
        r["v_cross_act"][:, columns] = gelu(hidden).astype(B16)

    each256(WIDE, up_step)
    store("cross_hidden", r["v_hidden"])
    share("cross_act", r["v_cross_act"])
    pass_on("attend1")

    def down_step(columns):
        r["v_after_mlp"][:, columns] = r["v_after_cross"][:, columns] + dot(
            r["v_cross_act"][...], r["w_cross_down"][:, columns]
        )

    each256(WIDE, down_step)
    store("after_mlp", r["v_after_mlp"])

    attend_in = r["v_attend_in"]
    norm_rows(r["v_after_mlp"], r["norm_gains"][2:3, :], attend_in)
    attend_copy = remote(attend_in.at[top], attend_in.at[low], sib)
    await_all("attend_own")
    pass_on("attend2")
    attend_copy.wait_recv()
    store("attend_in", attend_in)
    projected, probs = r["v_projected"], r["v_probs"]

    def project(weights, at):
        for k in range(3):
            projected[k, :, pl.ds(at, 256)] = dot(attend_in[...], weights[k]).astype(B16)

    def attend(h):
        columns = block(h, HEAD_WIDTH)
        dotted = dot_t(projected[0, :, columns], projected[1, :, columns]) * self_scale
        value = jnp.exp(dotted - jnp.max(dotted, axis=-1, keepdims=True))
        value = (value * (1.0 / jnp.sum(value, axis=-1, keepdims=True))).astype(B16)
        probs[2 * h] = value[:ROWS]
        probs[2 * h + 1] = value[ROWS:]
        r["v_self"][:, columns] = dot(value, projected[2, :, columns]).astype(B16)

    project(r["w_attend_own"], 0)
    loop(2, attend)
    pass_rest("attend0", "attend1", "attend2")
    project(attend_far, 256)
    loop(2, lambda i: attend(i + 2))
    store("mixed", r["v_self"])
    self_copy = remote(r["v_self"].at[low], r["v_self_in"], sib)
    store("projected", projected)
    store("probs", probs)
    store("attend_far", attend_far)

    @pl.when(c != t)
    def _():
        cot_move.wait_recv()

    @pl.when(c == t)
    def _():
        cot_stay.wait()

    share("cot", r["v_cot"])
    gather_pieces("out")
    await_all("out_own")
    arrived("out")
    store("out_mine", out_w.at[pl.ds(0, 512)])
    self_copy.wait_recv()

    def attended_step(columns):
        r["v_after_attend"][:, columns] = (
            r["v_after_mlp"][:, columns]
            + dot(r["v_self"][top, :], out_w[pl.ds(0, 512), columns])
            + dot(r["v_self_in"][...], out_w[pl.ds(512, 512), columns])
        )

    each256(WIDE, attended_step)
    store("after_attend", r["v_after_attend"])
    gather_pieces("up", "down")
    arrived("up", "down")
    store("up_far", up_far)
    store("down_far", down_far)

    @pl.when(c != t)
    def _():
        lat_move.wait_send()
        cot_move.wait_send()
        away[0].wait_send()

    @pl.when(c == t)
    def _():
        kept_move.wait_send()

    @pl.when(c == 0)
    def _():
        late_keep[0].wait()
        late_give[0].wait_send()
        late_give[1].wait_recv()

    @pl.when(c == 1)
    def _():
        late_keep[1].wait()
        late_give[1].wait_send()
        late_give[0].wait_recv()

    for k in range(1, seq):
        away[k].wait_send()
    for copy in shared:
        copy.wait_recv()
    for copy in waits:
        copy.wait_send()
    for copy in stores:
        copy.wait()
    assert not ready, tuple(ready)
    assert used[0] <= sems[0] and used[1] <= sems[1], used


def front(given):
    names, scratch = [], []

    def room(name, shape, dtype=B16):
        names.append(name)
        scratch.append(pltpu.VMEM(shape, dtype))

    sems = (101, 38)
    names += list(FRONT_HBM) + list(FRONT_VMEM) + list(FRONT_OUT)
    for name in ("send", "recv", "local"):
        names.append(name)
        scratch.append(pltpu.SemaphoreType.DMA((sems[1 if name == "local" else 0],)))
    for name in ("query", "cross_out", "cross_up", "cross_down", "out"):
        room("w_" + name, (WIDE, WIDE))
    for name in ("key", "value"):
        room("w_" + name, (PAD, WIDE))
    for name in ("attend_own", "attend_far"):
        room("w_" + name, (3, WIDE, 256))
    room("w_up_far", (WIDE, 512))
    room("w_down_far", (512, WIDE))
    room("v_picture", (PAD, 4096))
    room("v_pixels", (261, 16, LANES))
    room("v_normed", (PAD * 16, LANES), F32)
    room("v_home", (16, PAD, LANES))
    room("v_kept", (8, 4096), F32)
    room("v_kept_own", (8, 4096), F32)
    room("v_scores", (ROWS, 4096), F32)
    room("v_raised", (8, ROWS, 512))
    for name in ("lat", "cot", "query_low", "queries", "attended", "cross_in", "cross_act"):
        room("v_" + name, (ROWS, WIDE))
    for name in ("after_cross", "hidden", "after_mlp", "after_attend"):
        room("v_" + name, (ROWS, WIDE), F32)
    room("v_attend_in", (512, WIDE))
    room("v_projected", (3, 512, 512))
    room("v_probs", (8, ROWS, 512))
    room("v_self", (512, 512))
    room("v_self_in", (ROWS, 512))
    room("v_asked", (ROWS, PAD))
    room("v_top", (ROWS, 1), F32)
    room("v_total", (ROWS, 1), F32)
    room("v_mixed", (ROWS, PAD), F32)
    room("v_mixed_wide", (ROWS, 384), F32)
    room("v_mixed_pixels", (ROWS, 512))
    room("v_mixed_pixels_give", (ROWS, 512))
    anywhere = pl.BlockSpec(memory_space=pl.ANY)
    vmem = pl.BlockSpec(memory_space=pltpu.VMEM)
    result = pl.pallas_call(
        functools.partial(front_kernel, tuple(names), sems),
        out_shape=[jax.ShapeDtypeStruct(*spec) for spec in FRONT_OUT.values()],
        in_specs=[anywhere] * len(FRONT_HBM) + [vmem] * len(FRONT_VMEM),
        out_specs=[vmem if name in FRONT_OUT_VMEM else anywhere for name in FRONT_OUT],
        scratch_shapes=scratch,
        compiler_params=pltpu.CompilerParams(collective_id=0, has_side_effects=True, vmem_limit_bytes=63 * MIB),
        name="front",
    )(*[given[name] for name in FRONT_HBM + FRONT_VMEM])
    return dict(zip(FRONT_OUT, result))


LINKS = ("XA", "ZA", "L", "XB", "ZB", "O")
SETS = {"S": ((0, 1, 2, 3, 4, 5), 32), "P": ((0, 3, 1, 4), 16), "Q": ((2, 5, 0, 3), 16)}
BACK_HBM = (
    ("cot", "cross_act", "cross_in", "attended", "late_x", "mixed_pixels", "mixed", "attend_in", "projected", "probs")
    + ("out_mine", "attend_far", "up_far", "down_far", "after_mlp", "after_attend", "cross_hidden", "after_cross")
    + ("latents_turned", "picture", "raised", "mixed_f32", "asked", "self_attend", "self_up", "self_down")
    + ("cross_down", "cross_up", "cross_out", "query_weight", "key_wide", "value_wide")
)
BACK_VMEM = ("inverse_total", "any_kept", "norm_gains")
BACK_OUT = {
    "out_S": ((64, 2 * 6 * 256), B16),
    "out_P": ((32, 2 * 4 * 256), B16),
    "out_Q": ((32, 2 * 4 * 256), B16),
    "home": ((16, PAD, LANES), B16),
    "latents_home": ((ROWS, WIDE), B16),
    "latgrad_home": ((ROWS, WIDE), B16),
    "out_gains": ((8, WIDE), F32),
}


def back_kernel(names, sems, *refs):
    l, c, s, t = place()
    z, x = lax.div(s, 4), lax.rem(s, 4)
    seq = 16
    r = dict(zip(names, refs))
    send, recv, local = r["send"], r["recv"], r["local"]
    cross_scale = 1.0 / math.sqrt(WIDE)
    self_scale = 1.0 / math.sqrt(HEAD_WIDTH)

    partner = {
        "XA": (2 * l + c, z * 4 + flip(x), t),
        "XB": (2 * l + c, z * 4 + 3 - x, t),
        "ZA": (2 * l + c, flip(z) * 4 + x, t),
        "ZB": (2 * l + c, (3 - z) * 4 + x, t),
        "L": (2 * (1 - l) + c, s, t),
        "O": (2 * (1 - l) + c, s, 1 - t),
        "C": (2 * l + 1 - c, s, t),
        "D": (2 * (1 - l) + 1 - c, s, t),
    }

    def peer(k):
        return (2 * l + t, lax.rem(s + k, seq), c)

    barrier = pltpu.get_barrier_semaphore()
    for device in partner.values():
        pl.semaphore_signal(barrier, inc=1, device_id=device, device_id_type=MESH)
    for k in range(1, seq):
        pl.semaphore_signal(barrier, inc=1, device_id=peer(k), device_id_type=MESH)

    @pl.when(c != t)
    def _():
        pl.semaphore_signal(barrier, inc=1, device_id=peer(0), device_id_type=MESH)
        pl.semaphore_wait(barrier, len(partner) + seq)

    @pl.when(c == t)
    def _():
        pl.semaphore_wait(barrier, len(partner) + seq - 1)

    used = [0, 0]
    waits = []

    def remote_of(src, dst, device):
        i = used[0]
        used[0] += 1
        return pltpu.make_async_remote_copy(
            src_ref=src, dst_ref=dst, send_sem=send.at[i], recv_sem=recv.at[i], device_id=device, device_id_type=MESH
        )

    def remote(src, dst, device):
        copy = remote_of(src, dst, device)
        copy.start()
        waits.append(copy)
        return copy

    def sent(*copies):
        for copy in copies:
            copy.wait_send()
            waits[:] = [other for other in waits if other is not copy]

    def here_of(src, dst):
        i = used[1]
        used[1] += 1
        return pltpu.make_async_copy(src, dst, local.at[i])

    def here(src, dst):
        copy = here_of(src, dst)
        copy.start()
        return copy

    ready = {}

    def await_all(*wanted):
        for name in wanted:
            for wait in ready.pop(name):
                wait()

    def load(name, to, key=None):
        ready[key or name] = [here(r[name], to).wait]

    sib = partner["C"]
    top, low = pl.ds(0, ROWS), pl.ds(ROWS, ROWS)
    keep512 = pl.ds(pl.multiple_of(512 * c, LANES), 512)
    give512 = pl.ds(pl.multiple_of(512 * (1 - c), LANES), 512)
    keep256 = pl.ds(pl.multiple_of(256 * c, LANES), 256)
    give256 = pl.ds(pl.multiple_of(256 * (1 - c), LANES), 256)
    left, right = pl.ds(0, 256), pl.ds(256, 256)
    x1, x2, x3, x4, x5 = (r["x%d" % k] for k in range(1, 6))
    up_w, down_w, probs = r["w_up"], r["w_down"], r["v_probs"]

    load("after_attend", r["v_norm"])
    ready["up"] = [
        here(r["self_up"], up_w.at[:, pl.ds(0, 512)]).wait,
        here(r["up_far"], up_w.at[:, pl.ds(512, 512)]).wait,
    ]
    load("cot", x1)
    ready["down"] = [
        here(r["self_down"], down_w.at[pl.ds(0, 512)]).wait,
        here(r["down_far"], down_w.at[pl.ds(512, 512)]).wait,
    ]
    load("out_mine", r["w_out_mine"])
    load("projected", r["v_projected"])
    load("probs", probs)
    load("mixed", r["y_mixed"])
    ready["attend_own"] = [
        here(r["self_attend"].at[:, :, keep256], r["w_attend_own"]).wait
    ]
    load("attend_far", r["w_attend_far"])
    load("attend_in", x4)
    load("cross_hidden", r["v_hidden"])
    load("value_wide", r["w_value"])
    load("key_wide", r["w_key"])
    load("picture", r["v_picture"])
    load("mixed_f32", r["v_mixed"])
    load("asked", r["v_asked"])
    load("mixed_pixels", r["y_mixed_pixels"])

    class Part:
        def __init__(self, set_, q):
            first, self.depth = SETS[set_][0][q], SETS[set_][1]
            self.order = LINKS[first:] + LINKS[:first]
            self.set, self.q, self.stage, self.n = set_, q, -1, 64
            self.key = "%s%d_" % (set_, q)
            self.cur = r[self.key + "buf"]
            self.weight = {bit: 32 >> k for k, bit in enumerate(self.order)}

        def index(self, **bits):
            return sum(value * self.weight[bit] for bit, value in bits.items())

        def begin(self):
            self.stage += 1
            k, n = self.stage, self.n
            if k < 6:
                self.into = r[self.key + "in%d" % k]
                self.copies = [remote(self.cur.at[pl.ds(n // 2, n // 2)], self.into, partner[self.order[k]])]
                return
            count = len(SETS[self.set][0])
            dst = r["out_" + self.set].at[
                pl.ds(pl.multiple_of(l * self.depth, self.depth), self.depth),
                pl.ds(pl.multiple_of((count * c + self.q) * 256, LANES), 256),
            ]
            self.copies = [remote(self.cur.at[0], dst, partner[way]) for way in ("L", "C", "D")]
            self.copy_here = here(self.cur.at[0], dst)

        def finish(self):
            for copy in self.copies:
                copy.wait_recv()
            if self.stage == 6:
                self.copy_here.wait()
                return
            self.n //= 2
            cur, into = self.cur, self.into
            m = min(self.n, 4)

            def step(i):
                rows = pl.ds(i * m, m)
                cur[rows] = (cur[rows].astype(F32) + into[rows].astype(F32)).astype(B16)

            if self.n > m:
                loop(self.n // m, step)
            else:
                step(0)

        def advance(self):
            self.finish()
            if self.stage < 6:
                self.begin()

    parts = {(set_, q): Part(set_, q) for set_ in SETS for q in range(len(SETS[set_][0]))}

    def advance(set_, *some):
        for q in some or range(len(SETS[set_][0])):
            parts[set_, q].advance()

    def product(x_ref, y_ref, width, pieces, add=False):
        span = 512 if width <= 512 else 256
        per = span // 256

        def step(i):
            columns = block(i, span)
            whole = tdot(x_ref[:, columns], y_ref[...])
            for a in range(per):
                zz = i * per + a
                zb = lax.rem(lax.div(z, 2) + lax.div(zz, 2), 2)
                za = lax.rem(lax.rem(z, 2) + lax.rem(zz, 2) + zb, 2)
                for xx in range(4):
                    xb = lax.rem(lax.div(x, 2) + xx // 2, 2)
                    xa = lax.rem(lax.rem(x, 2) + xx % 2 + xb, 2)
                    at = (a * 4 + xx) * 64
                    for part, src, width_, half in pieces:
                        for k in range(64 // part.depth):
                            ll = k % 2
                            o = half if half is not None else lax.rem(k // 2 + t, 2)
                            idx = part.index(ZA=za, ZB=zb, XA=xa, XB=xb, O=o, L=lax.rem(ll + l + o, 2))
                            value = whole[at + k * part.depth : at + (k + 1) * part.depth, src : src + width_]
                            to = pl.ds(0, width_)
                            if add:
                                value = value + part.cur[idx, :, to].astype(F32)
                            part.cur[idx, :, to] = value.astype(B16)

        loop(WIDE // span, step)

    def heads(q, at=0):
        return [("S", q, at, 0), ("S", q, at + 256, 1)]

    def product_heads(x_ref, y_ref, width, wanted):
        product(x_ref, y_ref, width, [(parts["S", q], at, 256, half) for _, q, at, half in wanted])

    def product_rows(x_ref, y_ref, width, set_, q, add=False):
        pieces, at = [], 0
        while at < width:
            n = min(256, width - at)
            pieces.append((parts[set_, q + at // 256], at, n, None))
            at += n
        product(x_ref, y_ref, width, pieces, add)

    r["gains"][...] = jnp.zeros_like(r["gains"])

    def norm_grad(value_ref, gain, slot, after):
        def step(i):
            rows = block(i, 64)
            high, inverse = norm_parts(value_ref[rows, :].astype(F32))
            e = r["v_tmp"][rows, :]
            a = e * gain
            back = (
                a - jnp.mean(a, axis=-1, keepdims=True) - high * jnp.mean(a * high, axis=-1, keepdims=True)
            ) * inverse
            r["gains"][pl.ds(slot, 1), :] += jnp.sum(e * high, axis=0, keepdims=True)
            after(rows, back)

        loop(ROWS // 64, step)

    def add_grad(low_ref):
        def after(rows, back):
            total = r["v_grad"][rows, :] + back
            r["v_grad"][rows, :] = total
            low_ref[rows, :] = total.astype(B16)

        return after

    def pull(a_ref, w_ref, store):
        def step(i):
            rows = block(i, 256)
            store(rows, dot_t(a_ref[...], w_ref[rows, :]))

        loop(w_ref.shape[0] // 256, step)

    def to_tmp(columns, value):
        r["v_tmp"][:, columns] = value

    def halves(name, src, to):
        copy = remote(src.at[:, give512], to.at[low], sib)
        ready[name] = [here(src.at[:, keep512], to.at[top]).wait, copy.wait_recv]
        return copy

    await_all("after_attend")

    def feed_norm(i):
        rows = block(i, 64)
        high, _ = norm_parts(r["v_norm"][rows, :])
        x2[rows, :] = (high * r["norm_gains"][3:4, :]).astype(B16)

    loop(ROWS // 64, feed_norm)
    feed_in_copy = remote(x2.at[top], x2.at[low], sib)
    await_all("up", "cot", "down")

    def feed_step(i):
        columns = block(i, 256)
        hidden = dot(x2[top, :], up_w[:, columns])
        r["v_feed_act"][:, columns] = gelu(hidden).astype(B16)
        pulled = dot_t(x1[top, :], down_w[columns, :])
        r["v_feed_back"][:, columns] = (gelu_slope(hidden) * pulled).astype(B16)

    loop(4, feed_step)
    quarter_sends = []
    for name in ("feed_act", "feed_back"):
        ref, to = r["v_" + name], r["y_" + name]
        quarter_sends += [
            remote(ref.at[:, give256], to.at[low, left], sib),
            remote(ref.at[:, pl.ds(768, 256)], to.at[low, right], sib),
        ]
        ready["y_" + name] = [
            here(ref.at[:, keep256], to.at[top, left]).wait,
            here(ref.at[:, pl.ds(512, 256)], to.at[top, right]).wait,
        ] + [copy.wait_recv for copy in quarter_sends[-2:]]
    pull(r["v_feed_back"], up_w, to_tmp)

    def feed_after(rows, back):
        total = x1[rows, :].astype(F32) + back
        r["v_grad"][rows, :] = total
        x3[rows, :] = total.astype(B16)

    norm_grad(r["v_norm"], r["norm_gains"][3:4, :], 3, feed_after)
    branch_copy = remote(x3.at[top], x3.at[low], sib)
    load("cross_up", up_w, "cross_up")

    def latents_step(i):
        columns = block(i, 256)
        r["v_latents_out"][:, columns] = (
            r["v_norm"][:, columns] + dot(r["v_feed_act"][...], down_w[:, columns])
        ).astype(B16)

    loop(4, latents_step)
    load("cross_down", down_w, "cross_down")
    load("after_mlp", r["v_norm"], "after_mlp")
    out_move, out_stay = remote_of(r["v_latents_out"], r["latents_home"], peer(0)), here_of(r["v_latents_out"], r["latents_home"])

    @pl.when(c != t)
    def _():
        out_move.start()

    @pl.when(c == t)
    def _():
        out_stay.start()

    await_all("y_feed_act")
    product_heads(x1, r["y_feed_act"], 512, heads(0))
    parts["S", 0].begin()
    load("cross_act", x1, "x_cross_act")
    feed_in_copy.wait_recv()
    await_all("y_feed_back")
    product_heads(x2, r["y_feed_back"], 512, heads(1))
    parts["S", 1].begin()
    sent(feed_in_copy)
    load("late_x", x2, "x_late_x")

    branch_copy.wait_recv()
    await_all("out_mine", "projected", "probs", "mixed")

    def mixed_step(columns, value):
        r["v_self_grad"][:, columns] = value.astype(B16)

    pull(x3, r["w_out_mine"], mixed_step)
    product_heads(x3, r["y_mixed"], 512, heads(2))
    parts["S", 2].begin()
    sent(branch_copy)
    load("cross_in", x3, "x_cross_in")
    projected, y_back = r["v_projected"], r["y_back"]

    def attend_back(h):
        columns = block(h, HEAD_WIDTH)
        query, key, value = (projected[k, :, columns] for k in range(3))
        key_sum = value_sum = 0
        for j in range(2):
            rows = pl.ds(ROWS * j, ROWS)
            grad = r["v_self_grad"][rows, columns]
            p = probs[2 * h + j]
            g = dot_t(grad, value)
            p32 = p.astype(F32)
            change = (p32 * (g - jnp.sum(p32 * g, axis=-1, keepdims=True))).astype(B16)
            y_back[rows, columns] = (dot(change, key) * self_scale).astype(B16)
            key_sum = key_sum + tdot(change, projected[0, rows, columns])
            value_sum = value_sum + tdot(p, grad)
        y_back[:, pl.ds(pl.multiple_of(512 + h * HEAD_WIDTH, LANES), HEAD_WIDTH)] = (key_sum * self_scale).astype(B16)
        y_back[:, pl.ds(pl.multiple_of(1024 + h * HEAD_WIDTH, LANES), HEAD_WIDTH)] = value_sum.astype(B16)

    loop(4, attend_back)
    load("raised", probs)
    await_all("attend_own", "attend_far")

    def rows_step(i):
        rows = block(i, 256)
        total = 0
        for k in range(3):
            total = total + dot_t(y_back[:, pl.ds(512 * k, 256)], r["w_attend_own"][k, rows, :])
            total = total + dot_t(y_back[:, pl.ds(512 * k + 256, 256)], r["w_attend_far"][k, rows, :])
        r["v_tmp"][:, rows] = total[:ROWS]
        r["v_rows_give"][:, rows] = total[ROWS:].astype(B16)

    loop(4, rows_step)
    rows_copy = remote(r["v_rows_give"], r["v_rows_in"], sib)
    await_all("attend_in")
    product_heads(x4, y_back, 1536, [piece for k in range(3) for piece in heads(3 + k, 512 * k)])
    for q in (3, 4, 5):
        parts["S", q].begin()
    load("attended", x4, "x_attended")
    rows_copy.wait_recv()

    def sum_step(i):
        rows = block(i, 64)
        r["v_tmp"][rows, :] += r["v_rows_in"][rows, :].astype(F32)

    loop(ROWS // 64, sum_step)
    await_all("after_mlp")
    mlp_branch, cross_branch = r["v_branch"], r["v_rows_give"]
    norm_grad(r["v_norm"], r["norm_gains"][2:3, :], 2, add_grad(mlp_branch))
    load("after_cross", r["v_norm"], "after_cross")

    halves("y_mlp", mlp_branch, r["y_mlp"])
    await_all("cross_down", "cross_hidden")

    def hidden_store(columns, value):
        r["v_back"][:, columns] = (gelu_slope(r["v_hidden"][:, columns]) * value).astype(B16)

    pull(mlp_branch, down_w, hidden_store)
    load("cross_out", down_w, "cross_out")
    halves("y_hidden", r["v_back"], r["y_hidden"])
    await_all("cross_up")
    pull(r["v_back"], up_w, to_tmp)
    load("query_weight", up_w, "query_weight")
    advance("S", 0, 1)
    sent(rows_copy)
    await_all("after_cross")
    norm_grad(r["v_norm"], r["norm_gains"][1:2, :], 1, add_grad(cross_branch))
    halves("y_out", cross_branch, r["y_out"])
    await_all("cross_out")

    def attended_store(columns, value):
        x5[top, columns] = value.astype(B16)

    pull(cross_branch, down_w, attended_store)
    attended_copy = remote(x5.at[top], x5.at[low], sib)
    await_all("x_cross_act", "y_mlp")
    product_rows(x1, r["y_mlp"], 512, "P", 0)
    parts["P", 0].begin()
    parts["P", 1].begin()
    await_all("x_cross_in", "y_hidden")
    product_rows(x3, r["y_hidden"], 512, "P", 2)
    parts["P", 2].begin()
    parts["P", 3].begin()
    advance("S", 2)

    await_all("value_wide", "mixed_f32", "asked", "picture", "raised")
    pull_low = dot_t(x5[top, :], r["w_value"][...]).astype(B16)
    r["v_pull"][...] = pull_low
    pull_f32 = pull_low.astype(F32)
    r["v_dot"][...] = jnp.sum(pull_f32 * r["v_mixed"][...], axis=-1, keepdims=True)
    scale_any = r["inverse_total"][...] * r["any_kept"][...]
    r["v_asked_t"][...] = (r["v_asked"][...].astype(F32) * scale_any).T.astype(B16)
    r["v_pull_t"][...] = (pull_f32 * r["inverse_total"][...]).T.astype(B16)
    r["v_sum"][...] = jnp.zeros_like(r["v_sum"])

    def pixel_chunk(i, to, at):
        picture, raised = r["v_picture"][:, block(i, 512)], probs[i]
        change = (raised.astype(F32) * (dot(r["v_pull"][...], picture) - r["v_dot"][...])).astype(B16)
        r["v_sum"][...] += dot_t(change, picture)
        to[:, block(at, 512)] = (dot(r["v_asked_t"][...], change) + dot(r["v_pull_t"][...], raised)).astype(B16)

    loop(4, lambda i: pixel_chunk((1 - c) * 4 + i, r["grad_far"], i))
    grad_copy = remote(r["grad_far"], r["grad_in"], sib)
    loop(4, lambda i: pixel_chunk(c * 4 + i, r["grad_own"], i))

    turned_sum = r["v_sum"][...] * scale_any
    r["y_late_own"][...] = jnp.zeros_like(r["y_late_own"])
    r["y_late_own"][:, :PAD] = (turned_sum * cross_scale).astype(B16)
    ready["y_late"] = [
        here(r["y_late_own"], r["y_late"].at[top]).wait,
        remote(r["y_late_own"], r["y_late"].at[low], sib).wait_recv,
    ]
    r["gains"][4:5, :PAD] = jnp.sum(
        r["v_asked"][...].astype(F32) * turned_sum + pull_f32 * r["v_mixed"][...], axis=0, keepdims=True
    )

    grad_copy.wait_recv()

    def grad_step(i):
        rows = block(i, 16)
        r["grad_own"][rows, :] = (r["grad_own"][rows, :].astype(F32) + r["grad_in"][rows, :].astype(F32)).astype(B16)

    loop(PAD // 16, grad_step)

    def homeward_of(k):
        to = lax.rem(s + k, seq)
        return remote_of(r["grad_own"].at[:, block(to, LANES)], r["home"].at[s], peer(k))

    homeward = [homeward_of(k) for k in range(seq)]
    stay = here_of(r["grad_own"].at[:, block(s, LANES)], r["home"].at[s])

    @pl.when(c != t)
    def _():
        homeward[0].start()

    @pl.when(c == t)
    def _():
        stay.start()

    for k in range(1, seq):
        homeward[k].start()

    await_all("x_attended", "y_out")
    product_rows(x4, r["y_out"], 512, "Q", 0)
    parts["Q", 0].begin()
    parts["Q", 1].begin()
    attended_copy.wait_recv()
    await_all("mixed_pixels")
    product_rows(x5, r["y_mixed_pixels"], 512, "Q", 2)
    await_all("x_late_x", "y_late")
    product_rows(x2, r["y_late"], 384, "Q", 2, add=True)
    parts["Q", 2].begin()
    parts["Q", 3].begin()
    advance("S", 3, 4, 5)
    advance("S", 0, 1, 2)
    advance("P")

    sent(*quarter_sends)
    latents, latgrad = r["v_feed_act"], r["v_feed_back"]
    load("latents_turned", latents)
    await_all("key_wide", "query_weight", "latents_turned")
    r["v_rows_in"][...] = dot(r["y_late_own"][:, :PAD], r["w_key"][...]).astype(B16)
    pull(r["v_rows_in"], up_w, to_tmp)

    def latents_after(rows, back):
        latgrad[rows, :] = (r["v_grad"][rows, :] + back).astype(B16)

    norm_grad(latents, r["norm_gains"][0:1, :], 0, latents_after)
    grad_move, grad_stay = remote_of(latgrad, r["latgrad_home"], peer(0)), here_of(latgrad, r["latgrad_home"])

    @pl.when(c != t)
    def _():
        grad_move.start()

    @pl.when(c == t)
    def _():
        grad_stay.start()

    gain_buf, gain_in = r["gain_buf"], r["gain_in"]
    gain_buf[0] = r["gains"][...]
    gain_steps = LINKS + ("C",)
    gain_copy = remote(gain_buf.at[0], gain_in.at[0], partner[gain_steps[0]])
    live = [parts[key] for key in parts]
    k = 0
    while live or k < 7:
        if k < 7:
            gain_copy.wait_recv()
            total = gain_buf[k] + gain_in[k]
            k += 1
            if k < 7:
                gain_buf[k] = total
                gain_copy = remote(gain_buf.at[k], gain_in.at[k], partner[gain_steps[k]])
            else:
                r["out_gains"][...] = total
        left_over = []
        for part in live:
            last = part.stage == 6
            part.advance()
            if not last:
                left_over.append(part)
        live = left_over

    @pl.when(c != t)
    def _():
        out_move.wait()
        grad_move.wait()
        homeward[0].wait()

    @pl.when(c == t)
    def _():
        out_stay.wait()
        grad_stay.wait()
        stay.wait()

    for k in range(1, seq):
        homeward[k].wait()
    for copy in waits:
        copy.wait_send()
    assert not ready, tuple(ready)
    assert used[0] <= sems[0] and used[1] <= sems[1], used


def back_and_reduce(given):
    names, scratch = [], []

    def room(name, shape, dtype=B16):
        names.append(name)
        scratch.append(pltpu.VMEM(shape, dtype))

    sems = (200, 96)
    names += list(BACK_HBM) + list(BACK_VMEM) + list(BACK_OUT)
    for name in ("send", "recv", "local"):
        names.append(name)
        scratch.append(pltpu.SemaphoreType.DMA((sems[1 if name == "local" else 0],)))
    for k in range(1, 6):
        room("x%d" % k, (512, WIDE))
    for name in ("feed_act", "feed_back", "mixed", "mixed_pixels", "mlp", "hidden", "out"):
        room("y_" + name, (512, 512))
    room("y_back", (512, 1536))
    room("y_late", (512, 384))
    room("y_late_own", (ROWS, 384))
    for name in ("w_down", "w_up"):
        room(name, (WIDE, WIDE))
    room("w_out_mine", (512, WIDE))
    for name in ("w_attend_own", "w_attend_far"):
        room(name, (3, WIDE, 256))
    for name in ("w_key", "w_value"):
        room(name, (PAD, WIDE))
    for name in ("v_tmp", "v_norm", "v_grad", "v_hidden"):
        room(name, (ROWS, WIDE), F32)
    for name in ("rows_in", "rows_give", "branch", "back", "feed_act", "feed_back", "latents_out"):
        room("v_" + name, (ROWS, WIDE))
    room("v_projected", (3, 512, 512))
    room("v_probs", (8, ROWS, 512))
    room("v_self_grad", (512, 512))
    room("v_picture", (PAD, 4096))
    room("v_mixed", (ROWS, PAD), F32)
    room("v_sum", (ROWS, PAD), F32)
    room("v_asked", (ROWS, PAD))
    room("v_pull", (ROWS, PAD))
    room("v_asked_t", (PAD, ROWS))
    room("v_pull_t", (PAD, ROWS))
    room("v_dot", (ROWS, 1), F32)
    for name in ("grad_own", "grad_far", "grad_in"):
        room(name, (PAD, 16 * LANES))
    room("gains", (8, WIDE), F32)
    room("gain_buf", (7, 8, WIDE), F32)
    room("gain_in", (7, 8, WIDE), F32)
    for set_, (firsts, depth) in SETS.items():
        for q in range(len(firsts)):
            key = "%s%d_" % (set_, q)
            room(key + "buf", (64, depth, 256))
            for k in range(6):
                room(key + "in%d" % k, (32 >> k, depth, 256))
    anywhere = pl.BlockSpec(memory_space=pl.ANY)
    vmem = pl.BlockSpec(memory_space=pltpu.VMEM)
    result = pl.pallas_call(
        functools.partial(back_kernel, tuple(names), sems),
        out_shape=[jax.ShapeDtypeStruct(*spec) for spec in BACK_OUT.values()],
        in_specs=[anywhere] * len(BACK_HBM) + [vmem] * len(BACK_VMEM),
        out_specs=[anywhere] * (len(BACK_OUT) - 1) + [vmem],
        scratch_shapes=scratch,
        compiler_params=pltpu.CompilerParams(collective_id=1, has_side_effects=True, vmem_limit_bytes=63 * MIB),
        name="back_and_reduce",
    )(*[given[name] for name in BACK_HBM + BACK_VMEM])
    return dict(zip(BACK_OUT, result))


FINISH_IN = ("pixels", "home", "out_S", "out_P", "out_Q", "latgrad_home", "latents_home", "key_wide")
FINISH_OUT = ("pixels_grad", "latents_grad", "latents_out")


def finish_kernel(*refs):
    refs = list(refs)

    def take(n):
        part = refs[:n]
        del refs[:n]
        return part

    hbm = dict(zip(FINISH_IN, take(len(FINISH_IN))))
    gain, gains = take(2)
    results = dict(zip(FINISH_OUT, take(len(FINISH_OUT))))
    gain_rows, pixelgain, query_grad, key_grad, value_grad, crossout, crossup, crossdown = take(8)
    selfattend, selfout, selfup, selfdown = take(4)
    vmem = dict(zip(FINISH_IN, take(len(FINISH_IN))))
    turned, high, grad, latgrad, sems = take(5)
    pixels, home = vmem["pixels"], vmem["home"]
    channels = pixels.shape[0]

    copies = {
        name: pltpu.make_async_copy(hbm[name], vmem[name], sems.at[k])
        for k, name in enumerate(FINISH_IN)
    }
    last = len(FINISH_IN)
    straight = pltpu.make_async_copy(vmem["latents_home"], results["latents_out"], sems.at[last])
    for copy in copies.values():
        copy.start()

    some = 9

    def features(i):
        return pl.ds(i * some, some)

    steps = channels // some
    copies["pixels"].wait()
    zeros = jnp.zeros(pixels.shape[1:], F32)
    average = lax.fori_loop(
        0, steps, lambda i, total: total + jnp.sum(pixels[features(i)].astype(F32), axis=0), zeros
    ) * (1.0 / channels)

    def square_step(i, total):
        centered = pixels[features(i)].astype(F32) - average
        return total + jnp.sum(centered * centered, axis=0)

    inverse = lax.rsqrt(lax.fori_loop(0, steps, square_step, zeros) * (1.0 / channels) + EPS)
    copies["home"].wait()
    for image in range(16):
        turned[pl.ds(image, PAD, stride=16), :] = home[image].astype(F32)

    def mean_step(i, totals):
        h = (pixels[features(i)].astype(F32) - average) * inverse
        rows = pl.ds(pl.multiple_of(i * (some * 16), 16), some * 16)
        a = turned[rows, :].reshape(some, 16, LANES) * gain[features(i)]
        high[features(i)] = h
        grad[features(i)] = a
        return totals[0] + jnp.sum(a, axis=0), totals[1] + jnp.sum(a * h, axis=0)

    first, second = lax.fori_loop(0, steps, mean_step, (zeros, zeros))
    first, second = first * (1.0 / channels), second * (1.0 / channels)

    def grad_step(i):
        grad[features(i)] = (grad[features(i)] - first - high[features(i)] * second) * inverse

    loop(steps, grad_step)
    pixels_out = pltpu.make_async_copy(grad, results["pixels_grad"], sems.at[last + 1])
    pixels_out.start()
    copies["latents_home"].wait()
    straight.start()
    copies["latgrad_home"].wait()
    latgrad[...] = vmem["latgrad_home"][...].astype(F32)
    latents_out = pltpu.make_async_copy(latgrad, results["latents_grad"], sems.at[last + 2])
    latents_out.start()

    for name in ("out_S", "out_P", "out_Q", "key_wide"):
        copies[name].wait()
    out_s, out_p, out_q = vmem["out_S"], vmem["out_P"], vmem["out_Q"]
    late = [out_q[:, 512:1024], out_q[:, 1536:2048]]
    query_grad[...] = dot(late[0][:, :PAD], vmem["key_wide"][...])
    key_grad[...] = late[1][:, :channels].astype(F32)
    value_grad[:, :LANES] = late[0][:, 384:].astype(F32)
    value_grad[:, LANES : 2 * LANES] = late[1][:, 384:].astype(F32)
    value_grad[:, 2 * LANES :] = late[0][:, 256:384].astype(F32)[:, 16 : 16 + channels - 2 * LANES]
    for k, ref in enumerate((crossdown, crossup)):
        for core in range(2):
            ref[:, pl.ds(512 * core, 512)] = out_p[:, pl.ds(1024 * core + 512 * k, 512)].astype(F32)
    for core in range(2):
        crossout[:, pl.ds(512 * core, 512)] = out_q[:, pl.ds(1024 * core, 512)].astype(F32)

    def item(k, core):
        return out_s[:, pl.ds(1536 * core + 256 * k, 256)].astype(F32)

    for core in range(2):
        columns = pl.ds(256 * core, 256)
        selfdown[:, columns] = item(0, core)
        selfup[:, columns] = item(1, core)
        selfout[:, columns] = item(2, core)
        for k in range(3):
            selfattend[k, :, columns] = item(3 + k, core)

    mine = 2 * lax.axis_index("seq") + lax.axis_index("tensor")
    rolled = pltpu.roll(gains[...], lax.rem(WIDE - 32 * mine, WIDE), 1)
    for k, ref in enumerate(gain_rows_of(gain_rows)):
        ref[...] = rolled[k : k + 1, :32]
    pixelgain[...] = gains[4:5, :channels]
    straight.wait()
    pixels_out.wait()
    latents_out.wait()


def gain_rows_of(ref):
    return [ref.at[pl.ds(k, 1)] for k in range(4)]


def finish(given):
    pixels = given["pixels"]
    channels, images, rows = pixels.shape
    small = [
        (4, 32),
        (1, channels),
        (32, WIDE),
        (32, channels),
        (32, channels),
        (32, WIDE),
        (32, WIDE),
        (32, WIDE),
        (3, 64, 512),
        (64, 512),
        (64, 512),
        (64, 512),
    ]
    anywhere = pl.BlockSpec(memory_space=pl.ANY)
    vmem = pl.BlockSpec(memory_space=pltpu.VMEM)
    return pl.pallas_call(
        finish_kernel,
        out_shape=[
            jax.ShapeDtypeStruct(pixels.shape, F32),
            jax.ShapeDtypeStruct((ROWS, WIDE), F32),
            jax.ShapeDtypeStruct((ROWS, WIDE), B16),
        ]
        + [jax.ShapeDtypeStruct(shape, F32) for shape in small],
        in_specs=[anywhere] * len(FINISH_IN) + [vmem] * 2,
        out_specs=[anywhere] * 3 + [vmem] * len(small),
        scratch_shapes=[pltpu.VMEM(given[name].shape, given[name].dtype) for name in FINISH_IN]
        + [
            pltpu.VMEM((PAD * images, rows), F32),
            pltpu.VMEM(pixels.shape, F32),
            pltpu.VMEM(pixels.shape, F32),
            pltpu.VMEM((ROWS, WIDE), F32),
            pltpu.SemaphoreType.DMA((len(FINISH_IN) + 3,)),
        ],
        compiler_params=pltpu.CompilerParams(vmem_limit_bytes=60 * MIB),
        name="finish",
    )(*[given[name] for name in FINISH_IN], given["pixel_gain"], given["out_gains"])


def shards(
    latents,
    pixels,
    crop_bounds,
    key_mask,
    query_gain,
    pixel_gain,
    cross_gain,
    attend_gain,
    feed_gain,
    query_weight,
    key_weight,
    value_weight,
    cross_out,
    cross_up,
    cross_down,
    self_attend,
    self_out,
    self_up,
    self_down,
    cotangent,
):
    channels = pixels.shape[2]
    given = {
        "pixels": jnp.transpose(pixels, (2, 0, 1)),
        "latents": latents[0],
        "cotangent": cotangent[0],
        "query_weight": query_weight,
        "key_weight": key_weight,
        "value_weight": value_weight,
        "cross_out": cross_out,
        "cross_up": cross_up,
        "cross_down": cross_down,
        "self_attend": self_attend,
        "self_out": self_out,
        "self_up": self_up,
        "self_down": self_down,
        "norm_gains": jnp.stack([query_gain, cross_gain, attend_gain, feed_gain]).astype(F32),
        "pixel_gain": jnp.broadcast_to(pixel_gain.astype(F32)[:, None, None], (channels, 1, LANES)),
        "key_mask": key_mask,
        "crop_bounds": crop_bounds,
    }
    given |= front(given)
    given |= back_and_reduce(given)
    (
        pixels_grad,
        latents_grad,
        latents_out,
        gain_rows,
        pixelgain,
        queryweight_grad,
        keyweight_grad,
        valueweight_grad,
        crossout_grad,
        crossup_grad,
        crossdown_grad,
        selfattend_grad,
        selfout_grad,
        selfup_grad,
        selfdown_grad,
    ) = finish(given)
    return (
        latents_out[None],
        latents_grad[None],
        jnp.transpose(pixels_grad, (1, 2, 0)),
        gain_rows[0],
        pixelgain[0] / pixel_gain.astype(F32),
        gain_rows[1],
        gain_rows[2],
        gain_rows[3],
        queryweight_grad,
        keyweight_grad.T,
        valueweight_grad.T,
        crossout_grad,
        crossup_grad,
        crossdown_grad,
        selfattend_grad,
        selfout_grad.T,
        selfup_grad,
        selfdown_grad.T,
    )


def solution(mesh):
    in_specs = (
        P(("batch", "seq"), "tensor", None),
        P("batch", ("seq", "tensor"), None),
        P(("batch", "seq"), None),
        P(("batch", "seq"), None),
        P(),
        P(),
        P(),
        P(),
        P(),
        P(),
        P(),
        P(),
        P(),
        P(),
        P(),
        P(None, None, "tensor"),
        P("tensor", None),
        P(None, "tensor"),
        P("tensor", None),
        P(("batch", "seq"), "tensor", None),
    )
    out_specs = (
        P(("batch", "seq"), "tensor", None),
        P(("batch", "seq"), "tensor", None),
        P("batch", ("seq", "tensor"), None),
        P(("seq", "tensor")),
        P(),
        P(("seq", "tensor")),
        P(("seq", "tensor")),
        P(("seq", "tensor")),
        P(("seq", "tensor"), None),
        P(None, ("seq", "tensor")),
        P(None, ("seq", "tensor")),
        P(("seq", "tensor"), None),
        P(("seq", "tensor"), None),
        P(("seq", "tensor"), None),
        P(None, "seq", "tensor"),
        P("tensor", "seq"),
        P("seq", "tensor"),
        P("tensor", "seq"),
    )
    return jax.shard_map(shards, mesh=mesh, in_specs=in_specs, out_specs=out_specs, check_vma=False)
```

```python
import functools
import math

import jax
import jax.numpy as jnp
from jax import lax
from jax.experimental import pallas as pl
from jax.experimental.pallas import tpu as pltpu
from jax.sharding import PartitionSpec as P

HEAD_WIDTH = 128
EPS = 1e-05
MASKED = -1000000000.0
MESH = pl.DeviceIdType.MESH
F32 = jnp.float32
B16 = jnp.bfloat16
LANES = 128
PAD = 272
WIDE = 1024
CYCLE = ("XA", "XB", "ZA", "ZB", "T")

def norm_parts(values):
    average = jnp.mean(values, axis=-1, keepdims=True)
    centered = values - average
    spread = jnp.mean(centered * centered, axis=-1, keepdims=True)
    inverse = lax.rsqrt(spread + EPS)
    return centered * inverse, inverse


def dot(a, b):
    return jnp.dot(a, b, preferred_element_type=F32)


def dot_t(a, b):
    return lax.dot_general(a, b, (((1,), (1,)), ((), ())), preferred_element_type=F32)


def tdot(a, b):
    return lax.dot_general(a, b, (((0,), (0,)), ((), ())), preferred_element_type=F32)


def flip(p):
    return p + 1 - 2 * lax.rem(p, 2)


def place():
    b, s, t = lax.axis_index("batch"), lax.axis_index("seq"), lax.axis_index("tensor")
    return lax.div(b, 2), lax.rem(b, 2), s, t


MIB = 1024 * 1024
ROWS = 256
GELU_K = math.sqrt(2.0 / math.pi)


def gelu(u):
    return 0.5 * u * (1.0 + jnp.tanh(GELU_K * (u + 0.044715 * u * u * u)))


def gelu_slope(u):
    th = jnp.tanh(GELU_K * (u + 0.044715 * u * u * u))
    return 0.5 * (1.0 + th) + 0.5 * u * (1.0 - th * th) * GELU_K * (1.0 + 3.0 * 0.044715 * u * u)


def loop(n, step):
    lax.fori_loop(0, n, lambda i, carry: (step(i), carry)[1], 0)


def row_of(ref):
    return ref[...].astype(F32).reshape(1, ref.shape[0])


def per_feature(gain_ref, out_ref):
    channels = gain_ref.shape[0]
    wide = jnp.concatenate([row_of(gain_ref), jnp.zeros((1, 384 - channels), F32)], axis=1)
    out_ref[...] = jnp.broadcast_to(wide, (LANES, 384)).T


def block(i, n):
    return pl.ds(pl.multiple_of(i * n, n), n)


FRONT_HBM = (
    ("pixels", "latents", "cotangent", "self_attend", "self_out", "self_up", "self_down")
    + ("query_weight", "cross_out", "cross_up", "cross_down")
)
FRONT_VMEM = ("query_gain", "cross_gain", "attend_gain", "feed_gain", "pixel_gain", "key_weight", "value_weight", "key_mask", "crop_bounds")
FRONT_OUT = {
    "cot": ((512, WIDE), B16),
    "cross_act": ((512, WIDE), B16),
    "cross_in": ((512, WIDE), B16),
    "attended": ((512, WIDE), B16),
    "late_x": ((512, WIDE), B16),
    "mixed_pixels": ((512, 512), B16),
    "mixed": ((512, 512), B16),
    "attend_in": ((512, WIDE), B16),
    "projected": ((3, 512, 512), B16),
    "probs": ((8, ROWS, 512), B16),
    "out_mine": ((512, WIDE), B16),
    "attend_far": ((3, WIDE, 256), B16),
    "up_far": ((WIDE, 512), B16),
    "down_far": ((512, WIDE), B16),
    "after_mlp": ((ROWS, WIDE), F32),
    "after_attend": ((ROWS, WIDE), F32),
    "cross_hidden": ((ROWS, WIDE), F32),
    "after_cross": ((ROWS, WIDE), F32),
    "latents_turned": ((ROWS, WIDE), B16),
    "picture": ((PAD, 4096), B16),
    "raised": ((8, ROWS, 512), B16),
    "mixed_f32": ((ROWS, PAD), F32),
    "asked": ((ROWS, PAD), B16),
    "key_wide": ((PAD, WIDE), B16),
    "value_wide": ((PAD, WIDE), B16),
    "inverse_total": ((ROWS, 1), F32),
    "any_kept": ((1, 1), F32),
    "norm_gains": ((8, WIDE), F32),
}
FRONT_OUT_VMEM = ("inverse_total", "any_kept", "norm_gains")


def front_kernel(names, sems, *refs):
    l, c, s, t = place()
    seq = 16
    r = dict(zip(names, refs))
    send, recv, local = r["send"], r["recv"], r["local"]
    cross_scale = 1.0 / math.sqrt(WIDE)
    self_scale = 1.0 / math.sqrt(HEAD_WIDTH)
    sib = (2 * l + 1 - c, s, t)
    over = (2 * (1 - l) + c, s, 1 - t)

    def peer(k):
        return (2 * l + t, lax.rem(s + k, seq), c)

    barrier = pltpu.get_barrier_semaphore()
    for device in (sib, over):
        pl.semaphore_signal(barrier, inc=1, device_id=device, device_id_type=MESH)
    def plane(k):
        return (2 * l + c, lax.rem(s + k, seq), t)

    for k in range(1, seq):
        pl.semaphore_signal(barrier, inc=1, device_id=peer(k), device_id_type=MESH)
        pl.semaphore_signal(barrier, inc=1, device_id=plane(k), device_id_type=MESH)

    @pl.when(c != t)
    def _():
        pl.semaphore_signal(barrier, inc=1, device_id=peer(0), device_id_type=MESH)
        pl.semaphore_wait(barrier, 1 + 2 * seq)

    @pl.when(c == t)
    def _():
        pl.semaphore_wait(barrier, 2 * seq)

    used = [0, 0]
    waits, stores = [], []

    def remote_of(src, dst, device):
        i = used[0]
        used[0] += 1
        return pltpu.make_async_remote_copy(
            src_ref=src, dst_ref=dst, send_sem=send.at[i], recv_sem=recv.at[i], device_id=device, device_id_type=MESH
        )

    def remote(src, dst, device):
        copy = remote_of(src, dst, device)
        copy.start()
        waits.append(copy)
        return copy

    def here_of(src, dst):
        i = used[1]
        used[1] += 1
        return pltpu.make_async_copy(src, dst, local.at[i])

    def here(src, dst):
        copy = here_of(src, dst)
        copy.start()
        return copy

    def store(name, src):
        stores.append(here(src, r[name]))

    top, low = pl.ds(0, ROWS), pl.ds(ROWS, ROWS)
    shared = []

    def share(name, src, give=None):
        stores.append(here(src, r[name].at[top]))
        shared.append(remote(src if give is None else give, r[name].at[low], sib))

    ready = {}

    def await_all(*wanted):
        for name in wanted:
            for wait in ready.pop(name, ()):
                wait()

    base = pl.multiple_of(c * (seq * LANES), LANES)
    far = pl.multiple_of(t * (seq * LANES), LANES)
    picture = r["v_picture"]

    def away_of(k):
        return remote_of(
            r["v_home"].at[lax.rem(s + k, seq)],
            picture.at[:, pl.ds(pl.multiple_of(far + s * LANES, LANES), LANES)],
            peer(k),
        )

    away = [away_of(k) for k in range(seq)]
    lat_move, cot_move = remote_of(r["v_lat_own"], r["v_lat"], peer(0)), remote_of(r["cotangent"], r["v_cot"], peer(0))
    kept_move = remote_of(r["v_kept_own"], r["v_kept"], sib)
    cot_stay = here_of(r["cotangent"], r["v_cot"])
    lat_copy = here(r["latents"], r["v_lat_own"])
    asked_move = remote_of(r["v_asked_own"], r["v_asked"], peer(0))
    kept_stay = here_of(r["v_kept_own"], r["v_kept"])
    picture_stay = here_of(r["v_home"].at[s], picture.at[:, pl.ds(pl.multiple_of(base + s * LANES, LANES), LANES)])

    own256 = 256 * c
    own_columns = pl.ds(pl.multiple_of(own256, LANES), 256)
    attend_far, out_w, up_far, down_far = r["w_attend_far"], r["w_out"], r["w_up_far"], r["w_down_far"]
    left = pl.ds(0, 256)

    def rows16(base_row, piece):
        return pl.ds(pl.multiple_of(base_row + 16 * piece, 16), 16)

    shares = {
        "attend": (lambda p: r["self_attend"].at[:, block(p, 64), own_columns], lambda p: attend_far.at[:, block(p, 64)]),
        "out": (lambda p: r["self_out"].at[rows16(own256, p)], lambda p: out_w.at[rows16(256, p)]),
        "up": (lambda p: r["self_up"].at[block(p, 64), own_columns], lambda p: up_far.at[block(p, 64), left]),
        "down": (lambda p: r["self_down"].at[rows16(own256, p)], lambda p: down_far.at[rows16(0, p)]),
    }
    first_piece = {name: remote(src(s), dst(s), over) for name, (src, dst) in shares.items()}
    @pl.when(c == t)
    def _():
        cot_stay.start()

    pixels_copy = here(r["pixels"], r["v_pixels"])
    r["norm_gains"][...] = jnp.concatenate(
        [row_of(r[name + "_gain"]) for name in ("query", "cross", "attend", "feed")] + [jnp.zeros((4, WIDE), F32)],
        axis=0,
    )

    pieces = {}

    def spread_pieces(*wanted):
        for name in wanted:
            first_piece[name].wait_recv()
            dst = shares[name][1]
            pieces[name] = [remote(dst(s), dst(s), plane(k)) for k in range(1, seq)]

    def gathered(name):
        for copy in pieces[name]:
            copy.wait_recv()

    whole = {
        "out": (out_w.at[pl.ds(256, 256)], out_w.at[pl.ds(768, 256)]),
        "up": (up_far.at[:, left], up_far.at[:, pl.ds(256, 256)]),
        "down": (down_far.at[left], down_far.at[pl.ds(256, 256)]),
    }
    sib_quarter = {}

    def gather_pieces(*wanted):
        for name in wanted:
            gathered(name)
            sib_quarter[name] = remote(*whole[name], sib)

    def arrived(*wanted):
        for name in wanted:
            sib_quarter[name].wait_recv()

    pixels_copy.wait()
    pixels, normed = r["v_pixels"], r["v_normed"]
    channels = pixels.shape[0]
    some = 9

    def features(i):
        return pl.ds(i * some, some)

    def sum_step(i, total):
        return total + jnp.sum(pixels[features(i)].astype(F32), axis=0)

    per_feature(r["pixel_gain"], r["v_gain"])
    zeros = jnp.zeros(pixels.shape[1:], F32)
    average = lax.fori_loop(0, channels // some, sum_step, zeros) * (1.0 / channels)

    def square_step(i, total):
        centered = pixels[features(i)].astype(F32) - average
        return total + jnp.sum(centered * centered, axis=0)

    spread = lax.fori_loop(0, channels // some, square_step, zeros) * (1.0 / channels)
    inverse = lax.rsqrt(spread + EPS)

    def norm_step(i):
        value = (pixels[features(i)].astype(F32) - average) * inverse * r["v_gain"][features(i), :][:, None, :]
        normed[pl.ds(pl.multiple_of(i * (some * 16), 16), some * 16), :] = value.reshape(some * 16, LANES)

    loop(channels // some, norm_step)
    normed[channels * 16 :, :] = jnp.zeros(((PAD - channels) * 16, LANES), F32)

    def turn_image(k):
        image = lax.rem(s + k, seq)
        r["v_home"][image] = normed[pl.ds(image, PAD, stride=16), :].astype(B16)

    turn_image(0)

    @pl.when(c != t)
    def _():
        away[0].start()

    @pl.when(c == t)
    def _():
        picture_stay.start()

    for k in range(1, seq):
        turn_image(k)
        away[k].start()

    start, count = r["crop_bounds"][:, 0:1], r["crop_bounds"][:, 1:2]
    lanes = lax.broadcasted_iota(jnp.int32, (1, LANES), 1)
    for k in range(2 * seq):
        row = lanes + k * LANES
        keep = (row >= start) & (row < start + count) & (r["key_mask"][:, pl.ds(k * LANES, LANES)] == 1)
        to = pl.ds(((k % 2) * seq + k // 2) * LANES, LANES)
        r["v_kept_own"][:, to] = jnp.broadcast_to(jnp.where(keep, 1.0, 0.0), (8, LANES))

    @pl.when(c == t)
    def _():
        kept_stay.start()
        kept_move.start()

    for name in ("key", "value"):
        ref, to = r[name + "_weight"], r["w_" + name]
        to[:256, :] = ref[:256, :]
        to[256:, :] = jnp.concatenate(
            [ref[256:channels, :].astype(F32), jnp.zeros((PAD - channels, WIDE), F32)], axis=0
        ).astype(B16)
        store(name + "_wide", to)
    for name, to in (
        ("query_weight", "w_query"),
        ("cross_out", "w_cross_out"),
        ("cross_up", "w_cross_up"),
        ("cross_down", "w_cross_down"),
    ):
        ready[to] = [here(r[name], r[to]).wait]
    ready["attend_own"] = [here(r["self_attend"].at[:, :, own_columns], r["w_attend_own"]).wait]
    ready["out_own"] = [
        here(r["self_out"].at[pl.ds(pl.multiple_of(own256, LANES), 256)], out_w.at[pl.ds(0, 256)]).wait,
        here(r["self_out"].at[pl.ds(pl.multiple_of(256 - own256, LANES), 256)], out_w.at[pl.ds(512, 256)]).wait,
    ]

    def norm_rows(value_ref, gain, out_ref, also=None):
        def step(i):
            rows = block(i, 64)
            v = value_ref[rows, :].astype(F32)
            high, _ = norm_parts(v)
            out_ref[rows, :] = (high * gain).astype(B16)

        loop(ROWS // 64, step)

    def each256(n, step):
        loop(n // 256, lambda i: step(block(i, 256)))

    query_low, queries = r["v_query_low"], r["v_queries"]

    def ask(lat_ref):
        norm_rows(lat_ref, r["norm_gains"][0:1, :], query_low)

        def query_step(columns):
            queries[:, columns] = dot(query_low[...], r["w_query"][:, columns]).astype(B16)

        each256(WIDE, query_step)

    lat_copy.wait()
    await_all("w_query")
    ask(r["v_lat_own"])
    r["v_asked_own"][...] = (dot_t(queries[...], r["w_key"][...]) * cross_scale).astype(B16)

    @pl.when(c != t)
    def _():
        asked_move.start()
        lat_move.start()

    @pl.when(c == t)
    def _():
        r["v_asked"][...] = r["v_asked_own"][...]
        r["v_lat"][...] = r["v_lat_own"][...]

    spread_pieces("attend")

    def chunk(k):
        return picture.at[:, pl.ds(pl.multiple_of(base + lax.rem(s - k + seq, seq) * LANES, LANES), LANES)]

    @pl.when(c != t)
    def _():
        away[0].wait_recv()
        kept_move.wait_recv()

    @pl.when(c == t)
    def _():
        picture_stay.wait()
        kept_stay.wait()

    passed = [remote(chunk(0), chunk(0), sib)]
    for k in range(1, seq):
        away[k].wait_recv()
        passed.append(remote(chunk(k), chunk(k), sib))
    for copy in passed:
        copy.wait_recv()
    store("picture", picture)

    @pl.when(c != t)
    def _():
        cot_move.start()

    spread_pieces("out", "up", "down")
    @pl.when(c != t)
    def _():
        asked_move.wait_recv()

    store("asked", r["v_asked"])
    scores, raised = r["v_scores"], r["v_raised"]
    r["v_top"][...] = jnp.full((ROWS, 1), -3.0e38, F32)
    r["v_total"][...] = jnp.zeros((ROWS, 1), F32)
    r["v_mixed"][...] = jnp.zeros_like(r["v_mixed"])
    r["any_kept"][...] = jnp.max(r["v_kept"][0:1, :], axis=-1, keepdims=True)

    def score_step(i):
        columns = block(i, 512)
        value = dot(r["v_asked"][...], picture[:, columns])
        value = jnp.where(r["v_kept"][0:1, columns] > 0.5, value, MASKED)
        scores[:, columns] = value
        r["v_top"][...] = jnp.maximum(r["v_top"][...], jnp.max(value, axis=-1, keepdims=True))

    loop(8, score_step)

    def raise_step(i):
        columns = block(i, 512)
        value = jnp.exp(scores[:, columns] - r["v_top"][...])
        r["v_total"][...] += jnp.sum(value, axis=-1, keepdims=True)
        value = value.astype(B16)
        raised[i] = value
        r["v_mixed"][...] += dot_t(value, picture[:, columns])

    loop(8, raise_step)
    store("raised", raised)
    inverse_total = 1.0 / r["v_total"][...]
    r["inverse_total"][...] = inverse_total
    mixed = r["v_mixed"][...] * inverse_total
    r["v_mixed"][...] = mixed
    store("mixed_f32", r["v_mixed"])
    r["v_mixed_wide"][...] = jnp.zeros_like(r["v_mixed_wide"])
    r["v_mixed_wide"][:, :PAD] = mixed
    tail = pltpu.roll(r["v_mixed_wide"][:, 256:384], 16, 1).astype(B16)
    for name, core in (("mixed_pixels", c), ("mixed_pixels_give", 1 - c)):
        ref = r["v_" + name]
        ref[:, :256] = jnp.zeros((ROWS, 256), B16)
        ref[:, 256:384] = tail
        ref[:, 384:] = r["v_mixed_wide"][:, pl.ds(pl.multiple_of(LANES * core, LANES), LANES)].astype(B16)
    share("mixed_pixels", r["v_mixed_pixels"], r["v_mixed_pixels_give"])
    await_all("w_cross_out")
    r["v_attended"][...] = dot(mixed.astype(B16), r["w_value"][...]).astype(B16)
    share("attended", r["v_attended"])

    @pl.when(c != t)
    def _():
        lat_move.wait_recv()

    store("latents_turned", r["v_lat"])

    def out_step(columns):
        r["v_after_cross"][:, columns] = r["v_lat"][:, columns].astype(F32) + dot(
            r["v_attended"][...], r["w_cross_out"][:, columns]
        )

    each256(WIDE, out_step)
    store("after_cross", r["v_after_cross"])
    norm_rows(r["v_after_cross"], r["norm_gains"][1:2, :], r["v_cross_in"])
    share("cross_in", r["v_cross_in"])
    await_all("w_cross_up", "w_cross_down")

    def up_step(columns):
        hidden = dot(r["v_cross_in"][...], r["w_cross_up"][:, columns])
        r["v_hidden"][:, columns] = hidden
        r["v_cross_act"][:, columns] = gelu(hidden).astype(B16)

    each256(WIDE, up_step)
    store("cross_hidden", r["v_hidden"])
    share("cross_act", r["v_cross_act"])

    def down_step(columns):
        r["v_after_mlp"][:, columns] = r["v_after_cross"][:, columns] + dot(
            r["v_cross_act"][...], r["w_cross_down"][:, columns]
        )

    each256(WIDE, down_step)
    store("after_mlp", r["v_after_mlp"])

    attend_in = r["v_attend_in"]
    norm_rows(r["v_after_mlp"], r["norm_gains"][2:3, :], attend_in)
    attend_copy = remote(attend_in.at[top], attend_in.at[low], sib)
    @pl.when(c != t)
    def _():
        ask(r["v_lat"])

    late = r["late_x"]
    late_keep = [here_of(src, late.at[top]) for src in (query_low, queries)]
    late_give = [remote_of(src, late.at[low], sib) for src in (queries, query_low)]

    @pl.when(c == 0)
    def _():
        late_keep[0].start()
        late_give[0].start()

    @pl.when(c == 1)
    def _():
        late_keep[1].start()
        late_give[1].start()

    await_all("attend_own")
    attend_copy.wait_recv()
    store("attend_in", attend_in)
    projected, probs = r["v_projected"], r["v_probs"]

    def project(weights, at):
        for k in range(3):
            projected[k, :, pl.ds(at, 256)] = dot(attend_in[...], weights[k]).astype(B16)

    def attend(h):
        columns = block(h, HEAD_WIDTH)
        dotted = dot_t(projected[0, :, columns], projected[1, :, columns]) * self_scale
        value = jnp.exp(dotted - jnp.max(dotted, axis=-1, keepdims=True))
        value = (value * (1.0 / jnp.sum(value, axis=-1, keepdims=True))).astype(B16)
        probs[2 * h] = value[:ROWS]
        probs[2 * h + 1] = value[ROWS:]
        r["v_self"][:, columns] = dot(value, projected[2, :, columns]).astype(B16)

    project(r["w_attend_own"], 0)
    loop(2, attend)
    gathered("attend")
    project(attend_far, 256)
    loop(2, lambda i: attend(i + 2))
    store("mixed", r["v_self"])
    self_copy = remote(r["v_self"].at[low], r["v_self_in"], sib)
    store("projected", projected)
    store("probs", probs)
    store("attend_far", attend_far)

    @pl.when(c != t)
    def _():
        cot_move.wait_recv()

    @pl.when(c == t)
    def _():
        cot_stay.wait()

    share("cot", r["v_cot"])
    gather_pieces("out")
    await_all("out_own")
    arrived("out")
    store("out_mine", out_w.at[pl.ds(0, 512)])
    self_copy.wait_recv()

    def attended_step(columns):
        r["v_after_attend"][:, columns] = (
            r["v_after_mlp"][:, columns]
            + dot(r["v_self"][top, :], out_w[pl.ds(0, 512), columns])
            + dot(r["v_self_in"][...], out_w[pl.ds(512, 512), columns])
        )

    each256(WIDE, attended_step)
    store("after_attend", r["v_after_attend"])
    gather_pieces("up", "down")
    arrived("up", "down")
    store("up_far", up_far)
    store("down_far", down_far)

    @pl.when(c != t)
    def _():
        lat_move.wait_send()
        asked_move.wait_send()
        cot_move.wait_send()
        away[0].wait_send()

    @pl.when(c == t)
    def _():
        kept_move.wait_send()

    @pl.when(c == 0)
    def _():
        late_keep[0].wait()
        late_give[0].wait_send()
        late_give[1].wait_recv()

    @pl.when(c == 1)
    def _():
        late_keep[1].wait()
        late_give[1].wait_send()
        late_give[0].wait_recv()

    for k in range(1, seq):
        away[k].wait_send()
    for copy in shared:
        copy.wait_recv()
    for copy in waits:
        copy.wait_send()
    for copy in stores:
        copy.wait()
    assert not ready, tuple(ready)
    assert used[0] <= sems[0] and used[1] <= sems[1], used


def front(given):
    names, scratch = [], []

    def room(name, shape, dtype=B16):
        names.append(name)
        scratch.append(pltpu.VMEM(shape, dtype))

    sems = (112, 38)
    names += list(FRONT_HBM) + list(FRONT_VMEM) + list(FRONT_OUT)
    for name in ("send", "recv", "local"):
        names.append(name)
        scratch.append(pltpu.SemaphoreType.DMA((sems[1 if name == "local" else 0],)))
    for name in ("query", "cross_out", "cross_up", "cross_down", "out"):
        room("w_" + name, (WIDE, WIDE))
    for name in ("key", "value"):
        room("w_" + name, (PAD, WIDE))
    for name in ("attend_own", "attend_far"):
        room("w_" + name, (3, WIDE, 256))
    room("w_up_far", (WIDE, 512))
    room("w_down_far", (512, WIDE))
    room("v_picture", (PAD, 4096))
    room("v_pixels", (261, 16, LANES))
    room("v_normed", (PAD * 16, LANES), F32)
    room("v_gain", (384, LANES), F32)
    room("v_home", (16, PAD, LANES))
    room("v_kept", (8, 4096), F32)
    room("v_kept_own", (8, 4096), F32)
    room("v_scores", (ROWS, 4096), F32)
    room("v_raised", (8, ROWS, 512))
    room("v_asked_own", (ROWS, PAD))
    for name in ("lat_own", "lat", "cot", "query_low", "queries", "attended", "cross_in", "cross_act"):
        room("v_" + name, (ROWS, WIDE))
    for name in ("after_cross", "hidden", "after_mlp", "after_attend"):
        room("v_" + name, (ROWS, WIDE), F32)
    room("v_attend_in", (512, WIDE))
    room("v_projected", (3, 512, 512))
    room("v_probs", (8, ROWS, 512))
    room("v_self", (512, 512))
    room("v_self_in", (ROWS, 512))
    room("v_asked", (ROWS, PAD))
    room("v_top", (ROWS, 1), F32)
    room("v_total", (ROWS, 1), F32)
    room("v_mixed", (ROWS, PAD), F32)
    room("v_mixed_wide", (ROWS, 384), F32)
    room("v_mixed_pixels", (ROWS, 512))
    room("v_mixed_pixels_give", (ROWS, 512))
    anywhere = pl.BlockSpec(memory_space=pl.ANY)
    vmem = pl.BlockSpec(memory_space=pltpu.VMEM)
    result = pl.pallas_call(
        functools.partial(front_kernel, tuple(names), sems),
        out_shape=[jax.ShapeDtypeStruct(*spec) for spec in FRONT_OUT.values()],
        in_specs=[anywhere] * len(FRONT_HBM) + [vmem] * len(FRONT_VMEM),
        out_specs=[vmem if name in FRONT_OUT_VMEM else anywhere for name in FRONT_OUT],
        scratch_shapes=scratch,
        compiler_params=pltpu.CompilerParams(collective_id=0, has_side_effects=True, vmem_limit_bytes=63 * MIB),
        name="front",
    )(*[given[name] for name in FRONT_HBM + FRONT_VMEM])
    return dict(zip(FRONT_OUT, result))


X, Z, Y = ("XA", "XB"), ("ZA", "ZB"), ("L", "O")
def rotated(k):
    order = ("XA", "ZA", "L", "XB", "ZB", "O")
    return tuple((bit,) for bit in order[k:] + order[:k])


SETS = {
    "S": (tuple(rotated(k) for k in range(6)), 32),
    "P": (tuple(rotated(k) for k in (0, 3, 1, 4)), 16),
    "Q": (tuple(rotated(k) for k in (2, 5, 0, 3)), 16),
}
BOTH = {X: "X2", Z: "Z2", Y: "T"}
BACK_HBM = (
    ("cot", "cross_act", "cross_in", "attended", "late_x", "mixed_pixels", "mixed", "attend_in", "projected", "probs")
    + ("out_mine", "attend_far", "up_far", "down_far", "after_mlp", "after_attend", "cross_hidden", "after_cross")
    + ("latents_turned", "picture", "raised", "mixed_f32", "asked", "self_attend", "self_up", "self_down")
    + ("cross_down", "cross_up", "cross_out", "query_weight", "key_wide", "value_wide")
)
BACK_VMEM = ("inverse_total", "any_kept", "norm_gains")
BACK_OUT = {
    "out_S": ((64, 2 * 6 * 256), B16),
    "out_P": ((32, 2 * 4 * 256), B16),
    "out_Q": ((32, 2 * 4 * 256), B16),
    "home": ((16, PAD, LANES), B16),
    "latents_home": ((ROWS, WIDE), B16),
    "latgrad_home": ((ROWS, WIDE), B16),
    "out_gains": ((8, WIDE), F32),
}


def back_kernel(names, sems, *refs):
    l, c, s, t = place()
    z, x = lax.div(s, 4), lax.rem(s, 4)
    seq = 16
    r = dict(zip(names, refs))
    send, recv, local = r["send"], r["recv"], r["local"]
    cross_scale = 1.0 / math.sqrt(WIDE)
    self_scale = 1.0 / math.sqrt(HEAD_WIDTH)

    partner = {
        "XA": (2 * l + c, z * 4 + flip(x), t),
        "XB": (2 * l + c, z * 4 + 3 - x, t),
        "ZA": (2 * l + c, flip(z) * 4 + x, t),
        "ZB": (2 * l + c, (3 - z) * 4 + x, t),
        "L": (2 * (1 - l) + c, s, t),
        "O": (2 * (1 - l) + c, s, 1 - t),
        "X2": (2 * l + c, z * 4 + lax.rem(x + 2, 4), t),
        "Z2": (2 * l + c, lax.rem(z + 2, 4) * 4 + x, t),
        "T": (2 * l + c, s, 1 - t),
        "C": (2 * l + 1 - c, s, t),
        "D": (2 * (1 - l) + 1 - c, s, t),
    }

    def peer(k):
        return (2 * l + t, lax.rem(s + k, seq), c)

    barrier = pltpu.get_barrier_semaphore()
    for device in partner.values():
        pl.semaphore_signal(barrier, inc=1, device_id=device, device_id_type=MESH)
    def plane(k):
        return (2 * l + c, lax.rem(s + k, seq), t)

    for k in range(1, seq):
        pl.semaphore_signal(barrier, inc=1, device_id=plane(k), device_id_type=MESH)

    @pl.when(c != t)
    def _():
        pl.semaphore_signal(barrier, inc=1, device_id=peer(0), device_id_type=MESH)
        pl.semaphore_wait(barrier, len(partner) + seq)

    @pl.when(c == t)
    def _():
        pl.semaphore_wait(barrier, len(partner) + seq - 1)

    used = [0, 0]
    waits = []

    def remote_of(src, dst, device):
        i = used[0]
        used[0] += 1
        return pltpu.make_async_remote_copy(
            src_ref=src, dst_ref=dst, send_sem=send.at[i], recv_sem=recv.at[i], device_id=device, device_id_type=MESH
        )

    def remote(src, dst, device):
        copy = remote_of(src, dst, device)
        copy.start()
        waits.append(copy)
        return copy

    def sent(*copies):
        for copy in copies:
            copy.wait_send()
            waits[:] = [other for other in waits if other is not copy]

    def here_of(src, dst):
        i = used[1]
        used[1] += 1
        return pltpu.make_async_copy(src, dst, local.at[i])

    def here(src, dst):
        copy = here_of(src, dst)
        copy.start()
        return copy

    ready = {}

    def await_all(*wanted):
        for name in wanted:
            for wait in ready.pop(name):
                wait()

    def load(name, to, key=None):
        ready[key or name] = [here(r[name], to).wait]

    sib = partner["C"]
    top, low = pl.ds(0, ROWS), pl.ds(ROWS, ROWS)
    keep512 = pl.ds(pl.multiple_of(512 * c, LANES), 512)
    give512 = pl.ds(pl.multiple_of(512 * (1 - c), LANES), 512)
    keep256 = pl.ds(pl.multiple_of(256 * c, LANES), 256)
    give256 = pl.ds(pl.multiple_of(256 * (1 - c), LANES), 256)
    left, right = pl.ds(0, 256), pl.ds(256, 256)
    x1, x2, x3, x4, x5 = (r["x%d" % k] for k in range(1, 6))
    up_w, down_w, probs = r["w_up"], r["w_down"], r["v_probs"]

    load("after_attend", r["v_norm"])
    ready["up"] = [
        here(r["self_up"], up_w.at[:, pl.ds(0, 512)]).wait,
        here(r["up_far"], up_w.at[:, pl.ds(512, 512)]).wait,
    ]
    load("cot", x1)
    ready["down"] = [
        here(r["self_down"], down_w.at[pl.ds(0, 512)]).wait,
        here(r["down_far"], down_w.at[pl.ds(512, 512)]).wait,
    ]
    load("out_mine", r["w_out_mine"])
    load("projected", r["v_projected"])
    load("probs", probs)
    load("mixed", r["y_mixed"])
    ready["attend_own"] = [
        here(r["self_attend"].at[:, :, keep256], r["w_attend_own"]).wait
    ]
    load("attend_far", r["w_attend_far"])
    load("attend_in", x4)
    load("cross_hidden", r["v_hidden"])
    load("value_wide", r["w_value"])
    load("key_wide", r["w_key"])
    load("picture", r["v_picture"])
    load("mixed_f32", r["v_mixed"])
    load("asked", r["v_asked"])
    load("mixed_pixels", r["y_mixed_pixels"])

    class Part:
        def __init__(self, set_, q):
            self.stages, self.depth = SETS[set_][0][q], SETS[set_][1]
            self.set, self.q, self.stage, self.n = set_, q, -1, 64
            self.key = "%s%d_" % (set_, q)
            self.cur = r[self.key + "buf"]
            order = [bit for stage in self.stages for bit in stage]
            self.weight = {bit: 32 >> k for k, bit in enumerate(order)}
            self.done = False

        def index(self, **bits):
            return sum(value * self.weight[bit] for bit, value in bits.items())

        def begin(self):
            self.stage += 1
            k, n = self.stage, self.n
            if k < len(self.stages):
                bits = self.stages[k]
                self.into = r[self.key + "in%d" % k]
                if len(bits) == 1:
                    ways = bits
                else:
                    ways = (bits[1], bits[0], BOTH[bits])
                m = n // (len(ways) + 1)
                self.n = m
                self.copies = [
                    remote(self.cur.at[pl.ds((j + 1) * m, m)], self.into.at[j], partner[way])
                    for j, way in enumerate(ways)
                ]
                return
            count = len(SETS[self.set][0])
            dst = r["out_" + self.set].at[
                pl.ds(pl.multiple_of(l * self.depth, self.depth), self.depth),
                pl.ds(pl.multiple_of((count * c + self.q) * 256, LANES), 256),
            ]
            self.copies = [remote(self.cur.at[0], dst, partner[way]) for way in ("L", "C", "D")]
            self.copy_here = here(self.cur.at[0], dst)

        def finish(self):
            for copy in self.copies:
                copy.wait_recv()
            if self.stage == len(self.stages):
                self.copy_here.wait()
                self.done = True
                return
            cur, into, ways = self.cur, self.into, len(self.copies)
            m = min(self.n, 4)

            def step(i):
                rows = pl.ds(i * m, m)
                total = cur[rows].astype(F32)
                for j in range(ways):
                    total = total + into[j, rows].astype(F32)
                cur[rows] = total.astype(B16)

            if self.n > m:
                loop(self.n // m, step)
            else:
                step(0)

        def advance(self):
            if self.done:
                return
            self.finish()
            if not self.done:
                self.begin()

    parts = {(set_, q): Part(set_, q) for set_ in SETS for q in range(len(SETS[set_][0]))}

    def advance(set_, *some):
        for q in some or range(len(SETS[set_][0])):
            parts[set_, q].advance()

    def product(x_ref, y_ref, width, pieces, add=False):
        span = 512 if width <= 512 else 256
        per = span // 256

        def step(i):
            columns = block(i, span)
            whole = tdot(x_ref[:, columns], y_ref[...])
            for a in range(per):
                zz = i * per + a
                zb = lax.rem(lax.div(z, 2) + lax.div(zz, 2), 2)
                za = lax.rem(lax.rem(z, 2) + lax.rem(zz, 2) + zb, 2)
                for xx in range(4):
                    xb = lax.rem(lax.div(x, 2) + xx // 2, 2)
                    xa = lax.rem(lax.rem(x, 2) + xx % 2 + xb, 2)
                    at = (a * 4 + xx) * 64
                    for part, src, width_, half in pieces:
                        for k in range(64 // part.depth):
                            ll = k % 2
                            o = half if half is not None else lax.rem(k // 2 + t, 2)
                            idx = part.index(ZA=za, ZB=zb, XA=xa, XB=xb, O=o, L=lax.rem(ll + l + o, 2))
                            value = whole[at + k * part.depth : at + (k + 1) * part.depth, src : src + width_]
                            to = pl.ds(0, width_)
                            if add:
                                value = value + part.cur[idx, :, to].astype(F32)
                            part.cur[idx, :, to] = value.astype(B16)

        loop(WIDE // span, step)

    def heads(q, at=0):
        return [("S", q, at, 0), ("S", q, at + 256, 1)]

    def product_heads(x_ref, y_ref, width, wanted):
        product(x_ref, y_ref, width, [(parts["S", q], at, 256, half) for _, q, at, half in wanted])

    def product_rows(x_ref, y_ref, width, set_, q, add=False):
        pieces, at = [], 0
        while at < width:
            n = min(256, width - at)
            pieces.append((parts[set_, q + at // 256], at, n, None))
            at += n
        product(x_ref, y_ref, width, pieces, add)

    r["gains"][...] = jnp.zeros_like(r["gains"])

    def norm_grad(value_ref, gain, slot, after):
        def step(i):
            rows = block(i, 64)
            high, inverse = norm_parts(value_ref[rows, :].astype(F32))
            e = r["v_tmp"][rows, :]
            a = e * gain
            back = (
                a - jnp.mean(a, axis=-1, keepdims=True) - high * jnp.mean(a * high, axis=-1, keepdims=True)
            ) * inverse
            r["gains"][pl.ds(slot, 1), :] += jnp.sum(e * high, axis=0, keepdims=True)
            after(rows, back)

        loop(ROWS // 64, step)

    def add_grad(low_ref):
        def after(rows, back):
            total = r["v_grad"][rows, :] + back
            r["v_grad"][rows, :] = total
            low_ref[rows, :] = total.astype(B16)

        return after

    def pull(a_ref, w_ref, store):
        def step(i):
            rows = block(i, 256)
            store(rows, dot_t(a_ref[...], w_ref[rows, :]))

        loop(w_ref.shape[0] // 256, step)

    def to_tmp(columns, value):
        r["v_tmp"][:, columns] = value

    def halves(name, src, to):
        copy = remote(src.at[:, give512], to.at[low], sib)
        ready[name] = [here(src.at[:, keep512], to.at[top]).wait, copy.wait_recv]
        return copy

    await_all("after_attend")

    def feed_norm(i):
        rows = block(i, 64)
        high, _ = norm_parts(r["v_norm"][rows, :])
        x2[rows, :] = (high * r["norm_gains"][3:4, :]).astype(B16)

    loop(ROWS // 64, feed_norm)
    feed_in_copy = remote(x2.at[top], x2.at[low], sib)
    await_all("up", "cot", "down")

    def feed_step(i):
        columns = block(i, 256)
        hidden = dot(x2[top, :], up_w[:, columns])
        r["v_feed_act"][:, columns] = gelu(hidden).astype(B16)
        pulled = dot_t(x1[top, :], down_w[columns, :])
        r["v_feed_back"][:, columns] = (gelu_slope(hidden) * pulled).astype(B16)

    loop(4, feed_step)
    quarter_sends = []
    for name in ("feed_act", "feed_back"):
        ref, to = r["v_" + name], r["y_" + name]
        quarter_sends += [
            remote(ref.at[:, give256], to.at[low, left], sib),
            remote(ref.at[:, pl.ds(768, 256)], to.at[low, right], sib),
        ]
        ready["y_" + name] = [
            here(ref.at[:, keep256], to.at[top, left]).wait,
            here(ref.at[:, pl.ds(512, 256)], to.at[top, right]).wait,
        ] + [copy.wait_recv for copy in quarter_sends[-2:]]
    pull(r["v_feed_back"], up_w, to_tmp)

    def feed_after(rows, back):
        total = x1[rows, :].astype(F32) + back
        r["v_grad"][rows, :] = total
        x3[rows, :] = total.astype(B16)

    norm_grad(r["v_norm"], r["norm_gains"][3:4, :], 3, feed_after)
    branch_copy = remote(x3.at[top], x3.at[low], sib)
    load("cross_up", up_w, "cross_up")

    def latents_step(i):
        columns = block(i, 256)
        r["v_latents_out"][:, columns] = (
            r["v_norm"][:, columns] + dot(r["v_feed_act"][...], down_w[:, columns])
        ).astype(B16)

    loop(4, latents_step)
    load("cross_down", down_w, "cross_down")
    load("after_mlp", r["v_norm"], "after_mlp")
    out_move, out_stay = remote_of(r["v_latents_out"], r["latents_home"], peer(0)), here_of(r["v_latents_out"], r["latents_home"])

    @pl.when(c != t)
    def _():
        out_move.start()

    @pl.when(c == t)
    def _():
        out_stay.start()

    await_all("y_feed_act")
    product_heads(x1, r["y_feed_act"], 512, heads(0))
    parts["S", 0].begin()
    load("cross_act", x1, "x_cross_act")
    feed_in_copy.wait_recv()
    await_all("y_feed_back")
    product_heads(x2, r["y_feed_back"], 512, heads(1))
    parts["S", 1].begin()
    sent(feed_in_copy)
    load("late_x", x2, "x_late_x")

    branch_copy.wait_recv()
    await_all("out_mine", "projected", "probs", "mixed")

    def mixed_step(columns, value):
        r["v_self_grad"][:, columns] = value.astype(B16)

    pull(x3, r["w_out_mine"], mixed_step)
    product_heads(x3, r["y_mixed"], 512, heads(2))
    parts["S", 2].begin()
    sent(branch_copy)
    load("cross_in", x3, "x_cross_in")
    projected, y_back = r["v_projected"], r["y_back"]

    def attend_back(h):
        columns = block(h, HEAD_WIDTH)
        query, key, value = (projected[k, :, columns] for k in range(3))
        key_sum = value_sum = 0
        for j in range(2):
            rows = pl.ds(ROWS * j, ROWS)
            grad = r["v_self_grad"][rows, columns]
            p = probs[2 * h + j]
            g = dot_t(grad, value)
            p32 = p.astype(F32)
            change = (p32 * (g - jnp.sum(p32 * g, axis=-1, keepdims=True))).astype(B16)
            y_back[rows, columns] = (dot(change, key) * self_scale).astype(B16)
            key_sum = key_sum + tdot(change, projected[0, rows, columns])
            value_sum = value_sum + tdot(p, grad)
        y_back[:, pl.ds(pl.multiple_of(512 + h * HEAD_WIDTH, LANES), HEAD_WIDTH)] = (key_sum * self_scale).astype(B16)
        y_back[:, pl.ds(pl.multiple_of(1024 + h * HEAD_WIDTH, LANES), HEAD_WIDTH)] = value_sum.astype(B16)

    loop(4, attend_back)
    load("raised", probs)
    await_all("attend_own", "attend_far")

    def rows_step(i):
        rows = block(i, 256)
        total = 0
        for k in range(3):
            total = total + dot_t(y_back[:, pl.ds(512 * k, 256)], r["w_attend_own"][k, rows, :])
            total = total + dot_t(y_back[:, pl.ds(512 * k + 256, 256)], r["w_attend_far"][k, rows, :])
        r["v_tmp"][:, rows] = total[:ROWS]
        r["v_rows_give"][:, rows] = total[ROWS:].astype(B16)

    loop(4, rows_step)
    rows_copy = remote(r["v_rows_give"], r["v_rows_in"], sib)
    await_all("attend_in")
    product_heads(x4, y_back, 1536, [piece for k in range(3) for piece in heads(3 + k, 512 * k)])
    for q in (3, 4, 5):
        parts["S", q].begin()
    load("attended", x4, "x_attended")
    rows_copy.wait_recv()

    def sum_step(i):
        rows = block(i, 64)
        r["v_tmp"][rows, :] += r["v_rows_in"][rows, :].astype(F32)

    loop(ROWS // 64, sum_step)
    await_all("after_mlp")
    mlp_branch, cross_branch = r["v_branch"], r["v_rows_give"]
    norm_grad(r["v_norm"], r["norm_gains"][2:3, :], 2, add_grad(mlp_branch))
    load("after_cross", r["v_norm"], "after_cross")

    halves("y_mlp", mlp_branch, r["y_mlp"])
    await_all("cross_down", "cross_hidden")

    def hidden_store(columns, value):
        r["v_back"][:, columns] = (gelu_slope(r["v_hidden"][:, columns]) * value).astype(B16)

    pull(mlp_branch, down_w, hidden_store)
    load("cross_out", down_w, "cross_out")
    halves("y_hidden", r["v_back"], r["y_hidden"])
    await_all("cross_up")
    pull(r["v_back"], up_w, to_tmp)
    load("query_weight", up_w, "query_weight")
    advance("S", 0, 1)
    sent(rows_copy)
    await_all("after_cross")
    norm_grad(r["v_norm"], r["norm_gains"][1:2, :], 1, add_grad(cross_branch))
    halves("y_out", cross_branch, r["y_out"])
    await_all("cross_out")

    def attended_store(columns, value):
        x5[top, columns] = value.astype(B16)

    pull(cross_branch, down_w, attended_store)
    attended_copy = remote(x5.at[top], x5.at[low], sib)
    await_all("x_cross_act", "y_mlp")
    product_rows(x1, r["y_mlp"], 512, "P", 0)
    parts["P", 0].begin()
    parts["P", 1].begin()
    await_all("x_cross_in", "y_hidden")
    product_rows(x3, r["y_hidden"], 512, "P", 2)
    parts["P", 2].begin()
    parts["P", 3].begin()
    advance("S", 2)

    await_all("value_wide", "mixed_f32", "asked", "picture", "raised")
    pull_low = dot_t(x5[top, :], r["w_value"][...]).astype(B16)
    r["v_pull"][...] = pull_low
    pull_f32 = pull_low.astype(F32)
    r["v_dot"][...] = jnp.sum(pull_f32 * r["v_mixed"][...], axis=-1, keepdims=True)
    scale_any = r["inverse_total"][...] * r["any_kept"][...]
    r["v_asked_t"][...] = (r["v_asked"][...].astype(F32) * scale_any).T.astype(B16)
    r["v_pull_t"][...] = (pull_f32 * r["inverse_total"][...]).T.astype(B16)
    r["v_sum"][...] = jnp.zeros_like(r["v_sum"])

    def pixel_chunk(i, to, at):
        picture, raised = r["v_picture"][:, block(i, 512)], probs[i]
        change = (raised.astype(F32) * (dot(r["v_pull"][...], picture) - r["v_dot"][...])).astype(B16)
        r["v_sum"][...] += dot_t(change, picture)
        grad = (dot(r["v_asked_t"][...], change) + dot(r["v_pull_t"][...], raised)).astype(B16)
        for j in range(4):
            to[4 * at + j] = grad[:, j * LANES : (j + 1) * LANES]

    loop(4, lambda i: pixel_chunk((1 - c) * 4 + i, r["grad_far"], i))
    grad_copy = remote(r["grad_far"], r["grad_in"], sib)
    loop(4, lambda i: pixel_chunk(c * 4 + i, r["grad_own"], i))

    turned_sum = r["v_sum"][...] * scale_any
    r["y_late_own"][...] = jnp.zeros_like(r["y_late_own"])
    r["y_late_own"][:, :PAD] = (turned_sum * cross_scale).astype(B16)
    ready["y_late"] = [
        here(r["y_late_own"], r["y_late"].at[top]).wait,
        remote(r["y_late_own"], r["y_late"].at[low], sib).wait_recv,
    ]
    r["gains"][4:5, :PAD] = jnp.sum(
        r["v_asked"][...].astype(F32) * turned_sum + pull_f32 * r["v_mixed"][...], axis=0, keepdims=True
    )


    grad_copy.wait_recv()

    def grad_step(i):
        r["grad_own"][i] = (r["grad_own"][i].astype(F32) + r["grad_in"][i].astype(F32)).astype(B16)

    loop(seq, grad_step)

    hops = [(i, j) for i in range(4) for j in range(4)]

    def towards(i, j):
        return 4 * lax.rem(z + i, 4) + lax.rem(x + j, 4)

    def home_of(i, j, ref, sem):
        to = towards(i, j)
        return pltpu.make_async_remote_copy(
            src_ref=ref.at[to],
            dst_ref=r["home"].at[s],
            send_sem=send.at[sem],
            recv_sem=recv.at[sem],
            device_id=(2 * l + c, to, t),
            device_id_type=MESH,
        )

    first_sem = used[0]
    used[0] += len(hops)
    own_way = [home_of(i, j, r["grad_own"], first_sem + k) if k else None for k, (i, j) in enumerate(hops)]
    far_way = [home_of(i, j, r["grad_relay"], first_sem + k) if k else None for k, (i, j) in enumerate(hops)]

    def group(i):
        return block(lax.rem(z + i, 4), 4)

    crossing = [remote_of(r["grad_own"].at[group(i)], r["grad_relay"].at[group(i)], peer(0)) for i in range(4)]
    stay, stay_far = here_of(r["grad_own"].at[s], r["home"].at[s]), here_of(r["grad_relay"].at[s], r["home"].at[s])

    @pl.when(c != t)
    def _():
        for copy in crossing:
            copy.start()

    @pl.when(c == t)
    def _():
        stay.start()
        for copy in own_way[1:]:
            copy.start()

    await_all("x_attended", "y_out")
    product_rows(x4, r["y_out"], 512, "Q", 0)
    parts["Q", 0].begin()
    parts["Q", 1].begin()
    attended_copy.wait_recv()
    await_all("mixed_pixels")
    product_rows(x5, r["y_mixed_pixels"], 512, "Q", 2)
    await_all("x_late_x", "y_late")
    product_rows(x2, r["y_late"], 384, "Q", 2, add=True)
    parts["Q", 2].begin()
    parts["Q", 3].begin()
    advance("S", 3, 4, 5)
    advance("S", 0, 1, 2)
    advance("P")

    @pl.when(c != t)
    def _():
        for i in range(4):
            crossing[i].wait_recv()
            for j in range(4):
                (far_way[4 * i + j] if i or j else stay_far).start()

    sent(*quarter_sends)
    latents, latgrad = r["v_feed_act"], r["v_feed_back"]
    load("latents_turned", latents)
    await_all("key_wide", "query_weight", "latents_turned")
    r["v_rows_in"][...] = dot(r["y_late_own"][:, :PAD], r["w_key"][...]).astype(B16)
    pull(r["v_rows_in"], up_w, to_tmp)

    def latents_after(rows, back):
        latgrad[rows, :] = (r["v_grad"][rows, :] + back).astype(B16)

    norm_grad(latents, r["norm_gains"][0:1, :], 0, latents_after)
    grad_move, grad_stay = remote_of(latgrad, r["latgrad_home"], peer(0)), here_of(latgrad, r["latgrad_home"])

    @pl.when(c != t)
    def _():
        grad_move.start()

    @pl.when(c == t)
    def _():
        grad_stay.start()

    gain_buf, gain_in = r["gain_buf"], r["gain_in"]
    gain_stages = [tuple(bits) + (BOTH[bits],) for bits in (X, Z, Y)] + [("C",)]
    gain_buf[0] = r["gains"][...]

    def send_gains(k):
        return [remote(gain_buf.at[k], gain_in.at[k, j], partner[way]) for j, way in enumerate(gain_stages[k])]

    gain_copies = send_gains(0)
    live = [parts[key] for key in parts]
    k = 0
    while live or k < 4:
        if k < 4:
            for copy in gain_copies:
                copy.wait_recv()
            total = gain_buf[k] + gain_in[k, 0]
            if k < 3:
                total = total + (gain_in[k, 1] + gain_in[k, 2])
            k += 1
            if k < 4:
                gain_buf[k] = total
                gain_copies = send_gains(k)
            else:
                r["out_gains"][...] = total
        for part in live:
            part.advance()
        live = [part for part in live if not part.done]

    @pl.when(c != t)
    def _():
        out_move.wait()
        grad_move.wait()
        stay_far.wait()
        for copy in crossing:
            copy.wait_send()

    @pl.when(c == t)
    def _():
        out_stay.wait()
        grad_stay.wait()
        stay.wait()

    for copy in own_way[1:]:
        copy.wait()
    for copy in waits:
        copy.wait_send()
    assert not ready, tuple(ready)
    assert used[0] <= sems[0] and used[1] <= sems[1], used


def back_and_reduce(given):
    names, scratch = [], []

    def room(name, shape, dtype=B16):
        names.append(name)
        scratch.append(pltpu.VMEM(shape, dtype))

    sems = (210, 58)
    names += list(BACK_HBM) + list(BACK_VMEM) + list(BACK_OUT)
    for name in ("send", "recv", "local"):
        names.append(name)
        scratch.append(pltpu.SemaphoreType.DMA((sems[1 if name == "local" else 0],)))
    for k in range(1, 6):
        room("x%d" % k, (512, WIDE))
    for name in ("feed_act", "feed_back", "mixed", "mixed_pixels", "mlp", "hidden", "out"):
        room("y_" + name, (512, 512))
    room("y_back", (512, 1536))
    room("y_late", (512, 384))
    room("y_late_own", (ROWS, 384))
    for name in ("w_down", "w_up"):
        room(name, (WIDE, WIDE))
    room("w_out_mine", (512, WIDE))
    for name in ("w_attend_own", "w_attend_far"):
        room(name, (3, WIDE, 256))
    for name in ("w_key", "w_value"):
        room(name, (PAD, WIDE))
    for name in ("v_tmp", "v_norm", "v_grad", "v_hidden"):
        room(name, (ROWS, WIDE), F32)
    for name in ("rows_in", "rows_give", "branch", "back", "feed_act", "feed_back", "latents_out"):
        room("v_" + name, (ROWS, WIDE))
    room("v_projected", (3, 512, 512))
    room("v_probs", (8, ROWS, 512))
    room("v_self_grad", (512, 512))
    room("v_picture", (PAD, 4096))
    room("v_mixed", (ROWS, PAD), F32)
    room("v_sum", (ROWS, PAD), F32)
    room("v_asked", (ROWS, PAD))
    room("v_pull", (ROWS, PAD))
    room("v_asked_t", (PAD, ROWS))
    room("v_pull_t", (PAD, ROWS))
    room("v_dot", (ROWS, 1), F32)
    for name in ("grad_own", "grad_far", "grad_in", "grad_relay"):
        room(name, (16, PAD, LANES))
    room("gains", (8, WIDE), F32)
    room("gain_buf", (4, 8, WIDE), F32)
    room("gain_in", (4, 3, 8, WIDE), F32)
    for set_, (plans, depth) in SETS.items():
        for q, stages in enumerate(plans):
            key, n = "%s%d_" % (set_, q), 64
            room(key + "buf", (n, depth, 256))
            for k, bits in enumerate(stages):
                n >>= len(bits)
                room(key + "in%d" % k, (2 ** len(bits) - 1, n, depth, 256))
    anywhere = pl.BlockSpec(memory_space=pl.ANY)
    vmem = pl.BlockSpec(memory_space=pltpu.VMEM)
    result = pl.pallas_call(
        functools.partial(back_kernel, tuple(names), sems),
        out_shape=[jax.ShapeDtypeStruct(*spec) for spec in BACK_OUT.values()],
        in_specs=[anywhere] * len(BACK_HBM) + [vmem] * len(BACK_VMEM),
        out_specs=[anywhere] * (len(BACK_OUT) - 1) + [vmem],
        scratch_shapes=scratch,
        compiler_params=pltpu.CompilerParams(collective_id=1, has_side_effects=True, vmem_limit_bytes=63 * MIB),
        name="back_and_reduce",
    )(*[given[name] for name in BACK_HBM + BACK_VMEM])
    return dict(zip(BACK_OUT, result))


FINISH_IN = ("pixels", "home", "out_S", "out_P", "out_Q", "latgrad_home", "latents_home", "key_wide")
FINISH_OUT = ("pixels_grad", "latents_grad", "latents_out")


def finish_kernel(*refs):
    refs = list(refs)

    def take(n):
        part = refs[:n]
        del refs[:n]
        return part

    hbm = dict(zip(FINISH_IN, take(len(FINISH_IN))))
    gain, gains = take(2)
    results = dict(zip(FINISH_OUT, take(len(FINISH_OUT))))
    gain_rows, pixelgain, query_grad, key_grad, value_grad, crossout, crossup, crossdown = take(8)
    selfattend, selfout, selfup, selfdown = take(4)
    vmem = dict(zip(FINISH_IN, take(len(FINISH_IN))))
    turned, high, grad, latgrad, wide_gain, sems = take(6)
    pixels, home = vmem["pixels"], vmem["home"]
    channels = pixels.shape[0]

    copies = {
        name: pltpu.make_async_copy(hbm[name], vmem[name], sems.at[k])
        for k, name in enumerate(FINISH_IN)
    }
    last = len(FINISH_IN)
    straight = pltpu.make_async_copy(vmem["latents_home"], results["latents_out"], sems.at[last])
    for copy in copies.values():
        copy.start()

    some = 9

    def features(i):
        return pl.ds(i * some, some)

    steps = channels // some
    per_feature(gain, wide_gain)
    copies["pixels"].wait()
    zeros = jnp.zeros(pixels.shape[1:], F32)
    average = lax.fori_loop(
        0, steps, lambda i, total: total + jnp.sum(pixels[features(i)].astype(F32), axis=0), zeros
    ) * (1.0 / channels)

    def square_step(i, total):
        centered = pixels[features(i)].astype(F32) - average
        return total + jnp.sum(centered * centered, axis=0)

    inverse = lax.rsqrt(lax.fori_loop(0, steps, square_step, zeros) * (1.0 / channels) + EPS)
    copies["home"].wait()
    for image in range(16):
        turned[pl.ds(image, PAD, stride=16), :] = home[image].astype(F32)

    def mean_step(i, totals):
        h = (pixels[features(i)].astype(F32) - average) * inverse
        rows = pl.ds(pl.multiple_of(i * (some * 16), 16), some * 16)
        a = turned[rows, :].reshape(some, 16, LANES) * wide_gain[features(i), :][:, None, :]
        high[features(i)] = h
        grad[features(i)] = a
        return totals[0] + jnp.sum(a, axis=0), totals[1] + jnp.sum(a * h, axis=0)

    first, second = lax.fori_loop(0, steps, mean_step, (zeros, zeros))
    first, second = first * (1.0 / channels), second * (1.0 / channels)

    def grad_step(i):
        grad[features(i)] = (grad[features(i)] - first - high[features(i)] * second) * inverse

    loop(steps, grad_step)
    pixels_out = pltpu.make_async_copy(grad, results["pixels_grad"], sems.at[last + 1])
    pixels_out.start()
    copies["latents_home"].wait()
    straight.start()
    copies["latgrad_home"].wait()
    latgrad[...] = vmem["latgrad_home"][...].astype(F32)
    latents_out = pltpu.make_async_copy(latgrad, results["latents_grad"], sems.at[last + 2])
    latents_out.start()

    for name in ("out_S", "out_P", "out_Q", "key_wide"):
        copies[name].wait()
    out_s, out_p, out_q = vmem["out_S"], vmem["out_P"], vmem["out_Q"]
    late = [out_q[:, 512:1024], out_q[:, 1536:2048]]
    query_grad[...] = dot(late[0][:, :PAD], vmem["key_wide"][...])
    key_grad[...] = late[1][:, :channels].astype(F32)
    value_grad[:, :LANES] = late[0][:, 384:].astype(F32)
    value_grad[:, LANES : 2 * LANES] = late[1][:, 384:].astype(F32)
    value_grad[:, 2 * LANES :] = late[0][:, 256:384].astype(F32)[:, 16 : 16 + channels - 2 * LANES]
    for k, ref in enumerate((crossdown, crossup)):
        for core in range(2):
            ref[:, pl.ds(512 * core, 512)] = out_p[:, pl.ds(1024 * core + 512 * k, 512)].astype(F32)
    for core in range(2):
        crossout[:, pl.ds(512 * core, 512)] = out_q[:, pl.ds(1024 * core, 512)].astype(F32)

    def item(k, core):
        return out_s[:, pl.ds(1536 * core + 256 * k, 256)].astype(F32)

    for core in range(2):
        columns = pl.ds(256 * core, 256)
        selfdown[:, columns] = item(0, core)
        selfup[:, columns] = item(1, core)
        selfout[:, columns] = item(2, core)
        for k in range(3):
            selfattend[k, :, columns] = item(3 + k, core)

    mine = 2 * lax.axis_index("seq") + lax.axis_index("tensor")
    rolled = pltpu.roll(gains[...], lax.rem(WIDE - 32 * mine, WIDE), 1)
    for k, ref in enumerate(gain_rows_of(gain_rows)):
        ref[...] = rolled[k : k + 1, :32]
    pixelgain[...] = gains[4:5, :channels] / row_of(gain)
    straight.wait()
    pixels_out.wait()
    latents_out.wait()


def gain_rows_of(ref):
    return [ref.at[pl.ds(k, 1)] for k in range(4)]


def finish(given):
    pixels = given["pixels"]
    channels, images, rows = pixels.shape
    small = [
        (4, 32),
        (1, channels),
        (32, WIDE),
        (32, channels),
        (32, channels),
        (32, WIDE),
        (32, WIDE),
        (32, WIDE),
        (3, 64, 512),
        (64, 512),
        (64, 512),
        (64, 512),
    ]
    anywhere = pl.BlockSpec(memory_space=pl.ANY)
    vmem = pl.BlockSpec(memory_space=pltpu.VMEM)
    return pl.pallas_call(
        finish_kernel,
        out_shape=[
            jax.ShapeDtypeStruct(pixels.shape, F32),
            jax.ShapeDtypeStruct((ROWS, WIDE), F32),
            jax.ShapeDtypeStruct((ROWS, WIDE), B16),
        ]
        + [jax.ShapeDtypeStruct(shape, F32) for shape in small],
        in_specs=[anywhere] * len(FINISH_IN) + [vmem] * 2,
        out_specs=[anywhere] * 3 + [vmem] * len(small),
        scratch_shapes=[pltpu.VMEM(given[name].shape, given[name].dtype) for name in FINISH_IN]
        + [
            pltpu.VMEM((PAD * images, rows), F32),
            pltpu.VMEM(pixels.shape, F32),
            pltpu.VMEM(pixels.shape, F32),
            pltpu.VMEM((ROWS, WIDE), F32),
            pltpu.VMEM((384, LANES), F32),
            pltpu.SemaphoreType.DMA((len(FINISH_IN) + 3,)),
        ],
        compiler_params=pltpu.CompilerParams(vmem_limit_bytes=60 * MIB),
        name="finish",
    )(*[given[name] for name in FINISH_IN], given["pixel_gain"], given["out_gains"])


def shards(
    latents,
    pixels,
    crop_bounds,
    key_mask,
    query_gain,
    pixel_gain,
    cross_gain,
    attend_gain,
    feed_gain,
    query_weight,
    key_weight,
    value_weight,
    cross_out,
    cross_up,
    cross_down,
    self_attend,
    self_out,
    self_up,
    self_down,
    cotangent,
):
    channels = pixels.shape[2]
    given = {
        "pixels": jnp.transpose(pixels, (2, 0, 1)),
        "latents": latents[0],
        "cotangent": cotangent[0],
        "query_weight": query_weight,
        "key_weight": key_weight,
        "value_weight": value_weight,
        "cross_out": cross_out,
        "cross_up": cross_up,
        "cross_down": cross_down,
        "self_attend": self_attend,
        "self_out": self_out,
        "self_up": self_up,
        "self_down": self_down,
        "query_gain": query_gain,
        "cross_gain": cross_gain,
        "attend_gain": attend_gain,
        "feed_gain": feed_gain,
        "pixel_gain": pixel_gain,
        "key_mask": key_mask,
        "crop_bounds": crop_bounds,
    }
    given |= front(given)
    given |= back_and_reduce(given)
    (
        pixels_grad,
        latents_grad,
        latents_out,
        gain_rows,
        pixelgain,
        queryweight_grad,
        keyweight_grad,
        valueweight_grad,
        crossout_grad,
        crossup_grad,
        crossdown_grad,
        selfattend_grad,
        selfout_grad,
        selfup_grad,
        selfdown_grad,
    ) = finish(given)
    return (
        latents_out[None],
        latents_grad[None],
        jnp.transpose(pixels_grad, (1, 2, 0)),
        gain_rows[0],
        pixelgain[0],
        gain_rows[1],
        gain_rows[2],
        gain_rows[3],
        queryweight_grad,
        keyweight_grad.T,
        valueweight_grad.T,
        crossout_grad,
        crossup_grad,
        crossdown_grad,
        selfattend_grad,
        selfout_grad.T,
        selfup_grad,
        selfdown_grad.T,
    )


def solution(mesh):
    in_specs = (
        P(("batch", "seq"), "tensor", None),
        P("batch", ("seq", "tensor"), None),
        P(("batch", "seq"), None),
        P(("batch", "seq"), None),
        P(),
        P(),
        P(),
        P(),
        P(),
        P(),
        P(),
        P(),
        P(),
        P(),
        P(),
        P(None, None, "tensor"),
        P("tensor", None),
        P(None, "tensor"),
        P("tensor", None),
        P(("batch", "seq"), "tensor", None),
    )
    out_specs = (
        P(("batch", "seq"), "tensor", None),
        P(("batch", "seq"), "tensor", None),
        P("batch", ("seq", "tensor"), None),
        P(("seq", "tensor")),
        P(),
        P(("seq", "tensor")),
        P(("seq", "tensor")),
        P(("seq", "tensor")),
        P(("seq", "tensor"), None),
        P(None, ("seq", "tensor")),
        P(None, ("seq", "tensor")),
        P(("seq", "tensor"), None),
        P(("seq", "tensor"), None),
        P(("seq", "tensor"), None),
        P(None, "seq", "tensor"),
        P("tensor", "seq"),
        P("seq", "tensor"),
        P("tensor", "seq"),
    )
    return jax.shard_map(shards, mesh=mesh, in_specs=in_specs, out_specs=out_specs, check_vma=False)
```

```python
import functools
import math

import jax
import jax.numpy as jnp
from jax import lax
from jax.experimental import pallas as pl
from jax.experimental.pallas import tpu as pltpu
from jax.sharding import PartitionSpec as P

HEAD_WIDTH = 128
EPS = 1e-05
MASKED = -1000000000.0
MESH = pl.DeviceIdType.MESH
F32 = jnp.float32
B16 = jnp.bfloat16
LANES = 128
PAD = 272
WIDE = 1024
CYCLE = ("XA", "XB", "ZA", "ZB", "T")

def norm_parts(values):
    average = jnp.mean(values, axis=-1, keepdims=True)
    centered = values - average
    spread = jnp.mean(centered * centered, axis=-1, keepdims=True)
    inverse = lax.rsqrt(spread + EPS)
    return centered * inverse, inverse


def dot(a, b):
    return jnp.dot(a, b, preferred_element_type=F32)


def dot_t(a, b):
    return lax.dot_general(a, b, (((1,), (1,)), ((), ())), preferred_element_type=F32)


def tdot(a, b):
    return lax.dot_general(a, b, (((0,), (0,)), ((), ())), preferred_element_type=F32)


def flip(p):
    return p + 1 - 2 * lax.rem(p, 2)


def place():
    b, s, t = lax.axis_index("batch"), lax.axis_index("seq"), lax.axis_index("tensor")
    return lax.div(b, 2), lax.rem(b, 2), s, t


MIB = 1024 * 1024
ROWS = 256
GELU_K = math.sqrt(2.0 / math.pi)


def gelu(u):
    return 0.5 * u * (1.0 + jnp.tanh(GELU_K * (u + 0.044715 * u * u * u)))


def gelu_slope(u):
    th = jnp.tanh(GELU_K * (u + 0.044715 * u * u * u))
    return 0.5 * (1.0 + th) + 0.5 * u * (1.0 - th * th) * GELU_K * (1.0 + 3.0 * 0.044715 * u * u)


def loop(n, step):
    lax.fori_loop(0, n, lambda i, carry: (step(i), carry)[1], 0)


def row_of(ref):
    return ref[...].astype(F32).reshape(1, ref.shape[0])


def per_feature(gain_ref, out_ref):
    channels = gain_ref.shape[0]
    wide = jnp.concatenate([row_of(gain_ref), jnp.zeros((1, 384 - channels), F32)], axis=1)
    out_ref[...] = jnp.broadcast_to(wide, (LANES, 384)).T


def block(i, n):
    return pl.ds(pl.multiple_of(i * n, n), n)


FRONT_HBM = (
    ("pixels", "latents", "cotangent", "self_attend", "self_out", "self_up", "self_down")
    + ("query_weight", "cross_out", "cross_up", "cross_down")
)
FRONT_VMEM = ("query_gain", "cross_gain", "attend_gain", "feed_gain", "pixel_gain", "key_weight", "value_weight", "key_mask", "crop_bounds")
FRONT_OUT = {
    "cot": ((512, WIDE), B16),
    "cross_act": ((512, WIDE), B16),
    "cross_in": ((512, WIDE), B16),
    "attended": ((512, WIDE), B16),
    "late_x": ((512, WIDE), B16),
    "mixed_pixels": ((512, 512), B16),
    "mixed": ((512, 512), B16),
    "attend_in": ((512, WIDE), B16),
    "projected": ((3, 512, 512), B16),
    "probs": ((8, ROWS, 512), B16),
    "out_mine": ((512, WIDE), B16),
    "attend_far": ((3, WIDE, 256), B16),
    "up_far": ((WIDE, 512), B16),
    "down_far": ((512, WIDE), B16),
    "after_mlp": ((ROWS, WIDE), F32),
    "after_attend": ((ROWS, WIDE), F32),
    "cross_hidden": ((ROWS, WIDE), F32),
    "after_cross": ((ROWS, WIDE), F32),
    "latents_turned": ((ROWS, WIDE), B16),
    "picture": ((PAD, 4096), B16),
    "raised": ((8, ROWS, 512), B16),
    "mixed_f32": ((ROWS, PAD), F32),
    "asked": ((ROWS, PAD), B16),
    "key_wide": ((PAD, WIDE), B16),
    "value_wide": ((PAD, WIDE), B16),
    "inverse_total": ((ROWS, 1), F32),
    "any_kept": ((1, 1), F32),
    "norm_gains": ((8, WIDE), F32),
}
FRONT_OUT_VMEM = ("inverse_total", "any_kept", "norm_gains")


def front_kernel(names, sems, *refs):
    l, c, s, t = place()
    seq = 16
    r = dict(zip(names, refs))
    send, recv, local = r["send"], r["recv"], r["local"]
    cross_scale = 1.0 / math.sqrt(WIDE)
    self_scale = 1.0 / math.sqrt(HEAD_WIDTH)
    sib = (2 * l + 1 - c, s, t)
    over = (2 * (1 - l) + c, s, 1 - t)

    def peer(k):
        return (2 * l + t, lax.rem(s + k, seq), c)

    barrier = pltpu.get_barrier_semaphore()
    for device in (sib, over):
        pl.semaphore_signal(barrier, inc=1, device_id=device, device_id_type=MESH)
    def plane(k):
        return (2 * l + c, lax.rem(s + k, seq), t)

    for k in range(1, seq):
        pl.semaphore_signal(barrier, inc=1, device_id=peer(k), device_id_type=MESH)
        pl.semaphore_signal(barrier, inc=1, device_id=plane(k), device_id_type=MESH)

    @pl.when(c != t)
    def _():
        pl.semaphore_signal(barrier, inc=1, device_id=peer(0), device_id_type=MESH)
        pl.semaphore_wait(barrier, 1 + 2 * seq)

    @pl.when(c == t)
    def _():
        pl.semaphore_wait(barrier, 2 * seq)

    used = [0, 0]
    waits, stores = [], []

    def remote_of(src, dst, device):
        i = used[0]
        used[0] += 1
        return pltpu.make_async_remote_copy(
            src_ref=src, dst_ref=dst, send_sem=send.at[i], recv_sem=recv.at[i], device_id=device, device_id_type=MESH
        )

    def remote(src, dst, device):
        copy = remote_of(src, dst, device)
        copy.start()
        waits.append(copy)
        return copy

    def here_of(src, dst):
        i = used[1]
        used[1] += 1
        return pltpu.make_async_copy(src, dst, local.at[i])

    def here(src, dst):
        copy = here_of(src, dst)
        copy.start()
        return copy

    def store(name, src):
        stores.append(here(src, r[name]))

    top, low = pl.ds(0, ROWS), pl.ds(ROWS, ROWS)
    shared = []

    def share(name, src, give=None):
        stores.append(here(src, r[name].at[top]))
        shared.append(remote(src if give is None else give, r[name].at[low], sib))

    ready = {}

    def await_all(*wanted):
        for name in wanted:
            for wait in ready.pop(name, ()):
                wait()

    base = pl.multiple_of(c * (seq * LANES), LANES)
    far = pl.multiple_of(t * (seq * LANES), LANES)
    picture = r["v_picture"]

    def away_of(k):
        return remote_of(
            r["v_home"].at[lax.rem(s + k, seq)],
            picture.at[:, pl.ds(pl.multiple_of(far + s * LANES, LANES), LANES)],
            peer(k),
        )

    away = [away_of(k) for k in range(seq)]
    lat_move, cot_move = remote_of(r["v_lat_own"], r["v_lat"], peer(0)), remote_of(r["cotangent"], r["v_cot"], peer(0))
    kept_move = remote_of(r["v_kept_own"], r["v_kept"], sib)
    cot_stay = here_of(r["cotangent"], r["v_cot"])
    lat_copy = here(r["latents"], r["v_lat_own"])
    asked_move = remote_of(r["v_asked_own"], r["v_asked"], peer(0))
    kept_stay = here_of(r["v_kept_own"], r["v_kept"])
    picture_stay = here_of(r["v_home"].at[s], picture.at[:, pl.ds(pl.multiple_of(base + s * LANES, LANES), LANES)])

    own256 = 256 * c
    own_columns = pl.ds(pl.multiple_of(own256, LANES), 256)
    attend_far, out_w, up_far, down_far = r["w_attend_far"], r["w_out"], r["w_up_far"], r["w_down_far"]
    left = pl.ds(0, 256)

    def rows16(base_row, piece):
        return pl.ds(pl.multiple_of(base_row + 16 * piece, 16), 16)

    shares = {
        "attend": (lambda p: r["self_attend"].at[:, block(p, 64), own_columns], lambda p: attend_far.at[:, block(p, 64)]),
        "out": (lambda p: r["self_out"].at[rows16(own256, p)], lambda p: out_w.at[rows16(256, p)]),
        "up": (lambda p: r["self_up"].at[block(p, 64), own_columns], lambda p: up_far.at[block(p, 64), left]),
        "down": (lambda p: r["self_down"].at[rows16(own256, p)], lambda p: down_far.at[rows16(0, p)]),
    }
    first_piece = {name: remote(src(s), dst(s), over) for name, (src, dst) in shares.items()}
    @pl.when(c == t)
    def _():
        cot_stay.start()

    pixels_copy = here(r["pixels"], r["v_pixels"])
    r["norm_gains"][...] = jnp.concatenate(
        [row_of(r[name + "_gain"]) for name in ("query", "cross", "attend", "feed")] + [jnp.zeros((4, WIDE), F32)],
        axis=0,
    )

    pieces = {}

    def spread_pieces(*wanted):
        for name in wanted:
            first_piece[name].wait_recv()
            dst = shares[name][1]
            pieces[name] = [remote(dst(s), dst(s), plane(k)) for k in range(1, seq)]

    def gathered(name):
        for copy in pieces[name]:
            copy.wait_recv()

    whole = {
        "out": (out_w.at[pl.ds(256, 256)], out_w.at[pl.ds(768, 256)]),
        "up": (up_far.at[:, left], up_far.at[:, pl.ds(256, 256)]),
        "down": (down_far.at[left], down_far.at[pl.ds(256, 256)]),
    }
    sib_quarter = {}

    def gather_pieces(*wanted):
        for name in wanted:
            gathered(name)
            sib_quarter[name] = remote(*whole[name], sib)

    def arrived(*wanted):
        for name in wanted:
            sib_quarter[name].wait_recv()

    pixels_copy.wait()
    pixels, normed = r["v_pixels"], r["v_normed"]
    channels = pixels.shape[0]
    some = 9

    def features(i):
        return pl.ds(i * some, some)

    def sum_step(i, total):
        return total + jnp.sum(pixels[features(i)].astype(F32), axis=0)

    per_feature(r["pixel_gain"], r["v_gain"])
    zeros = jnp.zeros(pixels.shape[1:], F32)
    average = lax.fori_loop(0, channels // some, sum_step, zeros) * (1.0 / channels)

    def square_step(i, total):
        centered = pixels[features(i)].astype(F32) - average
        return total + jnp.sum(centered * centered, axis=0)

    spread = lax.fori_loop(0, channels // some, square_step, zeros) * (1.0 / channels)
    inverse = lax.rsqrt(spread + EPS)

    def norm_step(i):
        value = (pixels[features(i)].astype(F32) - average) * inverse * r["v_gain"][features(i), :][:, None, :]
        normed[pl.ds(pl.multiple_of(i * (some * 16), 16), some * 16), :] = value.reshape(some * 16, LANES)

    loop(channels // some, norm_step)
    normed[channels * 16 :, :] = jnp.zeros(((PAD - channels) * 16, LANES), F32)

    def turn_image(k):
        image = lax.rem(s + k, seq)
        r["v_home"][image] = normed[pl.ds(image, PAD, stride=16), :].astype(B16)

    turn_image(0)

    @pl.when(c != t)
    def _():
        away[0].start()

    @pl.when(c == t)
    def _():
        picture_stay.start()

    for k in range(1, seq):
        turn_image(k)
        away[k].start()

    start, count = r["crop_bounds"][:, 0:1], r["crop_bounds"][:, 1:2]
    lanes = lax.broadcasted_iota(jnp.int32, (1, LANES), 1)
    for k in range(2 * seq):
        row = lanes + k * LANES
        keep = (row >= start) & (row < start + count) & (r["key_mask"][:, pl.ds(k * LANES, LANES)] == 1)
        to = pl.ds(((k % 2) * seq + k // 2) * LANES, LANES)
        r["v_kept_own"][:, to] = jnp.broadcast_to(jnp.where(keep, 1.0, 0.0), (8, LANES))

    @pl.when(c == t)
    def _():
        kept_stay.start()
        kept_move.start()

    for name in ("key", "value"):
        ref, to = r[name + "_weight"], r["w_" + name]
        to[:256, :] = ref[:256, :]
        to[256:, :] = jnp.concatenate(
            [ref[256:channels, :].astype(F32), jnp.zeros((PAD - channels, WIDE), F32)], axis=0
        ).astype(B16)
        store(name + "_wide", to)
    for name, to in (
        ("query_weight", "w_query"),
        ("cross_out", "w_cross_out"),
        ("cross_up", "w_cross_up"),
        ("cross_down", "w_cross_down"),
    ):
        ready[to] = [here(r[name], r[to]).wait]
    ready["attend_own"] = [here(r["self_attend"].at[:, :, own_columns], r["w_attend_own"]).wait]
    ready["out_own"] = [
        here(r["self_out"].at[pl.ds(pl.multiple_of(own256, LANES), 256)], out_w.at[pl.ds(0, 256)]).wait,
        here(r["self_out"].at[pl.ds(pl.multiple_of(256 - own256, LANES), 256)], out_w.at[pl.ds(512, 256)]).wait,
    ]

    def norm_rows(value_ref, gain, out_ref, also=None):
        def step(i):
            rows = block(i, 64)
            v = value_ref[rows, :].astype(F32)
            high, _ = norm_parts(v)
            out_ref[rows, :] = (high * gain).astype(B16)

        loop(ROWS // 64, step)

    def each256(n, step):
        loop(n // 256, lambda i: step(block(i, 256)))

    query_low, queries = r["v_query_low"], r["v_queries"]

    def ask(lat_ref):
        norm_rows(lat_ref, r["norm_gains"][0:1, :], query_low)

        def query_step(columns):
            queries[:, columns] = dot(query_low[...], r["w_query"][:, columns]).astype(B16)

        each256(WIDE, query_step)

    lat_copy.wait()
    await_all("w_query")
    ask(r["v_lat_own"])
    r["v_asked_own"][...] = (dot_t(queries[...], r["w_key"][...]) * cross_scale).astype(B16)

    @pl.when(c != t)
    def _():
        asked_move.start()
        lat_move.start()

    @pl.when(c == t)
    def _():
        r["v_asked"][...] = r["v_asked_own"][...]
        r["v_lat"][...] = r["v_lat_own"][...]

    spread_pieces("attend")

    def chunk(k):
        return picture.at[:, pl.ds(pl.multiple_of(base + lax.rem(s - k + seq, seq) * LANES, LANES), LANES)]

    @pl.when(c != t)
    def _():
        away[0].wait_recv()
        kept_move.wait_recv()

    @pl.when(c == t)
    def _():
        picture_stay.wait()
        kept_stay.wait()

    passed = [remote(chunk(0), chunk(0), sib)]
    for k in range(1, seq):
        away[k].wait_recv()
        passed.append(remote(chunk(k), chunk(k), sib))
    for copy in passed:
        copy.wait_recv()
    store("picture", picture)

    @pl.when(c != t)
    def _():
        cot_move.start()

    spread_pieces("out", "up", "down")
    @pl.when(c != t)
    def _():
        asked_move.wait_recv()

    store("asked", r["v_asked"])
    scores, raised = r["v_scores"], r["v_raised"]
    r["v_top"][...] = jnp.full((ROWS, 1), -3.0e38, F32)
    r["v_total"][...] = jnp.zeros((ROWS, 1), F32)
    r["v_mixed"][...] = jnp.zeros_like(r["v_mixed"])
    r["any_kept"][...] = jnp.max(r["v_kept"][0:1, :], axis=-1, keepdims=True)

    def score_step(i):
        columns = block(i, 512)
        value = dot(r["v_asked"][...], picture[:, columns])
        value = jnp.where(r["v_kept"][0:1, columns] > 0.5, value, MASKED)
        scores[:, columns] = value
        r["v_top"][...] = jnp.maximum(r["v_top"][...], jnp.max(value, axis=-1, keepdims=True))

    loop(8, score_step)

    def raise_step(i):
        columns = block(i, 512)
        value = jnp.exp(scores[:, columns] - r["v_top"][...])
        r["v_total"][...] += jnp.sum(value, axis=-1, keepdims=True)
        value = value.astype(B16)
        raised[i] = value
        r["v_mixed"][...] += dot_t(value, picture[:, columns])

    loop(8, raise_step)
    store("raised", raised)
    inverse_total = 1.0 / r["v_total"][...]
    r["inverse_total"][...] = inverse_total
    mixed = r["v_mixed"][...] * inverse_total
    r["v_mixed"][...] = mixed
    store("mixed_f32", r["v_mixed"])
    r["v_mixed_wide"][...] = jnp.zeros_like(r["v_mixed_wide"])
    r["v_mixed_wide"][:, :PAD] = mixed
    tail = pltpu.roll(r["v_mixed_wide"][:, 256:384], 16, 1).astype(B16)
    for name, core in (("mixed_pixels", c), ("mixed_pixels_give", 1 - c)):
        ref = r["v_" + name]
        ref[:, :256] = jnp.zeros((ROWS, 256), B16)
        ref[:, 256:384] = tail
        ref[:, 384:] = r["v_mixed_wide"][:, pl.ds(pl.multiple_of(LANES * core, LANES), LANES)].astype(B16)
    share("mixed_pixels", r["v_mixed_pixels"], r["v_mixed_pixels_give"])
    await_all("w_cross_out")
    r["v_attended"][...] = dot(mixed.astype(B16), r["w_value"][...]).astype(B16)
    share("attended", r["v_attended"])

    @pl.when(c != t)
    def _():
        lat_move.wait_recv()

    store("latents_turned", r["v_lat"])

    def out_step(columns):
        r["v_after_cross"][:, columns] = r["v_lat"][:, columns].astype(F32) + dot(
            r["v_attended"][...], r["w_cross_out"][:, columns]
        )

    each256(WIDE, out_step)
    store("after_cross", r["v_after_cross"])
    norm_rows(r["v_after_cross"], r["norm_gains"][1:2, :], r["v_cross_in"])
    share("cross_in", r["v_cross_in"])
    await_all("w_cross_up", "w_cross_down")

    def up_step(columns):
        hidden = dot(r["v_cross_in"][...], r["w_cross_up"][:, columns])
        r["v_hidden"][:, columns] = hidden
        r["v_cross_act"][:, columns] = gelu(hidden).astype(B16)

    each256(WIDE, up_step)
    store("cross_hidden", r["v_hidden"])
    share("cross_act", r["v_cross_act"])

    def down_step(columns):
        r["v_after_mlp"][:, columns] = r["v_after_cross"][:, columns] + dot(
            r["v_cross_act"][...], r["w_cross_down"][:, columns]
        )

    each256(WIDE, down_step)
    store("after_mlp", r["v_after_mlp"])

    attend_in = r["v_attend_in"]
    norm_rows(r["v_after_mlp"], r["norm_gains"][2:3, :], attend_in)
    attend_copy = remote(attend_in.at[top], attend_in.at[low], sib)
    @pl.when(c != t)
    def _():
        ask(r["v_lat"])

    late = r["late_x"]
    late_keep = [here_of(src, late.at[top]) for src in (query_low, queries)]
    late_give = [remote_of(src, late.at[low], sib) for src in (queries, query_low)]

    @pl.when(c == 0)
    def _():
        late_keep[0].start()
        late_give[0].start()

    @pl.when(c == 1)
    def _():
        late_keep[1].start()
        late_give[1].start()

    await_all("attend_own")
    attend_copy.wait_recv()
    store("attend_in", attend_in)
    projected, probs = r["v_projected"], r["v_probs"]

    def project(weights, at):
        for k in range(3):
            projected[k, :, pl.ds(at, 256)] = dot(attend_in[...], weights[k]).astype(B16)

    def attend(h):
        columns = block(h, HEAD_WIDTH)
        dotted = dot_t(projected[0, :, columns], projected[1, :, columns]) * self_scale
        value = jnp.exp(dotted - jnp.max(dotted, axis=-1, keepdims=True))
        value = (value * (1.0 / jnp.sum(value, axis=-1, keepdims=True))).astype(B16)
        probs[2 * h] = value[:ROWS]
        probs[2 * h + 1] = value[ROWS:]
        r["v_self"][:, columns] = dot(value, projected[2, :, columns]).astype(B16)

    project(r["w_attend_own"], 0)
    loop(2, attend)
    gathered("attend")
    project(attend_far, 256)
    loop(2, lambda i: attend(i + 2))
    store("mixed", r["v_self"])
    self_copy = remote(r["v_self"].at[low], r["v_self_in"], sib)
    store("projected", projected)
    store("probs", probs)
    store("attend_far", attend_far)

    @pl.when(c != t)
    def _():
        cot_move.wait_recv()

    @pl.when(c == t)
    def _():
        cot_stay.wait()

    share("cot", r["v_cot"])
    gather_pieces("out")
    await_all("out_own")
    arrived("out")
    store("out_mine", out_w.at[pl.ds(0, 512)])
    self_copy.wait_recv()

    def attended_step(columns):
        r["v_after_attend"][:, columns] = (
            r["v_after_mlp"][:, columns]
            + dot(r["v_self"][top, :], out_w[pl.ds(0, 512), columns])
            + dot(r["v_self_in"][...], out_w[pl.ds(512, 512), columns])
        )

    each256(WIDE, attended_step)
    store("after_attend", r["v_after_attend"])
    gather_pieces("up", "down")
    arrived("up", "down")
    store("up_far", up_far)
    store("down_far", down_far)

    @pl.when(c != t)
    def _():
        lat_move.wait_send()
        asked_move.wait_send()
        cot_move.wait_send()
        away[0].wait_send()

    @pl.when(c == t)
    def _():
        kept_move.wait_send()

    @pl.when(c == 0)
    def _():
        late_keep[0].wait()
        late_give[0].wait_send()
        late_give[1].wait_recv()

    @pl.when(c == 1)
    def _():
        late_keep[1].wait()
        late_give[1].wait_send()
        late_give[0].wait_recv()

    for k in range(1, seq):
        away[k].wait_send()
    for copy in shared:
        copy.wait_recv()
    for copy in waits:
        copy.wait_send()
    for copy in stores:
        copy.wait()
    assert not ready, tuple(ready)
    assert used[0] <= sems[0] and used[1] <= sems[1], used


def front(given):
    names, scratch = [], []

    def room(name, shape, dtype=B16):
        names.append(name)
        scratch.append(pltpu.VMEM(shape, dtype))

    sems = (112, 38)
    names += list(FRONT_HBM) + list(FRONT_VMEM) + list(FRONT_OUT)
    for name in ("send", "recv", "local"):
        names.append(name)
        scratch.append(pltpu.SemaphoreType.DMA((sems[1 if name == "local" else 0],)))
    for name in ("query", "cross_out", "cross_up", "cross_down", "out"):
        room("w_" + name, (WIDE, WIDE))
    for name in ("key", "value"):
        room("w_" + name, (PAD, WIDE))
    for name in ("attend_own", "attend_far"):
        room("w_" + name, (3, WIDE, 256))
    room("w_up_far", (WIDE, 512))
    room("w_down_far", (512, WIDE))
    room("v_picture", (PAD, 4096))
    room("v_pixels", (261, 16, LANES))
    room("v_normed", (PAD * 16, LANES), F32)
    room("v_gain", (384, LANES), F32)
    room("v_home", (16, PAD, LANES))
    room("v_kept", (8, 4096), F32)
    room("v_kept_own", (8, 4096), F32)
    room("v_scores", (ROWS, 4096), F32)
    room("v_raised", (8, ROWS, 512))
    room("v_asked_own", (ROWS, PAD))
    for name in ("lat_own", "lat", "cot", "query_low", "queries", "attended", "cross_in", "cross_act"):
        room("v_" + name, (ROWS, WIDE))
    for name in ("after_cross", "hidden", "after_mlp", "after_attend"):
        room("v_" + name, (ROWS, WIDE), F32)
    room("v_attend_in", (512, WIDE))
    room("v_projected", (3, 512, 512))
    room("v_probs", (8, ROWS, 512))
    room("v_self", (512, 512))
    room("v_self_in", (ROWS, 512))
    room("v_asked", (ROWS, PAD))
    room("v_top", (ROWS, 1), F32)
    room("v_total", (ROWS, 1), F32)
    room("v_mixed", (ROWS, PAD), F32)
    room("v_mixed_wide", (ROWS, 384), F32)
    room("v_mixed_pixels", (ROWS, 512))
    room("v_mixed_pixels_give", (ROWS, 512))
    anywhere = pl.BlockSpec(memory_space=pl.ANY)
    vmem = pl.BlockSpec(memory_space=pltpu.VMEM)
    result = pl.pallas_call(
        functools.partial(front_kernel, tuple(names), sems),
        out_shape=[jax.ShapeDtypeStruct(*spec) for spec in FRONT_OUT.values()],
        in_specs=[anywhere] * len(FRONT_HBM) + [vmem] * len(FRONT_VMEM),
        out_specs=[vmem if name in FRONT_OUT_VMEM else anywhere for name in FRONT_OUT],
        scratch_shapes=scratch,
        compiler_params=pltpu.CompilerParams(collective_id=0, has_side_effects=True, vmem_limit_bytes=63 * MIB),
        name="front",
    )(*[given[name] for name in FRONT_HBM + FRONT_VMEM])
    return dict(zip(FRONT_OUT, result))


X, Z, Y = ("XA", "XB"), ("ZA", "ZB"), ("L", "O")
def rotated(k):
    order = ("XA", "ZA", "L", "XB", "ZB", "O")
    return tuple((bit,) for bit in order[k:] + order[:k])


SETS = {
    "S": (tuple(rotated(k) for k in range(6)), 32),
    "P": (tuple(rotated(k) for k in (0, 3, 1, 4)), 16),
    "Q": (tuple(rotated(k) for k in (2, 5, 0, 3)), 16),
}
BOTH = {X: "X2", Z: "Z2", Y: "T"}
BACK_HBM = (
    ("cot", "cross_act", "cross_in", "attended", "late_x", "mixed_pixels", "mixed", "attend_in", "projected", "probs")
    + ("out_mine", "attend_far", "up_far", "down_far", "after_mlp", "after_attend", "cross_hidden", "after_cross")
    + ("latents_turned", "picture", "raised", "mixed_f32", "asked", "self_attend", "self_up", "self_down")
    + ("cross_down", "cross_up", "cross_out", "query_weight", "key_wide", "value_wide")
)
BACK_VMEM = ("inverse_total", "any_kept", "norm_gains")
BACK_OUT = {
    "out_S": ((64, 2 * 6 * 256), B16),
    "out_P": ((32, 2 * 4 * 256), B16),
    "out_Q": ((32, 2 * 4 * 256), B16),
    "home": ((16, PAD, LANES), B16),
    "latents_home": ((ROWS, WIDE), B16),
    "latgrad_home": ((ROWS, WIDE), B16),
    "out_gains": ((8, WIDE), F32),
}


def back_kernel(names, sems, *refs):
    l, c, s, t = place()
    z, x = lax.div(s, 4), lax.rem(s, 4)
    seq = 16
    r = dict(zip(names, refs))
    send, recv, local = r["send"], r["recv"], r["local"]
    cross_scale = 1.0 / math.sqrt(WIDE)
    self_scale = 1.0 / math.sqrt(HEAD_WIDTH)

    partner = {
        "XA": (2 * l + c, z * 4 + flip(x), t),
        "XB": (2 * l + c, z * 4 + 3 - x, t),
        "ZA": (2 * l + c, flip(z) * 4 + x, t),
        "ZB": (2 * l + c, (3 - z) * 4 + x, t),
        "L": (2 * (1 - l) + c, s, t),
        "O": (2 * (1 - l) + c, s, 1 - t),
        "X2": (2 * l + c, z * 4 + lax.rem(x + 2, 4), t),
        "Z2": (2 * l + c, lax.rem(z + 2, 4) * 4 + x, t),
        "T": (2 * l + c, s, 1 - t),
        "C": (2 * l + 1 - c, s, t),
        "D": (2 * (1 - l) + 1 - c, s, t),
    }

    def peer(k):
        return (2 * l + t, lax.rem(s + k, seq), c)

    barrier = pltpu.get_barrier_semaphore()
    for device in partner.values():
        pl.semaphore_signal(barrier, inc=1, device_id=device, device_id_type=MESH)
    def plane(k):
        return (2 * l + c, lax.rem(s + k, seq), t)

    for k in range(1, seq):
        pl.semaphore_signal(barrier, inc=1, device_id=plane(k), device_id_type=MESH)

    @pl.when(c != t)
    def _():
        pl.semaphore_signal(barrier, inc=1, device_id=peer(0), device_id_type=MESH)
        pl.semaphore_wait(barrier, len(partner) + seq)

    @pl.when(c == t)
    def _():
        pl.semaphore_wait(barrier, len(partner) + seq - 1)

    used = [0, 0]
    waits = []

    def remote_of(src, dst, device):
        i = used[0]
        used[0] += 1
        return pltpu.make_async_remote_copy(
            src_ref=src, dst_ref=dst, send_sem=send.at[i], recv_sem=recv.at[i], device_id=device, device_id_type=MESH
        )

    def remote(src, dst, device):
        copy = remote_of(src, dst, device)
        copy.start()
        waits.append(copy)
        return copy

    def sent(*copies):
        for copy in copies:
            copy.wait_send()
            waits[:] = [other for other in waits if other is not copy]

    def here_of(src, dst):
        i = used[1]
        used[1] += 1
        return pltpu.make_async_copy(src, dst, local.at[i])

    def here(src, dst):
        copy = here_of(src, dst)
        copy.start()
        return copy

    ready = {}

    def await_all(*wanted):
        for name in wanted:
            for wait in ready.pop(name):
                wait()

    def load(name, to, key=None):
        ready[key or name] = [here(r[name], to).wait]

    sib = partner["C"]
    top, low = pl.ds(0, ROWS), pl.ds(ROWS, ROWS)
    keep512 = pl.ds(pl.multiple_of(512 * c, LANES), 512)
    give512 = pl.ds(pl.multiple_of(512 * (1 - c), LANES), 512)
    keep256 = pl.ds(pl.multiple_of(256 * c, LANES), 256)
    give256 = pl.ds(pl.multiple_of(256 * (1 - c), LANES), 256)
    left, right = pl.ds(0, 256), pl.ds(256, 256)
    x1, x2, x3, x4, x5 = (r["x%d" % k] for k in range(1, 6))
    up_w, down_w, probs = r["w_up"], r["w_down"], r["v_probs"]

    load("after_attend", r["v_norm"])
    ready["up"] = [
        here(r["self_up"], up_w.at[:, pl.ds(0, 512)]).wait,
        here(r["up_far"], up_w.at[:, pl.ds(512, 512)]).wait,
    ]
    load("cot", x1)
    ready["down"] = [
        here(r["self_down"], down_w.at[pl.ds(0, 512)]).wait,
        here(r["down_far"], down_w.at[pl.ds(512, 512)]).wait,
    ]
    load("out_mine", r["w_out_mine"])
    load("projected", r["v_projected"])
    load("probs", probs)
    load("mixed", r["y_mixed"])
    ready["attend_own"] = [
        here(r["self_attend"].at[:, :, keep256], r["w_attend_own"]).wait
    ]
    load("attend_far", r["w_attend_far"])
    load("attend_in", x4)
    load("cross_hidden", r["v_hidden"])
    load("value_wide", r["w_value"])
    load("key_wide", r["w_key"])
    load("picture", r["v_picture"])
    load("mixed_f32", r["v_mixed"])
    load("asked", r["v_asked"])
    load("mixed_pixels", r["y_mixed_pixels"])

    class Part:
        def __init__(self, set_, q):
            self.stages, self.depth = SETS[set_][0][q], SETS[set_][1]
            self.set, self.q, self.stage, self.n = set_, q, -1, 64
            self.key = "%s%d_" % (set_, q)
            self.cur = r[self.key + "buf"]
            order = [bit for stage in self.stages for bit in stage]
            self.weight = {bit: 32 >> k for k, bit in enumerate(order)}
            self.done = False

        def index(self, **bits):
            return sum(value * self.weight[bit] for bit, value in bits.items())

        def begin(self):
            self.stage += 1
            k, n = self.stage, self.n
            if k < len(self.stages):
                bits = self.stages[k]
                self.into = r[self.key + "in%d" % k]
                if len(bits) == 1:
                    ways = bits
                else:
                    ways = (bits[1], bits[0], BOTH[bits])
                m = n // (len(ways) + 1)
                self.n = m
                self.copies = [
                    remote(self.cur.at[pl.ds((j + 1) * m, m)], self.into.at[j], partner[way])
                    for j, way in enumerate(ways)
                ]
                return
            count = len(SETS[self.set][0])
            dst = r["out_" + self.set].at[
                pl.ds(pl.multiple_of(l * self.depth, self.depth), self.depth),
                pl.ds(pl.multiple_of((count * c + self.q) * 256, LANES), 256),
            ]
            self.copies = [remote(self.cur.at[0], dst, partner[way]) for way in ("L", "C", "D")]
            self.copy_here = here(self.cur.at[0], dst)

        def finish(self):
            for copy in self.copies:
                copy.wait_recv()
            if self.stage == len(self.stages):
                self.copy_here.wait()
                self.done = True
                return
            cur, into, ways = self.cur, self.into, len(self.copies)
            m = min(self.n, 4)

            def step(i):
                rows = pl.ds(i * m, m)
                total = cur[rows].astype(F32)
                for j in range(ways):
                    total = total + into[j, rows].astype(F32)
                cur[rows] = total.astype(B16)

            if self.n > m:
                loop(self.n // m, step)
            else:
                step(0)

        def advance(self):
            if self.done:
                return
            self.finish()
            if not self.done:
                self.begin()

    parts = {(set_, q): Part(set_, q) for set_ in SETS for q in range(len(SETS[set_][0]))}

    def advance(set_, *some):
        for q in some or range(len(SETS[set_][0])):
            parts[set_, q].advance()

    def product(x_ref, y_ref, width, pieces, add=False):
        span = 512 if width <= 512 else 256
        per = span // 256

        def step(i):
            columns = block(i, span)
            whole = tdot(x_ref[:, columns], y_ref[...])
            for a in range(per):
                zz = i * per + a
                zb = lax.rem(lax.div(z, 2) + lax.div(zz, 2), 2)
                za = lax.rem(lax.rem(z, 2) + lax.rem(zz, 2) + zb, 2)
                for xx in range(4):
                    xb = lax.rem(lax.div(x, 2) + xx // 2, 2)
                    xa = lax.rem(lax.rem(x, 2) + xx % 2 + xb, 2)
                    at = (a * 4 + xx) * 64
                    for part, src, width_, half in pieces:
                        for k in range(64 // part.depth):
                            ll = k % 2
                            o = half if half is not None else lax.rem(k // 2 + t, 2)
                            idx = part.index(ZA=za, ZB=zb, XA=xa, XB=xb, O=o, L=lax.rem(ll + l + o, 2))
                            value = whole[at + k * part.depth : at + (k + 1) * part.depth, src : src + width_]
                            to = pl.ds(0, width_)
                            if add:
                                value = value + part.cur[idx, :, to].astype(F32)
                            part.cur[idx, :, to] = value.astype(B16)

        loop(WIDE // span, step)

    def heads(q, at=0):
        return [("S", q, at, 0), ("S", q, at + 256, 1)]

    def product_heads(x_ref, y_ref, width, wanted):
        product(x_ref, y_ref, width, [(parts["S", q], at, 256, half) for _, q, at, half in wanted])

    def product_rows(x_ref, y_ref, width, set_, q, add=False):
        pieces, at = [], 0
        while at < width:
            n = min(256, width - at)
            pieces.append((parts[set_, q + at // 256], at, n, None))
            at += n
        product(x_ref, y_ref, width, pieces, add)

    r["gains"][...] = jnp.zeros_like(r["gains"])

    def norm_grad(value_ref, gain, slot, after):
        def step(i):
            rows = block(i, 64)
            high, inverse = norm_parts(value_ref[rows, :].astype(F32))
            e = r["v_tmp"][rows, :]
            a = e * gain
            back = (
                a - jnp.mean(a, axis=-1, keepdims=True) - high * jnp.mean(a * high, axis=-1, keepdims=True)
            ) * inverse
            r["gains"][pl.ds(slot, 1), :] += jnp.sum(e * high, axis=0, keepdims=True)
            after(rows, back)

        loop(ROWS // 64, step)

    def add_grad(low_ref):
        def after(rows, back):
            total = r["v_grad"][rows, :] + back
            r["v_grad"][rows, :] = total
            low_ref[rows, :] = total.astype(B16)

        return after

    def pull(a_ref, w_ref, store):
        def step(i):
            rows = block(i, 256)
            store(rows, dot_t(a_ref[...], w_ref[rows, :]))

        loop(w_ref.shape[0] // 256, step)

    def to_tmp(columns, value):
        r["v_tmp"][:, columns] = value

    def halves(name, src, to):
        copy = remote(src.at[:, give512], to.at[low], sib)
        ready[name] = [here(src.at[:, keep512], to.at[top]).wait, copy.wait_recv]
        return copy

    await_all("after_attend")

    def feed_norm(i):
        rows = block(i, 64)
        high, _ = norm_parts(r["v_norm"][rows, :])
        x2[rows, :] = (high * r["norm_gains"][3:4, :]).astype(B16)

    loop(ROWS // 64, feed_norm)
    feed_in_copy = remote(x2.at[top], x2.at[low], sib)
    await_all("up", "cot", "down")

    def feed_step(i):
        columns = block(i, 256)
        hidden = dot(x2[top, :], up_w[:, columns])
        r["v_feed_act"][:, columns] = gelu(hidden).astype(B16)
        pulled = dot_t(x1[top, :], down_w[columns, :])
        r["v_feed_back"][:, columns] = (gelu_slope(hidden) * pulled).astype(B16)

    loop(4, feed_step)
    quarter_sends = []
    for name in ("feed_act", "feed_back"):
        ref, to = r["v_" + name], r["y_" + name]
        quarter_sends += [
            remote(ref.at[:, give256], to.at[low, left], sib),
            remote(ref.at[:, pl.ds(768, 256)], to.at[low, right], sib),
        ]
        ready["y_" + name] = [
            here(ref.at[:, keep256], to.at[top, left]).wait,
            here(ref.at[:, pl.ds(512, 256)], to.at[top, right]).wait,
        ] + [copy.wait_recv for copy in quarter_sends[-2:]]
    pull(r["v_feed_back"], up_w, to_tmp)

    def feed_after(rows, back):
        total = x1[rows, :].astype(F32) + back
        r["v_grad"][rows, :] = total
        x3[rows, :] = total.astype(B16)

    norm_grad(r["v_norm"], r["norm_gains"][3:4, :], 3, feed_after)
    branch_copy = remote(x3.at[top], x3.at[low], sib)
    load("cross_up", up_w, "cross_up")

    def latents_step(i):
        columns = block(i, 256)
        r["v_latents_out"][:, columns] = (
            r["v_norm"][:, columns] + dot(r["v_feed_act"][...], down_w[:, columns])
        ).astype(B16)

    loop(4, latents_step)
    load("cross_down", down_w, "cross_down")
    load("after_mlp", r["v_norm"], "after_mlp")
    out_move, out_stay = remote_of(r["v_latents_out"], r["latents_home"], peer(0)), here_of(r["v_latents_out"], r["latents_home"])

    @pl.when(c != t)
    def _():
        out_move.start()

    @pl.when(c == t)
    def _():
        out_stay.start()

    await_all("y_feed_act")
    product_heads(x1, r["y_feed_act"], 512, heads(0))
    parts["S", 0].begin()
    load("cross_act", x1, "x_cross_act")
    feed_in_copy.wait_recv()
    await_all("y_feed_back")
    product_heads(x2, r["y_feed_back"], 512, heads(1))
    parts["S", 1].begin()
    sent(feed_in_copy)
    load("late_x", x2, "x_late_x")

    branch_copy.wait_recv()
    await_all("out_mine", "projected", "probs", "mixed")

    def mixed_step(columns, value):
        r["v_self_grad"][:, columns] = value.astype(B16)

    pull(x3, r["w_out_mine"], mixed_step)
    product_heads(x3, r["y_mixed"], 512, heads(2))
    parts["S", 2].begin()
    sent(branch_copy)
    load("cross_in", x3, "x_cross_in")
    projected, y_back = r["v_projected"], r["y_back"]

    def attend_back(h):
        columns = block(h, HEAD_WIDTH)
        query, key, value = (projected[k, :, columns] for k in range(3))
        key_sum = value_sum = 0
        for j in range(2):
            rows = pl.ds(ROWS * j, ROWS)
            grad = r["v_self_grad"][rows, columns]
            p = probs[2 * h + j]
            g = dot_t(grad, value)
            p32 = p.astype(F32)
            change = (p32 * (g - jnp.sum(p32 * g, axis=-1, keepdims=True))).astype(B16)
            y_back[rows, columns] = (dot(change, key) * self_scale).astype(B16)
            key_sum = key_sum + tdot(change, projected[0, rows, columns])
            value_sum = value_sum + tdot(p, grad)
        y_back[:, pl.ds(pl.multiple_of(512 + h * HEAD_WIDTH, LANES), HEAD_WIDTH)] = (key_sum * self_scale).astype(B16)
        y_back[:, pl.ds(pl.multiple_of(1024 + h * HEAD_WIDTH, LANES), HEAD_WIDTH)] = value_sum.astype(B16)

    loop(4, attend_back)
    load("raised", probs)
    await_all("attend_own", "attend_far")

    def rows_step(i):
        rows = block(i, 256)
        total = 0
        for k in range(3):
            total = total + dot_t(y_back[:, pl.ds(512 * k, 256)], r["w_attend_own"][k, rows, :])
            total = total + dot_t(y_back[:, pl.ds(512 * k + 256, 256)], r["w_attend_far"][k, rows, :])
        r["v_tmp"][:, rows] = total[:ROWS]
        r["v_rows_give"][:, rows] = total[ROWS:].astype(B16)

    loop(4, rows_step)
    rows_copy = remote(r["v_rows_give"], r["v_rows_in"], sib)
    await_all("attend_in")
    product_heads(x4, y_back, 1536, [piece for k in range(3) for piece in heads(3 + k, 512 * k)])
    for q in (3, 4, 5):
        parts["S", q].begin()
    load("attended", x4, "x_attended")
    rows_copy.wait_recv()

    def sum_step(i):
        rows = block(i, 64)
        r["v_tmp"][rows, :] += r["v_rows_in"][rows, :].astype(F32)

    loop(ROWS // 64, sum_step)
    await_all("after_mlp")
    mlp_branch, cross_branch = r["v_branch"], r["v_rows_give"]
    norm_grad(r["v_norm"], r["norm_gains"][2:3, :], 2, add_grad(mlp_branch))
    load("after_cross", r["v_norm"], "after_cross")

    halves("y_mlp", mlp_branch, r["y_mlp"])
    await_all("cross_down", "cross_hidden")

    def hidden_store(columns, value):
        r["v_back"][:, columns] = (gelu_slope(r["v_hidden"][:, columns]) * value).astype(B16)

    pull(mlp_branch, down_w, hidden_store)
    load("cross_out", down_w, "cross_out")
    halves("y_hidden", r["v_back"], r["y_hidden"])
    await_all("cross_up")
    pull(r["v_back"], up_w, to_tmp)
    load("query_weight", up_w, "query_weight")
    advance("S", 0, 1)
    sent(rows_copy)
    await_all("after_cross")
    norm_grad(r["v_norm"], r["norm_gains"][1:2, :], 1, add_grad(cross_branch))
    halves("y_out", cross_branch, r["y_out"])
    await_all("cross_out")

    def attended_store(columns, value):
        x5[top, columns] = value.astype(B16)

    pull(cross_branch, down_w, attended_store)
    attended_copy = remote(x5.at[top], x5.at[low], sib)
    await_all("x_cross_act", "y_mlp")
    product_rows(x1, r["y_mlp"], 512, "P", 0)
    parts["P", 0].begin()
    parts["P", 1].begin()
    await_all("x_cross_in", "y_hidden")
    product_rows(x3, r["y_hidden"], 512, "P", 2)
    parts["P", 2].begin()
    parts["P", 3].begin()
    advance("S", 2)

    await_all("value_wide", "mixed_f32", "asked", "picture", "raised")
    pull_low = dot_t(x5[top, :], r["w_value"][...]).astype(B16)
    r["v_pull"][...] = pull_low
    pull_f32 = pull_low.astype(F32)
    r["v_dot"][...] = jnp.sum(pull_f32 * r["v_mixed"][...], axis=-1, keepdims=True)
    scale_any = r["inverse_total"][...] * r["any_kept"][...]
    r["v_asked_t"][...] = (r["v_asked"][...].astype(F32) * scale_any).T.astype(B16)
    r["v_pull_t"][...] = (pull_f32 * r["inverse_total"][...]).T.astype(B16)
    r["v_sum"][...] = jnp.zeros_like(r["v_sum"])

    def pixel_chunk(i, to, at):
        picture, raised = r["v_picture"][:, block(i, 512)], probs[i]
        change = (raised.astype(F32) * (dot(r["v_pull"][...], picture) - r["v_dot"][...])).astype(B16)
        r["v_sum"][...] += dot_t(change, picture)
        grad = (dot(r["v_asked_t"][...], change) + dot(r["v_pull_t"][...], raised)).astype(B16)
        for j in range(4):
            to[4 * at + j] = grad[:, j * LANES : (j + 1) * LANES]

    loop(4, lambda i: pixel_chunk((1 - c) * 4 + i, r["grad_far"], i))
    grad_copy = remote(r["grad_far"], r["grad_in"], sib)
    loop(4, lambda i: pixel_chunk(c * 4 + i, r["grad_own"], i))

    turned_sum = r["v_sum"][...] * scale_any
    r["y_late_own"][...] = jnp.zeros_like(r["y_late_own"])
    r["y_late_own"][:, :PAD] = (turned_sum * cross_scale).astype(B16)
    ready["y_late"] = [
        here(r["y_late_own"], r["y_late"].at[top]).wait,
        remote(r["y_late_own"], r["y_late"].at[low], sib).wait_recv,
    ]
    r["gains"][4:5, :PAD] = jnp.sum(
        r["v_asked"][...].astype(F32) * turned_sum + pull_f32 * r["v_mixed"][...], axis=0, keepdims=True
    )


    grad_copy.wait_recv()

    def grad_step(i):
        r["grad_own"][i] = (r["grad_own"][i].astype(F32) + r["grad_in"][i].astype(F32)).astype(B16)

    loop(seq, grad_step)

    hops = [(i, j) for i in range(4) for j in range(4)]

    def towards(i, j):
        return 4 * lax.rem(z + i, 4) + lax.rem(x + j, 4)

    def home_of(i, j, ref, sem):
        to = towards(i, j)
        return pltpu.make_async_remote_copy(
            src_ref=ref.at[to],
            dst_ref=r["home"].at[s],
            send_sem=send.at[sem],
            recv_sem=recv.at[sem],
            device_id=(2 * l + c, to, t),
            device_id_type=MESH,
        )

    first_sem = used[0]
    used[0] += len(hops)
    own_way = [home_of(i, j, r["grad_own"], first_sem + k) if k else None for k, (i, j) in enumerate(hops)]
    far_way = [home_of(i, j, r["grad_relay"], first_sem + k) if k else None for k, (i, j) in enumerate(hops)]

    def group(i):
        return block(lax.rem(z + i, 4), 4)

    crossing = [remote_of(r["grad_own"].at[group(i)], r["grad_relay"].at[group(i)], peer(0)) for i in range(4)]
    stay, stay_far = here_of(r["grad_own"].at[s], r["home"].at[s]), here_of(r["grad_relay"].at[s], r["home"].at[s])

    @pl.when(c != t)
    def _():
        for copy in crossing:
            copy.start()

    @pl.when(c == t)
    def _():
        stay.start()
        for copy in own_way[1:]:
            copy.start()

    await_all("x_attended", "y_out")
    product_rows(x4, r["y_out"], 512, "Q", 0)
    parts["Q", 0].begin()
    parts["Q", 1].begin()
    attended_copy.wait_recv()
    await_all("mixed_pixels")
    product_rows(x5, r["y_mixed_pixels"], 512, "Q", 2)
    await_all("x_late_x", "y_late")
    product_rows(x2, r["y_late"], 384, "Q", 2, add=True)
    parts["Q", 2].begin()
    parts["Q", 3].begin()
    advance("S", 3, 4, 5)
    advance("S", 0, 1, 2)
    advance("P")

    @pl.when(c != t)
    def _():
        for i in range(4):
            crossing[i].wait_recv()
            for j in range(4):
                (far_way[4 * i + j] if i or j else stay_far).start()

    sent(*quarter_sends)
    latents, latgrad = r["v_feed_act"], r["v_feed_back"]
    load("latents_turned", latents)
    await_all("key_wide", "query_weight", "latents_turned")
    r["v_rows_in"][...] = dot(r["y_late_own"][:, :PAD], r["w_key"][...]).astype(B16)
    pull(r["v_rows_in"], up_w, to_tmp)

    def latents_after(rows, back):
        latgrad[rows, :] = (r["v_grad"][rows, :] + back).astype(B16)

    norm_grad(latents, r["norm_gains"][0:1, :], 0, latents_after)
    grad_move, grad_stay = remote_of(latgrad, r["latgrad_home"], peer(0)), here_of(latgrad, r["latgrad_home"])

    @pl.when(c != t)
    def _():
        grad_move.start()

    @pl.when(c == t)
    def _():
        grad_stay.start()

    gain_buf, gain_in = r["gain_buf"], r["gain_in"]
    gain_stages = [tuple(bits) + (BOTH[bits],) for bits in (X, Z, Y)] + [("C",)]
    gain_buf[0] = r["gains"][...]

    def send_gains(k):
        return [remote(gain_buf.at[k], gain_in.at[k, j], partner[way]) for j, way in enumerate(gain_stages[k])]

    gain_copies = send_gains(0)
    live = [parts[key] for key in parts]
    k = 0
    while live or k < 4:
        if k < 4:
            for copy in gain_copies:
                copy.wait_recv()
            total = gain_buf[k] + gain_in[k, 0]
            if k < 3:
                total = total + (gain_in[k, 1] + gain_in[k, 2])
            k += 1
            if k < 4:
                gain_buf[k] = total
                gain_copies = send_gains(k)
            else:
                r["out_gains"][...] = total
        for part in live:
            part.advance()
        live = [part for part in live if not part.done]

    @pl.when(c != t)
    def _():
        out_move.wait()
        grad_move.wait()
        stay_far.wait()
        for copy in crossing:
            copy.wait_send()

    @pl.when(c == t)
    def _():
        out_stay.wait()
        grad_stay.wait()
        stay.wait()

    for copy in own_way[1:]:
        copy.wait()
    for copy in waits:
        copy.wait_send()
    assert not ready, tuple(ready)
    assert used[0] <= sems[0] and used[1] <= sems[1], used


def back_and_reduce(given):
    names, scratch = [], []

    def room(name, shape, dtype=B16):
        names.append(name)
        scratch.append(pltpu.VMEM(shape, dtype))

    sems = (210, 58)
    names += list(BACK_HBM) + list(BACK_VMEM) + list(BACK_OUT)
    for name in ("send", "recv", "local"):
        names.append(name)
        scratch.append(pltpu.SemaphoreType.DMA((sems[1 if name == "local" else 0],)))
    for k in range(1, 6):
        room("x%d" % k, (512, WIDE))
    for name in ("feed_act", "feed_back", "mixed", "mixed_pixels", "mlp", "hidden", "out"):
        room("y_" + name, (512, 512))
    room("y_back", (512, 1536))
    room("y_late", (512, 384))
    room("y_late_own", (ROWS, 384))
    for name in ("w_down", "w_up"):
        room(name, (WIDE, WIDE))
    room("w_out_mine", (512, WIDE))
    for name in ("w_attend_own", "w_attend_far"):
        room(name, (3, WIDE, 256))
    for name in ("w_key", "w_value"):
        room(name, (PAD, WIDE))
    for name in ("v_tmp", "v_norm", "v_grad", "v_hidden"):
        room(name, (ROWS, WIDE), F32)
    for name in ("rows_in", "rows_give", "branch", "back", "feed_act", "feed_back", "latents_out"):
        room("v_" + name, (ROWS, WIDE))
    room("v_projected", (3, 512, 512))
    room("v_probs", (8, ROWS, 512))
    room("v_self_grad", (512, 512))
    room("v_picture", (PAD, 4096))
    room("v_mixed", (ROWS, PAD), F32)
    room("v_sum", (ROWS, PAD), F32)
    room("v_asked", (ROWS, PAD))
    room("v_pull", (ROWS, PAD))
    room("v_asked_t", (PAD, ROWS))
    room("v_pull_t", (PAD, ROWS))
    room("v_dot", (ROWS, 1), F32)
    for name in ("grad_own", "grad_far", "grad_in", "grad_relay"):
        room(name, (16, PAD, LANES))
    room("gains", (8, WIDE), F32)
    room("gain_buf", (4, 8, WIDE), F32)
    room("gain_in", (4, 3, 8, WIDE), F32)
    for set_, (plans, depth) in SETS.items():
        for q, stages in enumerate(plans):
            key, n = "%s%d_" % (set_, q), 64
            room(key + "buf", (n, depth, 256))
            for k, bits in enumerate(stages):
                n >>= len(bits)
                room(key + "in%d" % k, (2 ** len(bits) - 1, n, depth, 256))
    anywhere = pl.BlockSpec(memory_space=pl.ANY)
    vmem = pl.BlockSpec(memory_space=pltpu.VMEM)
    result = pl.pallas_call(
        functools.partial(back_kernel, tuple(names), sems),
        out_shape=[jax.ShapeDtypeStruct(*spec) for spec in BACK_OUT.values()],
        in_specs=[anywhere] * len(BACK_HBM) + [vmem] * len(BACK_VMEM),
        out_specs=[anywhere] * (len(BACK_OUT) - 1) + [vmem],
        scratch_shapes=scratch,
        compiler_params=pltpu.CompilerParams(collective_id=1, has_side_effects=True, vmem_limit_bytes=63 * MIB),
        name="back_and_reduce",
    )(*[given[name] for name in BACK_HBM + BACK_VMEM])
    return dict(zip(BACK_OUT, result))


FINISH_IN = ("pixels", "home", "out_S", "out_P", "out_Q", "latgrad_home", "latents_home", "key_wide")
FINISH_OUT = ("pixels_grad", "latents_grad", "latents_out")


def finish_kernel(*refs):
    refs = list(refs)

    def take(n):
        part = refs[:n]
        del refs[:n]
        return part

    hbm = dict(zip(FINISH_IN, take(len(FINISH_IN))))
    gain, gains = take(2)
    results = dict(zip(FINISH_OUT, take(len(FINISH_OUT))))
    gain_rows = take(4)
    pixelgain, query_grad, key_grad, value_grad, crossout, crossup, crossdown = take(7)
    selfattend, selfout, selfup, selfdown = take(4)
    vmem = dict(zip(FINISH_IN, take(len(FINISH_IN))))
    turned, high, grad, latgrad, wide_gain, sems = take(6)
    pixels, home = vmem["pixels"], vmem["home"]
    channels = pixels.shape[0]

    copies = {
        name: pltpu.make_async_copy(hbm[name], vmem[name], sems.at[k])
        for k, name in enumerate(FINISH_IN)
    }
    last = len(FINISH_IN)
    straight = pltpu.make_async_copy(vmem["latents_home"], results["latents_out"], sems.at[last])
    for copy in copies.values():
        copy.start()

    some = 29

    def features(i):
        return pl.ds(i * some, some)

    steps = channels // some
    per_feature(gain, wide_gain)
    copies["pixels"].wait()
    zeros = jnp.zeros(pixels.shape[1:], F32)
    average = lax.fori_loop(
        0, steps, lambda i, total: total + jnp.sum(pixels[features(i)].astype(F32), axis=0), zeros
    ) * (1.0 / channels)

    def square_step(i, total):
        centered = pixels[features(i)].astype(F32) - average
        return total + jnp.sum(centered * centered, axis=0)

    inverse = lax.rsqrt(lax.fori_loop(0, steps, square_step, zeros) * (1.0 / channels) + EPS)
    copies["home"].wait()
    for image in range(16):
        turned[pl.ds(image, PAD, stride=16), :] = home[image].astype(F32)

    def mean_step(i, totals):
        h = (pixels[features(i)].astype(F32) - average) * inverse
        rows = pl.ds(pl.multiple_of(i * (some * 16), 16), some * 16)
        a = turned[rows, :].reshape(some, 16, LANES) * wide_gain[features(i), :][:, None, :]
        high[features(i)] = h
        grad[features(i)] = a
        return totals[0] + jnp.sum(a, axis=0), totals[1] + jnp.sum(a * h, axis=0)

    first, second = lax.fori_loop(0, steps, mean_step, (zeros, zeros))
    first, second = first * (1.0 / channels), second * (1.0 / channels)

    def grad_step(i):
        grad[features(i)] = (grad[features(i)] - first - high[features(i)] * second) * inverse

    loop(steps, grad_step)
    pixels_out = pltpu.make_async_copy(grad, results["pixels_grad"], sems.at[last + 1])
    pixels_out.start()
    copies["latents_home"].wait()
    straight.start()
    copies["latgrad_home"].wait()
    latgrad[...] = vmem["latgrad_home"][...].astype(F32)
    latents_out = pltpu.make_async_copy(latgrad, results["latents_grad"], sems.at[last + 2])
    latents_out.start()

    for name in ("out_S", "out_P", "out_Q", "key_wide"):
        copies[name].wait()
    out_s, out_p, out_q = vmem["out_S"], vmem["out_P"], vmem["out_Q"]
    late = [out_q[:, 512:1024], out_q[:, 1536:2048]]
    query_grad[...] = dot(late[0][:, :PAD], vmem["key_wide"][...])
    key_grad[...] = late[1][:, :channels].astype(F32)
    value_grad[:, :LANES] = late[0][:, 384:].astype(F32)
    value_grad[:, LANES : 2 * LANES] = late[1][:, 384:].astype(F32)
    value_grad[:, 2 * LANES :] = late[0][:, 256:384].astype(F32)[:, 16 : 16 + channels - 2 * LANES]
    for k, ref in enumerate((crossdown, crossup)):
        for core in range(2):
            ref[:, pl.ds(512 * core, 512)] = out_p[:, pl.ds(1024 * core + 512 * k, 512)].astype(F32)
    for core in range(2):
        crossout[:, pl.ds(512 * core, 512)] = out_q[:, pl.ds(1024 * core, 512)].astype(F32)

    def item(k, core):
        return out_s[:, pl.ds(1536 * core + 256 * k, 256)].astype(F32)

    for core in range(2):
        columns = pl.ds(256 * core, 256)
        selfdown[:, columns] = item(0, core)
        selfup[:, columns] = item(1, core)
        selfout[:, columns] = item(2, core)
        for k in range(3):
            selfattend[k, :, columns] = item(3 + k, core)

    mine = 2 * lax.axis_index("seq") + lax.axis_index("tensor")
    rolled = pltpu.roll(gains[...], lax.rem(WIDE - 32 * mine, WIDE), 1)
    for k, ref in enumerate(gain_rows):
        ref[...] = rolled[k : k + 1, :32].reshape(32)
    pixelgain[...] = (gains[4:5, :channels] / row_of(gain)).reshape(channels)
    straight.wait()
    pixels_out.wait()
    latents_out.wait()


def finish(given):
    pixels = given["pixels"]
    channels, images, rows = pixels.shape
    small = [(32,)] * 4 + [
        (channels,),
        (32, WIDE),
        (32, channels),
        (32, channels),
        (32, WIDE),
        (32, WIDE),
        (32, WIDE),
        (3, 64, 512),
        (64, 512),
        (64, 512),
        (64, 512),
    ]
    anywhere = pl.BlockSpec(memory_space=pl.ANY)
    vmem = pl.BlockSpec(memory_space=pltpu.VMEM)
    return pl.pallas_call(
        finish_kernel,
        out_shape=[
            jax.ShapeDtypeStruct(pixels.shape, F32),
            jax.ShapeDtypeStruct((ROWS, WIDE), F32),
            jax.ShapeDtypeStruct((ROWS, WIDE), B16),
        ]
        + [jax.ShapeDtypeStruct(shape, F32) for shape in small],
        in_specs=[anywhere] * len(FINISH_IN) + [vmem] * 2,
        out_specs=[anywhere] * 3 + [vmem] * len(small),
        scratch_shapes=[pltpu.VMEM(given[name].shape, given[name].dtype) for name in FINISH_IN]
        + [
            pltpu.VMEM((PAD * images, rows), F32),
            pltpu.VMEM(pixels.shape, F32),
            pltpu.VMEM(pixels.shape, F32),
            pltpu.VMEM((ROWS, WIDE), F32),
            pltpu.VMEM((384, LANES), F32),
            pltpu.SemaphoreType.DMA((len(FINISH_IN) + 3,)),
        ],
        compiler_params=pltpu.CompilerParams(vmem_limit_bytes=60 * MIB),
        name="finish",
    )(*[given[name] for name in FINISH_IN], given["pixel_gain"], given["out_gains"])


def shards(
    latents,
    pixels,
    crop_bounds,
    key_mask,
    query_gain,
    pixel_gain,
    cross_gain,
    attend_gain,
    feed_gain,
    query_weight,
    key_weight,
    value_weight,
    cross_out,
    cross_up,
    cross_down,
    self_attend,
    self_out,
    self_up,
    self_down,
    cotangent,
):
    channels = pixels.shape[2]
    given = {
        "pixels": jnp.transpose(pixels, (2, 0, 1)),
        "latents": latents[0],
        "cotangent": cotangent[0],
        "query_weight": query_weight,
        "key_weight": key_weight,
        "value_weight": value_weight,
        "cross_out": cross_out,
        "cross_up": cross_up,
        "cross_down": cross_down,
        "self_attend": self_attend,
        "self_out": self_out,
        "self_up": self_up,
        "self_down": self_down,
        "query_gain": query_gain,
        "cross_gain": cross_gain,
        "attend_gain": attend_gain,
        "feed_gain": feed_gain,
        "pixel_gain": pixel_gain,
        "key_mask": key_mask,
        "crop_bounds": crop_bounds,
    }
    given |= front(given)
    given |= back_and_reduce(given)
    (
        pixels_grad,
        latents_grad,
        latents_out,
        querygain,
        crossgain,
        attendgain,
        feedgain,
        pixelgain,
        queryweight_grad,
        keyweight_grad,
        valueweight_grad,
        crossout_grad,
        crossup_grad,
        crossdown_grad,
        selfattend_grad,
        selfout_grad,
        selfup_grad,
        selfdown_grad,
    ) = finish(given)
    return (
        latents_out[None],
        latents_grad[None],
        jnp.transpose(pixels_grad, (1, 2, 0)),
        querygain,
        pixelgain,
        crossgain,
        attendgain,
        feedgain,
        queryweight_grad,
        keyweight_grad.T,
        valueweight_grad.T,
        crossout_grad,
        crossup_grad,
        crossdown_grad,
        selfattend_grad,
        selfout_grad.T,
        selfup_grad,
        selfdown_grad.T,
    )


def solution(mesh):
    in_specs = (
        P(("batch", "seq"), "tensor", None),
        P("batch", ("seq", "tensor"), None),
        P(("batch", "seq"), None),
        P(("batch", "seq"), None),
        P(),
        P(),
        P(),
        P(),
        P(),
        P(),
        P(),
        P(),
        P(),
        P(),
        P(),
        P(None, None, "tensor"),
        P("tensor", None),
        P(None, "tensor"),
        P("tensor", None),
        P(("batch", "seq"), "tensor", None),
    )
    out_specs = (
        P(("batch", "seq"), "tensor", None),
        P(("batch", "seq"), "tensor", None),
        P("batch", ("seq", "tensor"), None),
        P(("seq", "tensor")),
        P(),
        P(("seq", "tensor")),
        P(("seq", "tensor")),
        P(("seq", "tensor")),
        P(("seq", "tensor"), None),
        P(None, ("seq", "tensor")),
        P(None, ("seq", "tensor")),
        P(("seq", "tensor"), None),
        P(("seq", "tensor"), None),
        P(("seq", "tensor"), None),
        P(None, "seq", "tensor"),
        P("tensor", "seq"),
        P("seq", "tensor"),
        P("tensor", "seq"),
    )
    return jax.shard_map(shards, mesh=mesh, in_specs=in_specs, out_specs=out_specs, check_vma=False)
```

```python
import functools
import math

import jax
import jax.numpy as jnp
from jax import lax
from jax.experimental import pallas as pl
from jax.experimental.pallas import tpu as pltpu
from jax.sharding import PartitionSpec as P

HEAD_WIDTH = 128
EPS = 1e-05
MASKED = -1000000000.0
MESH = pl.DeviceIdType.MESH
F32 = jnp.float32
B16 = jnp.bfloat16
LANES = 128
PAD = 272
WIDE = 1024
CYCLE = ("XA", "XB", "ZA", "ZB", "T")

def norm_parts(values):
    average = jnp.mean(values, axis=-1, keepdims=True)
    centered = values - average
    spread = jnp.mean(centered * centered, axis=-1, keepdims=True)
    inverse = lax.rsqrt(spread + EPS)
    return centered * inverse, inverse


def dot(a, b):
    return jnp.dot(a, b, preferred_element_type=F32)


def dot_t(a, b):
    return lax.dot_general(a, b, (((1,), (1,)), ((), ())), preferred_element_type=F32)


def tdot(a, b):
    return lax.dot_general(a, b, (((0,), (0,)), ((), ())), preferred_element_type=F32)


def flip(p):
    return p + 1 - 2 * lax.rem(p, 2)


def place():
    b, s, t = lax.axis_index("batch"), lax.axis_index("seq"), lax.axis_index("tensor")
    return lax.div(b, 2), lax.rem(b, 2), s, t


MIB = 1024 * 1024
ROWS = 256
GELU_K = math.sqrt(2.0 / math.pi)


def gelu(u):
    return 0.5 * u * (1.0 + jnp.tanh(GELU_K * (u + 0.044715 * u * u * u)))


def gelu_slope(u):
    th = jnp.tanh(GELU_K * (u + 0.044715 * u * u * u))
    return 0.5 * (1.0 + th) + 0.5 * u * (1.0 - th * th) * GELU_K * (1.0 + 3.0 * 0.044715 * u * u)


def loop(n, step):
    lax.fori_loop(0, n, lambda i, carry: (step(i), carry)[1], 0)


def row_of(ref):
    return ref[...].astype(F32).reshape(1, ref.shape[0])


def per_feature(gain_ref, out_ref):
    channels = gain_ref.shape[0]
    wide = jnp.concatenate([row_of(gain_ref), jnp.zeros((1, 384 - channels), F32)], axis=1)
    out_ref[...] = jnp.broadcast_to(wide, (LANES, 384)).T


def block(i, n):
    return pl.ds(pl.multiple_of(i * n, n), n)


FRONT_HBM = (
    ("pixels", "latents", "cotangent", "self_attend", "self_out", "self_up", "self_down")
    + ("query_weight", "cross_out", "cross_up", "cross_down")
)
FRONT_VMEM = ("query_gain", "cross_gain", "attend_gain", "feed_gain", "pixel_gain", "key_weight", "value_weight", "key_mask", "crop_bounds")
FRONT_OUT = {
    "cot": ((512, WIDE), B16),
    "cross_act": ((512, WIDE), B16),
    "cross_in": ((512, WIDE), B16),
    "attended": ((512, WIDE), B16),
    "late_x": ((512, WIDE), B16),
    "mixed_pixels": ((512, 512), B16),
    "mixed": ((512, 512), B16),
    "attend_in": ((512, WIDE), B16),
    "projected": ((3, 512, 512), B16),
    "probs": ((8, ROWS, 512), B16),
    "out_mine": ((512, WIDE), B16),
    "attend_far": ((3, WIDE, 256), B16),
    "up_far": ((WIDE, 512), B16),
    "down_far": ((512, WIDE), B16),
    "after_mlp": ((ROWS, WIDE), F32),
    "after_attend": ((ROWS, WIDE), F32),
    "cross_hidden": ((ROWS, WIDE), F32),
    "after_cross": ((ROWS, WIDE), F32),
    "latents_turned": ((ROWS, WIDE), B16),
    "picture": ((PAD, 4096), B16),
    "raised": ((8, ROWS, 512), B16),
    "mixed_f32": ((ROWS, PAD), F32),
    "asked": ((ROWS, PAD), B16),
    "key_wide": ((PAD, WIDE), B16),
    "value_wide": ((PAD, WIDE), B16),
    "inverse_total": ((ROWS, 1), F32),
    "any_kept": ((1, 1), F32),
    "norm_gains": ((8, WIDE), F32),
}
FRONT_OUT_VMEM = ("inverse_total", "any_kept", "norm_gains")


def front_kernel(names, sems, *refs):
    l, c, s, t = place()
    seq = 16
    r = dict(zip(names, refs))
    send, recv, local = r["send"], r["recv"], r["local"]
    cross_scale = 1.0 / math.sqrt(WIDE)
    self_scale = 1.0 / math.sqrt(HEAD_WIDTH)
    sib = (2 * l + 1 - c, s, t)
    over = (2 * (1 - l) + c, s, 1 - t)

    def peer(k):
        return (2 * l + t, lax.rem(s + k, seq), c)

    barrier = pltpu.get_barrier_semaphore()
    for device in (sib, over):
        pl.semaphore_signal(barrier, inc=1, device_id=device, device_id_type=MESH)
    def plane(k):
        return (2 * l + c, lax.rem(s + k, seq), t)

    for k in range(1, seq):
        pl.semaphore_signal(barrier, inc=1, device_id=plane(k), device_id_type=MESH)

    @pl.when(c != t)
    def _():
        pl.semaphore_signal(barrier, inc=1, device_id=peer(0), device_id_type=MESH)
        pl.semaphore_wait(barrier, 2 + seq)

    @pl.when(c == t)
    def _():
        pl.semaphore_wait(barrier, 1 + seq)

    used = [0, 0]
    waits, stores = [], []

    def remote_of(src, dst, device):
        i = used[0]
        used[0] += 1
        return pltpu.make_async_remote_copy(
            src_ref=src, dst_ref=dst, send_sem=send.at[i], recv_sem=recv.at[i], device_id=device, device_id_type=MESH
        )

    def remote(src, dst, device):
        copy = remote_of(src, dst, device)
        copy.start()
        waits.append(copy)
        return copy

    def here_of(src, dst):
        i = used[1]
        used[1] += 1
        return pltpu.make_async_copy(src, dst, local.at[i])

    def here(src, dst):
        copy = here_of(src, dst)
        copy.start()
        return copy

    def store(name, src):
        stores.append(here(src, r[name]))

    top, low = pl.ds(0, ROWS), pl.ds(ROWS, ROWS)
    shared = []

    def share(name, src, give=None):
        stores.append(here(src, r[name].at[top]))
        shared.append(remote(src if give is None else give, r[name].at[low], sib))

    ready = {}

    def await_all(*wanted):
        for name in wanted:
            for wait in ready.pop(name, ()):
                wait()

    base = pl.multiple_of(c * (seq * LANES), LANES)
    picture = r["v_picture"]

    z, x = lax.div(s, 4), lax.rem(s, 4)
    hops = [(i, j) for i in range(4) for j in range(4)]

    def towards(i, j, sign=1):
        return 4 * lax.rem(z + sign * i + 4, 4) + lax.rem(x + sign * j + 4, 4)

    def columns_of(source):
        return picture.at[:, pl.ds(pl.multiple_of(base + source * LANES, LANES), LANES)]

    own_way = [remote_of(r["v_home"].at[towards(i, j)], columns_of(s), (2 * l + c, towards(i, j), t)) for i, j in hops]
    first_sem = used[0] - len(hops)
    far_way = [
        pltpu.make_async_remote_copy(
            src_ref=r["v_relay"].at[towards(i, j)],
            dst_ref=columns_of(s),
            send_sem=send.at[first_sem + k],
            recv_sem=recv.at[first_sem + k],
            device_id=(2 * l + c, towards(i, j), t),
            device_id_type=MESH,
        )
        for k, (i, j) in enumerate(hops)
    ]

    def group(i):
        return block(lax.rem(z + i, 4), 4)

    crossing = [remote_of(r["v_home"].at[group(i)], r["v_relay"].at[group(i)], peer(0)) for i in range(4)]
    lat_move, cot_move = remote_of(r["v_lat_own"], r["v_lat"], peer(0)), remote_of(r["cotangent"], r["v_cot"], peer(0))
    kept_move = remote_of(r["v_kept_own"], r["v_kept"], sib)
    cot_stay = here_of(r["cotangent"], r["v_cot"])
    lat_copy = here(r["latents"], r["v_lat_own"])
    asked_move = remote_of(r["v_asked_own"], r["v_asked"], peer(0))
    kept_stay = here_of(r["v_kept_own"], r["v_kept"])
    picture_stay = here_of(r["v_home"].at[s], columns_of(s))
    picture_cross = here_of(r["v_relay"].at[s], columns_of(s))

    z, x = lax.div(s, 4), lax.rem(s, 4)
    own256 = 256 * c
    own_columns = pl.ds(pl.multiple_of(own256, LANES), 256)
    attend_far, out_w, up_far, down_far = r["w_attend_far"], r["w_out"], r["w_up_far"], r["w_down_far"]
    left = pl.ds(0, 256)

    def rows16(base_row, piece):
        return pl.ds(pl.multiple_of(base_row + 16 * piece, 16), 16)

    shares = {
        "attend": (lambda p: r["self_attend"].at[:, block(p, 64), own_columns], lambda p, n=1: attend_far.at[:, block(p, 64 * n)]),
        "out": (lambda p: r["self_out"].at[rows16(own256, p)], lambda p, n=1: out_w.at[pl.ds(pl.multiple_of(256 + 16 * n * p, 16), 16 * n)]),
        "up": (lambda p: r["self_up"].at[block(p, 64), own_columns], lambda p, n=1: up_far.at[block(p, 64 * n), left]),
        "down": (lambda p: r["self_down"].at[rows16(own256, p)], lambda p, n=1: down_far.at[block(p, 16 * n)]),
    }

    def along(axis, k):
        at = z * 4 + lax.rem(x + k, 4) if axis == "x" else lax.rem(z + k, 4) * 4 + x
        return (2 * l + c, at, t)

    plans = {name: ("z", 4 * x + z, "x", x) if name == "attend" else ("x", 4 * z + x, "z", z) for name in shares}
    first_piece = {name: remote(src(plans[name][1]), dst(plans[name][1]), over) for name, (src, dst) in shares.items()}
    @pl.when(c == t)
    def _():
        cot_stay.start()

    pixels_copy = here(r["pixels"], r["v_pixels"])
    r["norm_gains"][...] = jnp.concatenate(
        [row_of(r[name + "_gain"]) for name in ("query", "cross", "attend", "feed")] + [jnp.zeros((4, WIDE), F32)],
        axis=0,
    )

    pieces, fours = {}, {}

    def spread_pieces(*wanted):
        for name in wanted:
            first_piece[name].wait_recv()
            axis, p, _, _ = plans[name]
            at = shares[name][1](p)
            pieces[name] = [remote(at, at, along(axis, k)) for k in range(1, 4)]

    def spread_fours(*wanted):
        for name in wanted:
            for copy in pieces[name]:
                copy.wait_recv()
            _, _, axis, p = plans[name]
            at = shares[name][1](p, 4)
            fours[name] = [remote(at, at, along(axis, k)) for k in range(1, 4)]

    def gathered(name):
        for copy in fours[name]:
            copy.wait_recv()

    whole = {
        "out": (out_w.at[pl.ds(256, 256)], out_w.at[pl.ds(768, 256)]),
        "up": (up_far.at[:, left], up_far.at[:, pl.ds(256, 256)]),
        "down": (down_far.at[left], down_far.at[pl.ds(256, 256)]),
    }
    sib_quarter = {}

    def gather_pieces(*wanted):
        for name in wanted:
            gathered(name)
            sib_quarter[name] = remote(*whole[name], sib)

    def arrived(*wanted):
        for name in wanted:
            sib_quarter[name].wait_recv()

    pixels_copy.wait()
    pixels, normed = r["v_pixels"], r["v_normed"]
    channels = pixels.shape[0]
    some = 9

    def features(i):
        return pl.ds(i * some, some)

    def sum_step(i, total):
        return total + jnp.sum(pixels[features(i)].astype(F32), axis=0)

    per_feature(r["pixel_gain"], r["v_gain"])
    zeros = jnp.zeros(pixels.shape[1:], F32)
    average = lax.fori_loop(0, channels // some, sum_step, zeros) * (1.0 / channels)

    def square_step(i, total):
        centered = pixels[features(i)].astype(F32) - average
        return total + jnp.sum(centered * centered, axis=0)

    spread = lax.fori_loop(0, channels // some, square_step, zeros) * (1.0 / channels)
    inverse = lax.rsqrt(spread + EPS)

    def norm_step(i):
        value = (pixels[features(i)].astype(F32) - average) * inverse * r["v_gain"][features(i), :][:, None, :]
        normed[pl.ds(pl.multiple_of(i * (some * 16), 16), some * 16), :] = value.reshape(some * 16, LANES)

    loop(channels // some, norm_step)
    normed[channels * 16 :, :] = jnp.zeros(((PAD - channels) * 16, LANES), F32)

    for i in range(4):
        for j in range(4):
            image = towards(i, j)
            r["v_home"][image] = normed[pl.ds(image, PAD, stride=16), :].astype(B16)

            @pl.when(c == t)
            def _():
                (own_way[4 * i + j] if i or j else picture_stay).start()

        @pl.when(c != t)
        def _():
            crossing[i].start()

    start, count = r["crop_bounds"][:, 0:1], r["crop_bounds"][:, 1:2]
    lanes = lax.broadcasted_iota(jnp.int32, (1, LANES), 1)
    for k in range(2 * seq):
        row = lanes + k * LANES
        keep = (row >= start) & (row < start + count) & (r["key_mask"][:, pl.ds(k * LANES, LANES)] == 1)
        to = pl.ds(((k % 2) * seq + k // 2) * LANES, LANES)
        r["v_kept_own"][:, to] = jnp.broadcast_to(jnp.where(keep, 1.0, 0.0), (8, LANES))

    @pl.when(c == t)
    def _():
        kept_stay.start()
        kept_move.start()

    for name in ("key", "value"):
        ref, to = r[name + "_weight"], r["w_" + name]
        to[:256, :] = ref[:256, :]
        to[256:, :] = jnp.concatenate(
            [ref[256:channels, :].astype(F32), jnp.zeros((PAD - channels, WIDE), F32)], axis=0
        ).astype(B16)
        store(name + "_wide", to)
    for name, to in (
        ("query_weight", "w_query"),
        ("cross_out", "w_cross_out"),
        ("cross_up", "w_cross_up"),
        ("cross_down", "w_cross_down"),
    ):
        ready[to] = [here(r[name], r[to]).wait]
    ready["attend_own"] = [here(r["self_attend"].at[:, :, own_columns], r["w_attend_own"]).wait]
    ready["out_own"] = [
        here(r["self_out"].at[pl.ds(pl.multiple_of(own256, LANES), 256)], out_w.at[pl.ds(0, 256)]).wait,
        here(r["self_out"].at[pl.ds(pl.multiple_of(256 - own256, LANES), 256)], out_w.at[pl.ds(512, 256)]).wait,
    ]

    def norm_rows(value_ref, gain, out_ref, also=None):
        def step(i):
            rows = block(i, 64)
            v = value_ref[rows, :].astype(F32)
            high, _ = norm_parts(v)
            out_ref[rows, :] = (high * gain).astype(B16)

        loop(ROWS // 64, step)

    def each256(n, step):
        loop(n // 256, lambda i: step(block(i, 256)))

    query_low, queries = r["v_query_low"], r["v_queries"]

    def ask(lat_ref):
        norm_rows(lat_ref, r["norm_gains"][0:1, :], query_low)

        def query_step(columns):
            queries[:, columns] = dot(query_low[...], r["w_query"][:, columns]).astype(B16)

        each256(WIDE, query_step)

    lat_copy.wait()
    await_all("w_query")
    ask(r["v_lat_own"])
    r["v_asked_own"][...] = (dot_t(queries[...], r["w_key"][...]) * cross_scale).astype(B16)

    @pl.when(c != t)
    def _():
        asked_move.start()
        lat_move.start()

    @pl.when(c == t)
    def _():
        r["v_asked"][...] = r["v_asked_own"][...]
        r["v_lat"][...] = r["v_lat_own"][...]

    @pl.when(c != t)
    def _():
        for i in range(4):
            crossing[i].wait_recv()
            for j in range(4):
                (far_way[4 * i + j] if i or j else picture_cross).start()
        kept_move.wait_recv()
        picture_cross.wait()

    @pl.when(c == t)
    def _():
        kept_stay.wait()
        picture_stay.wait()

    spread_pieces("attend", "out", "up", "down")
    passed = []
    for k, (i, j) in enumerate(hops):
        if k > 0:
            own_way[k].wait_recv()
        arrived_at = columns_of(towards(i, j, -1))
        passed.append(remote(arrived_at, arrived_at, sib))
    for copy in passed:
        copy.wait_recv()
    spread_fours("attend")
    store("picture", picture)

    @pl.when(c != t)
    def _():
        cot_move.start()

    @pl.when(c != t)
    def _():
        asked_move.wait_recv()

    store("asked", r["v_asked"])
    scores, raised = r["v_scores"], r["v_raised"]
    r["v_top"][...] = jnp.full((ROWS, 1), -3.0e38, F32)
    r["v_total"][...] = jnp.zeros((ROWS, 1), F32)
    r["v_mixed"][...] = jnp.zeros_like(r["v_mixed"])
    r["any_kept"][...] = jnp.max(r["v_kept"][0:1, :], axis=-1, keepdims=True)

    def score_step(i):
        columns = block(i, 512)
        value = dot(r["v_asked"][...], picture[:, columns])
        value = jnp.where(r["v_kept"][0:1, columns] > 0.5, value, MASKED)
        scores[:, columns] = value
        r["v_top"][...] = jnp.maximum(r["v_top"][...], jnp.max(value, axis=-1, keepdims=True))

    loop(8, score_step)

    def raise_step(i):
        columns = block(i, 512)
        value = jnp.exp(scores[:, columns] - r["v_top"][...])
        r["v_total"][...] += jnp.sum(value, axis=-1, keepdims=True)
        value = value.astype(B16)
        raised[i] = value
        r["v_mixed"][...] += dot_t(value, picture[:, columns])

    loop(8, raise_step)
    store("raised", raised)
    inverse_total = 1.0 / r["v_total"][...]
    r["inverse_total"][...] = inverse_total
    mixed = r["v_mixed"][...] * inverse_total
    r["v_mixed"][...] = mixed
    store("mixed_f32", r["v_mixed"])
    r["v_mixed_wide"][...] = jnp.zeros_like(r["v_mixed_wide"])
    r["v_mixed_wide"][:, :PAD] = mixed
    tail = pltpu.roll(r["v_mixed_wide"][:, 256:384], 16, 1).astype(B16)
    for name, core in (("mixed_pixels", c), ("mixed_pixels_give", 1 - c)):
        ref = r["v_" + name]
        ref[:, :256] = jnp.zeros((ROWS, 256), B16)
        ref[:, 256:384] = tail
        ref[:, 384:] = r["v_mixed_wide"][:, pl.ds(pl.multiple_of(LANES * core, LANES), LANES)].astype(B16)
    share("mixed_pixels", r["v_mixed_pixels"], r["v_mixed_pixels_give"])
    await_all("w_cross_out")
    r["v_attended"][...] = dot(mixed.astype(B16), r["w_value"][...]).astype(B16)
    spread_fours("out", "up", "down")
    share("attended", r["v_attended"])

    @pl.when(c != t)
    def _():
        lat_move.wait_recv()

    store("latents_turned", r["v_lat"])

    def out_step(columns):
        r["v_after_cross"][:, columns] = r["v_lat"][:, columns].astype(F32) + dot(
            r["v_attended"][...], r["w_cross_out"][:, columns]
        )

    each256(WIDE, out_step)
    store("after_cross", r["v_after_cross"])
    norm_rows(r["v_after_cross"], r["norm_gains"][1:2, :], r["v_cross_in"])
    share("cross_in", r["v_cross_in"])
    await_all("w_cross_up", "w_cross_down")

    def up_step(columns):
        hidden = dot(r["v_cross_in"][...], r["w_cross_up"][:, columns])
        r["v_hidden"][:, columns] = hidden
        r["v_cross_act"][:, columns] = gelu(hidden).astype(B16)

    each256(WIDE, up_step)
    store("cross_hidden", r["v_hidden"])
    share("cross_act", r["v_cross_act"])

    def down_step(columns):
        r["v_after_mlp"][:, columns] = r["v_after_cross"][:, columns] + dot(
            r["v_cross_act"][...], r["w_cross_down"][:, columns]
        )

    each256(WIDE, down_step)
    store("after_mlp", r["v_after_mlp"])

    attend_in = r["v_attend_in"]
    norm_rows(r["v_after_mlp"], r["norm_gains"][2:3, :], attend_in)
    attend_copy = remote(attend_in.at[top], attend_in.at[low], sib)
    @pl.when(c != t)
    def _():
        ask(r["v_lat"])

    late = r["late_x"]
    late_keep = [here_of(src, late.at[top]) for src in (query_low, queries)]
    late_give = [remote_of(src, late.at[low], sib) for src in (queries, query_low)]

    @pl.when(c == 0)
    def _():
        late_keep[0].start()
        late_give[0].start()

    @pl.when(c == 1)
    def _():
        late_keep[1].start()
        late_give[1].start()

    await_all("attend_own")
    attend_copy.wait_recv()
    store("attend_in", attend_in)
    projected, probs = r["v_projected"], r["v_probs"]

    def project(weights, at):
        for k in range(3):
            projected[k, :, pl.ds(at, 256)] = dot(attend_in[...], weights[k]).astype(B16)

    def attend(h):
        columns = block(h, HEAD_WIDTH)
        dotted = dot_t(projected[0, :, columns], projected[1, :, columns]) * self_scale
        value = jnp.exp(dotted - jnp.max(dotted, axis=-1, keepdims=True))
        value = (value * (1.0 / jnp.sum(value, axis=-1, keepdims=True))).astype(B16)
        probs[2 * h] = value[:ROWS]
        probs[2 * h + 1] = value[ROWS:]
        r["v_self"][:, columns] = dot(value, projected[2, :, columns]).astype(B16)

    project(r["w_attend_own"], 0)
    loop(2, attend)
    gathered("attend")
    project(attend_far, 256)
    loop(2, lambda i: attend(i + 2))
    store("mixed", r["v_self"])
    self_copy = remote(r["v_self"].at[low], r["v_self_in"], sib)
    store("projected", projected)
    store("probs", probs)
    store("attend_far", attend_far)

    @pl.when(c != t)
    def _():
        cot_move.wait_recv()

    @pl.when(c == t)
    def _():
        cot_stay.wait()

    share("cot", r["v_cot"])
    gather_pieces("out")
    await_all("out_own")
    arrived("out")
    store("out_mine", out_w.at[pl.ds(0, 512)])
    self_copy.wait_recv()

    def attended_step(columns):
        r["v_after_attend"][:, columns] = (
            r["v_after_mlp"][:, columns]
            + dot(r["v_self"][top, :], out_w[pl.ds(0, 512), columns])
            + dot(r["v_self_in"][...], out_w[pl.ds(512, 512), columns])
        )

    each256(WIDE, attended_step)
    store("after_attend", r["v_after_attend"])
    gather_pieces("up", "down")
    arrived("up", "down")
    store("up_far", up_far)
    store("down_far", down_far)

    @pl.when(c != t)
    def _():
        lat_move.wait_send()
        asked_move.wait_send()
        cot_move.wait_send()
        for copy in crossing:
            copy.wait_send()

    @pl.when(c == t)
    def _():
        kept_move.wait_send()

    @pl.when(c == 0)
    def _():
        late_keep[0].wait()
        late_give[0].wait_send()
        late_give[1].wait_recv()

    @pl.when(c == 1)
    def _():
        late_keep[1].wait()
        late_give[1].wait_send()
        late_give[0].wait_recv()

    for copy in own_way[1:]:
        copy.wait_send()
    for copy in shared:
        copy.wait_recv()
    for copy in waits:
        copy.wait_send()
    for copy in stores:
        copy.wait()
    assert not ready, tuple(ready)
    assert used[0] <= sems[0] and used[1] <= sems[1], used


def front(given):
    names, scratch = [], []

    def room(name, shape, dtype=B16):
        names.append(name)
        scratch.append(pltpu.VMEM(shape, dtype))

    sems = (80, 39)
    names += list(FRONT_HBM) + list(FRONT_VMEM) + list(FRONT_OUT)
    for name in ("send", "recv", "local"):
        names.append(name)
        scratch.append(pltpu.SemaphoreType.DMA((sems[1 if name == "local" else 0],)))
    for name in ("query", "cross_out", "cross_up", "cross_down", "out"):
        room("w_" + name, (WIDE, WIDE))
    for name in ("key", "value"):
        room("w_" + name, (PAD, WIDE))
    for name in ("attend_own", "attend_far"):
        room("w_" + name, (3, WIDE, 256))
    room("w_up_far", (WIDE, 512))
    room("w_down_far", (512, WIDE))
    room("v_picture", (PAD, 4096))
    room("v_pixels", (261, 16, LANES))
    room("v_normed", (PAD * 16, LANES), F32)
    room("v_gain", (384, LANES), F32)
    room("v_home", (16, PAD, LANES))
    room("v_relay", (16, PAD, LANES))
    room("v_kept", (8, 4096), F32)
    room("v_kept_own", (8, 4096), F32)
    room("v_scores", (ROWS, 4096), F32)
    room("v_raised", (8, ROWS, 512))
    room("v_asked_own", (ROWS, PAD))
    for name in ("lat_own", "lat", "cot", "query_low", "queries", "attended", "cross_in", "cross_act"):
        room("v_" + name, (ROWS, WIDE))
    for name in ("after_cross", "hidden", "after_mlp", "after_attend"):
        room("v_" + name, (ROWS, WIDE), F32)
    room("v_attend_in", (512, WIDE))
    room("v_projected", (3, 512, 512))
    room("v_probs", (8, ROWS, 512))
    room("v_self", (512, 512))
    room("v_self_in", (ROWS, 512))
    room("v_asked", (ROWS, PAD))
    room("v_top", (ROWS, 1), F32)
    room("v_total", (ROWS, 1), F32)
    room("v_mixed", (ROWS, PAD), F32)
    room("v_mixed_wide", (ROWS, 384), F32)
    room("v_mixed_pixels", (ROWS, 512))
    room("v_mixed_pixels_give", (ROWS, 512))
    anywhere = pl.BlockSpec(memory_space=pl.ANY)
    vmem = pl.BlockSpec(memory_space=pltpu.VMEM)
    result = pl.pallas_call(
        functools.partial(front_kernel, tuple(names), sems),
        out_shape=[jax.ShapeDtypeStruct(*spec) for spec in FRONT_OUT.values()],
        in_specs=[anywhere] * len(FRONT_HBM) + [vmem] * len(FRONT_VMEM),
        out_specs=[vmem if name in FRONT_OUT_VMEM else anywhere for name in FRONT_OUT],
        scratch_shapes=scratch,
        compiler_params=pltpu.CompilerParams(collective_id=0, has_side_effects=True, vmem_limit_bytes=63 * MIB),
        name="front",
    )(*[given[name] for name in FRONT_HBM + FRONT_VMEM])
    return dict(zip(FRONT_OUT, result))


X, Z, Y = ("XA", "XB"), ("ZA", "ZB"), ("L", "O")
def rotated(k):
    order = ("XA", "ZA", "L", "XB", "ZB", "O")
    return tuple((bit,) for bit in order[k:] + order[:k])


SETS = {
    "S": (tuple(rotated(k) for k in range(6)), 32),
    "P": (tuple(rotated(k) for k in (0, 3, 1, 4)), 16),
    "Q": (tuple(rotated(k) for k in (2, 5, 0, 3)), 16),
}
BOTH = {X: "X2", Z: "Z2", Y: "T"}
BACK_HBM = (
    ("cot", "cross_act", "cross_in", "attended", "late_x", "mixed_pixels", "mixed", "attend_in", "projected", "probs")
    + ("out_mine", "attend_far", "up_far", "down_far", "after_mlp", "after_attend", "cross_hidden", "after_cross")
    + ("latents_turned", "picture", "raised", "mixed_f32", "asked", "self_attend", "self_up", "self_down")
    + ("cross_down", "cross_up", "cross_out", "query_weight", "key_wide", "value_wide")
)
BACK_VMEM = ("inverse_total", "any_kept", "norm_gains")
BACK_OUT = {
    "out_S": ((64, 2 * 6 * 256), B16),
    "out_P": ((32, 2 * 4 * 256), B16),
    "out_Q": ((32, 2 * 4 * 256), B16),
    "home": ((16, PAD, LANES), B16),
    "latents_home": ((ROWS, WIDE), B16),
    "latgrad_home": ((ROWS, WIDE), B16),
    "out_gains": ((8, WIDE), F32),
}


def back_kernel(names, sems, *refs):
    l, c, s, t = place()
    z, x = lax.div(s, 4), lax.rem(s, 4)
    seq = 16
    r = dict(zip(names, refs))
    send, recv, local = r["send"], r["recv"], r["local"]
    cross_scale = 1.0 / math.sqrt(WIDE)
    self_scale = 1.0 / math.sqrt(HEAD_WIDTH)

    partner = {
        "XA": (2 * l + c, z * 4 + flip(x), t),
        "XB": (2 * l + c, z * 4 + 3 - x, t),
        "ZA": (2 * l + c, flip(z) * 4 + x, t),
        "ZB": (2 * l + c, (3 - z) * 4 + x, t),
        "L": (2 * (1 - l) + c, s, t),
        "O": (2 * (1 - l) + c, s, 1 - t),
        "X2": (2 * l + c, z * 4 + lax.rem(x + 2, 4), t),
        "Z2": (2 * l + c, lax.rem(z + 2, 4) * 4 + x, t),
        "T": (2 * l + c, s, 1 - t),
        "C": (2 * l + 1 - c, s, t),
        "D": (2 * (1 - l) + 1 - c, s, t),
    }

    def peer(k):
        return (2 * l + t, lax.rem(s + k, seq), c)

    barrier = pltpu.get_barrier_semaphore()
    for device in partner.values():
        pl.semaphore_signal(barrier, inc=1, device_id=device, device_id_type=MESH)
    def plane(k):
        return (2 * l + c, lax.rem(s + k, seq), t)

    for k in range(1, seq):
        pl.semaphore_signal(barrier, inc=1, device_id=plane(k), device_id_type=MESH)

    @pl.when(c != t)
    def _():
        pl.semaphore_signal(barrier, inc=1, device_id=peer(0), device_id_type=MESH)
        pl.semaphore_wait(barrier, len(partner) + seq)

    @pl.when(c == t)
    def _():
        pl.semaphore_wait(barrier, len(partner) + seq - 1)

    used = [0, 0]
    waits = []

    def remote_of(src, dst, device):
        i = used[0]
        used[0] += 1
        return pltpu.make_async_remote_copy(
            src_ref=src, dst_ref=dst, send_sem=send.at[i], recv_sem=recv.at[i], device_id=device, device_id_type=MESH
        )

    def remote(src, dst, device):
        copy = remote_of(src, dst, device)
        copy.start()
        waits.append(copy)
        return copy

    def sent(*copies):
        for copy in copies:
            copy.wait_send()
            waits[:] = [other for other in waits if other is not copy]

    def here_of(src, dst):
        i = used[1]
        used[1] += 1
        return pltpu.make_async_copy(src, dst, local.at[i])

    def here(src, dst):
        copy = here_of(src, dst)
        copy.start()
        return copy

    ready = {}

    def await_all(*wanted):
        for name in wanted:
            for wait in ready.pop(name):
                wait()

    def load(name, to, key=None):
        ready[key or name] = [here(r[name], to).wait]

    sib = partner["C"]
    top, low = pl.ds(0, ROWS), pl.ds(ROWS, ROWS)
    keep512 = pl.ds(pl.multiple_of(512 * c, LANES), 512)
    give512 = pl.ds(pl.multiple_of(512 * (1 - c), LANES), 512)
    keep256 = pl.ds(pl.multiple_of(256 * c, LANES), 256)
    give256 = pl.ds(pl.multiple_of(256 * (1 - c), LANES), 256)
    left, right = pl.ds(0, 256), pl.ds(256, 256)
    x1, x2, x3, x4, x5 = (r["x%d" % k] for k in range(1, 6))
    up_w, down_w, probs = r["w_up"], r["w_down"], r["v_probs"]

    load("after_attend", r["v_norm"])
    ready["up"] = [
        here(r["self_up"], up_w.at[:, pl.ds(0, 512)]).wait,
        here(r["up_far"], up_w.at[:, pl.ds(512, 512)]).wait,
    ]
    load("cot", x1)
    ready["down"] = [
        here(r["self_down"], down_w.at[pl.ds(0, 512)]).wait,
        here(r["down_far"], down_w.at[pl.ds(512, 512)]).wait,
    ]
    load("out_mine", r["w_out_mine"])
    load("projected", r["v_projected"])
    load("probs", probs)
    load("mixed", r["y_mixed"])
    ready["attend_own"] = [
        here(r["self_attend"].at[:, :, keep256], r["w_attend_own"]).wait
    ]
    load("attend_far", r["w_attend_far"])
    load("attend_in", x4)
    load("cross_hidden", r["v_hidden"])
    load("value_wide", r["w_value"])
    load("key_wide", r["w_key"])
    load("picture", r["v_picture"])
    load("mixed_f32", r["v_mixed"])
    load("asked", r["v_asked"])
    load("mixed_pixels", r["y_mixed_pixels"])

    class Part:
        def __init__(self, set_, q):
            self.stages, self.depth = SETS[set_][0][q], SETS[set_][1]
            self.set, self.q, self.stage, self.n = set_, q, -1, 64
            self.key = "%s%d_" % (set_, q)
            self.cur = r[self.key + "buf"]
            order = [bit for stage in self.stages for bit in stage]
            self.weight = {bit: 32 >> k for k, bit in enumerate(order)}
            self.done = False

        def index(self, **bits):
            return sum(value * self.weight[bit] for bit, value in bits.items())

        def begin(self):
            self.stage += 1
            k, n = self.stage, self.n
            if k < len(self.stages):
                bits = self.stages[k]
                self.into = r[self.key + "in%d" % k]
                if len(bits) == 1:
                    ways = bits
                else:
                    ways = (bits[1], bits[0], BOTH[bits])
                m = n // (len(ways) + 1)
                self.n = m
                self.copies = [
                    remote(self.cur.at[pl.ds((j + 1) * m, m)], self.into.at[j], partner[way])
                    for j, way in enumerate(ways)
                ]
                return
            count = len(SETS[self.set][0])
            dst = r["out_" + self.set].at[
                pl.ds(pl.multiple_of(l * self.depth, self.depth), self.depth),
                pl.ds(pl.multiple_of((count * c + self.q) * 256, LANES), 256),
            ]
            self.copies = [remote(self.cur.at[0], dst, partner[way]) for way in ("L", "C", "D")]
            self.copy_here = here(self.cur.at[0], dst)

        def finish(self):
            for copy in self.copies:
                copy.wait_recv()
            if self.stage == len(self.stages):
                self.copy_here.wait()
                self.done = True
                return
            cur, into, ways = self.cur, self.into, len(self.copies)
            m = min(self.n, 4)

            def step(i):
                rows = pl.ds(i * m, m)
                total = cur[rows].astype(F32)
                for j in range(ways):
                    total = total + into[j, rows].astype(F32)
                cur[rows] = total.astype(B16)

            if self.n > m:
                loop(self.n // m, step)
            else:
                step(0)

        def advance(self):
            if self.done:
                return
            self.finish()
            if not self.done:
                self.begin()

    parts = {(set_, q): Part(set_, q) for set_ in SETS for q in range(len(SETS[set_][0]))}

    def advance(set_, *some):
        for q in some or range(len(SETS[set_][0])):
            parts[set_, q].advance()

    def product(x_ref, y_ref, width, pieces, add=False):
        span = 512 if width <= 512 else 256
        per = span // 256

        def step(i):
            columns = block(i, span)
            whole = tdot(x_ref[:, columns], y_ref[...])
            for a in range(per):
                zz = i * per + a
                zb = lax.rem(lax.div(z, 2) + lax.div(zz, 2), 2)
                za = lax.rem(lax.rem(z, 2) + lax.rem(zz, 2) + zb, 2)
                for xx in range(4):
                    xb = lax.rem(lax.div(x, 2) + xx // 2, 2)
                    xa = lax.rem(lax.rem(x, 2) + xx % 2 + xb, 2)
                    at = (a * 4 + xx) * 64
                    for part, src, width_, half in pieces:
                        for k in range(64 // part.depth):
                            ll = k % 2
                            o = half if half is not None else lax.rem(k // 2 + t, 2)
                            idx = part.index(ZA=za, ZB=zb, XA=xa, XB=xb, O=o, L=lax.rem(ll + l + o, 2))
                            value = whole[at + k * part.depth : at + (k + 1) * part.depth, src : src + width_]
                            to = pl.ds(0, width_)
                            if add:
                                value = value + part.cur[idx, :, to].astype(F32)
                            part.cur[idx, :, to] = value.astype(B16)

        loop(WIDE // span, step)

    def heads(q, at=0):
        return [("S", q, at, 0), ("S", q, at + 256, 1)]

    def product_heads(x_ref, y_ref, width, wanted):
        product(x_ref, y_ref, width, [(parts["S", q], at, 256, half) for _, q, at, half in wanted])

    def product_rows(x_ref, y_ref, width, set_, q, add=False):
        pieces, at = [], 0
        while at < width:
            n = min(256, width - at)
            pieces.append((parts[set_, q + at // 256], at, n, None))
            at += n
        product(x_ref, y_ref, width, pieces, add)

    r["gains"][...] = jnp.zeros_like(r["gains"])

    def norm_grad(value_ref, gain, slot, after):
        def step(i):
            rows = block(i, 64)
            high, inverse = norm_parts(value_ref[rows, :].astype(F32))
            e = r["v_tmp"][rows, :]
            a = e * gain
            back = (
                a - jnp.mean(a, axis=-1, keepdims=True) - high * jnp.mean(a * high, axis=-1, keepdims=True)
            ) * inverse
            r["gains"][pl.ds(slot, 1), :] += jnp.sum(e * high, axis=0, keepdims=True)
            after(rows, back)

        loop(ROWS // 64, step)

    def add_grad(low_ref):
        def after(rows, back):
            total = r["v_grad"][rows, :] + back
            r["v_grad"][rows, :] = total
            low_ref[rows, :] = total.astype(B16)

        return after

    def pull(a_ref, w_ref, store):
        def step(i):
            rows = block(i, 256)
            store(rows, dot_t(a_ref[...], w_ref[rows, :]))

        loop(w_ref.shape[0] // 256, step)

    def to_tmp(columns, value):
        r["v_tmp"][:, columns] = value

    def halves(name, src, to):
        copy = remote(src.at[:, give512], to.at[low], sib)
        ready[name] = [here(src.at[:, keep512], to.at[top]).wait, copy.wait_recv]
        return copy

    await_all("after_attend")

    def feed_norm(i):
        rows = block(i, 64)
        high, _ = norm_parts(r["v_norm"][rows, :])
        x2[rows, :] = (high * r["norm_gains"][3:4, :]).astype(B16)

    loop(ROWS // 64, feed_norm)
    feed_in_copy = remote(x2.at[top], x2.at[low], sib)
    await_all("up", "cot", "down")

    def feed_step(i):
        columns = block(i, 256)
        hidden = dot(x2[top, :], up_w[:, columns])
        r["v_feed_act"][:, columns] = gelu(hidden).astype(B16)
        pulled = dot_t(x1[top, :], down_w[columns, :])
        r["v_feed_back"][:, columns] = (gelu_slope(hidden) * pulled).astype(B16)

    loop(4, feed_step)
    quarter_sends = []
    for name in ("feed_act", "feed_back"):
        ref, to = r["v_" + name], r["y_" + name]
        quarter_sends += [
            remote(ref.at[:, give256], to.at[low, left], sib),
            remote(ref.at[:, pl.ds(768, 256)], to.at[low, right], sib),
        ]
        ready["y_" + name] = [
            here(ref.at[:, keep256], to.at[top, left]).wait,
            here(ref.at[:, pl.ds(512, 256)], to.at[top, right]).wait,
        ] + [copy.wait_recv for copy in quarter_sends[-2:]]
    pull(r["v_feed_back"], up_w, to_tmp)

    def feed_after(rows, back):
        total = x1[rows, :].astype(F32) + back
        r["v_grad"][rows, :] = total
        x3[rows, :] = total.astype(B16)

    norm_grad(r["v_norm"], r["norm_gains"][3:4, :], 3, feed_after)
    branch_copy = remote(x3.at[top], x3.at[low], sib)
    load("cross_up", up_w, "cross_up")

    def latents_step(i):
        columns = block(i, 256)
        r["v_latents_out"][:, columns] = (
            r["v_norm"][:, columns] + dot(r["v_feed_act"][...], down_w[:, columns])
        ).astype(B16)

    loop(4, latents_step)
    load("cross_down", down_w, "cross_down")
    load("after_mlp", r["v_norm"], "after_mlp")
    out_move, out_stay = remote_of(r["v_latents_out"], r["latents_home"], peer(0)), here_of(r["v_latents_out"], r["latents_home"])

    @pl.when(c != t)
    def _():
        out_move.start()

    @pl.when(c == t)
    def _():
        out_stay.start()

    await_all("y_feed_act")
    product_heads(x1, r["y_feed_act"], 512, heads(0))
    parts["S", 0].begin()
    load("cross_act", x1, "x_cross_act")
    feed_in_copy.wait_recv()
    await_all("y_feed_back")
    product_heads(x2, r["y_feed_back"], 512, heads(1))
    parts["S", 1].begin()
    sent(feed_in_copy)
    load("late_x", x2, "x_late_x")

    branch_copy.wait_recv()
    await_all("out_mine", "projected", "probs", "mixed")

    def mixed_step(columns, value):
        r["v_self_grad"][:, columns] = value.astype(B16)

    pull(x3, r["w_out_mine"], mixed_step)
    product_heads(x3, r["y_mixed"], 512, heads(2))
    parts["S", 2].begin()
    sent(branch_copy)
    load("cross_in", x3, "x_cross_in")
    projected, y_back = r["v_projected"], r["y_back"]

    def attend_back(h):
        columns = block(h, HEAD_WIDTH)
        query, key, value = (projected[k, :, columns] for k in range(3))
        key_sum = value_sum = 0
        for j in range(2):
            rows = pl.ds(ROWS * j, ROWS)
            grad = r["v_self_grad"][rows, columns]
            p = probs[2 * h + j]
            g = dot_t(grad, value)
            p32 = p.astype(F32)
            change = (p32 * (g - jnp.sum(p32 * g, axis=-1, keepdims=True))).astype(B16)
            y_back[rows, columns] = (dot(change, key) * self_scale).astype(B16)
            key_sum = key_sum + tdot(change, projected[0, rows, columns])
            value_sum = value_sum + tdot(p, grad)
        y_back[:, pl.ds(pl.multiple_of(512 + h * HEAD_WIDTH, LANES), HEAD_WIDTH)] = (key_sum * self_scale).astype(B16)
        y_back[:, pl.ds(pl.multiple_of(1024 + h * HEAD_WIDTH, LANES), HEAD_WIDTH)] = value_sum.astype(B16)

    loop(4, attend_back)
    load("raised", probs)
    await_all("attend_own", "attend_far")

    def rows_step(i):
        rows = block(i, 256)
        total = 0
        for k in range(3):
            total = total + dot_t(y_back[:, pl.ds(512 * k, 256)], r["w_attend_own"][k, rows, :])
            total = total + dot_t(y_back[:, pl.ds(512 * k + 256, 256)], r["w_attend_far"][k, rows, :])
        r["v_tmp"][:, rows] = total[:ROWS]
        r["v_rows_give"][:, rows] = total[ROWS:].astype(B16)

    loop(4, rows_step)
    rows_copy = remote(r["v_rows_give"], r["v_rows_in"], sib)
    await_all("attend_in")
    product_heads(x4, y_back, 1536, [piece for k in range(3) for piece in heads(3 + k, 512 * k)])
    for q in (3, 4, 5):
        parts["S", q].begin()
    load("attended", x4, "x_attended")
    rows_copy.wait_recv()

    def sum_step(i):
        rows = block(i, 64)
        r["v_tmp"][rows, :] += r["v_rows_in"][rows, :].astype(F32)

    loop(ROWS // 64, sum_step)
    await_all("after_mlp")
    mlp_branch, cross_branch = r["v_branch"], r["v_rows_give"]
    norm_grad(r["v_norm"], r["norm_gains"][2:3, :], 2, add_grad(mlp_branch))
    load("after_cross", r["v_norm"], "after_cross")

    halves("y_mlp", mlp_branch, r["y_mlp"])
    await_all("cross_down", "cross_hidden")

    def hidden_store(columns, value):
        r["v_back"][:, columns] = (gelu_slope(r["v_hidden"][:, columns]) * value).astype(B16)

    pull(mlp_branch, down_w, hidden_store)
    load("cross_out", down_w, "cross_out")
    halves("y_hidden", r["v_back"], r["y_hidden"])
    await_all("cross_up")
    pull(r["v_back"], up_w, to_tmp)
    load("query_weight", up_w, "query_weight")
    advance("S", 0, 1)
    sent(rows_copy)
    await_all("after_cross")
    norm_grad(r["v_norm"], r["norm_gains"][1:2, :], 1, add_grad(cross_branch))
    halves("y_out", cross_branch, r["y_out"])
    await_all("cross_out")

    def attended_store(columns, value):
        x5[top, columns] = value.astype(B16)

    pull(cross_branch, down_w, attended_store)
    attended_copy = remote(x5.at[top], x5.at[low], sib)
    await_all("x_cross_act", "y_mlp")
    product_rows(x1, r["y_mlp"], 512, "P", 0)
    parts["P", 0].begin()
    parts["P", 1].begin()
    await_all("x_cross_in", "y_hidden")
    product_rows(x3, r["y_hidden"], 512, "P", 2)
    parts["P", 2].begin()
    parts["P", 3].begin()
    advance("S", 2)

    await_all("value_wide", "mixed_f32", "asked", "picture", "raised")
    pull_low = dot_t(x5[top, :], r["w_value"][...]).astype(B16)
    r["v_pull"][...] = pull_low
    pull_f32 = pull_low.astype(F32)
    r["v_dot"][...] = jnp.sum(pull_f32 * r["v_mixed"][...], axis=-1, keepdims=True)
    scale_any = r["inverse_total"][...] * r["any_kept"][...]
    r["v_asked_t"][...] = (r["v_asked"][...].astype(F32) * scale_any).T.astype(B16)
    r["v_pull_t"][...] = (pull_f32 * r["inverse_total"][...]).T.astype(B16)
    r["v_sum"][...] = jnp.zeros_like(r["v_sum"])

    def pixel_chunk(i, to, at):
        picture, raised = r["v_picture"][:, block(i, 512)], probs[i]
        change = (raised.astype(F32) * (dot(r["v_pull"][...], picture) - r["v_dot"][...])).astype(B16)
        r["v_sum"][...] += dot_t(change, picture)
        grad = (dot(r["v_asked_t"][...], change) + dot(r["v_pull_t"][...], raised)).astype(B16)
        for j in range(4):
            to[4 * at + j] = grad[:, j * LANES : (j + 1) * LANES]

    loop(4, lambda i: pixel_chunk((1 - c) * 4 + i, r["grad_far"], i))
    grad_copy = remote(r["grad_far"], r["grad_in"], sib)
    loop(4, lambda i: pixel_chunk(c * 4 + i, r["grad_own"], i))

    turned_sum = r["v_sum"][...] * scale_any
    r["y_late_own"][...] = jnp.zeros_like(r["y_late_own"])
    r["y_late_own"][:, :PAD] = (turned_sum * cross_scale).astype(B16)
    ready["y_late"] = [
        here(r["y_late_own"], r["y_late"].at[top]).wait,
        remote(r["y_late_own"], r["y_late"].at[low], sib).wait_recv,
    ]
    r["gains"][4:5, :PAD] = jnp.sum(
        r["v_asked"][...].astype(F32) * turned_sum + pull_f32 * r["v_mixed"][...], axis=0, keepdims=True
    )


    grad_copy.wait_recv()

    def grad_step(i):
        r["grad_own"][i] = (r["grad_own"][i].astype(F32) + r["grad_in"][i].astype(F32)).astype(B16)

    loop(seq, grad_step)

    hops = [(i, j) for i in range(4) for j in range(4)]

    def towards(i, j):
        return 4 * lax.rem(z + i, 4) + lax.rem(x + j, 4)

    def home_of(i, j, ref, sem):
        to = towards(i, j)
        return pltpu.make_async_remote_copy(
            src_ref=ref.at[to],
            dst_ref=r["home"].at[s],
            send_sem=send.at[sem],
            recv_sem=recv.at[sem],
            device_id=(2 * l + c, to, t),
            device_id_type=MESH,
        )

    first_sem = used[0]
    used[0] += len(hops)
    own_way = [home_of(i, j, r["grad_own"], first_sem + k) if k else None for k, (i, j) in enumerate(hops)]
    far_way = [home_of(i, j, r["grad_relay"], first_sem + k) if k else None for k, (i, j) in enumerate(hops)]

    def group(i):
        return block(lax.rem(z + i, 4), 4)

    crossing = [remote_of(r["grad_own"].at[group(i)], r["grad_relay"].at[group(i)], peer(0)) for i in range(4)]
    stay, stay_far = here_of(r["grad_own"].at[s], r["home"].at[s]), here_of(r["grad_relay"].at[s], r["home"].at[s])

    @pl.when(c != t)
    def _():
        for copy in crossing:
            copy.start()

    @pl.when(c == t)
    def _():
        stay.start()
        for copy in own_way[1:]:
            copy.start()

    await_all("x_attended", "y_out")
    product_rows(x4, r["y_out"], 512, "Q", 0)
    parts["Q", 0].begin()
    parts["Q", 1].begin()
    attended_copy.wait_recv()
    await_all("mixed_pixels")
    product_rows(x5, r["y_mixed_pixels"], 512, "Q", 2)
    await_all("x_late_x", "y_late")
    product_rows(x2, r["y_late"], 384, "Q", 2, add=True)
    parts["Q", 2].begin()
    parts["Q", 3].begin()
    advance("S", 3, 4, 5)
    advance("S", 0, 1, 2)
    advance("P")

    @pl.when(c != t)
    def _():
        for i in range(4):
            crossing[i].wait_recv()
            for j in range(4):
                (far_way[4 * i + j] if i or j else stay_far).start()

    sent(*quarter_sends)
    latents, latgrad = r["v_feed_act"], r["v_feed_back"]
    load("latents_turned", latents)
    await_all("key_wide", "query_weight", "latents_turned")
    r["v_rows_in"][...] = dot(r["y_late_own"][:, :PAD], r["w_key"][...]).astype(B16)
    pull(r["v_rows_in"], up_w, to_tmp)

    def latents_after(rows, back):
        latgrad[rows, :] = (r["v_grad"][rows, :] + back).astype(B16)

    norm_grad(latents, r["norm_gains"][0:1, :], 0, latents_after)
    grad_move, grad_stay = remote_of(latgrad, r["latgrad_home"], peer(0)), here_of(latgrad, r["latgrad_home"])

    @pl.when(c != t)
    def _():
        grad_move.start()

    @pl.when(c == t)
    def _():
        grad_stay.start()

    gain_buf, gain_in = r["gain_buf"], r["gain_in"]
    gain_stages = [tuple(bits) + (BOTH[bits],) for bits in (X, Z, Y)] + [("C",)]
    gain_buf[0] = r["gains"][...]

    def send_gains(k):
        return [remote(gain_buf.at[k], gain_in.at[k, j], partner[way]) for j, way in enumerate(gain_stages[k])]

    gain_copies = send_gains(0)
    live = [parts[key] for key in parts]
    k = 0
    while live or k < 4:
        if k < 4:
            for copy in gain_copies:
                copy.wait_recv()
            total = gain_buf[k] + gain_in[k, 0]
            if k < 3:
                total = total + (gain_in[k, 1] + gain_in[k, 2])
            k += 1
            if k < 4:
                gain_buf[k] = total
                gain_copies = send_gains(k)
            else:
                r["out_gains"][...] = total
        for part in live:
            part.advance()
        live = [part for part in live if not part.done]

    @pl.when(c != t)
    def _():
        out_move.wait()
        grad_move.wait()
        stay_far.wait()
        for copy in crossing:
            copy.wait_send()

    @pl.when(c == t)
    def _():
        out_stay.wait()
        grad_stay.wait()
        stay.wait()

    for copy in own_way[1:]:
        copy.wait()
    for copy in waits:
        copy.wait_send()
    assert not ready, tuple(ready)
    assert used[0] <= sems[0] and used[1] <= sems[1], used


def back_and_reduce(given):
    names, scratch = [], []

    def room(name, shape, dtype=B16):
        names.append(name)
        scratch.append(pltpu.VMEM(shape, dtype))

    sems = (210, 58)
    names += list(BACK_HBM) + list(BACK_VMEM) + list(BACK_OUT)
    for name in ("send", "recv", "local"):
        names.append(name)
        scratch.append(pltpu.SemaphoreType.DMA((sems[1 if name == "local" else 0],)))
    for k in range(1, 6):
        room("x%d" % k, (512, WIDE))
    for name in ("feed_act", "feed_back", "mixed", "mixed_pixels", "mlp", "hidden", "out"):
        room("y_" + name, (512, 512))
    room("y_back", (512, 1536))
    room("y_late", (512, 384))
    room("y_late_own", (ROWS, 384))
    for name in ("w_down", "w_up"):
        room(name, (WIDE, WIDE))
    room("w_out_mine", (512, WIDE))
    for name in ("w_attend_own", "w_attend_far"):
        room(name, (3, WIDE, 256))
    for name in ("w_key", "w_value"):
        room(name, (PAD, WIDE))
    for name in ("v_tmp", "v_norm", "v_grad", "v_hidden"):
        room(name, (ROWS, WIDE), F32)
    for name in ("rows_in", "rows_give", "branch", "back", "feed_act", "feed_back", "latents_out"):
        room("v_" + name, (ROWS, WIDE))
    room("v_projected", (3, 512, 512))
    room("v_probs", (8, ROWS, 512))
    room("v_self_grad", (512, 512))
    room("v_picture", (PAD, 4096))
    room("v_mixed", (ROWS, PAD), F32)
    room("v_sum", (ROWS, PAD), F32)
    room("v_asked", (ROWS, PAD))
    room("v_pull", (ROWS, PAD))
    room("v_asked_t", (PAD, ROWS))
    room("v_pull_t", (PAD, ROWS))
    room("v_dot", (ROWS, 1), F32)
    for name in ("grad_own", "grad_far", "grad_in", "grad_relay"):
        room(name, (16, PAD, LANES))
    room("gains", (8, WIDE), F32)
    room("gain_buf", (4, 8, WIDE), F32)
    room("gain_in", (4, 3, 8, WIDE), F32)
    for set_, (plans, depth) in SETS.items():
        for q, stages in enumerate(plans):
            key, n = "%s%d_" % (set_, q), 64
            room(key + "buf", (n, depth, 256))
            for k, bits in enumerate(stages):
                n >>= len(bits)
                room(key + "in%d" % k, (2 ** len(bits) - 1, n, depth, 256))
    anywhere = pl.BlockSpec(memory_space=pl.ANY)
    vmem = pl.BlockSpec(memory_space=pltpu.VMEM)
    result = pl.pallas_call(
        functools.partial(back_kernel, tuple(names), sems),
        out_shape=[jax.ShapeDtypeStruct(*spec) for spec in BACK_OUT.values()],
        in_specs=[anywhere] * len(BACK_HBM) + [vmem] * len(BACK_VMEM),
        out_specs=[anywhere] * (len(BACK_OUT) - 1) + [vmem],
        scratch_shapes=scratch,
        compiler_params=pltpu.CompilerParams(collective_id=1, has_side_effects=True, vmem_limit_bytes=63 * MIB),
        name="back_and_reduce",
    )(*[given[name] for name in BACK_HBM + BACK_VMEM])
    return dict(zip(BACK_OUT, result))


FINISH_IN = ("pixels", "home", "out_S", "out_P", "out_Q", "latgrad_home", "latents_home", "key_wide")
FINISH_OUT = ("pixels_grad", "latents_grad", "latents_out")


def finish_kernel(*refs):
    refs = list(refs)

    def take(n):
        part = refs[:n]
        del refs[:n]
        return part

    hbm = dict(zip(FINISH_IN, take(len(FINISH_IN))))
    gain, gains = take(2)
    results = dict(zip(FINISH_OUT, take(len(FINISH_OUT))))
    gain_rows = take(4)
    pixelgain, query_grad, key_grad, value_grad, crossout, crossup, crossdown = take(7)
    selfattend, selfout, selfup, selfdown = take(4)
    vmem = dict(zip(FINISH_IN, take(len(FINISH_IN))))
    turned, high, grad, latgrad, wide_gain, sems = take(6)
    pixels, home = vmem["pixels"], vmem["home"]
    channels = pixels.shape[0]

    copies = {
        name: pltpu.make_async_copy(hbm[name], vmem[name], sems.at[k])
        for k, name in enumerate(FINISH_IN)
    }
    last = len(FINISH_IN)
    straight = pltpu.make_async_copy(vmem["latents_home"], results["latents_out"], sems.at[last])
    for copy in copies.values():
        copy.start()

    some = 29

    def features(i):
        return pl.ds(i * some, some)

    steps = channels // some
    per_feature(gain, wide_gain)
    copies["pixels"].wait()
    zeros = jnp.zeros(pixels.shape[1:], F32)
    average = lax.fori_loop(
        0, steps, lambda i, total: total + jnp.sum(pixels[features(i)].astype(F32), axis=0), zeros
    ) * (1.0 / channels)

    def square_step(i, total):
        centered = pixels[features(i)].astype(F32) - average
        return total + jnp.sum(centered * centered, axis=0)

    inverse = lax.rsqrt(lax.fori_loop(0, steps, square_step, zeros) * (1.0 / channels) + EPS)
    copies["home"].wait()
    for image in range(16):
        turned[pl.ds(image, PAD, stride=16), :] = home[image].astype(F32)

    def mean_step(i, totals):
        h = (pixels[features(i)].astype(F32) - average) * inverse
        rows = pl.ds(pl.multiple_of(i * (some * 16), 16), some * 16)
        a = turned[rows, :].reshape(some, 16, LANES) * wide_gain[features(i), :][:, None, :]
        high[features(i)] = h
        grad[features(i)] = a
        return totals[0] + jnp.sum(a, axis=0), totals[1] + jnp.sum(a * h, axis=0)

    first, second = lax.fori_loop(0, steps, mean_step, (zeros, zeros))
    first, second = first * (1.0 / channels), second * (1.0 / channels)

    def grad_step(i):
        grad[features(i)] = (grad[features(i)] - first - high[features(i)] * second) * inverse

    loop(steps, grad_step)
    pixels_out = pltpu.make_async_copy(grad, results["pixels_grad"], sems.at[last + 1])
    pixels_out.start()
    copies["latents_home"].wait()
    straight.start()
    copies["latgrad_home"].wait()
    latgrad[...] = vmem["latgrad_home"][...].astype(F32)
    latents_out = pltpu.make_async_copy(latgrad, results["latents_grad"], sems.at[last + 2])
    latents_out.start()

    for name in ("out_S", "out_P", "out_Q", "key_wide"):
        copies[name].wait()
    out_s, out_p, out_q = vmem["out_S"], vmem["out_P"], vmem["out_Q"]
    late = [out_q[:, 512:1024], out_q[:, 1536:2048]]
    query_grad[...] = dot(late[0][:, :PAD], vmem["key_wide"][...])
    key_grad[...] = late[1][:, :channels].astype(F32)
    value_grad[:, :LANES] = late[0][:, 384:].astype(F32)
    value_grad[:, LANES : 2 * LANES] = late[1][:, 384:].astype(F32)
    value_grad[:, 2 * LANES :] = late[0][:, 256:384].astype(F32)[:, 16 : 16 + channels - 2 * LANES]
    for k, ref in enumerate((crossdown, crossup)):
        for core in range(2):
            ref[:, pl.ds(512 * core, 512)] = out_p[:, pl.ds(1024 * core + 512 * k, 512)].astype(F32)
    for core in range(2):
        crossout[:, pl.ds(512 * core, 512)] = out_q[:, pl.ds(1024 * core, 512)].astype(F32)

    def item(k, core):
        return out_s[:, pl.ds(1536 * core + 256 * k, 256)].astype(F32)

    for core in range(2):
        columns = pl.ds(256 * core, 256)
        selfdown[:, columns] = item(0, core)
        selfup[:, columns] = item(1, core)
        selfout[:, columns] = item(2, core)
        for k in range(3):
            selfattend[k, :, columns] = item(3 + k, core)

    mine = 2 * lax.axis_index("seq") + lax.axis_index("tensor")
    rolled = pltpu.roll(gains[...], lax.rem(WIDE - 32 * mine, WIDE), 1)
    for k, ref in enumerate(gain_rows):
        ref[...] = rolled[k : k + 1, :32].reshape(32)
    pixelgain[...] = (gains[4:5, :channels] / row_of(gain)).reshape(channels)
    straight.wait()
    pixels_out.wait()
    latents_out.wait()


def finish(given):
    pixels = given["pixels"]
    channels, images, rows = pixels.shape
    small = [(32,)] * 4 + [
        (channels,),
        (32, WIDE),
        (32, channels),
        (32, channels),
        (32, WIDE),
        (32, WIDE),
        (32, WIDE),
        (3, 64, 512),
        (64, 512),
        (64, 512),
        (64, 512),
    ]
    anywhere = pl.BlockSpec(memory_space=pl.ANY)
    vmem = pl.BlockSpec(memory_space=pltpu.VMEM)
    return pl.pallas_call(
        finish_kernel,
        out_shape=[
            jax.ShapeDtypeStruct(pixels.shape, F32),
            jax.ShapeDtypeStruct((ROWS, WIDE), F32),
            jax.ShapeDtypeStruct((ROWS, WIDE), B16),
        ]
        + [jax.ShapeDtypeStruct(shape, F32) for shape in small],
        in_specs=[anywhere] * len(FINISH_IN) + [vmem] * 2,
        out_specs=[anywhere] * 3 + [vmem] * len(small),
        scratch_shapes=[pltpu.VMEM(given[name].shape, given[name].dtype) for name in FINISH_IN]
        + [
            pltpu.VMEM((PAD * images, rows), F32),
            pltpu.VMEM(pixels.shape, F32),
            pltpu.VMEM(pixels.shape, F32),
            pltpu.VMEM((ROWS, WIDE), F32),
            pltpu.VMEM((384, LANES), F32),
            pltpu.SemaphoreType.DMA((len(FINISH_IN) + 3,)),
        ],
        compiler_params=pltpu.CompilerParams(vmem_limit_bytes=60 * MIB),
        name="finish",
    )(*[given[name] for name in FINISH_IN], given["pixel_gain"], given["out_gains"])


def shards(
    latents,
    pixels,
    crop_bounds,
    key_mask,
    query_gain,
    pixel_gain,
    cross_gain,
    attend_gain,
    feed_gain,
    query_weight,
    key_weight,
    value_weight,
    cross_out,
    cross_up,
    cross_down,
    self_attend,
    self_out,
    self_up,
    self_down,
    cotangent,
):
    channels = pixels.shape[2]
    given = {
        "pixels": jnp.transpose(pixels, (2, 0, 1)),
        "latents": latents[0],
        "cotangent": cotangent[0],
        "query_weight": query_weight,
        "key_weight": key_weight,
        "value_weight": value_weight,
        "cross_out": cross_out,
        "cross_up": cross_up,
        "cross_down": cross_down,
        "self_attend": self_attend,
        "self_out": self_out,
        "self_up": self_up,
        "self_down": self_down,
        "query_gain": query_gain,
        "cross_gain": cross_gain,
        "attend_gain": attend_gain,
        "feed_gain": feed_gain,
        "pixel_gain": pixel_gain,
        "key_mask": key_mask,
        "crop_bounds": crop_bounds,
    }
    given |= front(given)
    given |= back_and_reduce(given)
    (
        pixels_grad,
        latents_grad,
        latents_out,
        querygain,
        crossgain,
        attendgain,
        feedgain,
        pixelgain,
        queryweight_grad,
        keyweight_grad,
        valueweight_grad,
        crossout_grad,
        crossup_grad,
        crossdown_grad,
        selfattend_grad,
        selfout_grad,
        selfup_grad,
        selfdown_grad,
    ) = finish(given)
    return (
        latents_out[None],
        latents_grad[None],
        jnp.transpose(pixels_grad, (1, 2, 0)),
        querygain,
        pixelgain,
        crossgain,
        attendgain,
        feedgain,
        queryweight_grad,
        keyweight_grad.T,
        valueweight_grad.T,
        crossout_grad,
        crossup_grad,
        crossdown_grad,
        selfattend_grad,
        selfout_grad.T,
        selfup_grad,
        selfdown_grad.T,
    )


def solution(mesh):
    in_specs = (
        P(("batch", "seq"), "tensor", None),
        P("batch", ("seq", "tensor"), None),
        P(("batch", "seq"), None),
        P(("batch", "seq"), None),
        P(),
        P(),
        P(),
        P(),
        P(),
        P(),
        P(),
        P(),
        P(),
        P(),
        P(),
        P(None, None, "tensor"),
        P("tensor", None),
        P(None, "tensor"),
        P("tensor", None),
        P(("batch", "seq"), "tensor", None),
    )
    out_specs = (
        P(("batch", "seq"), "tensor", None),
        P(("batch", "seq"), "tensor", None),
        P("batch", ("seq", "tensor"), None),
        P(("seq", "tensor")),
        P(),
        P(("seq", "tensor")),
        P(("seq", "tensor")),
        P(("seq", "tensor")),
        P(("seq", "tensor"), None),
        P(None, ("seq", "tensor")),
        P(None, ("seq", "tensor")),
        P(("seq", "tensor"), None),
        P(("seq", "tensor"), None),
        P(("seq", "tensor"), None),
        P(None, "seq", "tensor"),
        P("tensor", "seq"),
        P("seq", "tensor"),
        P("tensor", "seq"),
    )
    return jax.shard_map(shards, mesh=mesh, in_specs=in_specs, out_specs=out_specs, check_vma=False)
```

```python
import functools
import math

import jax
import jax.numpy as jnp
from jax import lax
from jax.experimental import pallas as pl
from jax.experimental.pallas import tpu as pltpu
from jax.sharding import PartitionSpec as P

HEAD_WIDTH = 128
EPS = 1e-05
MASKED = -1000000000.0
MESH = pl.DeviceIdType.MESH
F32 = jnp.float32
B16 = jnp.bfloat16
LANES = 128
PAD = 272
WIDE = 1024
CYCLE = ("XA", "XB", "ZA", "ZB", "T")

def norm_parts(values):
    average = jnp.mean(values, axis=-1, keepdims=True)
    centered = values - average
    spread = jnp.mean(centered * centered, axis=-1, keepdims=True)
    inverse = lax.rsqrt(spread + EPS)
    return centered * inverse, inverse


def dot(a, b):
    return jnp.dot(a, b, preferred_element_type=F32)


def dot_t(a, b):
    return lax.dot_general(a, b, (((1,), (1,)), ((), ())), preferred_element_type=F32)


def tdot(a, b):
    return lax.dot_general(a, b, (((0,), (0,)), ((), ())), preferred_element_type=F32)


def flip(p):
    return p + 1 - 2 * lax.rem(p, 2)


def place():
    b, s, t = lax.axis_index("batch"), lax.axis_index("seq"), lax.axis_index("tensor")
    return lax.div(b, 2), lax.rem(b, 2), s, t


MIB = 1024 * 1024
ROWS = 256
GELU_K = math.sqrt(2.0 / math.pi)


def gelu(u):
    return 0.5 * u * (1.0 + jnp.tanh(GELU_K * (u + 0.044715 * u * u * u)))


def gelu_slope(u):
    th = jnp.tanh(GELU_K * (u + 0.044715 * u * u * u))
    return 0.5 * (1.0 + th) + 0.5 * u * (1.0 - th * th) * GELU_K * (1.0 + 3.0 * 0.044715 * u * u)


def loop(n, step):
    lax.fori_loop(0, n, lambda i, carry: (step(i), carry)[1], 0)


def row_of(ref):
    return ref[...].astype(F32).reshape(1, ref.shape[0])


def per_feature(gain_ref, out_ref):
    channels = gain_ref.shape[0]
    wide = jnp.concatenate([row_of(gain_ref), jnp.zeros((1, 384 - channels), F32)], axis=1)
    out_ref[...] = jnp.broadcast_to(wide, (LANES, 384)).T


def block(i, n):
    return pl.ds(pl.multiple_of(i * n, n), n)


FRONT_HBM = (
    ("pixels", "latents", "cotangent", "self_attend", "self_out", "self_up", "self_down")
    + ("query_weight", "cross_out", "cross_up", "cross_down")
)
FRONT_VMEM = ("query_gain", "cross_gain", "attend_gain", "feed_gain", "pixel_gain", "key_weight", "value_weight", "key_mask", "crop_bounds")
FRONT_OUT = {
    "cot": ((512, WIDE), B16),
    "cross_act": ((512, WIDE), B16),
    "cross_in": ((512, WIDE), B16),
    "attended": ((512, WIDE), B16),
    "late_x": ((512, WIDE), B16),
    "mixed_pixels": ((512, 512), B16),
    "mixed": ((512, 512), B16),
    "attend_in": ((512, WIDE), B16),
    "projected": ((3, 512, 512), B16),
    "probs": ((8, ROWS, 512), B16),
    "out_mine": ((512, WIDE), B16),
    "attend_far": ((3, WIDE, 256), B16),
    "up_far": ((WIDE, 512), B16),
    "down_far": ((512, WIDE), B16),
    "after_mlp": ((ROWS, WIDE), F32),
    "after_attend": ((ROWS, WIDE), F32),
    "cross_hidden": ((ROWS, WIDE), F32),
    "after_cross": ((ROWS, WIDE), F32),
    "latents_turned": ((ROWS, WIDE), B16),
    "picture": ((PAD, 4096), B16),
    "raised": ((8, ROWS, 512), B16),
    "mixed_f32": ((ROWS, PAD), F32),
    "asked": ((ROWS, PAD), B16),
    "key_wide": ((PAD, WIDE), B16),
    "value_wide": ((PAD, WIDE), B16),
    "inverse_total": ((ROWS, 1), F32),
    "any_kept": ((1, 1), F32),
    "norm_gains": ((8, WIDE), F32),
}
FRONT_OUT_VMEM = ("inverse_total", "any_kept", "norm_gains")


def front_kernel(names, sems, *refs):
    l, c, s, t = place()
    seq = 16
    r = dict(zip(names, refs))
    send, recv, local = r["send"], r["recv"], r["local"]
    cross_scale = 1.0 / math.sqrt(WIDE)
    self_scale = 1.0 / math.sqrt(HEAD_WIDTH)
    sib = (2 * l + 1 - c, s, t)
    over = (2 * (1 - l) + c, s, 1 - t)

    def peer(k):
        return (2 * l + t, lax.rem(s + k, seq), c)

    barrier = pltpu.get_barrier_semaphore()
    for device in (sib, over):
        pl.semaphore_signal(barrier, inc=1, device_id=device, device_id_type=MESH)
    def plane(k):
        return (2 * l + c, lax.rem(s + k, seq), t)

    for k in range(1, seq):
        pl.semaphore_signal(barrier, inc=1, device_id=plane(k), device_id_type=MESH)

    @pl.when(c != t)
    def _():
        pl.semaphore_signal(barrier, inc=1, device_id=peer(0), device_id_type=MESH)
        pl.semaphore_wait(barrier, 2 + seq)

    @pl.when(c == t)
    def _():
        pl.semaphore_wait(barrier, 1 + seq)

    used = [0, 0]
    waits, stores = [], []

    def remote_of(src, dst, device):
        i = used[0]
        used[0] += 1
        return pltpu.make_async_remote_copy(
            src_ref=src, dst_ref=dst, send_sem=send.at[i], recv_sem=recv.at[i], device_id=device, device_id_type=MESH
        )

    def remote(src, dst, device):
        copy = remote_of(src, dst, device)
        copy.start()
        waits.append(copy)
        return copy

    def here_of(src, dst):
        i = used[1]
        used[1] += 1
        return pltpu.make_async_copy(src, dst, local.at[i])

    def here(src, dst):
        copy = here_of(src, dst)
        copy.start()
        return copy

    def store(name, src):
        stores.append(here(src, r[name]))

    top, low = pl.ds(0, ROWS), pl.ds(ROWS, ROWS)
    shared = []

    def share(name, src, give=None):
        stores.append(here(src, r[name].at[top]))
        shared.append(remote(src if give is None else give, r[name].at[low], sib))

    ready = {}

    def await_all(*wanted):
        for name in wanted:
            for wait in ready.pop(name, ()):
                wait()

    base = pl.multiple_of(c * (seq * LANES), LANES)
    picture = r["v_picture"]

    z, x = lax.div(s, 4), lax.rem(s, 4)
    hops = [(i, j) for i in range(4) for j in range(4)]

    def towards(i, j, sign=1):
        return 4 * lax.rem(z + sign * i + 4, 4) + lax.rem(x + sign * j + 4, 4)

    def columns_of(source):
        return picture.at[:, pl.ds(pl.multiple_of(base + source * LANES, LANES), LANES)]

    own_way = [remote_of(r["v_home"].at[towards(i, j)], columns_of(s), (2 * l + c, towards(i, j), t)) for i, j in hops]
    first_sem = used[0] - len(hops)
    far_way = [
        pltpu.make_async_remote_copy(
            src_ref=r["v_relay"].at[towards(i, j)],
            dst_ref=columns_of(s),
            send_sem=send.at[first_sem + k],
            recv_sem=recv.at[first_sem + k],
            device_id=(2 * l + c, towards(i, j), t),
            device_id_type=MESH,
        )
        for k, (i, j) in enumerate(hops)
    ]

    def group(i):
        return block(lax.rem(z + i, 4), 4)

    crossing = [remote_of(r["v_home"].at[group(i)], r["v_relay"].at[group(i)], peer(0)) for i in range(4)]
    lat_move, cot_move = remote_of(r["v_lat_own"], r["v_lat"], peer(0)), remote_of(r["cotangent"], r["v_cot"], peer(0))
    kept_move = remote_of(r["v_kept_own"], r["v_kept"], sib)
    cot_stay = here_of(r["cotangent"], r["v_cot"])
    lat_copy = here(r["latents"], r["v_lat_own"])
    asked_move = remote_of(r["v_asked_own"], r["v_asked"], peer(0))
    kept_stay = here_of(r["v_kept_own"], r["v_kept"])
    picture_stay = here_of(r["v_home"].at[s], columns_of(s))
    picture_cross = here_of(r["v_relay"].at[s], columns_of(s))

    z, x = lax.div(s, 4), lax.rem(s, 4)
    own256 = 256 * c
    own_columns = pl.ds(pl.multiple_of(own256, LANES), 256)
    attend_far, out_w, up_far, down_far = r["w_attend_far"], r["w_out"], r["w_up_far"], r["w_down_far"]
    left = pl.ds(0, 256)

    def rows16(base_row, piece):
        return pl.ds(pl.multiple_of(base_row + 16 * piece, 16), 16)

    shares = {
        "attend": (lambda p: r["self_attend"].at[:, block(p, 64), own_columns], lambda p, n=1: attend_far.at[:, block(p, 64 * n)]),
        "out": (lambda p: r["self_out"].at[rows16(own256, p)], lambda p, n=1: out_w.at[pl.ds(pl.multiple_of(256 + 16 * n * p, 16), 16 * n)]),
        "up": (lambda p: r["self_up"].at[block(p, 64), own_columns], lambda p, n=1: up_far.at[block(p, 64 * n), left]),
        "down": (lambda p: r["self_down"].at[rows16(own256, p)], lambda p, n=1: down_far.at[block(p, 16 * n)]),
    }

    def along(axis, k):
        at = z * 4 + lax.rem(x + k, 4) if axis == "x" else lax.rem(z + k, 4) * 4 + x
        return (2 * l + c, at, t)

    plans = {name: ("z", 4 * x + z, "x", x) if name == "attend" else ("x", 4 * z + x, "z", z) for name in shares}
    first_piece = {name: remote(src(plans[name][1]), dst(plans[name][1]), over) for name, (src, dst) in shares.items()}
    @pl.when(c == t)
    def _():
        cot_stay.start()

    pixels_copy = here(r["pixels"], r["v_pixels"])
    r["norm_gains"][...] = jnp.concatenate(
        [row_of(r[name + "_gain"]) for name in ("query", "cross", "attend", "feed")] + [jnp.zeros((4, WIDE), F32)],
        axis=0,
    )

    pieces, fours = {}, {}

    def spread_pieces(*wanted):
        for name in wanted:
            first_piece[name].wait_recv()
            axis, p, _, _ = plans[name]
            at = shares[name][1](p)
            pieces[name] = [remote(at, at, along(axis, k)) for k in range(1, 4)]

    def spread_fours(*wanted):
        for name in wanted:
            for copy in pieces[name]:
                copy.wait_recv()
            _, _, axis, p = plans[name]
            at = shares[name][1](p, 4)
            fours[name] = [remote(at, at, along(axis, k)) for k in range(1, 4)]

    def gathered(name):
        for copy in fours[name]:
            copy.wait_recv()

    whole = {
        "out": (out_w.at[pl.ds(256, 256)], out_w.at[pl.ds(768, 256)]),
        "up": (up_far.at[:, left], up_far.at[:, pl.ds(256, 256)]),
        "down": (down_far.at[left], down_far.at[pl.ds(256, 256)]),
    }
    sib_quarter = {}

    def gather_pieces(*wanted):
        for name in wanted:
            gathered(name)
            sib_quarter[name] = remote(*whole[name], sib)

    def arrived(*wanted):
        for name in wanted:
            sib_quarter[name].wait_recv()

    pixels_copy.wait()
    pixels, normed = r["v_pixels"], r["v_normed"]
    channels = pixels.shape[0]
    some = 9

    def features(i):
        return pl.ds(i * some, some)

    def sum_step(i, total):
        return total + jnp.sum(pixels[features(i)].astype(F32), axis=0)

    per_feature(r["pixel_gain"], r["v_gain"])
    zeros = jnp.zeros(pixels.shape[1:], F32)
    average = lax.fori_loop(0, channels // some, sum_step, zeros) * (1.0 / channels)

    def square_step(i, total):
        centered = pixels[features(i)].astype(F32) - average
        return total + jnp.sum(centered * centered, axis=0)

    spread = lax.fori_loop(0, channels // some, square_step, zeros) * (1.0 / channels)
    inverse = lax.rsqrt(spread + EPS)

    def norm_step(i):
        value = (pixels[features(i)].astype(F32) - average) * inverse * r["v_gain"][features(i), :][:, None, :]
        normed[pl.ds(pl.multiple_of(i * (some * 16), 16), some * 16), :] = value.reshape(some * 16, LANES)

    loop(channels // some, norm_step)
    normed[channels * 16 :, :] = jnp.zeros(((PAD - channels) * 16, LANES), F32)

    for i in range(4):
        for j in range(4):
            image = towards(i, j)
            r["v_home"][image] = normed[pl.ds(image, PAD, stride=16), :].astype(B16)

            @pl.when(c == t)
            def _():
                (own_way[4 * i + j] if i or j else picture_stay).start()

        @pl.when(c != t)
        def _():
            crossing[i].start()

    start, count = r["crop_bounds"][:, 0:1], r["crop_bounds"][:, 1:2]
    lanes = lax.broadcasted_iota(jnp.int32, (1, LANES), 1)
    for k in range(2 * seq):
        row = lanes + k * LANES
        keep = (row >= start) & (row < start + count) & (r["key_mask"][:, pl.ds(k * LANES, LANES)] == 1)
        to = pl.ds(((k % 2) * seq + k // 2) * LANES, LANES)
        r["v_kept_own"][:, to] = jnp.broadcast_to(jnp.where(keep, 1.0, 0.0), (8, LANES))

    @pl.when(c == t)
    def _():
        kept_stay.start()
        kept_move.start()

    for name in ("key", "value"):
        ref, to = r[name + "_weight"], r["w_" + name]
        to[:256, :] = ref[:256, :]
        to[256:, :] = jnp.concatenate(
            [ref[256:channels, :].astype(F32), jnp.zeros((PAD - channels, WIDE), F32)], axis=0
        ).astype(B16)
        store(name + "_wide", to)
    for name, to in (
        ("query_weight", "w_query"),
        ("cross_out", "w_cross_out"),
        ("cross_up", "w_cross_up"),
        ("cross_down", "w_cross_down"),
    ):
        ready[to] = [here(r[name], r[to]).wait]
    ready["attend_own"] = [here(r["self_attend"].at[:, :, own_columns], r["w_attend_own"]).wait]
    ready["out_own"] = [
        here(r["self_out"].at[pl.ds(pl.multiple_of(own256, LANES), 256)], out_w.at[pl.ds(0, 256)]).wait,
        here(r["self_out"].at[pl.ds(pl.multiple_of(256 - own256, LANES), 256)], out_w.at[pl.ds(512, 256)]).wait,
    ]

    def norm_rows(value_ref, gain, out_ref, also=None):
        def step(i):
            rows = block(i, 64)
            v = value_ref[rows, :].astype(F32)
            high, _ = norm_parts(v)
            out_ref[rows, :] = (high * gain).astype(B16)

        loop(ROWS // 64, step)

    def each256(n, step):
        loop(n // 256, lambda i: step(block(i, 256)))

    query_low, queries = r["v_query_low"], r["v_queries"]

    def ask(lat_ref):
        norm_rows(lat_ref, r["norm_gains"][0:1, :], query_low)

        def query_step(columns):
            queries[:, columns] = dot(query_low[...], r["w_query"][:, columns]).astype(B16)

        each256(WIDE, query_step)

    lat_copy.wait()
    await_all("w_query")
    ask(r["v_lat_own"])
    r["v_asked_own"][...] = (dot_t(queries[...], r["w_key"][...]) * cross_scale).astype(B16)

    @pl.when(c != t)
    def _():
        asked_move.start()
        lat_move.start()

    @pl.when(c == t)
    def _():
        r["v_asked"][...] = r["v_asked_own"][...]
        r["v_lat"][...] = r["v_lat_own"][...]

    @pl.when(c != t)
    def _():
        for i in range(4):
            crossing[i].wait_recv()
            for j in range(4):
                (far_way[4 * i + j] if i or j else picture_cross).start()
        kept_move.wait_recv()
        picture_cross.wait()

    @pl.when(c == t)
    def _():
        kept_stay.wait()
        picture_stay.wait()

    spread_pieces("attend", "out", "up", "down")
    passed = []
    for k, (i, j) in enumerate(hops):
        if k > 0:
            own_way[k].wait_recv()
        arrived_at = columns_of(towards(i, j, -1))
        passed.append(remote(arrived_at, arrived_at, sib))
    for copy in passed:
        copy.wait_recv()
    spread_fours("attend")
    store("picture", picture)

    @pl.when(c != t)
    def _():
        cot_move.start()

    @pl.when(c != t)
    def _():
        asked_move.wait_recv()

    store("asked", r["v_asked"])
    scores, raised = r["v_scores"], r["v_raised"]
    r["v_top"][...] = jnp.full((ROWS, 1), -3.0e38, F32)
    r["v_total"][...] = jnp.zeros((ROWS, 1), F32)
    r["v_mixed"][...] = jnp.zeros_like(r["v_mixed"])
    r["any_kept"][...] = jnp.max(r["v_kept"][0:1, :], axis=-1, keepdims=True)

    def score_step(i):
        columns = block(i, 512)
        value = dot(r["v_asked"][...], picture[:, columns])
        value = jnp.where(r["v_kept"][0:1, columns] > 0.5, value, MASKED)
        scores[:, columns] = value
        r["v_top"][...] = jnp.maximum(r["v_top"][...], jnp.max(value, axis=-1, keepdims=True))

    loop(8, score_step)

    def raise_step(i):
        columns = block(i, 512)
        value = jnp.exp(scores[:, columns] - r["v_top"][...])
        r["v_total"][...] += jnp.sum(value, axis=-1, keepdims=True)
        value = value.astype(B16)
        raised[i] = value
        r["v_mixed"][...] += dot_t(value, picture[:, columns])

    loop(8, raise_step)
    store("raised", raised)
    inverse_total = 1.0 / r["v_total"][...]
    r["inverse_total"][...] = inverse_total
    mixed = r["v_mixed"][...] * inverse_total
    r["v_mixed"][...] = mixed
    store("mixed_f32", r["v_mixed"])
    r["v_mixed_wide"][...] = jnp.zeros_like(r["v_mixed_wide"])
    r["v_mixed_wide"][:, :PAD] = mixed
    tail = pltpu.roll(r["v_mixed_wide"][:, 256:384], 16, 1).astype(B16)
    for name, core in (("mixed_pixels", c), ("mixed_pixels_give", 1 - c)):
        ref = r["v_" + name]
        ref[:, :256] = jnp.zeros((ROWS, 256), B16)
        ref[:, 256:384] = tail
        ref[:, 384:] = r["v_mixed_wide"][:, pl.ds(pl.multiple_of(LANES * core, LANES), LANES)].astype(B16)
    share("mixed_pixels", r["v_mixed_pixels"], r["v_mixed_pixels_give"])
    await_all("w_cross_out")
    r["v_attended"][...] = dot(mixed.astype(B16), r["w_value"][...]).astype(B16)
    spread_fours("out", "up", "down")
    share("attended", r["v_attended"])

    @pl.when(c != t)
    def _():
        lat_move.wait_recv()

    store("latents_turned", r["v_lat"])

    def out_step(columns):
        r["v_after_cross"][:, columns] = r["v_lat"][:, columns].astype(F32) + dot(
            r["v_attended"][...], r["w_cross_out"][:, columns]
        )

    each256(WIDE, out_step)
    store("after_cross", r["v_after_cross"])
    norm_rows(r["v_after_cross"], r["norm_gains"][1:2, :], r["v_cross_in"])
    share("cross_in", r["v_cross_in"])
    await_all("w_cross_up", "w_cross_down")

    def up_step(columns):
        hidden = dot(r["v_cross_in"][...], r["w_cross_up"][:, columns])
        r["v_hidden"][:, columns] = hidden
        r["v_cross_act"][:, columns] = gelu(hidden).astype(B16)

    each256(WIDE, up_step)
    store("cross_hidden", r["v_hidden"])
    share("cross_act", r["v_cross_act"])

    def down_step(columns):
        r["v_after_mlp"][:, columns] = r["v_after_cross"][:, columns] + dot(
            r["v_cross_act"][...], r["w_cross_down"][:, columns]
        )

    each256(WIDE, down_step)
    store("after_mlp", r["v_after_mlp"])

    attend_in = r["v_attend_in"]
    norm_rows(r["v_after_mlp"], r["norm_gains"][2:3, :], attend_in)
    attend_copy = remote(attend_in.at[top], attend_in.at[low], sib)
    @pl.when(c != t)
    def _():
        ask(r["v_lat"])

    late = r["late_x"]
    late_keep = [here_of(src, late.at[top]) for src in (query_low, queries)]
    late_give = [remote_of(src, late.at[low], sib) for src in (queries, query_low)]

    @pl.when(c == 0)
    def _():
        late_keep[0].start()
        late_give[0].start()

    @pl.when(c == 1)
    def _():
        late_keep[1].start()
        late_give[1].start()

    await_all("attend_own")
    attend_copy.wait_recv()
    store("attend_in", attend_in)
    projected, probs = r["v_projected"], r["v_probs"]

    def project(weights, at):
        for k in range(3):
            projected[k, :, pl.ds(at, 256)] = dot(attend_in[...], weights[k]).astype(B16)

    def attend(h):
        columns = block(h, HEAD_WIDTH)
        dotted = dot_t(projected[0, :, columns], projected[1, :, columns]) * self_scale
        value = jnp.exp(dotted - jnp.max(dotted, axis=-1, keepdims=True))
        value = (value * (1.0 / jnp.sum(value, axis=-1, keepdims=True))).astype(B16)
        probs[2 * h] = value[:ROWS]
        probs[2 * h + 1] = value[ROWS:]
        r["v_self"][:, columns] = dot(value, projected[2, :, columns]).astype(B16)

    project(r["w_attend_own"], 0)
    loop(2, attend)
    gathered("attend")
    project(attend_far, 256)
    loop(2, lambda i: attend(i + 2))
    store("mixed", r["v_self"])
    self_copy = remote(r["v_self"].at[low], r["v_self_in"], sib)
    store("projected", projected)
    store("probs", probs)
    store("attend_far", attend_far)

    @pl.when(c != t)
    def _():
        cot_move.wait_recv()

    @pl.when(c == t)
    def _():
        cot_stay.wait()

    share("cot", r["v_cot"])
    gather_pieces("out")
    await_all("out_own")
    arrived("out")
    store("out_mine", out_w.at[pl.ds(0, 512)])
    self_copy.wait_recv()

    def attended_step(columns):
        r["v_after_attend"][:, columns] = (
            r["v_after_mlp"][:, columns]
            + dot(r["v_self"][top, :], out_w[pl.ds(0, 512), columns])
            + dot(r["v_self_in"][...], out_w[pl.ds(512, 512), columns])
        )

    each256(WIDE, attended_step)
    store("after_attend", r["v_after_attend"])
    gather_pieces("up", "down")
    arrived("up", "down")
    store("up_far", up_far)
    store("down_far", down_far)

    @pl.when(c != t)
    def _():
        lat_move.wait_send()
        asked_move.wait_send()
        cot_move.wait_send()
        for copy in crossing:
            copy.wait_send()

    @pl.when(c == t)
    def _():
        kept_move.wait_send()

    @pl.when(c == 0)
    def _():
        late_keep[0].wait()
        late_give[0].wait_send()
        late_give[1].wait_recv()

    @pl.when(c == 1)
    def _():
        late_keep[1].wait()
        late_give[1].wait_send()
        late_give[0].wait_recv()

    for copy in own_way[1:]:
        copy.wait_send()
    for copy in shared:
        copy.wait_recv()
    for copy in waits:
        copy.wait_send()
    for copy in stores:
        copy.wait()
    assert not ready, tuple(ready)
    assert used[0] <= sems[0] and used[1] <= sems[1], used


def front(given):
    names, scratch = [], []

    def room(name, shape, dtype=B16):
        names.append(name)
        scratch.append(pltpu.VMEM(shape, dtype))

    sems = (80, 39)
    names += list(FRONT_HBM) + list(FRONT_VMEM) + list(FRONT_OUT)
    for name in ("send", "recv", "local"):
        names.append(name)
        scratch.append(pltpu.SemaphoreType.DMA((sems[1 if name == "local" else 0],)))
    for name in ("query", "cross_out", "cross_up", "cross_down", "out"):
        room("w_" + name, (WIDE, WIDE))
    for name in ("key", "value"):
        room("w_" + name, (PAD, WIDE))
    for name in ("attend_own", "attend_far"):
        room("w_" + name, (3, WIDE, 256))
    room("w_up_far", (WIDE, 512))
    room("w_down_far", (512, WIDE))
    room("v_picture", (PAD, 4096))
    room("v_pixels", (261, 16, LANES))
    room("v_normed", (PAD * 16, LANES), F32)
    room("v_gain", (384, LANES), F32)
    room("v_home", (16, PAD, LANES))
    room("v_relay", (16, PAD, LANES))
    room("v_kept", (8, 4096), F32)
    room("v_kept_own", (8, 4096), F32)
    room("v_scores", (ROWS, 4096), F32)
    room("v_raised", (8, ROWS, 512))
    room("v_asked_own", (ROWS, PAD))
    for name in ("lat_own", "lat", "cot", "query_low", "queries", "attended", "cross_in", "cross_act"):
        room("v_" + name, (ROWS, WIDE))
    for name in ("after_cross", "hidden", "after_mlp", "after_attend"):
        room("v_" + name, (ROWS, WIDE), F32)
    room("v_attend_in", (512, WIDE))
    room("v_projected", (3, 512, 512))
    room("v_probs", (8, ROWS, 512))
    room("v_self", (512, 512))
    room("v_self_in", (ROWS, 512))
    room("v_asked", (ROWS, PAD))
    room("v_top", (ROWS, 1), F32)
    room("v_total", (ROWS, 1), F32)
    room("v_mixed", (ROWS, PAD), F32)
    room("v_mixed_wide", (ROWS, 384), F32)
    room("v_mixed_pixels", (ROWS, 512))
    room("v_mixed_pixels_give", (ROWS, 512))
    anywhere = pl.BlockSpec(memory_space=pl.ANY)
    vmem = pl.BlockSpec(memory_space=pltpu.VMEM)
    result = pl.pallas_call(
        functools.partial(front_kernel, tuple(names), sems),
        out_shape=[jax.ShapeDtypeStruct(*spec) for spec in FRONT_OUT.values()],
        in_specs=[anywhere] * len(FRONT_HBM) + [vmem] * len(FRONT_VMEM),
        out_specs=[vmem if name in FRONT_OUT_VMEM else anywhere for name in FRONT_OUT],
        scratch_shapes=scratch,
        compiler_params=pltpu.CompilerParams(collective_id=0, has_side_effects=True, vmem_limit_bytes=63 * MIB),
        name="front",
    )(*[given[name] for name in FRONT_HBM + FRONT_VMEM])
    return dict(zip(FRONT_OUT, result))


X, Z, Y = ("XA", "XB"), ("ZA", "ZB"), ("L", "O")
def rotated(k):
    order = ("XA", "ZA", "L", "XB", "ZB", "O")
    return tuple((bit,) for bit in order[k:] + order[:k])


SETS = {
    "S": (tuple(rotated(k) for k in range(6)), 32),
    "P": (tuple(rotated(k) for k in (0, 3, 1, 4)), 16),
    "Q": (tuple(rotated(k) for k in (2, 5, 0, 3)), 16),
}
BOTH = {X: "X2", Z: "Z2", Y: "T"}
BACK_HBM = (
    ("cot", "cross_act", "cross_in", "attended", "late_x", "mixed_pixels", "mixed", "attend_in", "projected", "probs")
    + ("out_mine", "attend_far", "up_far", "down_far", "after_mlp", "after_attend", "cross_hidden", "after_cross")
    + ("latents_turned", "picture", "raised", "mixed_f32", "asked", "self_attend", "self_up", "self_down")
    + ("cross_down", "cross_up", "cross_out", "query_weight", "key_wide", "value_wide")
)
BACK_VMEM = ("inverse_total", "any_kept", "norm_gains")
BACK_OUT = {
    "out_S": ((6, 64, 512), B16),
    "out_P": ((4, 32, 512), B16),
    "out_Q": ((4, 32, 512), B16),
    "home": ((16, PAD, LANES), B16),
    "latents_home": ((ROWS, WIDE), B16),
    "latgrad_home": ((ROWS, WIDE), B16),
    "out_gains": ((8, WIDE), F32),
}


def back_kernel(names, sems, *refs):
    l, c, s, t = place()
    z, x = lax.div(s, 4), lax.rem(s, 4)
    seq = 16
    r = dict(zip(names, refs))
    send, recv, local = r["send"], r["recv"], r["local"]
    cross_scale = 1.0 / math.sqrt(WIDE)
    self_scale = 1.0 / math.sqrt(HEAD_WIDTH)

    partner = {
        "XA": (2 * l + c, z * 4 + flip(x), t),
        "XB": (2 * l + c, z * 4 + 3 - x, t),
        "ZA": (2 * l + c, flip(z) * 4 + x, t),
        "ZB": (2 * l + c, (3 - z) * 4 + x, t),
        "L": (2 * (1 - l) + c, s, t),
        "O": (2 * (1 - l) + c, s, 1 - t),
        "X2": (2 * l + c, z * 4 + lax.rem(x + 2, 4), t),
        "Z2": (2 * l + c, lax.rem(z + 2, 4) * 4 + x, t),
        "T": (2 * l + c, s, 1 - t),
        "C": (2 * l + 1 - c, s, t),
        "D": (2 * (1 - l) + 1 - c, s, t),
    }

    def peer(k):
        return (2 * l + t, lax.rem(s + k, seq), c)

    barrier = pltpu.get_barrier_semaphore()
    for device in partner.values():
        pl.semaphore_signal(barrier, inc=1, device_id=device, device_id_type=MESH)
    def plane(k):
        return (2 * l + c, lax.rem(s + k, seq), t)

    for k in range(1, seq):
        pl.semaphore_signal(barrier, inc=1, device_id=plane(k), device_id_type=MESH)

    @pl.when(c != t)
    def _():
        pl.semaphore_signal(barrier, inc=1, device_id=peer(0), device_id_type=MESH)
        pl.semaphore_wait(barrier, len(partner) + seq)

    @pl.when(c == t)
    def _():
        pl.semaphore_wait(barrier, len(partner) + seq - 1)

    used = [0, 0]
    waits = []

    def remote_of(src, dst, device):
        i = used[0]
        used[0] += 1
        return pltpu.make_async_remote_copy(
            src_ref=src, dst_ref=dst, send_sem=send.at[i], recv_sem=recv.at[i], device_id=device, device_id_type=MESH
        )

    def remote(src, dst, device):
        copy = remote_of(src, dst, device)
        copy.start()
        waits.append(copy)
        return copy

    def sent(*copies):
        for copy in copies:
            copy.wait_send()
            waits[:] = [other for other in waits if other is not copy]

    def here_of(src, dst):
        i = used[1]
        used[1] += 1
        return pltpu.make_async_copy(src, dst, local.at[i])

    def here(src, dst):
        copy = here_of(src, dst)
        copy.start()
        return copy

    ready = {}

    def await_all(*wanted):
        for name in wanted:
            for wait in ready.pop(name):
                wait()

    def load(name, to, key=None):
        ready[key or name] = [here(r[name], to).wait]

    sib = partner["C"]
    top, low = pl.ds(0, ROWS), pl.ds(ROWS, ROWS)
    keep512 = pl.ds(pl.multiple_of(512 * c, LANES), 512)
    give512 = pl.ds(pl.multiple_of(512 * (1 - c), LANES), 512)
    keep256 = pl.ds(pl.multiple_of(256 * c, LANES), 256)
    give256 = pl.ds(pl.multiple_of(256 * (1 - c), LANES), 256)
    left, right = pl.ds(0, 256), pl.ds(256, 256)
    x1, x2, x3, x4, x5 = (r["x%d" % k] for k in range(1, 6))
    up_w, down_w, probs = r["w_up"], r["w_down"], r["v_probs"]

    load("after_attend", r["v_norm"])
    ready["up"] = [
        here(r["self_up"], up_w.at[:, pl.ds(0, 512)]).wait,
        here(r["up_far"], up_w.at[:, pl.ds(512, 512)]).wait,
    ]
    load("cot", x1)
    ready["down"] = [
        here(r["self_down"], down_w.at[pl.ds(0, 512)]).wait,
        here(r["down_far"], down_w.at[pl.ds(512, 512)]).wait,
    ]
    load("out_mine", r["w_out_mine"])
    load("projected", r["v_projected"])
    load("probs", probs)
    load("mixed", r["y_mixed"])
    ready["attend_own"] = [
        here(r["self_attend"].at[:, :, keep256], r["w_attend_own"]).wait
    ]
    load("attend_far", r["w_attend_far"])
    load("attend_in", x4)
    load("cross_hidden", r["v_hidden"])
    load("value_wide", r["w_value"])
    load("key_wide", r["w_key"])
    load("picture", r["v_picture"])
    load("mixed_f32", r["v_mixed"])
    load("asked", r["v_asked"])
    load("mixed_pixels", r["y_mixed_pixels"])

    missing, ends = {set_: len(SETS[set_][0]) for set_ in SETS}, []

    class Part:
        def __init__(self, set_, q):
            self.stages, self.depth = SETS[set_][0][q], SETS[set_][1]
            self.set, self.q, self.stage, self.n = set_, q, -1, 64
            self.key = "%s%d_" % (set_, q)
            self.cur = r[self.key + "buf"]
            order = [bit for stage in self.stages for bit in stage]
            self.weight = {bit: 32 >> k for k, bit in enumerate(order)}
            self.done = False

        def index(self, **bits):
            return sum(value * self.weight[bit] for bit, value in bits.items())

        def begin(self):
            self.stage += 1
            k, n = self.stage, self.n
            if k < len(self.stages):
                bits = self.stages[k]
                self.into = r[self.key + "in%d" % k]
                if len(bits) == 1:
                    ways = bits
                else:
                    ways = (bits[1], bits[0], BOTH[bits])
                m = n // (len(ways) + 1)
                self.n = m
                self.copies = [
                    remote(self.cur.at[pl.ds((j + 1) * m, m)], self.into.at[j], partner[way])
                    for j, way in enumerate(ways)
                ]
                return
            r["fin_" + self.set][self.q] = self.cur[0]
            self.done = True
            missing[self.set] -= 1
            if not missing[self.set]:
                src = r["fin_" + self.set]
                dst = r["out_" + self.set].at[
                    :,
                    pl.ds(pl.multiple_of(l * self.depth, self.depth), self.depth),
                    pl.ds(pl.multiple_of(c * 256, LANES), 256),
                ]
                ends.extend(remote(src, dst, partner[way]).wait_recv for way in ("L", "C", "D"))
                ends.append(here(src, dst).wait)

        def finish(self):
            for copy in self.copies:
                copy.wait_recv()
            cur, into, ways = self.cur, self.into, len(self.copies)
            m = min(self.n, 4)

            def step(i):
                rows = pl.ds(i * m, m)
                total = cur[rows].astype(F32)
                for j in range(ways):
                    total = total + into[j, rows].astype(F32)
                cur[rows] = total.astype(B16)

            if self.n > m:
                loop(self.n // m, step)
            else:
                step(0)

        def advance(self):
            if self.done:
                return
            self.finish()
            if not self.done:
                self.begin()

    parts = {(set_, q): Part(set_, q) for set_ in SETS for q in range(len(SETS[set_][0]))}

    def advance(set_, *some):
        for q in some or range(len(SETS[set_][0])):
            parts[set_, q].advance()

    def product(x_ref, y_ref, width, pieces, add=False):
        span = 512 if width <= 512 else 256
        per = span // 256

        def step(i):
            columns = block(i, span)
            whole = tdot(x_ref[:, columns], y_ref[...])
            for a in range(per):
                zz = i * per + a
                zb = lax.rem(lax.div(z, 2) + lax.div(zz, 2), 2)
                za = lax.rem(lax.rem(z, 2) + lax.rem(zz, 2) + zb, 2)
                for xx in range(4):
                    xb = lax.rem(lax.div(x, 2) + xx // 2, 2)
                    xa = lax.rem(lax.rem(x, 2) + xx % 2 + xb, 2)
                    at = (a * 4 + xx) * 64
                    for part, src, width_, half in pieces:
                        for k in range(64 // part.depth):
                            ll = k % 2
                            o = half if half is not None else lax.rem(k // 2 + t, 2)
                            idx = part.index(ZA=za, ZB=zb, XA=xa, XB=xb, O=o, L=lax.rem(ll + l + o, 2))
                            value = whole[at + k * part.depth : at + (k + 1) * part.depth, src : src + width_]
                            to = pl.ds(0, width_)
                            if add:
                                value = value + part.cur[idx, :, to].astype(F32)
                            part.cur[idx, :, to] = value.astype(B16)

        loop(WIDE // span, step)

    def heads(q, at=0):
        return [("S", q, at, 0), ("S", q, at + 256, 1)]

    def product_heads(x_ref, y_ref, width, wanted):
        product(x_ref, y_ref, width, [(parts["S", q], at, 256, half) for _, q, at, half in wanted])

    def product_rows(x_ref, y_ref, width, set_, q, add=False):
        pieces, at = [], 0
        while at < width:
            n = min(256, width - at)
            pieces.append((parts[set_, q + at // 256], at, n, None))
            at += n
        product(x_ref, y_ref, width, pieces, add)

    r["gains"][...] = jnp.zeros_like(r["gains"])

    def norm_grad(value_ref, gain, slot, after):
        def step(i):
            rows = block(i, 64)
            high, inverse = norm_parts(value_ref[rows, :].astype(F32))
            e = r["v_tmp"][rows, :]
            a = e * gain
            back = (
                a - jnp.mean(a, axis=-1, keepdims=True) - high * jnp.mean(a * high, axis=-1, keepdims=True)
            ) * inverse
            r["gains"][pl.ds(slot, 1), :] += jnp.sum(e * high, axis=0, keepdims=True)
            after(rows, back)

        loop(ROWS // 64, step)

    def add_grad(low_ref):
        def after(rows, back):
            total = r["v_grad"][rows, :] + back
            r["v_grad"][rows, :] = total
            low_ref[rows, :] = total.astype(B16)

        return after

    def pull(a_ref, w_ref, store):
        def step(i):
            rows = block(i, 256)
            store(rows, dot_t(a_ref[...], w_ref[rows, :]))

        loop(w_ref.shape[0] // 256, step)

    def to_tmp(columns, value):
        r["v_tmp"][:, columns] = value

    def halves(name, src, to):
        copy = remote(src.at[:, give512], to.at[low], sib)
        ready[name] = [here(src.at[:, keep512], to.at[top]).wait, copy.wait_recv]
        return copy

    await_all("after_attend")

    def feed_norm(i):
        rows = block(i, 64)
        high, _ = norm_parts(r["v_norm"][rows, :])
        x2[rows, :] = (high * r["norm_gains"][3:4, :]).astype(B16)

    loop(ROWS // 64, feed_norm)
    feed_in_copy = remote(x2.at[top], x2.at[low], sib)
    await_all("up", "cot", "down")

    def feed_step(i):
        columns = block(i, 256)
        hidden = dot(x2[top, :], up_w[:, columns])
        r["v_feed_act"][:, columns] = gelu(hidden).astype(B16)
        pulled = dot_t(x1[top, :], down_w[columns, :])
        r["v_feed_back"][:, columns] = (gelu_slope(hidden) * pulled).astype(B16)

    loop(4, feed_step)
    quarter_sends = []
    for name in ("feed_act", "feed_back"):
        ref, to = r["v_" + name], r["y_" + name]
        quarter_sends += [
            remote(ref.at[:, give256], to.at[low, left], sib),
            remote(ref.at[:, pl.ds(768, 256)], to.at[low, right], sib),
        ]
        ready["y_" + name] = [
            here(ref.at[:, keep256], to.at[top, left]).wait,
            here(ref.at[:, pl.ds(512, 256)], to.at[top, right]).wait,
        ] + [copy.wait_recv for copy in quarter_sends[-2:]]
    pull(r["v_feed_back"], up_w, to_tmp)

    def feed_after(rows, back):
        total = x1[rows, :].astype(F32) + back
        r["v_grad"][rows, :] = total
        x3[rows, :] = total.astype(B16)

    norm_grad(r["v_norm"], r["norm_gains"][3:4, :], 3, feed_after)
    branch_copy = remote(x3.at[top], x3.at[low], sib)
    load("cross_up", up_w, "cross_up")

    def latents_step(i):
        columns = block(i, 256)
        r["v_latents_out"][:, columns] = (
            r["v_norm"][:, columns] + dot(r["v_feed_act"][...], down_w[:, columns])
        ).astype(B16)

    loop(4, latents_step)
    load("cross_down", down_w, "cross_down")
    load("after_mlp", r["v_norm"], "after_mlp")
    out_move, out_stay = remote_of(r["v_latents_out"], r["latents_home"], peer(0)), here_of(r["v_latents_out"], r["latents_home"])

    @pl.when(c != t)
    def _():
        out_move.start()

    @pl.when(c == t)
    def _():
        out_stay.start()

    await_all("y_feed_act")
    product_heads(x1, r["y_feed_act"], 512, heads(0))
    parts["S", 0].begin()
    load("cross_act", x1, "x_cross_act")
    feed_in_copy.wait_recv()
    await_all("y_feed_back")
    product_heads(x2, r["y_feed_back"], 512, heads(1))
    parts["S", 1].begin()
    sent(feed_in_copy)
    load("late_x", x2, "x_late_x")

    branch_copy.wait_recv()
    await_all("out_mine", "projected", "probs", "mixed")

    def mixed_step(columns, value):
        r["v_self_grad"][:, columns] = value.astype(B16)

    pull(x3, r["w_out_mine"], mixed_step)
    product_heads(x3, r["y_mixed"], 512, heads(2))
    parts["S", 2].begin()
    sent(branch_copy)
    load("cross_in", x3, "x_cross_in")
    projected, y_back = r["v_projected"], r["y_back"]

    def attend_back(h):
        columns = block(h, HEAD_WIDTH)
        query, key, value = (projected[k, :, columns] for k in range(3))
        key_sum = value_sum = 0
        for j in range(2):
            rows = pl.ds(ROWS * j, ROWS)
            grad = r["v_self_grad"][rows, columns]
            p = probs[2 * h + j]
            g = dot_t(grad, value)
            p32 = p.astype(F32)
            change = (p32 * (g - jnp.sum(p32 * g, axis=-1, keepdims=True))).astype(B16)
            y_back[rows, columns] = (dot(change, key) * self_scale).astype(B16)
            key_sum = key_sum + tdot(change, projected[0, rows, columns])
            value_sum = value_sum + tdot(p, grad)
        y_back[:, pl.ds(pl.multiple_of(512 + h * HEAD_WIDTH, LANES), HEAD_WIDTH)] = (key_sum * self_scale).astype(B16)
        y_back[:, pl.ds(pl.multiple_of(1024 + h * HEAD_WIDTH, LANES), HEAD_WIDTH)] = value_sum.astype(B16)

    loop(4, attend_back)
    load("raised", probs)
    await_all("attend_own", "attend_far")

    def rows_step(i):
        rows = block(i, 256)
        total = 0
        for k in range(3):
            total = total + dot_t(y_back[:, pl.ds(512 * k, 256)], r["w_attend_own"][k, rows, :])
            total = total + dot_t(y_back[:, pl.ds(512 * k + 256, 256)], r["w_attend_far"][k, rows, :])
        r["v_tmp"][:, rows] = total[:ROWS]
        r["v_rows_give"][:, rows] = total[ROWS:].astype(B16)

    loop(4, rows_step)
    rows_copy = remote(r["v_rows_give"], r["v_rows_in"], sib)
    await_all("attend_in")
    product_heads(x4, y_back, 1536, [piece for k in range(3) for piece in heads(3 + k, 512 * k)])
    for q in (3, 4, 5):
        parts["S", q].begin()
    load("attended", x4, "x_attended")
    rows_copy.wait_recv()

    def sum_step(i):
        rows = block(i, 64)
        r["v_tmp"][rows, :] += r["v_rows_in"][rows, :].astype(F32)

    loop(ROWS // 64, sum_step)
    await_all("after_mlp")
    mlp_branch, cross_branch = r["v_branch"], r["v_rows_give"]
    norm_grad(r["v_norm"], r["norm_gains"][2:3, :], 2, add_grad(mlp_branch))
    load("after_cross", r["v_norm"], "after_cross")

    halves("y_mlp", mlp_branch, r["y_mlp"])
    await_all("cross_down", "cross_hidden")

    def hidden_store(columns, value):
        r["v_back"][:, columns] = (gelu_slope(r["v_hidden"][:, columns]) * value).astype(B16)

    pull(mlp_branch, down_w, hidden_store)
    load("cross_out", down_w, "cross_out")
    halves("y_hidden", r["v_back"], r["y_hidden"])
    await_all("cross_up")
    pull(r["v_back"], up_w, to_tmp)
    load("query_weight", up_w, "query_weight")
    advance("S", 0, 1)
    sent(rows_copy)
    await_all("after_cross")
    norm_grad(r["v_norm"], r["norm_gains"][1:2, :], 1, add_grad(cross_branch))
    halves("y_out", cross_branch, r["y_out"])
    await_all("cross_out")

    def attended_store(columns, value):
        x5[top, columns] = value.astype(B16)

    pull(cross_branch, down_w, attended_store)
    attended_copy = remote(x5.at[top], x5.at[low], sib)
    await_all("x_cross_act", "y_mlp")
    product_rows(x1, r["y_mlp"], 512, "P", 0)
    parts["P", 0].begin()
    parts["P", 1].begin()
    await_all("x_cross_in", "y_hidden")
    product_rows(x3, r["y_hidden"], 512, "P", 2)
    parts["P", 2].begin()
    parts["P", 3].begin()
    advance("S", 2)

    await_all("value_wide", "mixed_f32", "asked", "picture", "raised")
    pull_low = dot_t(x5[top, :], r["w_value"][...]).astype(B16)
    r["v_pull"][...] = pull_low
    pull_f32 = pull_low.astype(F32)
    r["v_dot"][...] = jnp.sum(pull_f32 * r["v_mixed"][...], axis=-1, keepdims=True)
    scale_any = r["inverse_total"][...] * r["any_kept"][...]
    r["v_asked_t"][...] = (r["v_asked"][...].astype(F32) * scale_any).T.astype(B16)
    r["v_pull_t"][...] = (pull_f32 * r["inverse_total"][...]).T.astype(B16)
    r["v_sum"][...] = jnp.zeros_like(r["v_sum"])

    def pixel_chunk(i, to, at):
        picture, raised = r["v_picture"][:, block(i, 512)], probs[i]
        change = (raised.astype(F32) * (dot(r["v_pull"][...], picture) - r["v_dot"][...])).astype(B16)
        r["v_sum"][...] += dot_t(change, picture)
        grad = (dot(r["v_asked_t"][...], change) + dot(r["v_pull_t"][...], raised)).astype(B16)
        for j in range(4):
            to[4 * at + j] = grad[:, j * LANES : (j + 1) * LANES]

    loop(4, lambda i: pixel_chunk((1 - c) * 4 + i, r["grad_far"], i))
    grad_copy = remote(r["grad_far"], r["grad_in"], sib)
    loop(4, lambda i: pixel_chunk(c * 4 + i, r["grad_own"], i))

    turned_sum = r["v_sum"][...] * scale_any
    r["y_late_own"][...] = jnp.zeros_like(r["y_late_own"])
    r["y_late_own"][:, :PAD] = (turned_sum * cross_scale).astype(B16)
    ready["y_late"] = [
        here(r["y_late_own"], r["y_late"].at[top]).wait,
        remote(r["y_late_own"], r["y_late"].at[low], sib).wait_recv,
    ]
    r["gains"][4:5, :PAD] = jnp.sum(
        r["v_asked"][...].astype(F32) * turned_sum + pull_f32 * r["v_mixed"][...], axis=0, keepdims=True
    )


    grad_copy.wait_recv()

    def grad_step(i):
        r["grad_own"][i] = (r["grad_own"][i].astype(F32) + r["grad_in"][i].astype(F32)).astype(B16)

    loop(seq, grad_step)

    hops = [(i, j) for i in range(4) for j in range(4)]

    def towards(i, j):
        return 4 * lax.rem(z + i, 4) + lax.rem(x + j, 4)

    def home_of(i, j, ref, sem):
        to = towards(i, j)
        return pltpu.make_async_remote_copy(
            src_ref=ref.at[to],
            dst_ref=r["home"].at[s],
            send_sem=send.at[sem],
            recv_sem=recv.at[sem],
            device_id=(2 * l + c, to, t),
            device_id_type=MESH,
        )

    first_sem = used[0]
    used[0] += len(hops)
    own_way = [home_of(i, j, r["grad_own"], first_sem + k) if k else None for k, (i, j) in enumerate(hops)]
    far_way = [home_of(i, j, r["grad_relay"], first_sem + k) if k else None for k, (i, j) in enumerate(hops)]

    def group(i):
        return block(lax.rem(z + i, 4), 4)

    crossing = [remote_of(r["grad_own"].at[group(i)], r["grad_relay"].at[group(i)], peer(0)) for i in range(4)]
    stay, stay_far = here_of(r["grad_own"].at[s], r["home"].at[s]), here_of(r["grad_relay"].at[s], r["home"].at[s])

    @pl.when(c != t)
    def _():
        for copy in crossing:
            copy.start()

    @pl.when(c == t)
    def _():
        stay.start()
        for copy in own_way[1:]:
            copy.start()

    await_all("x_attended", "y_out")
    product_rows(x4, r["y_out"], 512, "Q", 0)
    parts["Q", 0].begin()
    parts["Q", 1].begin()
    attended_copy.wait_recv()
    await_all("mixed_pixels")
    product_rows(x5, r["y_mixed_pixels"], 512, "Q", 2)
    await_all("x_late_x", "y_late")
    product_rows(x2, r["y_late"], 384, "Q", 2, add=True)
    parts["Q", 2].begin()
    parts["Q", 3].begin()
    advance("S", 3, 4, 5)
    advance("S", 0, 1, 2)
    advance("P")

    @pl.when(c != t)
    def _():
        for i in range(4):
            crossing[i].wait_recv()
            for j in range(4):
                (far_way[4 * i + j] if i or j else stay_far).start()

    sent(*quarter_sends)
    latents, latgrad = r["v_feed_act"], r["v_feed_back"]
    load("latents_turned", latents)
    await_all("key_wide", "query_weight", "latents_turned")
    r["v_rows_in"][...] = dot(r["y_late_own"][:, :PAD], r["w_key"][...]).astype(B16)
    pull(r["v_rows_in"], up_w, to_tmp)

    def latents_after(rows, back):
        latgrad[rows, :] = (r["v_grad"][rows, :] + back).astype(B16)

    norm_grad(latents, r["norm_gains"][0:1, :], 0, latents_after)
    grad_move, grad_stay = remote_of(latgrad, r["latgrad_home"], peer(0)), here_of(latgrad, r["latgrad_home"])

    @pl.when(c != t)
    def _():
        grad_move.start()

    @pl.when(c == t)
    def _():
        grad_stay.start()

    gain_buf, gain_in = r["gain_buf"], r["gain_in"]
    gain_stages = [tuple(bits) + (BOTH[bits],) for bits in (X, Z, Y)] + [("C",)]
    gain_buf[0] = r["gains"][...]

    def send_gains(k):
        return [remote(gain_buf.at[k], gain_in.at[k, j], partner[way]) for j, way in enumerate(gain_stages[k])]

    gain_copies = send_gains(0)
    live = [parts[key] for key in parts]
    k = 0
    while live or k < 4:
        if k < 4:
            for copy in gain_copies:
                copy.wait_recv()
            total = gain_buf[k] + gain_in[k, 0]
            if k < 3:
                total = total + (gain_in[k, 1] + gain_in[k, 2])
            k += 1
            if k < 4:
                gain_buf[k] = total
                gain_copies = send_gains(k)
            else:
                r["out_gains"][...] = total
        for part in live:
            part.advance()
        live = [part for part in live if not part.done]
    for wait in ends:
        wait()

    @pl.when(c != t)
    def _():
        out_move.wait()
        grad_move.wait()
        stay_far.wait()
        for copy in crossing:
            copy.wait_send()

    @pl.when(c == t)
    def _():
        out_stay.wait()
        grad_stay.wait()
        stay.wait()

    for copy in own_way[1:]:
        copy.wait()
    for copy in waits:
        copy.wait_send()
    assert not ready, tuple(ready)
    assert used[0] <= sems[0] and used[1] <= sems[1], used


def back_and_reduce(given):
    names, scratch = [], []

    def room(name, shape, dtype=B16):
        names.append(name)
        scratch.append(pltpu.VMEM(shape, dtype))

    sems = (177, 47)
    names += list(BACK_HBM) + list(BACK_VMEM) + list(BACK_OUT)
    for name in ("send", "recv", "local"):
        names.append(name)
        scratch.append(pltpu.SemaphoreType.DMA((sems[1 if name == "local" else 0],)))
    for k in range(1, 6):
        room("x%d" % k, (512, WIDE))
    for name in ("feed_act", "feed_back", "mixed", "mixed_pixels", "mlp", "hidden", "out"):
        room("y_" + name, (512, 512))
    room("y_back", (512, 1536))
    room("y_late", (512, 384))
    room("y_late_own", (ROWS, 384))
    for name in ("w_down", "w_up"):
        room(name, (WIDE, WIDE))
    room("w_out_mine", (512, WIDE))
    for name in ("w_attend_own", "w_attend_far"):
        room(name, (3, WIDE, 256))
    for name in ("w_key", "w_value"):
        room(name, (PAD, WIDE))
    for name in ("v_tmp", "v_norm", "v_grad", "v_hidden"):
        room(name, (ROWS, WIDE), F32)
    for name in ("rows_in", "rows_give", "branch", "back", "feed_act", "feed_back", "latents_out"):
        room("v_" + name, (ROWS, WIDE))
    room("v_projected", (3, 512, 512))
    room("v_probs", (8, ROWS, 512))
    room("v_self_grad", (512, 512))
    room("v_picture", (PAD, 4096))
    room("v_mixed", (ROWS, PAD), F32)
    room("v_sum", (ROWS, PAD), F32)
    room("v_asked", (ROWS, PAD))
    room("v_pull", (ROWS, PAD))
    room("v_asked_t", (PAD, ROWS))
    room("v_pull_t", (PAD, ROWS))
    room("v_dot", (ROWS, 1), F32)
    for name in ("grad_own", "grad_far", "grad_in", "grad_relay"):
        room(name, (16, PAD, LANES))
    room("gains", (8, WIDE), F32)
    room("gain_buf", (4, 8, WIDE), F32)
    room("gain_in", (4, 3, 8, WIDE), F32)
    for set_, (plans, depth) in SETS.items():
        room("fin_" + set_, (len(plans), depth, 256))
        for q, stages in enumerate(plans):
            key, n = "%s%d_" % (set_, q), 64
            room(key + "buf", (n, depth, 256))
            for k, bits in enumerate(stages):
                n >>= len(bits)
                room(key + "in%d" % k, (2 ** len(bits) - 1, n, depth, 256))
    anywhere = pl.BlockSpec(memory_space=pl.ANY)
    vmem = pl.BlockSpec(memory_space=pltpu.VMEM)
    result = pl.pallas_call(
        functools.partial(back_kernel, tuple(names), sems),
        out_shape=[jax.ShapeDtypeStruct(*spec) for spec in BACK_OUT.values()],
        in_specs=[anywhere] * len(BACK_HBM) + [vmem] * len(BACK_VMEM),
        out_specs=[anywhere] * (len(BACK_OUT) - 1) + [vmem],
        scratch_shapes=scratch,
        compiler_params=pltpu.CompilerParams(collective_id=1, has_side_effects=True, vmem_limit_bytes=63 * MIB),
        name="back_and_reduce",
    )(*[given[name] for name in BACK_HBM + BACK_VMEM])
    return dict(zip(BACK_OUT, result))


FINISH_IN = ("pixels", "home", "out_S", "out_P", "out_Q", "latgrad_home", "latents_home", "key_wide")
FINISH_OUT = ("pixels_grad", "latents_grad", "latents_out")


def finish_kernel(*refs):
    refs = list(refs)

    def take(n):
        part = refs[:n]
        del refs[:n]
        return part

    hbm = dict(zip(FINISH_IN, take(len(FINISH_IN))))
    gain, gains = take(2)
    results = dict(zip(FINISH_OUT, take(len(FINISH_OUT))))
    gain_rows = take(4)
    pixelgain, query_grad, key_grad, value_grad, crossout, crossup, crossdown = take(7)
    selfattend, selfout, selfup, selfdown = take(4)
    vmem = dict(zip(FINISH_IN, take(len(FINISH_IN))))
    turned, high, grad, latgrad, wide_gain, sems = take(6)
    pixels, home = vmem["pixels"], vmem["home"]
    channels = pixels.shape[0]

    copies = {
        name: pltpu.make_async_copy(hbm[name], vmem[name], sems.at[k])
        for k, name in enumerate(FINISH_IN)
    }
    last = len(FINISH_IN)
    straight = pltpu.make_async_copy(vmem["latents_home"], results["latents_out"], sems.at[last])
    for copy in copies.values():
        copy.start()

    some = 29

    def features(i):
        return pl.ds(i * some, some)

    steps = channels // some
    per_feature(gain, wide_gain)
    copies["pixels"].wait()
    zeros = jnp.zeros(pixels.shape[1:], F32)
    average = lax.fori_loop(
        0, steps, lambda i, total: total + jnp.sum(pixels[features(i)].astype(F32), axis=0), zeros
    ) * (1.0 / channels)

    def square_step(i, total):
        centered = pixels[features(i)].astype(F32) - average
        return total + jnp.sum(centered * centered, axis=0)

    inverse = lax.rsqrt(lax.fori_loop(0, steps, square_step, zeros) * (1.0 / channels) + EPS)
    copies["home"].wait()
    for image in range(16):
        turned[pl.ds(image, PAD, stride=16), :] = home[image].astype(F32)

    def mean_step(i, totals):
        h = (pixels[features(i)].astype(F32) - average) * inverse
        rows = pl.ds(pl.multiple_of(i * (some * 16), 16), some * 16)
        a = turned[rows, :].reshape(some, 16, LANES) * wide_gain[features(i), :][:, None, :]
        high[features(i)] = h
        grad[features(i)] = a
        return totals[0] + jnp.sum(a, axis=0), totals[1] + jnp.sum(a * h, axis=0)

    first, second = lax.fori_loop(0, steps, mean_step, (zeros, zeros))
    first, second = first * (1.0 / channels), second * (1.0 / channels)

    def grad_step(i):
        grad[features(i)] = (grad[features(i)] - first - high[features(i)] * second) * inverse

    loop(steps, grad_step)
    pixels_out = pltpu.make_async_copy(grad, results["pixels_grad"], sems.at[last + 1])
    pixels_out.start()
    copies["latents_home"].wait()
    straight.start()
    copies["latgrad_home"].wait()
    latgrad[...] = vmem["latgrad_home"][...].astype(F32)
    latents_out = pltpu.make_async_copy(latgrad, results["latents_grad"], sems.at[last + 2])
    latents_out.start()

    for name in ("out_S", "out_P", "out_Q", "key_wide"):
        copies[name].wait()
    out_s, out_p, out_q = vmem["out_S"], vmem["out_P"], vmem["out_Q"]
    late = [[out_q[2 + k, :, pl.ds(256 * core, 256)] for k in range(2)] for core in range(2)]
    key_wide = vmem["key_wide"]
    query_grad[...] = dot(late[0][0], key_wide[:256, :]) + dot(late[0][1][:, :16], key_wide[256:, :])
    key_grad[:, : 2 * LANES] = late[1][0].astype(F32)
    key_grad[:, 2 * LANES :] = late[1][1].astype(F32)[:, : channels - 2 * LANES]
    value_grad[:, :LANES] = late[0][1][:, LANES:].astype(F32)
    value_grad[:, LANES : 2 * LANES] = late[1][1][:, LANES:].astype(F32)
    value_grad[:, 2 * LANES :] = late[0][1].astype(F32)[:, 16 : 16 + channels - 2 * LANES]
    for ref, out, first in ((crossdown, out_p, 0), (crossup, out_p, 2), (crossout, out_q, 0)):
        for core in range(2):
            for k in range(2):
                ref[:, pl.ds(512 * core + 256 * k, 256)] = out[first + k, :, pl.ds(256 * core, 256)].astype(F32)
    selfdown[...] = out_s[0].astype(F32)
    selfup[...] = out_s[1].astype(F32)
    selfout[...] = out_s[2].astype(F32)
    for k in range(3):
        selfattend[k] = out_s[3 + k].astype(F32)

    mine = 2 * lax.axis_index("seq") + lax.axis_index("tensor")
    rolled = pltpu.roll(gains[...], lax.rem(WIDE - 32 * mine, WIDE), 1)
    for k, ref in enumerate(gain_rows):
        ref[...] = rolled[k : k + 1, :32].reshape(32)
    pixelgain[...] = (gains[4:5, :channels] / row_of(gain)).reshape(channels)
    straight.wait()
    pixels_out.wait()
    latents_out.wait()


def finish(given):
    pixels = given["pixels"]
    channels, images, rows = pixels.shape
    small = [(32,)] * 4 + [
        (channels,),
        (32, WIDE),
        (32, channels),
        (32, channels),
        (32, WIDE),
        (32, WIDE),
        (32, WIDE),
        (3, 64, 512),
        (64, 512),
        (64, 512),
        (64, 512),
    ]
    anywhere = pl.BlockSpec(memory_space=pl.ANY)
    vmem = pl.BlockSpec(memory_space=pltpu.VMEM)
    return pl.pallas_call(
        finish_kernel,
        out_shape=[
            jax.ShapeDtypeStruct(pixels.shape, F32),
            jax.ShapeDtypeStruct((ROWS, WIDE), F32),
            jax.ShapeDtypeStruct((ROWS, WIDE), B16),
        ]
        + [jax.ShapeDtypeStruct(shape, F32) for shape in small],
        in_specs=[anywhere] * len(FINISH_IN) + [vmem] * 2,
        out_specs=[anywhere] * 3 + [vmem] * len(small),
        scratch_shapes=[pltpu.VMEM(given[name].shape, given[name].dtype) for name in FINISH_IN]
        + [
            pltpu.VMEM((PAD * images, rows), F32),
            pltpu.VMEM(pixels.shape, F32),
            pltpu.VMEM(pixels.shape, F32),
            pltpu.VMEM((ROWS, WIDE), F32),
            pltpu.VMEM((384, LANES), F32),
            pltpu.SemaphoreType.DMA((len(FINISH_IN) + 3,)),
        ],
        compiler_params=pltpu.CompilerParams(vmem_limit_bytes=60 * MIB),
        name="finish",
    )(*[given[name] for name in FINISH_IN], given["pixel_gain"], given["out_gains"])


def shards(
    latents,
    pixels,
    crop_bounds,
    key_mask,
    query_gain,
    pixel_gain,
    cross_gain,
    attend_gain,
    feed_gain,
    query_weight,
    key_weight,
    value_weight,
    cross_out,
    cross_up,
    cross_down,
    self_attend,
    self_out,
    self_up,
    self_down,
    cotangent,
):
    channels = pixels.shape[2]
    given = {
        "pixels": jnp.transpose(pixels, (2, 0, 1)),
        "latents": latents[0],
        "cotangent": cotangent[0],
        "query_weight": query_weight,
        "key_weight": key_weight,
        "value_weight": value_weight,
        "cross_out": cross_out,
        "cross_up": cross_up,
        "cross_down": cross_down,
        "self_attend": self_attend,
        "self_out": self_out,
        "self_up": self_up,
        "self_down": self_down,
        "query_gain": query_gain,
        "cross_gain": cross_gain,
        "attend_gain": attend_gain,
        "feed_gain": feed_gain,
        "pixel_gain": pixel_gain,
        "key_mask": key_mask,
        "crop_bounds": crop_bounds,
    }
    given |= front(given)
    given |= back_and_reduce(given)
    (
        pixels_grad,
        latents_grad,
        latents_out,
        querygain,
        crossgain,
        attendgain,
        feedgain,
        pixelgain,
        queryweight_grad,
        keyweight_grad,
        valueweight_grad,
        crossout_grad,
        crossup_grad,
        crossdown_grad,
        selfattend_grad,
        selfout_grad,
        selfup_grad,
        selfdown_grad,
    ) = finish(given)
    return (
        latents_out[None],
        latents_grad[None],
        jnp.transpose(pixels_grad, (1, 2, 0)),
        querygain,
        pixelgain,
        crossgain,
        attendgain,
        feedgain,
        queryweight_grad,
        keyweight_grad.T,
        valueweight_grad.T,
        crossout_grad,
        crossup_grad,
        crossdown_grad,
        selfattend_grad,
        selfout_grad.T,
        selfup_grad,
        selfdown_grad.T,
    )


def solution(mesh):
    in_specs = (
        P(("batch", "seq"), "tensor", None),
        P("batch", ("seq", "tensor"), None),
        P(("batch", "seq"), None),
        P(("batch", "seq"), None),
        P(),
        P(),
        P(),
        P(),
        P(),
        P(),
        P(),
        P(),
        P(),
        P(),
        P(),
        P(None, None, "tensor"),
        P("tensor", None),
        P(None, "tensor"),
        P("tensor", None),
        P(("batch", "seq"), "tensor", None),
    )
    out_specs = (
        P(("batch", "seq"), "tensor", None),
        P(("batch", "seq"), "tensor", None),
        P("batch", ("seq", "tensor"), None),
        P(("seq", "tensor")),
        P(),
        P(("seq", "tensor")),
        P(("seq", "tensor")),
        P(("seq", "tensor")),
        P(("seq", "tensor"), None),
        P(None, ("seq", "tensor")),
        P(None, ("seq", "tensor")),
        P(("seq", "tensor"), None),
        P(("seq", "tensor"), None),
        P(("seq", "tensor"), None),
        P(None, "seq", "tensor"),
        P("tensor", "seq"),
        P("seq", "tensor"),
        P("tensor", "seq"),
    )
    return jax.shard_map(shards, mesh=mesh, in_specs=in_specs, out_specs=out_specs, check_vma=False)
```
